32 devices in a mesh: tower: 2 (over core), batch: 16 (over z, y, x).
Axes of the slice: x: 2, y: 2, z: 4, core: 2. Of those that a mesh axis runs over, the one named last changes fastest.
Arguments:
- root_state: bfloat16 [4096, 256], P('batch', 'tower'), may hold values from -6 to 6
- cond_table: bfloat16 [36, 256], replicated, may hold values from -6 to 6
- block_gain: bfloat16 [2, 3, 256], P('tower'), may hold values from 0.25 to 1.75
- w_in: bfloat16 [2, 3, 256, 256], P('tower'), may hold values from -0.375 to 0.375
- w_out: bfloat16 [2, 3, 256, 256], P('tower'), may hold values from -0.375 to 0.375
- value_head: bfloat16 [2, 256, 601], P('tower'), may hold values from -0.75 to 0.75
- reward_head: bfloat16 [256, 601], replicated, may hold values from -0.75 to 0.75
- small_head: bfloat16 [256, 36], replicated, may hold values from -0.75 to 0.75
- unroll_len: int32 [4096], P('batch'), may hold values from 5 to 10, as said below
- actions: int32 [10, 4096], P(None, 'batch'), may hold values from 0 to 3
- codes: int32 [10, 4096], P(None, 'batch'), may hold values from 0 to 31
- policy_target: int32 [10, 4096], P(None, 'batch'), may hold values from 0 to 3
- value_bins: int32 [2, 10, 4096], P(None, None, 'batch'), may hold values from 0 to 600
- reward_bins: int32 [10, 4096], P(None, 'batch'), may hold values from 0 to 600
Outputs:
- latents: bfloat16 [2, 10, 4096, 256], P('tower', None, 'batch')
- value_logits: bfloat16 [2, 10, 4096, 601], P('tower', None, 'batch')
- row_loss: float32 [4096], P('batch')
- layer_rms: float32 [2, 10, 3, 2], P('tower')
- grad_root: float32 [4096, 256], P('batch', 'tower')
- grad_cond: float32 [36, 256], replicated
- grad_gain: float32 [2, 3, 256], P('tower')
- grad_w_in: float32 [2, 3, 256, 256], P('tower')
- grad_w_out: float32 [2, 3, 256, 256], P('tower')
- grad_value_head: float32 [2, 256, 601], P('tower')
- grad_reward_head: float32 [256, 601], replicated
- grad_small_head: float32 [256, 36], replicated
The draws below stay inside these ranges and needn't reach their ends.
Inputs may be any that keep to these rules, and one draw needn't show every extreme that they name: `unroll_len`: each position unrolls either 10 or 5 steps.
All inputs are finite; a program needn't handle non-finite values.
Results may differ from the reference program's by a relative error of at most 0.013.
Values may be sent and summed in bfloat16 or wider, within the bound.
No kernel may reach another device: no remote copies, remote signals or barrier semaphores. Data moves between devices by JAX's collectives and lax.ppermute only.
A program may use at most 64 MiB of HBM per device.

```python
from functools import partial
import jax
import jax.numpy as jnp
from jax import lax

D = 256
BINS = 601
ACTIONS = 4
CODES = 32
BLOCKS = 3
UNROLL = 10
B_DEV = 256
POSITIONS = 4096
N_BATCH = 16


def draw_unroll_len(key, part):
    key = jax.random.fold_in(key, 7)
    position = jnp.arange(POSITIONS)
    coin_draw = jax.random.randint(key, (POSITIONS,), 0, POSITIONS)
    longer = (coin_draw < position) | (position == POSITIONS - 1)
    return jnp.where(longer, UNROLL, UNROLL // 2).astype(jnp.int32)


def plant(result, rng, smallest, largest):
    longest = result.shape.index(max(result.shape))
    spots = []
    for shift in (0, 1):
        where = [jax.random.randint(jax.random.fold_in(rng, axis), (), 0, length) for axis, length in enumerate(result.shape)]
        where[longest] = (where[longest] + shift) % result.shape[longest]
        spots.append(tuple(where))
    return result.at[spots[0]].set(smallest).at[spots[1]].set(largest)


def shard_levels(stream_key, shape, pieces, least, largest):
    def one(dim, shards_of):
        draws = jax.random.uniform(jax.random.fold_in(jax.random.fold_in(stream_key, 6), dim), (shards_of,), jnp.float32, least / len(pieces), largest / len(pieces))
        return jnp.repeat(jnp.exp(draws), shape[dim] // shards_of).reshape((-1,) + (1,) * (len(shape) - dim - 1))

    gain = one(*pieces[0])
    for cut in pieces[1:]:
        gain = gain * one(*cut)
    return gain


def gaussian(own_key, dims, deviation, most, split=(), held_as=jnp.bfloat16):
    values = jax.random.normal(own_key, dims, jnp.float32) * deviation
    if len(split) > 0:
        values = shard_levels(own_key, dims, split, -0.22, 0.18) * values
    return jnp.clip(values, min=-most, max=most).astype(held_as)


def setup_inputs(seed: int = 0) -> dict:
    splits = jax.random.split(jax.random.key(seed), 15)
    root_state = gaussian(splits[0], (POSITIONS, D), 1.0, 6.0, ((0, 16), (1, 2)))
    cond_table = gaussian(splits[1], (ACTIONS + CODES, D), 1.0, 6.0)
    block_gain = jnp.clip(1.0 + 0.15 * jax.random.normal(splits[2], (2, BLOCKS, D), jnp.float32), 0.25, 1.75).astype(jnp.bfloat16)
    w_in = gaussian(splits[3], (2, BLOCKS, D, D), D ** -0.5, 0.375, ((0, 2),))
    w_out = gaussian(splits[4], (2, BLOCKS, D, D), D ** -0.5, 0.375, ((0, 2),))
    value_head = gaussian(splits[5], (2, D, BINS), (D // 4) ** -0.5, 0.75, ((0, 2),))
    reward_head = gaussian(splits[6], (D, BINS), (D // 4) ** -0.5, 0.75)
    small_head = gaussian(splits[7], (D, ACTIONS + CODES), (D // 4) ** -0.5, 0.75)
    unroll_len = draw_unroll_len(jax.random.fold_in(splits[14], 71), 0)
    actions = plant(jax.random.randint(splits[9], (UNROLL, POSITIONS), 0, ACTIONS), jax.random.fold_in(splits[9], 1), 0, ACTIONS - 1).astype(jnp.int32)
    codes = plant(jax.random.randint(splits[10], (UNROLL, POSITIONS), 0, CODES), jax.random.fold_in(splits[10], 1), 0, CODES - 1).astype(jnp.int32)
    policy_target = plant(jax.random.randint(splits[11], (UNROLL, POSITIONS), 0, ACTIONS), jax.random.fold_in(splits[11], 1), 0, ACTIONS - 1).astype(jnp.int32)
    value_bins = plant(jax.random.randint(splits[12], (2, UNROLL, POSITIONS), 0, BINS), jax.random.fold_in(splits[12], 1), 0, BINS - 1).astype(jnp.int32)
    reward_bins = plant(jax.random.randint(splits[13], (UNROLL, POSITIONS), 0, BINS), jax.random.fold_in(splits[13], 1), 0, BINS - 1).astype(jnp.int32)
    return {"root_state": root_state, "cond_table": cond_table, "block_gain": block_gain, "w_in": w_in, "w_out": w_out, "value_head": value_head, "reward_head": reward_head, "small_head": small_head, "unroll_len": unroll_len, "actions": actions, "codes": codes, "policy_target": policy_target, "value_bins": value_bins, "reward_bins": reward_bins}


@jax.custom_vjp
def low(v):
    return lax.optimization_barrier(v.astype(jnp.bfloat16)).astype(jnp.float32)

@jax.custom_vjp
def low_back(v):
    return v

def low_keep(v):
    return (low(v), None)

def low_pass(kept, grad):
    return (grad,)

def back_keep(v):
    return (v, None)

def back_low(kept, grad):
    return (low(grad),)
low.defvjp(low_keep, low_pass)
low_back.defvjp(back_keep, back_low)
epsilon = 1e-06
very_negative = -1e+30

def norm_rows(hidden):
    return hidden * lax.rsqrt(lax.optimization_barrier(jnp.mean(hidden * hidden, axis=-1, keepdims=True)) + epsilon)

def product(left_rows, right_rows):
    return jnp.dot(left_rows, right_rows, precision=lax.Precision.HIGHEST, preferred_element_type=jnp.float32)

def cross_entropy(logits, target, allowed):
    masked = jnp.where(allowed, logits, very_negative)
    top_logit = lax.optimization_barrier(jnp.max(masked, axis=-1, keepdims=True))
    log_total = jnp.log(lax.optimization_barrier(jnp.sum(jnp.exp(masked - top_logit), axis=-1))) + top_logit[:, 0]
    picked = jnp.take_along_axis(logits, target[:, None], axis=1)[:, 0]
    return log_total - picked

def tower_step(tower_id, x_in, code_index, small_target, value_target, reward_target, live_rows, table, gains, first, second, value_w, reward_w, small_w):
    hidden = low_back(x_in) + table[code_index]
    squares = []
    for block_index in range(BLOCKS):
        entry_rows = low(norm_rows(hidden) * gains[block_index])
        before = low_back(product(entry_rows, first[block_index]))
        branch = low_back(product(low(jax.nn.silu(before)), second[block_index]))
        hidden = hidden + branch
        squares.append(jnp.stack([jnp.sum(live_rows[:, None] * hidden * hidden), jnp.sum(live_rows[:, None] * branch * branch)]))
    latent = low(norm_rows(hidden))
    value_logit = low_back(product(latent, value_w))
    reward_logit = low_back(product(latent, reward_w))
    small_logit = low_back(product(latent, small_w))
    columns = jnp.arange(small_logit.shape[1])[None, :]
    allowed = (columns >= ACTIONS) == (tower_id == 0)
    reward_weight = float(tower_id)
    row_terms = cross_entropy(value_logit, value_target, True) + reward_weight * cross_entropy(reward_logit, reward_target, True) + cross_entropy(small_logit, small_target, allowed)
    return (latent, value_logit, live_rows * row_terms, jnp.stack(squares))
first_tower = jax.checkpoint(partial(tower_step, 0))
second_tower = jax.checkpoint(partial(tower_step, 1))

def unroll(weights, root_rows, lengths, action_rows, code_rows, policy_rows, value_rows, reward_rows):
    table, gains, first, second, value_w, reward_w, small_w = weights
    state = root_rows
    after_list, state_list, first_logits, second_logits, first_sq, second_sq = ([], [], [], [], [], [])
    row_total = jnp.zeros((root_rows.shape[0],), jnp.float32)
    for unroll_section in range(UNROLL):
        live_rows = (unroll_section < lengths).astype(jnp.float32)
        after, q_logit, loss_first, sq_first = first_tower(state, action_rows[unroll_section], ACTIONS + code_rows[unroll_section], value_rows[0, unroll_section], reward_rows[unroll_section], live_rows, table, gains[0], first[0], second[0], value_w[0], reward_w, small_w)
        state, v_logit, loss_second, sq_second = second_tower(after, ACTIONS + code_rows[unroll_section], policy_rows[unroll_section], value_rows[1, unroll_section], reward_rows[unroll_section], live_rows, table, gains[1], first[1], second[1], value_w[1], reward_w, small_w)
        after_list.append(after)
        state_list.append(state)
        first_logits.append(q_logit)
        second_logits.append(v_logit)
        first_sq.append(sq_first)
        second_sq.append(sq_second)
        row_total = row_total + loss_first + loss_second
    latents = jnp.stack([jnp.stack(after_list), jnp.stack(state_list)])
    logits = jnp.stack([jnp.stack(first_logits), jnp.stack(second_logits)])
    squares = jnp.stack([jnp.stack(first_sq), jnp.stack(second_sq)])
    return (jnp.sum(row_total), (latents, logits, row_total, squares))

def reference(root_state, cond_table, block_gain, w_in, w_out, value_head, reward_head, small_head, unroll_len, actions, codes, policy_target, value_bins, reward_bins):
    weights = tuple((weight.astype(jnp.float32) for weight in (cond_table, block_gain, w_in, w_out, value_head, reward_head, small_head)))
    root = root_state.astype(jnp.float32)

    def one_block(carried, row_start):
        grad_sum, square_sum = carried

        def rows_of(array, axis_number):
            return lax.dynamic_slice_in_dim(array, row_start, B_DEV, axis_number)
        lengths = rows_of(unroll_len, 0)
        action_rows = rows_of(actions, 1)
        code_rows = rows_of(codes, 1)
        policy_rows = rows_of(policy_target, 1)
        value_rows = rows_of(value_bins, 2)
        reward_rows = rows_of(reward_bins, 1)

        def objective(weights_in, root_in):
            return unroll(weights_in, root_in, lengths, action_rows, code_rows, policy_rows, value_rows, reward_rows)
        total, pullback, extras = jax.vjp(objective, weights, rows_of(root, 0), has_aux=True)
        weight_grads, root_grad = pullback(jnp.ones_like(total))
        grad_sum = jax.tree.map(jnp.add, grad_sum, weight_grads)
        return ((grad_sum, square_sum + extras[3]), (extras[0], extras[1], extras[2], root_grad))
    starts = jnp.arange(N_BATCH, dtype=jnp.int32) * B_DEV
    initial = (jax.tree.map(jnp.zeros_like, weights), jnp.zeros((2, UNROLL, BLOCKS, 2), jnp.float32))
    (grad_sum, square_sum), stacked = lax.scan(one_block, initial, starts)
    latents = jnp.moveaxis(stacked[0], 0, 2).reshape(2, UNROLL, POSITIONS, D)
    logits = jnp.moveaxis(stacked[1], 0, 2).reshape(2, UNROLL, POSITIONS, BINS)
    row_loss = stacked[2].reshape(POSITIONS)
    grad_root = stacked[3].reshape(POSITIONS, D)
    counts = lax.optimization_barrier(jnp.sum((jnp.arange(UNROLL)[:, None] < unroll_len[None, :]).astype(jnp.float32), axis=1))
    layer_rms = jnp.sqrt(square_sum / (jnp.maximum(counts, 1.0)[None, :, None, None] * D))
    return (latents.astype(jnp.bfloat16), logits.astype(jnp.bfloat16), row_loss, layer_rms, grad_root, grad_sum[0], grad_sum[1], grad_sum[2], grad_sum[3], grad_sum[4], grad_sum[5], grad_sum[6])
```

```python
import functools

import jax
import jax.numpy as jnp
from jax import lax
from jax.experimental import pallas as pl
from jax.experimental.pallas import tpu as pltpu
from jax.sharding import PartitionSpec as P

ACTIONS = 4
LANES = 128
SIDE = 32
epsilon = 1e-06
very_negative = -1e30
F32 = jnp.float32
BF16 = jnp.bfloat16


def natural(left, right):
    return lax.dot_general(left, right, (((1,), (0,)), ((), ())), preferred_element_type=F32)


def by_rows(left, right):
    return lax.dot_general(left, right, (((0,), (0,)), ((), ())), preferred_element_type=F32)


def by_lanes(left, right):
    return lax.dot_general(left, right, (((1,), (1,)), ((), ())), preferred_element_type=F32)


def round_up(value, unit):
    return (value + unit - 1) // unit * unit


def lane_sum(value):
    return jnp.sum(value, axis=-1, keepdims=True)


def inverse_rms(hidden):
    return lax.rsqrt(lane_sum(hidden * hidden) * (1.0 / hidden.shape[-1]) + epsilon)


def cross_entropy(logits, target, live, first, last):
    column = lax.broadcasted_iota(jnp.int32, logits.shape, 1)
    inside = column < last
    if first > 0:
        inside = inside & (column >= first)
    masked = jnp.where(inside, logits, very_negative)
    top = jnp.max(masked, axis=-1, keepdims=True)
    exp_terms = jnp.exp(masked - top)
    total = lane_sum(exp_terms)
    is_target = column == target
    picked = lane_sum(jnp.where(is_target, logits, 0.0))
    cotangent = exp_terms * (live / total) - jnp.where(is_target, live, 0.0)
    return jnp.log(total) + top - picked, cotangent.astype(BF16)


def forward_kernel(
    sizes,
    root, now, before, table, gains, w_in, w_out, value_w, reward_w, small_w,
    lat, entry, after, slope, side, dlat, dlast, loss, g_value, g_reward, g_small,
    state,
):
    steps, blocks, bins, table_rows = sizes
    step = pl.program_id(0)

    @pl.when(step == 0)
    def _():
        state[...] = root[...]
        loss[...] = jnp.zeros_like(loss)
        g_value[...] = jnp.zeros_like(g_value)
        g_reward[...] = jnp.zeros_like(g_reward)
        g_small[...] = jnp.zeros_like(g_small)

    def heads(tower, latent, columns, live):
        small_target = columns[:, 1:2] + ACTIONS if tower == 0 else columns[:, 2:3]
        value_logit = natural(latent, value_w[tower])
        small_logit = natural(latent, small_w[...])
        value_loss, value_cot = cross_entropy(
            value_logit, columns[:, 3 + tower : 4 + tower], live, 0, bins
        )
        small_loss, small_cot = cross_entropy(
            small_logit, small_target, live,
            ACTIONS if tower == 0 else 0, table_rows if tower == 0 else ACTIONS,
        )
        g_value[tower] += by_rows(latent, value_cot)
        g_small[...] += by_rows(small_cot, latent)
        d_latent = by_lanes(value_cot, value_w[tower]) + by_lanes(small_cot, small_w[...])
        row_loss = value_loss + small_loss
        if tower == 1:
            reward_logit = natural(latent, reward_w[...])
            reward_loss, reward_cot = cross_entropy(
                reward_logit, columns[:, 5:6], live, 0, bins
            )
            g_reward[...] += by_rows(latent, reward_cot)
            d_latent += by_lanes(reward_cot, reward_w[...])
            row_loss += reward_loss
        loss[:, 0:1] += live * row_loss
        return d_latent

    def tower_call(tower, x_in, code, live):
        columns = lax.broadcasted_iota(jnp.int32, (x_in.shape[0], table.shape[0]), 1)
        onehot = jnp.where(columns == code, 1.0, 0.0).astype(BF16)
        hidden = x_in.astype(F32) + natural(onehot, table[...])
        for block in range(blocks):
            place = tower * blocks + block
            inv_scale = inverse_rms(hidden)
            entry_rows = (hidden * inv_scale * gains[place : place + 1, :]).astype(BF16)
            u = natural(entry_rows, w_in[tower, block])
            gate = 0.5 * jnp.tanh(0.5 * u) + 0.5
            after_rows = (u * gate).astype(BF16)
            branch = natural(after_rows, w_out[tower, block])
            hidden = hidden + branch
            entry[0, place] = entry_rows
            after[0, place] = after_rows
            slope[0, place] = gate * (1.0 + u * (1.0 - gate))
            side[0, :, place : place + 1] = inv_scale
            spot = 2 * blocks + 2 + 2 * place
            side[0, :, spot : spot + 1] = live * lane_sum(hidden * hidden)
            side[0, :, spot + 1 : spot + 2] = live * lane_sum(branch * branch)
        inv_scale = inverse_rms(hidden)
        spot = 2 * blocks + tower
        side[0, :, spot : spot + 1] = inv_scale
        latent = (hidden * inv_scale).astype(BF16)
        lat[0, tower] = latent
        return latent

    columns = now[0]
    live = columns[:, 6:7].astype(F32)
    earlier = before[0]
    live_earlier = jnp.where(step > 0, earlier[:, 6:7], 0).astype(F32)
    x_in = state[...]
    dlat[0, 1] = heads(1, x_in, earlier, live_earlier)
    after_state = tower_call(0, x_in, columns[:, 0:1], live)
    dlat[0, 0] = heads(0, after_state, columns, live)
    next_state = tower_call(1, after_state, columns[:, 1:2] + ACTIONS, live)
    state[...] = next_state

    @pl.when(step == steps - 1)
    def _():
        dlast[...] = heads(1, next_state, columns, live)


def backward_kernel(
    sizes,
    lat, entry, after, slope, side, dlat, dlast, lanes, gains, w_in, w_out, g_small,
    grads, root_grad,
    carry, gain_sum, cond_sum,
):
    blocks, table_rows, width = sizes
    turn = pl.program_id(0)
    last = pl.num_programs(0) - 1

    @pl.when(turn == 0)
    def _():
        carry[...] = dlast[...]
        grads[...] = jnp.zeros_like(grads)
        gain_sum[...] = jnp.zeros_like(gain_sum)
        cond_sum[...] = jnp.zeros_like(cond_sum)

    def tower_back(tower, d_latent, code):
        normed = lat[0, tower].astype(F32)
        spot = 2 * blocks + tower
        inv_scale = side[0, :, spot : spot + 1]
        d_hidden = inv_scale * (
            d_latent - normed * (lane_sum(d_latent * normed) * (1.0 / width))
        )
        for block in reversed(range(blocks)):
            place = tower * blocks + block
            gain = gains[place : place + 1, :]
            entry_rows = entry[0, place]
            d_branch = d_hidden.astype(BF16)
            at_out = pl.ds((blocks + block) * width, width)
            grads[tower, at_out, :] += by_rows(after[0, place], d_branch)
            d_after = by_lanes(d_branch, w_out[tower, block])
            d_before = (d_after * slope[0, place]).astype(BF16)
            at_in = pl.ds(block * width, width)
            grads[tower, at_in, :] += by_rows(entry_rows, d_before)
            d_entry = by_lanes(d_before, w_in[tower, block])
            entry_wide = entry_rows.astype(F32)
            product = d_entry * entry_wide
            gain_sum[place : place + 1, :] += jnp.sum(product, axis=0, keepdims=True)
            mean = lane_sum(product) * (1.0 / width)
            inv_scale = side[0, :, place : place + 1]
            d_hidden = d_hidden + inv_scale * (
                d_entry * gain - (entry_wide / gain) * mean
            )
        rows = lax.broadcasted_iota(jnp.int32, (cond_sum.shape[0], d_hidden.shape[0]), 0)
        onehot = jnp.where(rows == code, 1.0, 0.0).astype(BF16)
        cond_sum[...] += natural(onehot, d_hidden.astype(BF16))
        return d_hidden

    code = lanes[0]
    d_after = tower_back(1, carry[...], code[1:2, :] + ACTIONS)
    d_state = tower_back(0, d_after + dlat[0, 0], code[0:1, :])
    carry[...] = d_state + dlat[0, 1]
    root_grad[...] = d_state

    @pl.when(turn == last)
    def _():
        start = 2 * blocks * width
        held = table_rows
        grads[0, pl.ds(start, held), :] = g_small[0:held, :]
        grads[0, pl.ds(start + held, held), :] = cond_sum[0:held, :]
        for tower in range(2):
            mine = slice(tower * blocks, (tower + 1) * blocks)
            grads[tower, pl.ds(start + 2 * held, blocks), :] = gain_sum[mine, :] / gains[mine, :]


def whole(shape):
    return pl.BlockSpec(shape, lambda step: (0,) * len(shape))


def factors_of(size):
    found = []
    while size > 1:
        found.append(4 if size % 4 == 0 else 2)
        size //= found[-1]
    return found


def swap(value, axis, mask):
    pairs = [(source, source ^ mask) for source in range(lax.axis_size(axis))]
    return lax.ppermute(value, axis, pairs)


def scatter_sum(pieces, axis):
    index, stride = lax.axis_index(axis), 1
    tail = pieces.shape[1:]
    for factor in factors_of(pieces.shape[0]):
        digit = (index // stride) % factor
        view = pieces.reshape((-1, factor) + tail)
        total = lax.dynamic_index_in_dim(view, digit, 1, keepdims=False)
        for other in range(1, factor):
            leaving = lax.dynamic_index_in_dim(view, digit ^ other, 1, keepdims=False)
            total = total + swap(leaving.astype(BF16), axis, other * stride).astype(F32)
        pieces, stride = total, stride * factor
    return pieces[0]


def gather_pieces(piece, axis):
    size = lax.axis_size(axis)
    index, stride = lax.axis_index(axis), size
    value = piece.astype(BF16)[None]
    tail = piece.shape
    for factor in reversed(factors_of(size)):
        stride //= factor
        digit = (index // stride) % factor
        held = jnp.stack(
            [value] + [swap(value, axis, other * stride) for other in range(1, factor)]
        )
        value = jnp.stack(
            [
                lax.dynamic_index_in_dim(held, digit ^ other, 0, keepdims=False)
                for other in range(factor)
            ],
            axis=1,
        ).reshape((-1,) + tail)
    return value


def body(
    root_state, cond_table, block_gain, w_in, w_out, value_head, reward_head, small_head,
    unroll_len, actions, codes, policy_target, value_bins, reward_bins,
):
    tower_id = lax.axis_index("tower")
    other_id = 1 - tower_id
    steps, batch_rows = actions.shape
    blocks, width = block_gain.shape[1:]
    bins = value_head.shape[2]
    table_rows = cond_table.shape[0]
    rows = batch_rows // 2
    wide = round_up(bins, LANES)
    row_start = tower_id * rows

    root_whole = lax.all_gather(root_state, "tower", axis=1, tiled=True)
    root = lax.dynamic_slice_in_dim(root_whole, row_start, rows, 0)
    gains = lax.all_gather(block_gain[0], "tower").reshape(2 * blocks, width).astype(F32)
    w_in_all = lax.all_gather(w_in[0], "tower")
    w_out_all = lax.all_gather(w_out[0], "tower")
    value_mine = jnp.pad(value_head[0], ((0, 0), (0, wide - bins)))
    value_all = lax.all_gather(value_mine, "tower")
    reward_w = jnp.pad(reward_head, ((0, 0), (0, wide - bins)))
    small_w = jnp.pad(small_head, ((0, 0), (0, LANES - table_rows)))
    table = jnp.pad(cond_table, ((0, LANES - table_rows), (0, 0)))

    live_all = (jnp.arange(steps)[:, None] < unroll_len[None, :]).astype(jnp.int32)
    counts = jnp.sum(live_all.astype(F32), axis=1)

    def mine(value):
        return lax.dynamic_slice_in_dim(value, row_start, rows, value.ndim - 1)

    kinds = [actions, codes, policy_target, value_bins[0], value_bins[1], reward_bins, live_all]
    kinds = [mine(kind) for kind in kinds] + [jnp.zeros((steps, rows), jnp.int32)]
    lane_kinds = jnp.stack(kinds, axis=1)
    column_kinds = jnp.swapaxes(lane_kinds, 1, 2)

    calls = 2 * blocks
    per_step = lambda *tail: pl.BlockSpec(
        (1,) + tail, lambda step: (step,) + (0,) * len(tail)
    )
    shape = jax.ShapeDtypeStruct
    limit = 56 * 1024 * 1024
    products = steps * rows * (4 * blocks * width * width + 9 * width * wide)
    (
        lat, entry, after, slope, side, dlat, dlast, loss, g_value, g_reward, g_small,
    ) = pl.pallas_call(
        functools.partial(forward_kernel, (steps, blocks, bins, table_rows)),
        grid=(steps,),
        in_specs=[
            whole((rows, width)),
            per_step(rows, 8),
            pl.BlockSpec((1, rows, 8), lambda step: (jnp.maximum(step - 1, 0), 0, 0)),
            whole((LANES, width)),
            whole((calls, width)),
            whole((2, blocks, width, width)),
            whole((2, blocks, width, width)),
            whole((2, width, wide)),
            whole((width, wide)),
            whole((width, LANES)),
        ],
        out_specs=[
            per_step(2, rows, width),
            per_step(calls, rows, width),
            per_step(calls, rows, width),
            per_step(calls, rows, width),
            per_step(rows, SIDE),
            per_step(2, rows, width),
            whole((rows, width)),
            whole((rows, 8)),
            whole((2, width, wide)),
            whole((width, wide)),
            whole((LANES, width)),
        ],
        out_shape=[
            shape((steps, 2, rows, width), BF16),
            shape((steps, calls, rows, width), BF16),
            shape((steps, calls, rows, width), BF16),
            shape((steps, calls, rows, width), F32),
            shape((steps, rows, SIDE), F32),
            shape((steps, 2, rows, width), F32),
            shape((rows, width), F32),
            shape((rows, 8), F32),
            shape((2, width, wide), F32),
            shape((width, wide), F32),
            shape((LANES, width), F32),
        ],
        scratch_shapes=[pltpu.VMEM((rows, width), BF16)],
        compiler_params=pltpu.CompilerParams(vmem_limit_bytes=limit),
        cost_estimate=pl.CostEstimate(
            flops=2 * products, bytes_accessed=40 * 2**20, transcendentals=0
        ),
        name="unroll_forward",
    )(root, column_kinds, column_kinds, table, gains, w_in_all, w_out_all, value_all, reward_w, small_w)

    lat_own = lax.dynamic_index_in_dim(lat, tower_id, 1, keepdims=False)
    lat_away = lax.dynamic_index_in_dim(lat, other_id, 1, keepdims=False)
    lat_got = swap(lat_away, "tower", 1)

    start = 2 * blocks * width
    parts = lax.axis_size("batch")
    grad_rows = round_up(start + 2 * table_rows + blocks, 8 * parts)
    descending = lambda *tail: pl.BlockSpec(
        (1,) + tail, lambda step: (steps - 1 - step,) + (0,) * len(tail)
    )
    grads, root_grad = pl.pallas_call(
        functools.partial(backward_kernel, (blocks, table_rows, width)),
        grid=(steps,),
        in_specs=[
            descending(2, rows, width),
            descending(calls, rows, width),
            descending(calls, rows, width),
            descending(calls, rows, width),
            descending(rows, SIDE),
            descending(2, rows, width),
            whole((rows, width)),
            descending(8, rows),
            whole((calls, width)),
            whole((2, blocks, width, width)),
            whole((2, blocks, width, width)),
            whole((LANES, width)),
        ],
        out_specs=[whole((2, grad_rows, width)), whole((rows, width))],
        out_shape=[shape((2, grad_rows, width), F32), shape((rows, width), F32)],
        scratch_shapes=[
            pltpu.VMEM((rows, width), F32),
            pltpu.VMEM((8, width), F32),
            pltpu.VMEM((round_up(table_rows, 16), width), F32),
        ],
        compiler_params=pltpu.CompilerParams(vmem_limit_bytes=limit),
        cost_estimate=pl.CostEstimate(
            flops=2 * products, bytes_accessed=40 * 2**20, transcendentals=0
        ),
        name="unroll_backward",
    )(lat, entry, after, slope, side, dlat, dlast, lane_kinds, gains, w_in_all, w_out_all, g_small)

    latents = jnp.where(
        tower_id == 0,
        jnp.concatenate([lat_own, lat_got], axis=1),
        jnp.concatenate([lat_got, lat_own], axis=1),
    )
    logits = lax.dot_general(
        latents, value_head[0], (((2,), (0,)), ((), ())), preferred_element_type=F32
    ).astype(BF16)
    row_loss = lax.all_gather(loss[:, 0], "tower", tiled=True)
    half = width // 2
    root_bf = root_grad.astype(BF16)
    leaving = lax.dynamic_slice_in_dim(root_bf, other_id * half, half, 1)
    staying = lax.dynamic_slice_in_dim(root_bf, tower_id * half, half, 1)
    arrived = swap(leaving, "tower", 1)
    grad_root = jnp.where(
        tower_id == 0,
        jnp.concatenate([staying, arrived], axis=0),
        jnp.concatenate([arrived, staying], axis=0),
    ).astype(F32)

    sums = jnp.sum(side[:, :, calls + 2 : calls + 2 + 2 * calls], axis=1)
    sums = sums.reshape(steps, 2, 2 * blocks)
    sums_own = lax.dynamic_index_in_dim(sums, tower_id, 1, keepdims=False)
    sums_away = lax.dynamic_index_in_dim(sums, other_id, 1, keepdims=False)
    sums_own = sums_own + swap(sums_away, "tower", 1)
    small_sums = jnp.concatenate([sums_own, counts[:, None]], axis=1)
    stride = 1
    while stride < parts:
        small_sums = small_sums + swap(small_sums, "batch", stride)
        stride *= 2
    layer_rms = jnp.sqrt(
        small_sums[:, : 2 * blocks] / (jnp.maximum(small_sums[:, 2 * blocks :], 1.0) * width)
    ).reshape(1, steps, blocks, 2)

    def both(own, away):
        return own + swap(away.astype(BF16), "tower", 1).astype(F32)

    grads_own = both(
        lax.dynamic_index_in_dim(grads, tower_id, 0, keepdims=False),
        lax.dynamic_index_in_dim(grads, other_id, 0, keepdims=False),
    )
    reward_halves = g_reward.reshape(2, half, wide)
    head_grads = jnp.concatenate([g_value, reward_halves], axis=1)
    head_own = both(
        lax.dynamic_index_in_dim(head_grads, tower_id, 0, keepdims=False),
        lax.dynamic_index_in_dim(head_grads, other_id, 0, keepdims=False),
    )
    head_sum = gather_pieces(scatter_sum(head_own.reshape(parts, -1, wide), "batch"), "batch")
    head_sum = head_sum.reshape(-1, wide)
    grad_sum = gather_pieces(scatter_sum(grads_own.reshape(parts, -1, width), "batch"), "batch")
    grad_sum = grad_sum.reshape(-1, width)
    grad_value = head_sum[:width, :bins].astype(F32)[None]
    reward_own = head_sum[width:]
    reward_got = swap(reward_own, "tower", 1)
    grad_reward = jnp.where(
        tower_id == 0,
        jnp.concatenate([reward_own, reward_got], axis=0),
        jnp.concatenate([reward_got, reward_own], axis=0),
    )[:, :bins].astype(F32)
    matrices = grad_sum[:start].reshape(2, 1, blocks, width, width).astype(F32)
    shared = grad_sum[start : start + 2 * table_rows]
    shared_got = swap(shared, "tower", 1)
    shared = jnp.where(tower_id == 0, shared, shared_got).astype(F32)
    grad_gain = grad_sum[start + 2 * table_rows :][:blocks].astype(F32)[None]
    return (
        latents[None],
        logits[None],
        row_loss,
        layer_rms,
        grad_root,
        shared[table_rows:],
        grad_gain,
        matrices[0],
        matrices[1],
        grad_value,
        grad_reward,
        shared[:table_rows].T,
    )


def solution(mesh):
    placed = (
        P("batch", "tower"),
        P(),
        P("tower", None, None),
        P("tower", None, None, None),
        P("tower", None, None, None),
        P("tower", None, None),
        P(),
        P(),
        P("batch"),
        P(None, "batch"),
        P(None, "batch"),
        P(None, "batch"),
        P(None, None, "batch"),
        P(None, "batch"),
    )
    return jax.shard_map(
        body,
        mesh=mesh,
        in_specs=placed,
        out_specs=(
            P("tower", None, "batch", None),
            P("tower", None, "batch", None),
            P("batch"),
            P("tower", None, None, None),
            P("batch", "tower"),
            P(),
            P("tower", None, None),
            P("tower", None, None, None),
            P("tower", None, None, None),
            P("tower", None, None),
            P(),
            P(),
        ),
        check_vma=False,
    )
```

```python
import functools

import jax
import jax.numpy as jnp
from jax import lax
from jax.experimental import pallas as pl
from jax.experimental.pallas import tpu as pltpu
from jax.sharding import PartitionSpec as P

ACTIONS = 4
LANES = 128
SIDE = 32
CHUNK = 32
VMEM_LIMIT = 56 * 1024 * 1024
epsilon = 1e-06
very_negative = -1e30
F32 = jnp.float32
BF16 = jnp.bfloat16


def natural(left, right):
    return lax.dot_general(left, right, (((1,), (0,)), ((), ())), preferred_element_type=F32)


def by_rows(left, right):
    return lax.dot_general(left, right, (((0,), (0,)), ((), ())), preferred_element_type=F32)


def by_lanes(left, right):
    return lax.dot_general(left, right, (((1,), (1,)), ((), ())), preferred_element_type=F32)


def round_up(value, unit):
    return (value + unit - 1) // unit * unit


def lane_sum(value):
    return jnp.sum(value, axis=-1, keepdims=True)


def inverse_rms(hidden):
    return lax.rsqrt(lane_sum(hidden * hidden) * (1.0 / hidden.shape[-1]) + epsilon)


def weave(*tasks):
    tasks = [(list(task)) for task in tasks]
    longest = max(len(task) for task in tasks)
    done = [0] * len(tasks)
    for turn in range(longest):
        for which, task in enumerate(tasks):
            until = (turn + 1) * len(task) // longest
            while done[which] < until:
                task[done[which]]()
                done[which] += 1


def place_weights(tower_id, own, got, held):
    held[tower_id] = own[...]
    held[1 - tower_id] = got[...]


class Sizes:
    def __init__(self, steps, rows, blocks, width, bins, table_rows, parts):
        self.steps, self.rows, self.blocks, self.width = steps, rows, blocks, width
        self.bins, self.table_rows, self.parts = bins, table_rows, parts
        self.calls = 2 * blocks
        self.wide = round_up(bins, LANES)
        self.tiles = self.wide // LANES
        self.split = width // LANES
        self.pitch = round_up(steps, 8)
        self.held = round_up(table_rows, 8)
        self.matrix_rows = self.calls * width * self.split
        self.value_at = self.matrix_rows
        self.gain_at = self.value_at + width * self.tiles
        self.sums_at = self.gain_at + 8 * self.split
        self.reward_at = self.sums_at + self.pitch
        self.small_at = self.reward_at + (width // 2) * self.tiles
        self.cond_at = self.small_at + self.held * self.split
        self.shared_end = self.cond_at + self.held * self.split
        self.total = round_up(self.shared_end, 8 * parts)
        self.head_rows = (
            width * self.tiles + self.pitch + (width // 2) * self.tiles + self.held * self.split
        )


def forward_kernel(
    sizes, tower_ref,
    root_own, root_got, lengths, actions, codes, policy, value_bins, reward_bins,
    table_in, gains_own, gains_got, in_own, in_got, out_own, out_got,
    value_own, value_got, reward_in, small_in,
    lat, lat_own, lat_away, entry, after, slope, side, dlat, dlast, loss, head_grads,
    state, columns, table, gains, w_in, w_out, heads0, heads1, acc0, acc1,
    logits0, logits1, cot0, cot1,
):
    s = sizes
    step = pl.program_id(0)
    tower_id = tower_ref[0]
    rows, width, wide = s.rows, s.width, s.wide

    @pl.when(step == 0)
    def _():
        first = tower_id == 0
        state[:, 0 : width // 2] = jnp.where(first, root_own[...], root_got[...])
        state[:, width // 2 : width] = jnp.where(first, root_got[...], root_own[...])
        place_weights(tower_id, in_own, in_got, w_in)
        place_weights(tower_id, out_own, out_got, w_out)
        gains[...] = jnp.zeros_like(gains)
        gains[tower_id, 0 : s.blocks, :] = gains_own[...].astype(F32)
        gains[1 - tower_id, 0 : s.blocks, :] = gains_got[...].astype(F32)
        table[...] = jnp.zeros_like(table)
        table[0 : s.table_rows, :] = table_in[...]
        heads0[...] = jnp.zeros_like(heads0)
        heads1[...] = jnp.zeros_like(heads1)
        heads0[:, 0 : s.bins] = jnp.where(first, value_own[...], value_got[...])
        heads1[:, 0 : s.bins] = jnp.where(first, value_got[...], value_own[...])
        heads1[:, wide : wide + s.bins] = reward_in[...]
        heads0[:, wide : wide + s.table_rows] = small_in[...]
        heads1[:, 2 * wide : 2 * wide + s.table_rows] = small_in[...]
        acc0[...] = jnp.zeros_like(acc0)
        acc1[...] = jnp.zeros_like(acc1)
        loss[...] = jnp.zeros_like(loss)
        head_grads[...] = jnp.zeros_like(head_grads)
        columns[...] = jnp.zeros_like(columns)
        kinds = [actions[...], codes[...], policy[...], value_bins[0], value_bins[1], reward_bins[...]]
        count = lax.broadcasted_iota(jnp.int32, (s.steps, rows), 0)
        kinds.append((count < lengths[...]).astype(jnp.int32))
        for place, kind in enumerate(kinds):
            columns[place * s.pitch : place * s.pitch + s.steps, :] = kind
        columns[...] = columns[...].T

    rolled = pltpu.roll(columns[...], (LANES - step) % LANES, 1)

    def column(kind, back=0):
        lane = (kind * s.pitch - back) % LANES
        return rolled[:, lane : lane + 1]

    live = column(6).astype(F32)
    live_earlier = jnp.where(step > 0, column(6, 1), 0).astype(F32)
    lane = lax.broadcasted_iota(jnp.int32, (CHUNK, LANES), 1)

    def cross_entropy(logits, cot, at, bins_first, bins_last, target, live_col):
        losses = []
        tiles = (bins_last + LANES - 1) // LANES
        for start in range(0, rows, CHUNK):
            some = slice(start, start + CHUNK)
            goal = target[some]
            weight = live_col[some]
            values = [
                logits[some, at + tile * LANES : at + (tile + 1) * LANES] for tile in range(tiles)
            ]
            inside = lane < bins_last - (tiles - 1) * LANES
            if bins_first > 0:
                inside = inside & (lane >= bins_first)
            masked = values[:-1] + [jnp.where(inside, values[-1], very_negative)]
            top = functools.reduce(jnp.maximum, masked)
            top = jnp.max(top, axis=-1, keepdims=True)
            exp_terms = [jnp.exp(value - top) for value in masked]
            total = lane_sum(functools.reduce(jnp.add, exp_terms))
            hits = [lane == goal - tile * LANES for tile in range(tiles)]
            picked = lane_sum(
                functools.reduce(
                    jnp.add, [jnp.where(hit, value, 0.0) for hit, value in zip(hits, values)]
                )
            )
            scale = weight / total
            for tile, (hit, term) in enumerate(zip(hits, exp_terms)):
                cot[some, at + tile * LANES : at + (tile + 1) * LANES] = (
                    term * scale - jnp.where(hit, weight, 0.0)
                ).astype(BF16)
            losses.append(weight * (jnp.log(total) + top - picked))
        return losses

    def heads(tower, latent, live_col, back, put):
        weights, logits, cot, acc = (
            (heads0, logits0, cot0, acc0) if tower == 0 else (heads1, logits1, cot1, acc1)
        )
        spans = [(0, 0, s.bins, column(3 + tower, back))]
        if tower == 1:
            spans.append((wide, 0, s.bins, column(5, back)))
            spans.append((2 * wide, 0, ACTIONS, column(2, back)))
        else:
            spans.append((wide, ACTIONS, s.table_rows, column(1, back) + ACTIONS))
        pieces = []

        def make_logits(at, length):
            logits[:, at : at + length] = natural(latent(), weights[:, at : at + length])

        def make_cotangent(span):
            losses = cross_entropy(logits, cot, *span, live_col)
            for place, part in enumerate(losses):
                loss[place * CHUNK : (place + 1) * CHUNK, 0:1] += part

        def make_latent():
            put(by_lanes(cot[...], weights[...]))

        def make_grads(at, length):
            acc[:, at : at + length] += by_rows(latent(), cot[:, at : at + length])

        for span in spans:
            length = wide if span[2] == s.bins else LANES
            pieces.append(functools.partial(make_logits, span[0], length))
            pieces.append(functools.partial(make_cotangent, span))
            pieces.append(functools.partial(make_grads, span[0], length))
        pieces.append(make_latent)
        return pieces

    def tower_call(tower, x_in, code, done):
        kept = {}

        def begin():
            spot = lax.broadcasted_iota(jnp.int32, (rows, table.shape[0]), 1)
            onehot = jnp.where(spot == code, 1.0, 0.0).astype(BF16)
            kept["hidden"] = x_in().astype(F32) + natural(onehot, table[...])

        def into(block):
            place = tower * s.blocks + block
            hidden = kept["hidden"]
            inv_scale = inverse_rms(hidden)
            entry_rows = (hidden * inv_scale * gains[tower, block : block + 1, :]).astype(BF16)
            kept["u"] = natural(entry_rows, w_in[tower, block])
            entry[0, place] = entry_rows
            side[0, :, place : place + 1] = inv_scale

        def out_of(block):
            place = tower * s.blocks + block
            u = kept["u"]
            gate = 0.5 * jnp.tanh(0.5 * u) + 0.5
            after_rows = (u * gate).astype(BF16)
            branch = natural(after_rows, w_out[tower, block])
            hidden = kept["hidden"] + branch
            kept["hidden"] = hidden
            after[0, place] = after_rows
            slope[0, place] = gate * (1.0 + u * (1.0 - gate))
            spot = s.calls + 2 + 2 * place
            side[0, :, spot : spot + 1] = live * lane_sum(hidden * hidden)
            side[0, :, spot + 1 : spot + 2] = live * lane_sum(branch * branch)

        def finish():
            inv_scale = inverse_rms(kept["hidden"])
            spot = s.calls + tower
            side[0, :, spot : spot + 1] = inv_scale
            latent = (kept["hidden"] * inv_scale).astype(BF16)
            lat[0, tower] = latent
            done(latent)

        pieces = [begin]
        for block in range(s.blocks):
            pieces += [functools.partial(into, block), functools.partial(out_of, block)]
        return pieces + [finish]

    found = {"s": state[...]}

    def put_state(value):
        dlat[0, 1] = value

    def put_after(value):
        dlat[0, 0] = value

    def put_last(value):
        dlast[...] = value

    weave(
        tower_call(0, lambda: found["s"], column(0), lambda y: found.update(a=y)),
        heads(1, lambda: found["s"], live_earlier, 1, put_state),
    )
    weave(
        tower_call(1, lambda: found["a"], column(1) + ACTIONS, lambda y: found.update(n=y)),
        heads(0, lambda: found["a"], live, 0, put_after),
    )
    state[...] = found["n"]
    first = tower_id == 0
    lat_own[0] = jnp.where(first, found["a"], found["n"])
    lat_away[0] = jnp.where(first, found["n"], found["a"])
    side[0, :, SIDE - 1 : SIDE] = live
    sums_at = width * s.tiles
    sums = jnp.sum(side[0], axis=0, keepdims=True)
    for tower in range(2):
        head_grads[tower, pl.ds(sums_at + step, 1), 0:SIDE] = sums

    @pl.when(step == s.steps - 1)
    def _():
        for piece in heads(1, lambda: found["n"], live, 0, put_last):
            piece()
        for tile in range(s.tiles):
            lanes = slice(tile * LANES, (tile + 1) * LANES)
            head_grads[0, tile * width : (tile + 1) * width, :] = acc0[:, lanes]
            head_grads[1, tile * width : (tile + 1) * width, :] = acc1[:, lanes]
            half = width // 2
            at = sums_at + s.pitch + tile * half
            lanes = slice(wide + tile * LANES, wide + (tile + 1) * LANES)
            for tower in range(2):
                head_grads[tower, at : at + half, :] = acc1[tower * half : (tower + 1) * half, lanes]
        small = acc0[:, wide : wide + LANES] + acc1[:, 2 * wide : 2 * wide + LANES]
        small = small.T
        at = sums_at + s.pitch + half * s.tiles
        for part in range(s.split):
            head_grads[0, at + part * s.held : at + (part + 1) * s.held, :] = small[
                0 : s.held, part * LANES : (part + 1) * LANES
            ]


def backward_kernel(
    sizes, tower_ref,
    lat, entry, after, slope, side, dlat, dlast, actions, codes,
    gains_own, gains_got, in_own, in_got, out_own, out_got, head_grads,
    own, away, root_own, root_away,
    carry, gain_sum, cond_sum, grads, gains, w_in, w_out,
):
    s = sizes
    turn = pl.program_id(0)
    step = s.steps - 1 - turn
    tower_id = tower_ref[0]
    blocks, width = s.blocks, s.width

    @pl.when(turn == 0)
    def _():
        place_weights(tower_id, in_own, in_got, w_in)
        place_weights(tower_id, out_own, out_got, w_out)
        gains[...] = jnp.ones_like(gains)
        gains[tower_id, 0:blocks, :] = gains_own[...].astype(F32)
        gains[1 - tower_id, 0:blocks, :] = gains_got[...].astype(F32)
        carry[...] = dlast[...]
        grads[...] = jnp.zeros_like(grads)
        gain_sum[...] = jnp.zeros_like(gain_sum)
        cond_sum[...] = jnp.zeros_like(cond_sum)

    def tower_back(tower, d_latent, code):
        normed = lat[0, tower].astype(F32)
        spot = s.calls + tower
        inv_scale = side[0, :, spot : spot + 1]
        d_hidden = inv_scale * (
            d_latent - normed * (lane_sum(d_latent * normed) * (1.0 / width))
        )
        for block in reversed(range(blocks)):
            place = tower * blocks + block
            gain = gains[tower, block : block + 1, :]
            entry_rows = entry[0, place]
            d_branch = d_hidden.astype(BF16)
            grads[tower, blocks + block] += by_rows(after[0, place], d_branch)
            d_after = by_lanes(d_branch, w_out[tower, block])
            d_before = (d_after * slope[0, place]).astype(BF16)
            grads[tower, block] += by_rows(entry_rows, d_before)
            d_entry = by_lanes(d_before, w_in[tower, block])
            entry_wide = entry_rows.astype(F32)
            product = d_entry * entry_wide
            gain_sum[tower, block : block + 1, :] += jnp.sum(product, axis=0, keepdims=True)
            mean = lane_sum(product) * (1.0 / width)
            inv_scale = side[0, :, place : place + 1]
            d_hidden = d_hidden + inv_scale * (
                d_entry * gain - (entry_wide / gain) * mean
            )
        spots = lax.broadcasted_iota(jnp.int32, (cond_sum.shape[0], d_hidden.shape[0]), 0)
        onehot = jnp.where(spots == code, 1.0, 0.0).astype(BF16)
        cond_sum[...] += natural(onehot, d_hidden.astype(BF16))
        return d_hidden

    d_after = tower_back(1, carry[...], codes[pl.ds(step, 1), :] + ACTIONS)
    d_state = tower_back(0, d_after + dlat[0, 0], actions[pl.ds(step, 1), :])
    carry[...] = d_state + dlat[0, 1]

    @pl.when(turn == s.steps - 1)
    def _():
        left = d_state[:, 0 : width // 2].astype(BF16)
        right = d_state[:, width // 2 : width].astype(BF16)
        root_own[...] = jnp.where(tower_id == 0, left, right)
        root_away[...] = jnp.where(tower_id == 0, right, left)
        gain_sum[...] = gain_sum[...] / gains[...]
        value_rows = width * s.tiles
        for target, which in ((own, tower_id), (away, 1 - tower_id)):
            kind = target.dtype
            if s.total > s.shared_end:
                target[s.shared_end :, :] = jnp.zeros((s.total - s.shared_end, LANES), kind)
            for part in range(s.split):
                lanes = slice(part * LANES, (part + 1) * LANES)
                for matrix in range(s.calls):
                    at = (matrix * s.split + part) * width
                    target[at : at + width, :] = grads[which, matrix, :, lanes].astype(kind)
                at = s.gain_at + 8 * part
                target[at : at + 8, :] = gain_sum[which, :, lanes].astype(kind)
                at = s.cond_at + s.held * part
                here = jnp.where(which == 0, cond_sum[0 : s.held, lanes], 0.0)
                target[at : at + s.held, :] = here.astype(kind)
            target[s.value_at : s.value_at + value_rows, :] = head_grads[
                which, 0:value_rows, :
            ].astype(kind)
            target[s.sums_at : s.cond_at, :] = head_grads[
                which, value_rows : s.head_rows, :
            ].astype(kind)


def logits_kernel(sizes, tower_ref, lat_own, lat_got, value_own, latents, logits):
    rows = sizes.rows
    tower_id = tower_ref[0]
    at_own = pl.ds(pl.multiple_of(tower_id * rows, rows), rows)
    at_got = pl.ds(pl.multiple_of((1 - tower_id) * rows, rows), rows)
    for at, source in ((at_own, lat_own), (at_got, lat_got)):
        latents[0, at, :] = source[0]
        logits[0, at, :] = natural(source[0], value_own[...]).astype(BF16)


def unpack_kernel(
    sizes, tower_ref, summed, shared,
    cond, gain, w_in, w_out, value, reward, small, rms,
):
    s = sizes
    tower_id = tower_ref[0]
    width, half = s.width, s.width // 2
    for part in range(s.split):
        lanes = slice(part * LANES, (part + 1) * LANES)
        for block in range(s.blocks):
            at = (block * s.split + part) * width
            w_in[block, :, lanes] = summed[at : at + width, :].astype(F32)
            at = ((s.blocks + block) * s.split + part) * width
            w_out[block, :, lanes] = summed[at : at + width, :].astype(F32)
        at = s.gain_at + 8 * part
        gain[:, lanes] = summed[at : at + 8, :].astype(F32)[0 : s.blocks]
        at = s.cond_at + s.held * part
        both = summed[at : at + s.held, :].astype(F32)
        both += shared[at - s.reward_at : at - s.reward_at + s.held, :].astype(F32)
        cond[:, lanes] = both[0 : s.table_rows]
        at = s.small_at + s.held * part
        both = summed[at : at + s.held, :].astype(F32)
        both += shared[at - s.reward_at : at - s.reward_at + s.held, :].astype(F32)
        small[:, lanes] = both[0 : s.table_rows]
    at_own = pl.ds(pl.multiple_of(tower_id * half, half), half)
    at_got = pl.ds(pl.multiple_of((1 - tower_id) * half, half), half)
    for tile in range(s.tiles):
        stop = min((tile + 1) * LANES, s.bins)
        lanes = slice(tile * LANES, stop)
        kept = slice(0, stop - tile * LANES)
        at = s.value_at + tile * width
        value[:, lanes] = summed[at : at + width, :].astype(F32)[:, kept]
        at = s.reward_at + tile * half
        reward[at_own, lanes] = summed[at : at + half, :].astype(F32)[:, kept]
        at = tile * half
        reward[at_got, lanes] = shared[at : at + half, :].astype(F32)[:, kept]
    sums = summed[s.sums_at : s.sums_at + s.pitch, :].astype(F32)
    count = jnp.maximum(sums[:, SIDE - 1 : SIDE], 1.0)
    rms[...] = jnp.sqrt(jnp.maximum(sums, 0.0) / (count * width))


def whole(shape):
    return pl.BlockSpec(shape, lambda step, tower: (0,) * len(shape))


def per_step(*tail):
    return pl.BlockSpec((1,) + tail, lambda step, tower: (step,) + (0,) * len(tail))


def swap(value, axis, mask):
    pairs = [(source, source ^ mask) for source in range(lax.axis_size(axis))]
    return lax.ppermute(value, axis, pairs)


def exchange_groups(batch_size):
    factors = []
    left = batch_size
    while left > 1:
        factors.append(4 if left % 4 == 0 else 2)
        left //= factors[-1]
    rounds = []
    for tower in range(2):
        mine = []
        stride = 1
        for factor in factors:
            groups = [
                [tower * batch_size + base + stride * digit for digit in range(factor)]
                for base in range(batch_size)
                if (base // stride) % factor == 0
            ]
            mine.append((factor, groups))
            stride *= factor
        if tower == 1 and len(set(factors)) == 1:
            mine.reverse()
        rounds.append(mine)
    return [
        (first[0], first[1] + second[1]) for first, second in zip(rounds[0], rounds[1])
    ]


AXES = ("tower", "batch")


def scatter_sum(pieces, rounds):
    for factor, groups in rounds:
        view = pieces.reshape((factor, -1) + pieces.shape[1:]).astype(BF16)
        got = lax.all_to_all(view, AXES, 0, 0, axis_index_groups=groups)
        pieces = jnp.sum(got.astype(F32), axis=0)
    return pieces


def gather_pieces(pieces, rounds):
    value = pieces.astype(BF16)
    for factor, groups in reversed(rounds):
        spread = jnp.broadcast_to(value[None], (factor,) + value.shape)
        got = lax.all_to_all(spread, AXES, 0, 0, axis_index_groups=groups)
        value = got.reshape((-1,) + value.shape[1:])
    return value


def body(
    root_state, cond_table, block_gain, w_in, w_out, value_head, reward_head, small_head,
    unroll_len, actions, codes, policy_target, value_bins, reward_bins,
):
    tower_id = lax.axis_index("tower")
    other_id = 1 - tower_id
    tower_ref = tower_id.astype(jnp.int32)[None]
    steps, batch_rows = actions.shape
    blocks, width = block_gain.shape[1:]
    bins = value_head.shape[2]
    table_rows = cond_table.shape[0]
    rows = batch_rows // 2
    half = width // 2
    parts = lax.axis_size("batch")
    s = Sizes(steps, rows, blocks, width, bins, table_rows, parts)
    calls, wide = s.calls, s.wide

    root_mine = lax.dynamic_slice_in_dim(root_state, tower_id * rows, rows, 0)
    root_away = lax.dynamic_slice_in_dim(root_state, other_id * rows, rows, 0)
    root_got = swap(root_away, "tower", 1)
    in_own, out_own, gains_own, value_own = w_in[0], w_out[0], block_gain[0], value_head[0]
    in_got = swap(in_own, "tower", 1)
    out_got = swap(out_own, "tower", 1)
    gains_got = swap(gains_own, "tower", 1)
    value_got = swap(value_own, "tower", 1)
    lengths = unroll_len.reshape(1, batch_rows)

    shape = jax.ShapeDtypeStruct
    params = pltpu.CompilerParams(vmem_limit_bytes=VMEM_LIMIT)
    products = steps * rows * (4 * blocks * width * width + 9 * width * wide)
    cost = pl.CostEstimate(flops=2 * products, bytes_accessed=40 * 2**20, transcendentals=0)
    mine = lambda *lead: pl.BlockSpec(
        lead + (rows,), lambda step, tower: (0,) * len(lead) + (tower[0],)
    )
    (
        lat, lat_own, lat_away, entry, after, slope, side, dlat, dlast, loss, head_grads,
    ) = pl.pallas_call(
        functools.partial(forward_kernel, s),
        grid_spec=pltpu.PrefetchScalarGridSpec(
            num_scalar_prefetch=1,
            grid=(steps,),
            in_specs=[
                whole((rows, half)),
                whole((rows, half)),
                mine(1),
                mine(steps),
                mine(steps),
                mine(steps),
                mine(2, steps),
                mine(steps),
                whole((table_rows, width)),
                whole((blocks, width)),
                whole((blocks, width)),
                whole((blocks, width, width)),
                whole((blocks, width, width)),
                whole((blocks, width, width)),
                whole((blocks, width, width)),
                whole((width, bins)),
                whole((width, bins)),
                whole((width, bins)),
                whole((width, table_rows)),
            ],
            out_specs=[
                per_step(2, rows, width),
                per_step(rows, width),
                per_step(rows, width),
                per_step(calls, rows, width),
                per_step(calls, rows, width),
                per_step(calls, rows, width),
                per_step(rows, SIDE),
                per_step(2, rows, width),
                whole((rows, width)),
                whole((rows, 8)),
                whole((2, s.head_rows, LANES)),
            ],
            scratch_shapes=[
                pltpu.VMEM((rows, width), BF16),
                pltpu.VMEM((LANES, rows), jnp.int32),
                pltpu.VMEM((LANES, width), BF16),
                pltpu.VMEM((2, 8, width), F32),
                pltpu.VMEM((2, blocks, width, width), BF16),
                pltpu.VMEM((2, blocks, width, width), BF16),
                pltpu.VMEM((width, wide + LANES), BF16),
                pltpu.VMEM((width, 2 * wide + LANES), BF16),
                pltpu.VMEM((width, wide + LANES), F32),
                pltpu.VMEM((width, 2 * wide + LANES), F32),
                pltpu.VMEM((rows, wide + LANES), F32),
                pltpu.VMEM((rows, 2 * wide + LANES), F32),
                pltpu.VMEM((rows, wide + LANES), BF16),
                pltpu.VMEM((rows, 2 * wide + LANES), BF16),
            ],
        ),
        out_shape=[
            shape((steps, 2, rows, width), BF16),
            shape((steps, rows, width), BF16),
            shape((steps, rows, width), BF16),
            shape((steps, calls, rows, width), BF16),
            shape((steps, calls, rows, width), BF16),
            shape((steps, calls, rows, width), F32),
            shape((steps, rows, SIDE), F32),
            shape((steps, 2, rows, width), F32),
            shape((rows, width), F32),
            shape((rows, 8), F32),
            shape((2, s.head_rows, LANES), F32),
        ],
        compiler_params=params,
        cost_estimate=cost,
        name="unroll_forward",
    )(
        tower_ref, root_mine, root_got, lengths, actions, codes, policy_target, value_bins,
        reward_bins, cond_table, gains_own, gains_got, in_own, in_got, out_own, out_got,
        value_own, value_got, reward_head, small_head,
    )
    lat_got = swap(lat_away, "tower", 1)
    loss_own = loss[:, 0]
    loss_got = swap(loss_own, "tower", 1)

    descending = lambda *tail: pl.BlockSpec(
        (1,) + tail, lambda step, tower: (steps - 1 - step,) + (0,) * len(tail)
    )
    own, away, root_own, root_away = pl.pallas_call(
        functools.partial(backward_kernel, s),
        grid_spec=pltpu.PrefetchScalarGridSpec(
            num_scalar_prefetch=1,
            grid=(steps,),
            in_specs=[
                descending(2, rows, width),
                descending(calls, rows, width),
                descending(calls, rows, width),
                descending(calls, rows, width),
                descending(rows, SIDE),
                descending(2, rows, width),
                whole((rows, width)),
                mine(steps),
                mine(steps),
                whole((blocks, width)),
                whole((blocks, width)),
                whole((blocks, width, width)),
                whole((blocks, width, width)),
                whole((blocks, width, width)),
                whole((blocks, width, width)),
                whole((2, s.head_rows, LANES)),
            ],
            out_specs=[
                whole((s.total, LANES)),
                whole((s.total, LANES)),
                whole((rows, half)),
                whole((rows, half)),
            ],
            scratch_shapes=[
                pltpu.VMEM((rows, width), F32),
                pltpu.VMEM((2, 8, width), F32),
                pltpu.VMEM((round_up(table_rows, 16), width), F32),
                pltpu.VMEM((2, calls, width, width), F32),
                pltpu.VMEM((2, 8, width), F32),
                pltpu.VMEM((2, blocks, width, width), BF16),
                pltpu.VMEM((2, blocks, width, width), BF16),
            ],
        ),
        out_shape=[
            shape((s.total, LANES), F32),
            shape((s.total, LANES), BF16),
            shape((rows, half), BF16),
            shape((rows, half), BF16),
        ],
        compiler_params=params,
        cost_estimate=cost,
        name="unroll_backward",
    )(
        tower_ref, lat, entry, after, slope, side, dlat, dlast, actions, codes,
        gains_own, gains_got, in_own, in_got, out_own, out_got, head_grads,
    )
    got = swap(away, "tower", 1)
    root_got = swap(root_away, "tower", 1)

    latents, logits = pl.pallas_call(
        functools.partial(logits_kernel, s),
        grid_spec=pltpu.PrefetchScalarGridSpec(
            num_scalar_prefetch=1,
            grid=(steps,),
            in_specs=[per_step(rows, width), per_step(rows, width), whole((width, bins))],
            out_specs=[per_step(batch_rows, width), per_step(batch_rows, bins)],
        ),
        out_shape=[
            shape((steps, batch_rows, width), BF16),
            shape((steps, batch_rows, bins), BF16),
        ],
        compiler_params=params,
        cost_estimate=pl.CostEstimate(
            flops=2 * steps * batch_rows * width * wide, bytes_accessed=6 * 2**20, transcendentals=0
        ),
        name="latents_and_logits",
    )(tower_ref, lat_own, lat_got, value_own)

    def in_order(mine_value, got_value, axis):
        return jnp.where(
            tower_id == 0,
            jnp.concatenate([mine_value, got_value], axis=axis),
            jnp.concatenate([got_value, mine_value], axis=axis),
        )

    row_loss = in_order(loss_own, loss_got, 0)
    grad_root = in_order(root_own, root_got, 0).astype(F32)

    rounds = exchange_groups(parts)
    chip_sum = own + got.astype(F32)
    pieces = scatter_sum(chip_sum, rounds)
    summed = gather_pieces(pieces, rounds)
    shared = swap(summed[s.reward_at : s.shared_end], "tower", 1)

    outs = pl.pallas_call(
        functools.partial(unpack_kernel, s),
        grid_spec=pltpu.PrefetchScalarGridSpec(
            num_scalar_prefetch=1,
            grid=(1,),
            in_specs=[whole((s.total, LANES)), whole((s.shared_end - s.reward_at, LANES))],
            out_specs=[
                whole((table_rows, width)),
                whole((blocks, width)),
                whole((blocks, width, width)),
                whole((blocks, width, width)),
                whole((width, bins)),
                whole((width, bins)),
                whole((table_rows, width)),
                whole((s.pitch, LANES)),
            ],
        ),
        out_shape=[
            shape((table_rows, width), F32),
            shape((blocks, width), F32),
            shape((blocks, width, width), F32),
            shape((blocks, width, width), F32),
            shape((width, bins), F32),
            shape((width, bins), F32),
            shape((table_rows, width), F32),
            shape((s.pitch, LANES), F32),
        ],
        compiler_params=params,
        name="unpack_gradients",
    )(tower_ref, summed, shared)
    grad_cond, grad_gain, grad_in, grad_out, grad_value, grad_reward, small_t, rms = outs
    spot = calls + 2 + tower_id * calls
    layer_rms = lax.dynamic_slice(rms, (0, spot), (steps, calls)).reshape(1, steps, blocks, 2)
    return (
        latents[None],
        logits[None],
        row_loss,
        layer_rms,
        grad_root,
        grad_cond,
        grad_gain[None],
        grad_in[None],
        grad_out[None],
        grad_value[None],
        grad_reward,
        small_t.T,
    )


def solution(mesh):
    placed = (
        P("batch", "tower"),
        P(),
        P("tower", None, None),
        P("tower", None, None, None),
        P("tower", None, None, None),
        P("tower", None, None),
        P(),
        P(),
        P("batch"),
        P(None, "batch"),
        P(None, "batch"),
        P(None, "batch"),
        P(None, None, "batch"),
        P(None, "batch"),
    )
    return jax.shard_map(
        body,
        mesh=mesh,
        in_specs=placed,
        out_specs=(
            P("tower", None, "batch", None),
            P("tower", None, "batch", None),
            P("batch"),
            P("tower", None, None, None),
            P("batch", "tower"),
            P(),
            P("tower", None, None),
            P("tower", None, None, None),
            P("tower", None, None, None),
            P("tower", None, None),
            P(),
            P(),
        ),
        check_vma=False,
    )
```

```python
import functools

import jax
import jax.numpy as jnp
from jax import lax
from jax.experimental import pallas as pl
from jax.experimental.pallas import tpu as pltpu
from jax.sharding import PartitionSpec as P

ACTIONS = 4
LANES = 128
SIDE = 32
VMEM_LIMIT = 56 * 1024 * 1024
epsilon = 1e-06
very_negative = -1e30
F32 = jnp.float32
BF16 = jnp.bfloat16


def natural(left, right):
    return lax.dot_general(left, right, (((1,), (0,)), ((), ())), preferred_element_type=F32)


def by_rows(left, right):
    return lax.dot_general(left, right, (((0,), (0,)), ((), ())), preferred_element_type=F32)


def by_lanes(left, right):
    return lax.dot_general(left, right, (((1,), (1,)), ((), ())), preferred_element_type=F32)


def round_up(value, unit):
    return (value + unit - 1) // unit * unit


def lane_sum(value):
    return jnp.sum(value, axis=-1, keepdims=True)


def inverse_rms(hidden):
    return lax.rsqrt(lane_sum(hidden * hidden) * (1.0 / hidden.shape[-1]) + epsilon)


def weave(*tasks):
    tasks = [(list(task)) for task in tasks]
    longest = max(len(task) for task in tasks)
    done = [0] * len(tasks)
    for turn in range(longest):
        for which, task in enumerate(tasks):
            until = (turn + 1) * len(task) // longest
            while done[which] < until:
                task[done[which]]()
                done[which] += 1


def place_weights(tower_id, own, got, held):
    held[tower_id] = own[...]
    held[1 - tower_id] = got[...]


def cuts(length, unit=160):
    return [(start, min(start + unit, length)) for start in range(0, length, unit)]


class Sizes:
    def __init__(self, steps, rows, blocks, width, bins, table_rows, parts):
        self.steps, self.rows, self.blocks, self.width = steps, rows, blocks, width
        self.bins, self.table_rows, self.parts = bins, table_rows, parts
        self.calls = 2 * blocks
        self.wide = round_up(bins, 32)
        self.held = round_up(table_rows, 16)
        self.stack = (self.wide + self.held, 2 * self.wide + self.held)
        self.depth = tuple(round_up(rows_in, LANES) for rows_in in self.stack)
        half = self.wide // 2
        self.value_at = self.calls * width
        self.sums_at = self.value_at + self.wide
        self.gain_row = steps
        self.reward_at = self.sums_at + round_up(steps + blocks, 16)
        self.small_at = self.reward_at + half
        self.cond_at = self.small_at + self.held
        self.shared_end = self.cond_at + self.held
        self.total = round_up(self.shared_end, 16 * parts)
        self.head_rows = self.cond_at - self.value_at


def forward_kernel(
    sizes, tower_ref,
    root_own, root_got, lengths, actions, codes, policy, value_bins, reward_bins,
    table_in, gains_own, gains_got, in_own, in_got, out_own, out_got,
    value_own, value_got, reward_in, small_in,
    lat, lat_own, lat_away, entry, after, slope, side, dlat, dlast, loss, head_grads,
    state, table, gains, w_in, w_out, heads0, heads1, flip0, flip1, acc0, acc1,
    logits0, logits1, cot0, cot1, sums,
):
    s = sizes
    step = pl.program_id(0)
    tower_id = tower_ref[0]
    rows, width, wide = s.rows, s.width, s.wide

    @pl.when(step == 0)
    def _():
        first = tower_id == 0
        state[:, 0 : width // 2] = jnp.where(first, root_own[...], root_got[...])
        state[:, width // 2 : width] = jnp.where(first, root_got[...], root_own[...])
        place_weights(tower_id, in_own, in_got, w_in)
        place_weights(tower_id, out_own, out_got, w_out)
        gains[...] = jnp.zeros_like(gains)
        gains[tower_id, 0 : s.blocks, :] = gains_own[...].astype(F32)
        gains[1 - tower_id, 0 : s.blocks, :] = gains_got[...].astype(F32)
        table[...] = jnp.zeros_like(table)
        table[0 : s.table_rows, :] = table_in[...]
        heads0[...] = jnp.zeros_like(heads0)
        heads1[...] = jnp.zeros_like(heads1)
        heads0[0 : s.bins, :] = jnp.where(first, value_own[...], value_got[...])
        heads1[0 : s.bins, :] = jnp.where(first, value_got[...], value_own[...])
        heads1[wide : wide + s.bins, :] = reward_in[...]
        heads0[wide : wide + s.table_rows, :] = small_in[...]
        heads1[2 * wide : 2 * wide + s.table_rows, :] = small_in[...]
        down = lax.broadcasted_iota(jnp.int32, (width, width), 0)
        across = lax.broadcasted_iota(jnp.int32, (width, width), 1)
        identity = jnp.where(down == across, 1.0, 0.0).astype(BF16)
        flip0[...] = by_lanes(identity, heads0[...]).astype(BF16)
        flip1[...] = by_lanes(identity, heads1[...]).astype(BF16)
        cot0[...] = jnp.zeros_like(cot0)
        cot1[...] = jnp.zeros_like(cot1)
        acc0[...] = jnp.zeros_like(acc0)
        acc1[...] = jnp.zeros_like(acc1)
        sums[...] = jnp.zeros_like(sums)
        loss[...] = jnp.zeros_like(loss)

    earlier = jnp.maximum(step - 1, 0)
    live_now = (step < lengths[...]).astype(F32)
    live_before = ((step - 1 < lengths[...]) & (step > 0)).astype(F32)
    action_now = actions[pl.ds(step, 1), :]
    code_now = codes[pl.ds(step, 1), :]
    kinds = jnp.concatenate(
        [live_now, action_now.astype(F32), code_now.astype(F32), jnp.zeros((5, rows), F32)], axis=0
    )
    columns = kinds.T
    live = columns[:, 0:1]
    eights = lax.broadcasted_iota(jnp.int32, (8, rows), 0)

    def heads(tower, latent, live_row, at_step, put):
        weights, flip, logits, cot, acc = (
            (heads0, flip0, logits0, cot0, acc0)
            if tower == 0
            else (heads1, flip1, logits1, cot1, acc1)
        )
        pick = lambda kind: kind[pl.ds(at_step, 1), :]
        value_goal = value_bins[pl.ds(at_step, 1), tower, :]
        spans = [(0, wide, 0, s.bins, value_goal)]
        if tower == 1:
            spans.append((wide, wide, 0, s.bins, pick(reward_bins)))
            spans.append((2 * wide, s.held, 0, ACTIONS, pick(policy)))
        else:
            spans.append((wide, s.held, ACTIONS, s.table_rows, pick(codes) + ACTIONS))
        pieces = []

        def make_logits(at, length):
            logits[at : at + length, :] = by_lanes(weights[at : at + length, :], latent())

        def eight_rows(value):
            return value.reshape(-1, 8, rows)

        def find_top(at, length, first, last, kept):
            for start in range(0, length, 8):
                if start < first or start + 8 > last:
                    inside = (eights >= first - start) & (eights < last - start)
                    place = slice(at + start, at + start + 8)
                    logits[place, :] = jnp.where(inside, logits[place, :], very_negative)
            top = functools.reduce(
                jnp.maximum,
                [
                    jnp.max(eight_rows(logits[at + start : at + stop, :]), axis=0)
                    for start, stop in cuts(length)
                ],
            )
            kept["top"] = jnp.max(top, axis=0, keepdims=True)

        def make_terms(at, length, goal, kept):
            total, picked = 0.0, 0.0
            for start, stop in cuts(length):
                place = slice(at + start, at + stop)
                value = logits[place, :]
                spot = lax.broadcasted_iota(jnp.int32, value.shape, 0)
                term = jnp.exp(value - kept["top"])
                logits[place, :] = term
                hit = spot == goal - start
                total += jnp.sum(eight_rows(term), axis=0)
                picked += jnp.sum(eight_rows(jnp.where(hit, value, 0.0)), axis=0)
            total = jnp.sum(total, axis=0, keepdims=True)
            picked = jnp.sum(picked, axis=0, keepdims=True)
            kept["scale"] = live_row / total
            loss[0:1, :] += live_row * (jnp.log(total) + kept["top"] - picked)

        def make_cotangent(at, length, goal, kept):
            for start, stop in cuts(length):
                place = slice(at + start, at + stop)
                term = logits[place, :]
                spot = lax.broadcasted_iota(jnp.int32, term.shape, 0)
                hit = spot == goal - start
                cot[place, :] = (
                    term * kept["scale"] - jnp.where(hit, live_row, 0.0)
                ).astype(BF16)

        def make_grads(at, length):
            acc[at : at + length, :] += natural(cot[at : at + length, :], latent())

        def make_latent():
            put(natural(flip[...], cot[...]).T)

        later = []
        for at, length, first, last, goal in spans:
            kept = {}
            pieces += [
                functools.partial(make_logits, at, length),
                functools.partial(find_top, at, length, first, last, kept),
                functools.partial(make_terms, at, length, goal, kept),
                functools.partial(make_cotangent, at, length, goal, kept),
            ]
            later.append(functools.partial(make_grads, at, length))
        return pieces + [make_latent] + later

    def tower_call(tower, x_in, code, done):
        kept = {}

        def begin():
            spot = lax.broadcasted_iota(jnp.int32, (rows, table.shape[0]), 1).astype(F32)
            onehot = jnp.where(spot == code, 1.0, 0.0).astype(BF16)
            kept["hidden"] = x_in().astype(F32) + natural(onehot, table[...])

        def into(block):
            place = tower * s.blocks + block
            hidden = kept["hidden"]
            inv_scale = inverse_rms(hidden)
            entry_rows = (hidden * inv_scale * gains[tower, block : block + 1, :]).astype(BF16)
            kept["u"] = natural(entry_rows, w_in[tower, block])
            entry[0, place] = entry_rows
            side[0, :, place : place + 1] = inv_scale

        def out_of(block):
            place = tower * s.blocks + block
            u = kept["u"]
            gate = 0.5 * jnp.tanh(0.5 * u) + 0.5
            after_rows = (u * gate).astype(BF16)
            branch = natural(after_rows, w_out[tower, block])
            hidden = kept["hidden"] + branch
            kept["hidden"] = hidden
            after[0, place] = after_rows
            slope[0, place] = gate * (1.0 + u * (1.0 - gate))
            spot = s.calls + 2 + 2 * place
            side[0, :, spot : spot + 1] = live * lane_sum(hidden * hidden)
            side[0, :, spot + 1 : spot + 2] = live * lane_sum(branch * branch)

        def finish():
            inv_scale = inverse_rms(kept["hidden"])
            spot = s.calls + tower
            side[0, :, spot : spot + 1] = inv_scale
            latent = (kept["hidden"] * inv_scale).astype(BF16)
            lat[0, tower] = latent
            done(latent)

        pieces = [begin]
        for block in range(s.blocks):
            pieces += [functools.partial(into, block), functools.partial(out_of, block)]
        return pieces + [finish]

    found = {"s": state[...]}

    def put_state(value):
        dlat[0, 1] = value

    def put_after(value):
        dlat[0, 0] = value

    def put_last(value):
        dlast[...] = value

    weave(
        tower_call(0, lambda: found["s"], columns[:, 1:2], lambda y: found.update(a=y)),
        heads(1, lambda: found["s"], live_before, earlier, put_state),
    )
    weave(
        tower_call(1, lambda: found["a"], columns[:, 2:3] + ACTIONS, lambda y: found.update(n=y)),
        heads(0, lambda: found["a"], live_now, step, put_after),
    )
    state[...] = found["n"]
    first = tower_id == 0
    lat_own[0] = jnp.where(first, found["a"], found["n"])
    lat_away[0] = jnp.where(first, found["n"], found["a"])
    side[0, :, SIDE - 1 : SIDE] = live
    sums[pl.ds(step, 1), 0:SIDE] = jnp.sum(side[0], axis=0, keepdims=True)

    @pl.when(step == s.steps - 1)
    def _():
        for piece in heads(1, lambda: found["n"], live_now, step, put_last):
            piece()
        half = wide // 2
        head_grads[...] = jnp.zeros_like(head_grads)
        head_grads[0, 0:wide, :] = acc0[0:wide, :].astype(BF16)
        head_grads[1, 0:wide, :] = acc1[0:wide, :].astype(BF16)
        small = acc0[wide : wide + s.held, :] + acc1[2 * wide : 2 * wide + s.held, :]
        at = s.small_at - s.value_at
        head_grads[0, at : at + s.held, :] = small.astype(BF16)
        for tower in range(2):
            put = s.reward_at - s.value_at
            at = wide + tower * half
            head_grads[tower, put : put + half, :] = acc1[at : at + half, :].astype(BF16)
            head_grads[tower, wide : wide + sums.shape[0], 0:LANES] = sums[...].astype(BF16)


def backward_kernel(
    sizes, tower_ref,
    lat, entry, after, slope, side, dlat, dlast, actions, codes,
    gains_own, gains_got, in_own, in_got, out_own, out_got, head_grads,
    own, away, root_own, root_away,
    carry, gain_sum, cond_sum, grads, gains, w_in, w_out,
):
    s = sizes
    turn = pl.program_id(0)
    step = s.steps - 1 - turn
    tower_id = tower_ref[0]
    blocks, width = s.blocks, s.width

    @pl.when(turn == 0)
    def _():
        place_weights(tower_id, in_own, in_got, w_in)
        place_weights(tower_id, out_own, out_got, w_out)
        gains[...] = jnp.ones_like(gains)
        gains[tower_id, 0:blocks, :] = gains_own[...].astype(F32)
        gains[1 - tower_id, 0:blocks, :] = gains_got[...].astype(F32)
        carry[...] = dlast[...]
        grads[...] = jnp.zeros_like(grads)
        gain_sum[...] = jnp.zeros_like(gain_sum)
        cond_sum[...] = jnp.zeros_like(cond_sum)

    def tower_back(tower, d_latent, code):
        normed = lat[0, tower].astype(F32)
        spot = s.calls + tower
        inv_scale = side[0, :, spot : spot + 1]
        d_hidden = inv_scale * (
            d_latent - normed * (lane_sum(d_latent * normed) * (1.0 / width))
        )
        for block in reversed(range(blocks)):
            place = tower * blocks + block
            gain = gains[tower, block : block + 1, :]
            entry_rows = entry[0, place]
            d_branch = d_hidden.astype(BF16)
            grads[tower, blocks + block] += by_rows(after[0, place], d_branch)
            d_after = by_lanes(d_branch, w_out[tower, block])
            d_before = (d_after * slope[0, place]).astype(BF16)
            grads[tower, block] += by_rows(entry_rows, d_before)
            d_entry = by_lanes(d_before, w_in[tower, block])
            entry_wide = entry_rows.astype(F32)
            product = d_entry * entry_wide
            gain_sum[tower, block : block + 1, :] += jnp.sum(product, axis=0, keepdims=True)
            mean = lane_sum(product) * (1.0 / width)
            inv_scale = side[0, :, place : place + 1]
            d_hidden = d_hidden + inv_scale * (
                d_entry * gain - (entry_wide / gain) * mean
            )
        spots = lax.broadcasted_iota(jnp.int32, (cond_sum.shape[0], d_hidden.shape[0]), 0)
        onehot = jnp.where(spots == code, 1.0, 0.0).astype(BF16)
        cond_sum[...] += natural(onehot, d_hidden.astype(BF16))
        return d_hidden

    d_after = tower_back(1, carry[...], codes[pl.ds(step, 1), :] + ACTIONS)
    d_state = tower_back(0, d_after + dlat[0, 0], actions[pl.ds(step, 1), :])
    carry[...] = d_state + dlat[0, 1]

    @pl.when(turn == s.steps - 1)
    def _():
        left = d_state[:, 0 : width // 2].astype(BF16)
        right = d_state[:, width // 2 : width].astype(BF16)
        root_own[...] = jnp.where(tower_id == 0, left, right)
        root_away[...] = jnp.where(tower_id == 0, right, left)
        gain_sum[...] = gain_sum[...] / gains[...]
        lines = lax.broadcasted_iota(jnp.int32, (s.reward_at - s.sums_at, width), 0)
        for target, which in ((own, tower_id), (away, 1 - tower_id)):
            for matrix in range(s.calls):
                at = matrix * width
                target[at : at + width, :] = grads[which, matrix].astype(BF16)
            target[s.value_at : s.cond_at, :] = head_grads[which]
            sums = head_grads[which, s.wide : s.wide + lines.shape[0], :].astype(F32)
            for block in range(blocks):
                gain = gain_sum[which, block : block + 1, :]
                sums = jnp.where(lines == s.gain_row + block, gain, sums)
            target[s.sums_at : s.reward_at, :] = sums.astype(BF16)
            here = jnp.where(which == 0, cond_sum[...], 0.0)
            target[s.cond_at : s.shared_end, :] = here.astype(BF16)
            if s.total > s.shared_end:
                target[s.shared_end :, :] = jnp.zeros((s.total - s.shared_end, width), BF16)


def logits_kernel(sizes, tower_ref, lat_own, lat_got, value_own, latents, logits):
    rows = sizes.rows
    tower_id = tower_ref[0]
    at_own = pl.ds(pl.multiple_of(tower_id * rows, rows), rows)
    at_got = pl.ds(pl.multiple_of((1 - tower_id) * rows, rows), rows)
    latents[0, at_own, :] = lat_own[0]
    latents[0, at_got, :] = lat_got[0]
    logits[0] = by_lanes(value_own[...], latents[0]).astype(BF16)


def add_and_split_kernel(count, digit_ref, *refs):
    inputs, outputs = refs[:count], refs[count:]
    digit = digit_ref[0]
    for other, target in enumerate(outputs):
        part = digit ^ other
        total = inputs[0][part].astype(F32)
        for source in inputs[1:]:
            total = total + source[part].astype(F32)
        target[...] = total.astype(BF16)


def in_order_kernel(digit_ref, *refs):
    digit = digit_ref[0]
    for other, source in enumerate(refs[:-1]):
        refs[-1][digit ^ other] = source[...]


def unpack_own_kernel(sizes, scalars, *refs):
    s = sizes
    factor = len(refs) - 8
    digit, tower_id = scalars[0], scalars[1]
    w_in, w_out, value, gain, rms, shared, flat, turned = refs[factor:]
    width = s.width
    length = refs[0].shape[0]
    for other, source in enumerate(refs[:factor]):
        at = pl.multiple_of((digit ^ other) * length, 16)
        flat[pl.ds(at, length), :] = source[...]
    for block in range(s.blocks):
        at = block * width
        w_in[block] = flat[at : at + width, :].astype(F32)
        at = (s.blocks + block) * width
        w_out[block] = flat[at : at + width, :].astype(F32)
    value[:, 0, :] = flat[s.value_at : s.sums_at, :].astype(F32)[0 : s.bins]
    shared[...] = flat[s.reward_at : s.shared_end, :]
    sums = flat[s.sums_at : s.reward_at, :].astype(F32)
    for block in range(s.blocks):
        gain[block] = sums[s.gain_row + block : s.gain_row + block + 1, :]
    turned[...] = sums[:, 0:LANES].T
    count = jnp.maximum(turned[SIDE - 1 : SIDE, 0 : s.steps], 1.0)
    spot = s.calls + 2 + tower_id * s.calls
    for block in range(s.blocks):
        for kind in range(2):
            square = turned[pl.ds(spot + 2 * block + kind, 1), 0 : s.steps]
            rms[block, kind : kind + 1, :] = jnp.sqrt(jnp.maximum(square, 0.0) / (count * width))


def unpack_shared_kernel(sizes, tower_ref, mine, got, reward, small, cond, joined):
    s = sizes
    tower_id = tower_ref[0]
    half = s.wide // 2
    joined[pl.ds(pl.multiple_of(tower_id * half, 8), half), :] = mine[0:half, :].astype(F32)
    joined[pl.ds(pl.multiple_of((1 - tower_id) * half, 8), half), :] = got[0:half, :].astype(F32)
    reward[...] = joined[0 : s.bins, :]
    for target, at in ((small, s.small_at), (cond, s.cond_at)):
        rows = slice(at - s.reward_at, at - s.reward_at + s.held)
        target[...] = (mine[rows, :].astype(F32) + got[rows, :].astype(F32))[0 : s.table_rows]


def whole(shape):
    return pl.BlockSpec(shape, lambda step, tower: (0,) * len(shape))


def per_step(*tail):
    return pl.BlockSpec((1,) + tail, lambda step, tower: (step,) + (0,) * len(tail))


def swap(value, axis, mask):
    pairs = [(source, source ^ mask) for source in range(lax.axis_size(axis))]
    return lax.ppermute(value, axis, pairs)


AXES = ("tower", "batch")


def exchange_rounds(batch_size):
    factors, left = [], batch_size
    while left > 1:
        factors.append(4 if left % 4 == 0 else 2)
        left //= factors[-1]
    rounds, stride = [], 1
    for factor in factors:
        rounds.append((factor, stride))
        stride *= factor
    turned = rounds[::-1] if len(set(factors)) == 1 else rounds
    return [(one[0], (one[1], two[1])) for one, two in zip(rounds, turned)]


def swap_within(value, strides, other, batch_size):
    pairs = [
        (tower * batch_size + index, tower * batch_size + (index ^ (other * strides[tower])))
        for tower in range(2)
        for index in range(batch_size)
    ]
    return lax.ppermute(value, AXES, pairs)


def my_digit(factor, strides):
    stride = jnp.where(lax.axis_index("tower") == 0, strides[0], strides[1])
    return (lax.axis_index("batch") // stride) % factor


def exchange(value, rounds, batch_size, beside, given, last_kernel):
    shape = jax.ShapeDtypeStruct
    held = value
    digits = []
    for factor, strides in rounds:
        digit = my_digit(factor, strides)
        digits.append(digit)
        rows, width = held[0].shape
        rows = rows // factor
        split = pl.pallas_call(
            functools.partial(add_and_split_kernel, len(held)),
            grid_spec=pltpu.PrefetchScalarGridSpec(
                num_scalar_prefetch=1,
                grid=(1,),
                in_specs=[whole((factor, rows, width))] * len(held),
                out_specs=[whole((rows, width))] * factor,
            ),
            out_shape=[shape((rows, width), BF16)] * factor,
            compiler_params=pltpu.CompilerParams(vmem_limit_bytes=VMEM_LIMIT // 2),
            name="add_and_split",
        )(digit[None], *[part.reshape(factor, rows, width) for part in held])
        first = len(digits) == 1
        if first:
            split, given = lax.optimization_barrier((split, given))
        held = [split[0]] + [
            swap_within(split[other], strides, other, batch_size) for other in range(1, factor)
        ]
        if first:
            done = beside(given)
            held, done = lax.optimization_barrier((held, done))
    piece = functools.reduce(jnp.add, [part.astype(F32) for part in held]).astype(BF16)
    for place in reversed(range(len(rounds))):
        factor, strides = rounds[place]
        rows, width = piece.shape
        held = [piece] + [
            swap_within(piece, strides, other, batch_size) for other in range(1, factor)
        ]
        if place == 0:
            return last_kernel(digits[0], held), done
        piece = pl.pallas_call(
            in_order_kernel,
            grid_spec=pltpu.PrefetchScalarGridSpec(
                num_scalar_prefetch=1,
                grid=(1,),
                in_specs=[whole((rows, width))] * factor,
                out_specs=whole((factor, rows, width)),
            ),
            out_shape=shape((factor, rows, width), BF16),
            compiler_params=pltpu.CompilerParams(vmem_limit_bytes=VMEM_LIMIT // 2),
            name="in_order",
        )(digits[place][None], *held).reshape(factor * rows, width)


def body(
    root_state, cond_table, block_gain, w_in, w_out, value_head, reward_head, small_head,
    unroll_len, actions, codes, policy_target, value_bins, reward_bins,
):
    tower_id = lax.axis_index("tower")
    other_id = 1 - tower_id
    tower_ref = tower_id.astype(jnp.int32)[None]
    steps, batch_rows = actions.shape
    blocks, width = block_gain.shape[1:]
    bins = value_head.shape[2]
    table_rows = cond_table.shape[0]
    rows = batch_rows // 2
    half = width // 2
    parts = lax.axis_size("batch")
    s = Sizes(steps, rows, blocks, width, bins, table_rows, parts)
    calls, wide = s.calls, s.wide

    root_mine = lax.dynamic_slice_in_dim(root_state, tower_id * rows, rows, 0)
    root_away = lax.dynamic_slice_in_dim(root_state, other_id * rows, rows, 0)
    root_got = swap(root_away, "tower", 1)
    in_own, out_own, gains_own = w_in[0], w_out[0], block_gain[0]
    value_own = value_head[0].T
    in_got = swap(in_own, "tower", 1)
    out_got = swap(out_own, "tower", 1)
    gains_got = swap(gains_own, "tower", 1)
    value_got = swap(value_own, "tower", 1)
    lengths = unroll_len.reshape(1, batch_rows)

    shape = jax.ShapeDtypeStruct
    params = pltpu.CompilerParams(vmem_limit_bytes=VMEM_LIMIT)
    products = steps * rows * (4 * blocks * width * width + 9 * width * wide)
    cost = pl.CostEstimate(flops=2 * products, bytes_accessed=40 * 2**20, transcendentals=0)
    mine = lambda *lead: pl.BlockSpec(
        lead + (rows,), lambda step, tower: (0,) * len(lead) + (tower[0],)
    )
    (
        lat, lat_own, lat_away, entry, after, slope, side, dlat, dlast, loss, head_grads,
    ) = pl.pallas_call(
        functools.partial(forward_kernel, s),
        grid_spec=pltpu.PrefetchScalarGridSpec(
            num_scalar_prefetch=1,
            grid=(steps,),
            in_specs=[
                whole((rows, half)),
                whole((rows, half)),
                mine(1),
                mine(steps),
                mine(steps),
                mine(steps),
                mine(steps, 2),
                mine(steps),
                whole((table_rows, width)),
                whole((blocks, width)),
                whole((blocks, width)),
                whole((blocks, width, width)),
                whole((blocks, width, width)),
                whole((blocks, width, width)),
                whole((blocks, width, width)),
                whole((bins, width)),
                whole((bins, width)),
                whole((bins, width)),
                whole((table_rows, width)),
            ],
            out_specs=[
                per_step(2, rows, width),
                per_step(rows, width),
                per_step(rows, width),
                per_step(calls, rows, width),
                per_step(calls, rows, width),
                per_step(calls, rows, width),
                per_step(rows, SIDE),
                per_step(2, rows, width),
                whole((rows, width)),
                whole((8, rows)),
                whole((2, s.head_rows, width)),
            ],
            scratch_shapes=[
                pltpu.VMEM((rows, width), BF16),
                pltpu.VMEM((LANES, width), BF16),
                pltpu.VMEM((2, 8, width), F32),
                pltpu.VMEM((2, blocks, width, width), BF16),
                pltpu.VMEM((2, blocks, width, width), BF16),
                pltpu.VMEM((s.depth[0], width), BF16),
                pltpu.VMEM((s.depth[1], width), BF16),
                pltpu.VMEM((width, s.depth[0]), BF16),
                pltpu.VMEM((width, s.depth[1]), BF16),
                pltpu.VMEM((s.stack[0], width), F32),
                pltpu.VMEM((s.stack[1], width), F32),
                pltpu.VMEM((s.stack[0], rows), F32),
                pltpu.VMEM((s.stack[1], rows), F32),
                pltpu.VMEM((s.depth[0], rows), BF16),
                pltpu.VMEM((s.depth[1], rows), BF16),
                pltpu.VMEM((s.reward_at - s.sums_at, LANES), F32),
            ],
        ),
        out_shape=[
            shape((steps, 2, rows, width), BF16),
            shape((steps, rows, width), BF16),
            shape((steps, rows, width), BF16),
            shape((steps, calls, rows, width), BF16),
            shape((steps, calls, rows, width), BF16),
            shape((steps, calls, rows, width), F32),
            shape((steps, rows, SIDE), F32),
            shape((steps, 2, rows, width), F32),
            shape((rows, width), F32),
            shape((8, rows), F32),
            shape((2, s.head_rows, width), BF16),
        ],
        compiler_params=params,
        cost_estimate=cost,
        name="unroll_forward",
    )(
        tower_ref, root_mine, root_got, lengths, actions, codes, policy_target,
        jnp.swapaxes(value_bins, 0, 1), reward_bins, cond_table, gains_own, gains_got, in_own, in_got, out_own, out_got,
        value_own, value_got, reward_head.T, small_head.T,
    )
    descending = lambda *tail: pl.BlockSpec(
        (1,) + tail, lambda step, tower: (steps - 1 - step,) + (0,) * len(tail)
    )
    own, away, root_own, root_away = pl.pallas_call(
        functools.partial(backward_kernel, s),
        grid_spec=pltpu.PrefetchScalarGridSpec(
            num_scalar_prefetch=1,
            grid=(steps,),
            in_specs=[
                descending(2, rows, width),
                descending(calls, rows, width),
                descending(calls, rows, width),
                descending(calls, rows, width),
                descending(rows, SIDE),
                descending(2, rows, width),
                whole((rows, width)),
                mine(steps),
                mine(steps),
                whole((blocks, width)),
                whole((blocks, width)),
                whole((blocks, width, width)),
                whole((blocks, width, width)),
                whole((blocks, width, width)),
                whole((blocks, width, width)),
                whole((2, s.head_rows, width)),
            ],
            out_specs=[
                whole((s.total, width)),
                whole((s.total, width)),
                whole((rows, half)),
                whole((rows, half)),
            ],
            scratch_shapes=[
                pltpu.VMEM((rows, width), F32),
                pltpu.VMEM((2, 16, width), F32),
                pltpu.VMEM((s.held, width), F32),
                pltpu.VMEM((2, calls, width, width), F32),
                pltpu.VMEM((2, 16, width), F32),
                pltpu.VMEM((2, blocks, width, width), BF16),
                pltpu.VMEM((2, blocks, width, width), BF16),
            ],
        ),
        out_shape=[
            shape((s.total, width), BF16),
            shape((s.total, width), BF16),
            shape((rows, half), BF16),
            shape((rows, half), BF16),
        ],
        compiler_params=params,
        cost_estimate=cost,
        name="unroll_backward",
    )(
        tower_ref, lat, entry, after, slope, side, dlat, dlast, actions, codes,
        gains_own, gains_got, in_own, in_got, out_own, out_got, head_grads,
    )
    got = swap(away, "tower", 1)

    def beside(given):
        lat_own, lat_away, loss, root_own, root_away = given
        lat_got = swap(lat_away, "tower", 1)
        loss_own = loss[0]
        loss_got = swap(loss_own, "tower", 1)
        root_got = swap(root_away, "tower", 1)

        latents, logits = pl.pallas_call(
            functools.partial(logits_kernel, s),
            grid_spec=pltpu.PrefetchScalarGridSpec(
                num_scalar_prefetch=1,
                grid=(steps,),
                in_specs=[per_step(rows, width), per_step(rows, width), whole((bins, width))],
                out_specs=[per_step(batch_rows, width), per_step(bins, batch_rows)],
            ),
            out_shape=[
                shape((steps, batch_rows, width), BF16),
                shape((steps, bins, batch_rows), BF16),
            ],
            compiler_params=params,
            cost_estimate=pl.CostEstimate(
                flops=2 * steps * batch_rows * width * wide, bytes_accessed=6 * 2**20, transcendentals=0
            ),
            name="latents_and_logits",
        )(tower_ref, lat_own, lat_got, value_own)

        def in_order(mine_value, got_value, axis):
            return jnp.where(
                tower_id == 0,
                jnp.concatenate([mine_value, got_value], axis=axis),
                jnp.concatenate([got_value, mine_value], axis=axis),
            )

        row_loss = in_order(loss_own, loss_got, 0)
        grad_root = in_order(root_own, root_got, 0).astype(F32)
        return latents, logits, row_loss, grad_root

    rounds = exchange_rounds(parts)

    def unpack(digit, held):
        scalars = jnp.stack([digit, tower_id]).astype(jnp.int32)
        shared_rows = s.shared_end - s.reward_at
        return pl.pallas_call(
            functools.partial(unpack_own_kernel, s),
            grid_spec=pltpu.PrefetchScalarGridSpec(
                num_scalar_prefetch=1,
                grid=(1,),
                in_specs=[whole(part.shape) for part in held],
                out_specs=[
                    whole((blocks, width, width)),
                    whole((blocks, width, width)),
                    whole((bins, 1, width)),
                    whole((blocks, 1, width)),
                    whole((blocks, 2, steps)),
                    whole((shared_rows, width)),
                ],
                scratch_shapes=[
                    pltpu.VMEM((s.total, width), BF16),
                    pltpu.VMEM((LANES, s.reward_at - s.sums_at), F32),
                ],
            ),
            out_shape=[
                shape((blocks, width, width), F32),
                shape((blocks, width, width), F32),
                shape((bins, 1, width), F32),
                shape((blocks, 1, width), F32),
                shape((blocks, 2, steps), F32),
                shape((shared_rows, width), BF16),
            ],
            compiler_params=params,
            name="unpack_own",
        )(scalars, *held)

    given = (lat_own, lat_away, loss, root_own, root_away)
    unpacked, done = exchange([own, got], rounds, parts, beside, given, unpack)
    grad_in, grad_out, value_t, gain_t, rms_t, shared = unpacked
    latents, logits, row_loss, grad_root = done
    shared_got = swap(shared, "tower", 1)
    reward_t, small_t, grad_cond = pl.pallas_call(
        functools.partial(unpack_shared_kernel, s),
        grid_spec=pltpu.PrefetchScalarGridSpec(
            num_scalar_prefetch=1,
            grid=(1,),
            in_specs=[whole(shared.shape), whole(shared.shape)],
            out_specs=[
                whole((bins, width)),
                whole((table_rows, width)),
                whole((table_rows, width)),
            ],
            scratch_shapes=[pltpu.VMEM((s.wide, width), F32)],
        ),
        out_shape=[
            shape((bins, width), F32),
            shape((table_rows, width), F32),
            shape((table_rows, width), F32),
        ],
        compiler_params=params,
        name="unpack_shared",
    )(tower_ref, shared, shared_got)
    layer_rms = jnp.transpose(rms_t, (2, 0, 1))[None]
    return (
        latents[None],
        jnp.swapaxes(logits, 1, 2)[None],
        row_loss,
        layer_rms,
        grad_root,
        grad_cond,
        jnp.swapaxes(gain_t, 0, 1),
        grad_in[None],
        grad_out[None],
        jnp.transpose(value_t, (1, 2, 0)),
        reward_t.T,
        small_t.T,
    )


def solution(mesh):
    placed = (
        P("batch", "tower"),
        P(),
        P("tower", None, None),
        P("tower", None, None, None),
        P("tower", None, None, None),
        P("tower", None, None),
        P(),
        P(),
        P("batch"),
        P(None, "batch"),
        P(None, "batch"),
        P(None, "batch"),
        P(None, None, "batch"),
        P(None, "batch"),
    )
    return jax.shard_map(
        body,
        mesh=mesh,
        in_specs=placed,
        out_specs=(
            P("tower", None, "batch", None),
            P("tower", None, "batch", None),
            P("batch"),
            P("tower", None, None, None),
            P("batch", "tower"),
            P(),
            P("tower", None, None),
            P("tower", None, None, None),
            P("tower", None, None, None),
            P("tower", None, None),
            P(),
            P(),
        ),
        check_vma=False,
    )
```

```python
import functools

import jax
import jax.numpy as jnp
from jax import lax
from jax.experimental import pallas as pl
from jax.experimental.pallas import tpu as pltpu
from jax.sharding import PartitionSpec as P

ACTIONS = 4
LANES = 128
VMEM_LIMIT = 56 * 1024 * 1024
epsilon = 1e-06
very_negative = -1e30
F32 = jnp.float32
BF16 = jnp.bfloat16


def natural(left, right):
    return lax.dot_general(left, right, (((1,), (0,)), ((), ())), preferred_element_type=F32)


def by_rows(left, right):
    return lax.dot_general(left, right, (((0,), (0,)), ((), ())), preferred_element_type=F32)


def by_lanes(left, right):
    return lax.dot_general(left, right, (((1,), (1,)), ((), ())), preferred_element_type=F32)


def round_up(value, unit):
    return (value + unit - 1) // unit * unit


def lane_sum(value):
    return jnp.sum(value, axis=-1, keepdims=True)


def inverse_rms(hidden):
    return lax.rsqrt(lane_sum(hidden * hidden) * (1.0 / hidden.shape[-1]) + epsilon)


def weave(*tasks):
    tasks = [(list(task)) for task in tasks]
    longest = max(len(task) for task in tasks)
    done = [0] * len(tasks)
    for turn in range(longest):
        for which, task in enumerate(tasks):
            until = (turn + 1) * len(task) // longest
            while done[which] < until:
                task[done[which]]()
                done[which] += 1


def place_weights(tower_id, own, got, held):
    held[tower_id] = own[...]
    held[1 - tower_id] = got[...]


def cuts(length, unit=160):
    return [(start, min(start + unit, length)) for start in range(0, length, unit)]


class Sizes:
    def __init__(self, steps, rows, blocks, width, bins, table_rows, parts):
        self.steps, self.rows, self.blocks, self.width = steps, rows, blocks, width
        self.bins, self.table_rows, self.parts = bins, table_rows, parts
        self.calls = 2 * blocks
        self.wide = round_up(bins, 32)
        self.held = round_up(table_rows, 16)
        self.stack = (self.wide + self.held, 2 * self.wide + self.held)
        self.depth = tuple(round_up(rows_in, LANES) for rows_in in self.stack)
        half = self.wide // 2
        self.value_at = self.calls * width
        self.sums_at = self.value_at + self.wide
        self.kinds = 2 * self.calls
        self.gain_row = self.kinds + 1
        self.reward_at = self.sums_at + round_up(self.gain_row + blocks, 16)
        self.small_at = self.reward_at + half
        self.cond_at = self.small_at + self.held
        self.shared_end = self.cond_at + self.held
        self.total = round_up(self.shared_end, 16 * parts)
        self.head_rows = self.cond_at - self.value_at


def forward_kernel(
    sizes, tower_ref,
    root_own, root_got, lengths, actions, codes, policy, value_bins, reward_bins,
    table_in, gains_own, gains_got, in_own, in_got, out_own, out_got,
    value_own, value_got, reward_in, small_in,
    lat, lat_own, lat_away, entry, after, slope, side, dlat, dlast, loss, head_grads,
    state, table, gains, w_in, w_out, heads0, heads1, flip0, flip1, acc0, acc1,
    logits0, logits1, cot0, cot1, sums, squares,
):
    s = sizes
    step = pl.program_id(0)
    tower_id = tower_ref[0]
    rows, width, wide = s.rows, s.width, s.wide

    @pl.when(step == 0)
    def _():
        first = tower_id == 0
        state[:, 0 : width // 2] = jnp.where(first, root_own[...], root_got[...])
        state[:, width // 2 : width] = jnp.where(first, root_got[...], root_own[...])
        place_weights(tower_id, in_own, in_got, w_in)
        place_weights(tower_id, out_own, out_got, w_out)
        gains[...] = jnp.zeros_like(gains)
        gains[tower_id, 0 : s.blocks, :] = gains_own[...].astype(F32)
        gains[1 - tower_id, 0 : s.blocks, :] = gains_got[...].astype(F32)
        table[...] = jnp.zeros_like(table)
        table[0 : s.table_rows, :] = table_in[...]
        heads0[...] = jnp.zeros_like(heads0)
        heads1[...] = jnp.zeros_like(heads1)
        heads0[0 : s.bins, :] = jnp.where(first, value_own[...], value_got[...])
        heads1[0 : s.bins, :] = jnp.where(first, value_got[...], value_own[...])
        heads1[wide : wide + s.bins, :] = reward_in[...]
        heads0[wide : wide + s.table_rows, :] = small_in[...]
        heads1[2 * wide : 2 * wide + s.table_rows, :] = small_in[...]
        down = lax.broadcasted_iota(jnp.int32, (width, width), 0)
        across = lax.broadcasted_iota(jnp.int32, (width, width), 1)
        identity = jnp.where(down == across, 1.0, 0.0).astype(BF16)
        flip0[...] = by_lanes(identity, heads0[...]).astype(BF16)
        flip1[...] = by_lanes(identity, heads1[...]).astype(BF16)
        cot0[...] = jnp.zeros_like(cot0)
        cot1[...] = jnp.zeros_like(cot1)
        acc0[...] = jnp.zeros_like(acc0)
        acc1[...] = jnp.zeros_like(acc1)
        sums[...] = jnp.zeros_like(sums)
        squares[...] = jnp.zeros_like(squares)
        loss[...] = jnp.zeros_like(loss)

    earlier = jnp.maximum(step - 1, 0)
    live_now = (step < lengths[...]).astype(F32)
    live_before = ((step - 1 < lengths[...]) & (step > 0)).astype(F32)
    action_now = actions[pl.ds(step, 1), :]
    code_now = codes[pl.ds(step, 1), :]
    kinds = jnp.concatenate(
        [live_now, action_now.astype(F32), code_now.astype(F32), jnp.zeros((5, rows), F32)], axis=0
    )
    columns = kinds.T
    live = columns[:, 0:1]
    eights = lax.broadcasted_iota(jnp.int32, (8, rows), 0)

    def heads(tower, latent, live_row, at_step, put):
        weights, flip, logits, cot, acc = (
            (heads0, flip0, logits0, cot0, acc0)
            if tower == 0
            else (heads1, flip1, logits1, cot1, acc1)
        )
        pick = lambda kind: kind[pl.ds(at_step, 1), :]
        value_goal = value_bins[pl.ds(at_step, 1), tower, :]
        spans = [(0, wide, 0, s.bins, value_goal)]
        if tower == 1:
            spans.append((wide, wide, 0, s.bins, pick(reward_bins)))
            spans.append((2 * wide, s.held, 0, ACTIONS, pick(policy)))
        else:
            spans.append((wide, s.held, ACTIONS, s.table_rows, pick(codes) + ACTIONS))
        pieces = []

        def make_logits(at, length):
            logits[at : at + length, :] = by_lanes(weights[at : at + length, :], latent())

        def eight_rows(value):
            return value.reshape(-1, 8, rows)

        def mask(at, length, first, last):
            for start in range(0, length, 8):
                if start < first or start + 8 > last:
                    inside = (eights >= first - start) & (eights < last - start)
                    place = slice(at + start, at + start + 8)
                    logits[place, :] = jnp.where(inside, logits[place, :], very_negative)

        def find_top(at, start, stop, kept):
            top = jnp.max(eight_rows(logits[at + start : at + stop, :]), axis=0)
            kept["top"] = jnp.maximum(kept["top"], top) if "top" in kept else top

        def end_top(kept):
            kept["top"] = jnp.max(kept["top"], axis=0, keepdims=True)

        def make_terms(at, start, stop, goal, kept):
            place = slice(at + start, at + stop)
            value = logits[place, :]
            spot = lax.broadcasted_iota(jnp.int32, value.shape, 0)
            term = jnp.exp(value - kept["top"])
            logits[place, :] = term
            hit = spot == goal - start
            total = jnp.sum(eight_rows(term), axis=0)
            picked = jnp.sum(eight_rows(jnp.where(hit, value, 0.0)), axis=0)
            kept["total"] = kept["total"] + total if "total" in kept else total
            kept["picked"] = kept["picked"] + picked if "picked" in kept else picked

        def end_terms(kept):
            total = jnp.sum(kept["total"], axis=0, keepdims=True)
            picked = jnp.sum(kept["picked"], axis=0, keepdims=True)
            kept["scale"] = live_row / total
            loss[0:1, :] += live_row * (jnp.log(total) + kept["top"] - picked)

        def make_cotangent(at, start, stop, goal, kept):
            place = slice(at + start, at + stop)
            term = logits[place, :]
            spot = lax.broadcasted_iota(jnp.int32, term.shape, 0)
            hit = spot == goal - start
            cot[place, :] = (term * kept["scale"] - jnp.where(hit, live_row, 0.0)).astype(BF16)

        def make_grads(at, start, stop):
            place = slice(at + start, at + stop)
            acc[place, :] += natural(cot[place, :], latent())

        def make_latent():
            put(natural(flip[...], cot[...]).T)

        later = []
        for at, length, first, last, goal in spans:
            kept = {}
            each = cuts(length)
            pieces.append(functools.partial(make_logits, at, length))
            pieces.append(functools.partial(mask, at, length, first, last))
            pieces += [functools.partial(find_top, at, *cut, kept) for cut in each]
            pieces.append(functools.partial(end_top, kept))
            pieces += [functools.partial(make_terms, at, *cut, goal, kept) for cut in each]
            pieces.append(functools.partial(end_terms, kept))
            pieces += [functools.partial(make_cotangent, at, *cut, goal, kept) for cut in each]
            later += [functools.partial(make_grads, at, *cut) for cut in each]
        return pieces + [make_latent] + later

    def tower_call(tower, x_in, code, done):
        kept = {}

        def begin():
            spot = lax.broadcasted_iota(jnp.int32, (rows, table.shape[0]), 1).astype(F32)
            onehot = jnp.where(spot == code, 1.0, 0.0).astype(BF16)
            kept["hidden"] = x_in().astype(F32) + natural(onehot, table[...])

        def scale_rows():
            row_squares = lane_sum(kept["hidden"] * kept["hidden"])
            return row_squares, lax.rsqrt(row_squares * (1.0 / width) + epsilon)

        def keep_squares(block, row_squares):
            place = 2 * (tower * s.blocks + block)
            total = jnp.sum(live * row_squares, axis=0, keepdims=True) * (1.0 / LANES)
            squares[place : place + 1, 0:LANES] = jnp.broadcast_to(total, (1, LANES))

        def into(block):
            place = tower * s.blocks + block
            gained = kept["hidden"] * gains[tower, block : block + 1, :]
            product = natural(gained.astype(BF16), w_in[tower, block])
            row_squares, inv_scale = scale_rows()
            kept["u"] = product * inv_scale
            entry[0, place] = (gained * inv_scale).astype(BF16)
            side[0, place] = jnp.broadcast_to(inv_scale, (rows, LANES))
            if block > 0:
                keep_squares(block - 1, row_squares)

        def out_of(block):
            place = tower * s.blocks + block
            u = kept["u"]
            gate = 0.5 * jnp.tanh(0.5 * u) + 0.5
            after_rows = (u * gate).astype(BF16)
            branch = natural(after_rows, w_out[tower, block])
            kept["hidden"] = kept["hidden"] + branch
            after[0, place] = after_rows
            slope[0, place] = gate * (1.0 + u * (1.0 - gate))
            spot = 2 * place + 1
            squares[spot : spot + 1, :] = jnp.sum(
                branch * branch * live, axis=0, keepdims=True
            )

        def finish():
            row_squares, inv_scale = scale_rows()
            side[0, s.calls + tower] = jnp.broadcast_to(inv_scale, (rows, LANES))
            latent = (kept["hidden"] * inv_scale).astype(BF16)
            lat[0, tower] = latent
            keep_squares(s.blocks - 1, row_squares)
            done(latent)

        pieces = [begin]
        for block in range(s.blocks):
            pieces += [functools.partial(into, block), functools.partial(out_of, block)]
        return pieces + [finish]

    found = {"s": state[...]}

    def put_state(value):
        dlat[0, 1] = value

    def put_after(value):
        dlat[0, 0] = value

    def put_last(value):
        dlast[...] = value

    chain = tower_call(0, lambda: found["s"], columns[:, 1:2], lambda y: found.update(a=y))
    chain += tower_call(
        1, lambda: found["a"], columns[:, 2:3] + ACTIONS, lambda y: found.update(n=y)
    )
    weave(
        chain,
        heads(1, lambda: found["s"], live_before, earlier, put_state)
        + heads(0, lambda: found["a"], live_now, step, put_after),
    )
    state[...] = found["n"]
    first = tower_id == 0
    lat_own[0] = jnp.where(first, found["a"], found["n"])
    lat_away[0] = jnp.where(first, found["n"], found["a"])
    total = jnp.sum(live, axis=0, keepdims=True) * (1.0 / LANES)
    squares[s.kinds : s.kinds + 1, 0:LANES] = jnp.broadcast_to(total, (1, LANES))
    at_lane = lax.broadcasted_iota(jnp.int32, sums.shape, 1) == step
    sums[...] = jnp.where(at_lane, lane_sum(squares[...]), sums[...])

    @pl.when(step == s.steps - 1)
    def _():
        for piece in heads(1, lambda: found["n"], live_now, step, put_last):
            piece()
        half = wide // 2
        head_grads[...] = jnp.zeros_like(head_grads)
        head_grads[0, 0:wide, :] = acc0[0:wide, :].astype(BF16)
        head_grads[1, 0:wide, :] = acc1[0:wide, :].astype(BF16)
        small = acc0[wide : wide + s.held, :] + acc1[2 * wide : 2 * wide + s.held, :]
        at = s.small_at - s.value_at
        head_grads[0, at : at + s.held, :] = small.astype(BF16)
        for tower in range(2):
            put = s.reward_at - s.value_at
            at = wide + tower * half
            head_grads[tower, put : put + half, :] = acc1[at : at + half, :].astype(BF16)
            head_grads[tower, wide : wide + sums.shape[0], 0:LANES] = sums[...].astype(BF16)


def backward_kernel(
    sizes, tower_ref,
    lat, entry, after, slope, side, dlat, dlast, actions, codes,
    gains_own, gains_got, in_own, in_got, out_own, out_got, head_grads,
    own, away, root_own, root_away,
    carry, gain_sum, cond_sum, grads, gains, inverse_gains, w_in, w_out,
):
    s = sizes
    turn = pl.program_id(0)
    step = s.steps - 1 - turn
    tower_id = tower_ref[0]
    blocks, width = s.blocks, s.width

    @pl.when(turn == 0)
    def _():
        place_weights(tower_id, in_own, in_got, w_in)
        place_weights(tower_id, out_own, out_got, w_out)
        gains[...] = jnp.ones_like(gains)
        gains[tower_id, 0:blocks, :] = gains_own[...].astype(F32)
        gains[1 - tower_id, 0:blocks, :] = gains_got[...].astype(F32)
        inverse_gains[...] = 1.0 / gains[...]
        carry[...] = dlast[...]
        grads[...] = jnp.zeros_like(grads)
        gain_sum[...] = jnp.zeros_like(gain_sum)
        cond_sum[...] = jnp.zeros_like(cond_sum)

    def over_lanes(column):
        return jnp.concatenate([column] * (width // LANES), axis=1)

    def tower_back(tower, d_latent, code):
        normed = lat[0, tower]
        normed_wide = normed.astype(F32)
        inv_scale = over_lanes(side[0, s.calls + tower])
        base = inv_scale * d_latent
        slant = inv_scale * (lane_sum(d_latent * normed_wide) * (1.0 / width))
        for block in reversed(range(blocks)):
            place = tower * blocks + block
            gain = gains[tower, block : block + 1, :]
            entry_rows = entry[0, place]
            entry_wide = entry_rows.astype(F32)
            inv_scale = over_lanes(side[0, place])
            beside = by_lanes(normed, w_out[tower, block])
            d_after = by_lanes(base.astype(BF16), w_out[tower, block]) - slant * beside
            d_hidden = base - slant * normed_wide
            d_before = (d_after * slope[0, place]).astype(BF16)
            d_entry = by_lanes(d_before, w_in[tower, block])
            grads[tower, blocks + block] += by_rows(after[0, place], d_hidden.astype(BF16))
            grads[tower, block] += by_rows(entry_rows, d_before)
            product = d_entry * entry_wide
            gain_sum[tower, block : block + 1, :] += jnp.sum(product, axis=0, keepdims=True)
            base = d_hidden + inv_scale * (d_entry * gain)
            slant = inv_scale * (lane_sum(product) * (1.0 / width))
            normed_wide = entry_wide * inverse_gains[tower, block : block + 1, :]
            normed = normed_wide.astype(BF16)
        d_hidden = base - slant * normed_wide
        spots = lax.broadcasted_iota(jnp.int32, (cond_sum.shape[0], d_hidden.shape[0]), 0)
        onehot = jnp.where(spots == code, 1.0, 0.0).astype(BF16)
        cond_sum[...] += natural(onehot, d_hidden.astype(BF16))
        return d_hidden

    d_after = tower_back(1, carry[...], codes[pl.ds(step, 1), :] + ACTIONS)
    d_state = tower_back(0, d_after + dlat[0, 0], actions[pl.ds(step, 1), :])
    carry[...] = d_state + dlat[0, 1]

    @pl.when(turn == s.steps - 1)
    def _():
        left = d_state[:, 0 : width // 2].astype(BF16)
        right = d_state[:, width // 2 : width].astype(BF16)
        root_own[...] = jnp.where(tower_id == 0, left, right)
        root_away[...] = jnp.where(tower_id == 0, right, left)
        gain_sum[...] = gain_sum[...] * inverse_gains[...]
        lines = lax.broadcasted_iota(jnp.int32, (s.reward_at - s.sums_at, width), 0)
        for target, which in ((own, tower_id), (away, 1 - tower_id)):
            for matrix in range(s.calls):
                at = matrix * width
                target[at : at + width, :] = grads[which, matrix].astype(BF16)
            target[s.value_at : s.cond_at, :] = head_grads[which]
            sums = head_grads[which, s.wide : s.wide + lines.shape[0], :].astype(F32)
            for block in range(blocks):
                gain = gain_sum[which, block : block + 1, :]
                sums = jnp.where(lines == s.gain_row + block, gain, sums)
            target[s.sums_at : s.reward_at, :] = sums.astype(BF16)
            here = jnp.where(which == 0, cond_sum[...], 0.0)
            target[s.cond_at : s.shared_end, :] = here.astype(BF16)
            if s.total > s.shared_end:
                target[s.shared_end :, :] = jnp.zeros((s.total - s.shared_end, width), BF16)


def logits_kernel(sizes, tower_ref, lat_own, lat_got, value_own, latents, logits):
    rows = sizes.rows
    tower_id = tower_ref[0]
    at_own = pl.ds(pl.multiple_of(tower_id * rows, rows), rows)
    at_got = pl.ds(pl.multiple_of((1 - tower_id) * rows, rows), rows)
    latents[0, at_own, :] = lat_own[0]
    latents[0, at_got, :] = lat_got[0]
    logits[0] = by_lanes(value_own[...], latents[0]).astype(BF16)


def add_and_split_kernel(count, digit_ref, *refs):
    inputs, outputs = refs[:count], refs[count:]
    digit = digit_ref[0]
    for other, target in enumerate(outputs):
        part = digit ^ other
        total = inputs[0][part].astype(F32)
        for source in inputs[1:]:
            total = total + source[part].astype(F32)
        target[...] = total.astype(BF16)


def in_order_kernel(digit_ref, *refs):
    digit = digit_ref[0]
    for other, source in enumerate(refs[:-1]):
        refs[-1][digit ^ other] = source[...]


def unpack_own_kernel(sizes, scalars, *refs):
    s = sizes
    factor = len(refs) - 8
    digit, tower_id = scalars[0], scalars[1]
    w_in, w_out, value, gain, rms, shared, flat, held = refs[factor:]
    width = s.width
    length = refs[0].shape[0]
    for other, source in enumerate(refs[:factor]):
        at = pl.multiple_of((digit ^ other) * length, 16)
        flat[pl.ds(at, length), :] = source[...]
    for block in range(s.blocks):
        at = block * width
        w_in[block] = flat[at : at + width, :].astype(F32)
        at = (s.blocks + block) * width
        w_out[block] = flat[at : at + width, :].astype(F32)
    value[:, 0, :] = flat[s.value_at : s.sums_at, :].astype(F32)[0 : s.bins]
    shared[...] = flat[s.reward_at : s.shared_end, :]
    sums = flat[s.sums_at : s.reward_at, :].astype(F32)
    for block in range(s.blocks):
        gain[block] = sums[s.gain_row + block : s.gain_row + block + 1, :]
    held[...] = sums[:, 0:LANES]
    count = jnp.maximum(held[s.kinds : s.kinds + 1, 0 : s.steps], 1.0)
    for block in range(s.blocks):
        for kind in range(2):
            spot = tower_id * s.calls + 2 * block + kind
            square = held[pl.ds(spot, 1), 0 : s.steps]
            rms[block, kind : kind + 1, :] = jnp.sqrt(jnp.maximum(square, 0.0) / (count * width))


def unpack_shared_kernel(sizes, tower_ref, mine, got, reward, small, cond, joined):
    s = sizes
    tower_id = tower_ref[0]
    half = s.wide // 2
    joined[pl.ds(pl.multiple_of(tower_id * half, 8), half), :] = mine[0:half, :].astype(F32)
    joined[pl.ds(pl.multiple_of((1 - tower_id) * half, 8), half), :] = got[0:half, :].astype(F32)
    reward[...] = joined[0 : s.bins, :]
    for target, at in ((small, s.small_at), (cond, s.cond_at)):
        rows = slice(at - s.reward_at, at - s.reward_at + s.held)
        target[...] = (mine[rows, :].astype(F32) + got[rows, :].astype(F32))[0 : s.table_rows]


def whole(shape):
    return pl.BlockSpec(shape, lambda step, tower: (0,) * len(shape))


def per_step(*tail):
    return pl.BlockSpec((1,) + tail, lambda step, tower: (step,) + (0,) * len(tail))


def swap(value, axis, mask):
    pairs = [(source, source ^ mask) for source in range(lax.axis_size(axis))]
    return lax.ppermute(value, axis, pairs)


AXES = ("tower", "batch")


def exchange_rounds(batch_size):
    factors, left = [], batch_size
    while left > 1:
        factors.append(4 if left % 4 == 0 else 2)
        left //= factors[-1]
    rounds, stride = [], 1
    for factor in factors:
        rounds.append((factor, stride))
        stride *= factor
    turned = rounds[::-1] if len(set(factors)) == 1 else rounds
    return [(one[0], (one[1], two[1])) for one, two in zip(rounds, turned)]


def swap_within(value, strides, other, batch_size):
    pairs = [
        (tower * batch_size + index, tower * batch_size + (index ^ (other * strides[tower])))
        for tower in range(2)
        for index in range(batch_size)
    ]
    return lax.ppermute(value, AXES, pairs)


def my_digit(factor, strides):
    stride = jnp.where(lax.axis_index("tower") == 0, strides[0], strides[1])
    return (lax.axis_index("batch") // stride) % factor


def exchange(value, rounds, batch_size, beside, given, last_kernel):
    shape = jax.ShapeDtypeStruct
    held = value
    digits = []
    for factor, strides in rounds:
        digit = my_digit(factor, strides)
        digits.append(digit)
        rows, width = held[0].shape
        rows = rows // factor
        split = pl.pallas_call(
            functools.partial(add_and_split_kernel, len(held)),
            grid_spec=pltpu.PrefetchScalarGridSpec(
                num_scalar_prefetch=1,
                grid=(1,),
                in_specs=[whole((factor, rows, width))] * len(held),
                out_specs=[whole((rows, width))] * factor,
            ),
            out_shape=[shape((rows, width), BF16)] * factor,
            compiler_params=pltpu.CompilerParams(vmem_limit_bytes=VMEM_LIMIT // 2),
            name="add_and_split",
        )(digit[None], *[part.reshape(factor, rows, width) for part in held])
        first = len(digits) == 1
        if first:
            split, given = lax.optimization_barrier((split, given))
        held = [split[0]] + [
            swap_within(split[other], strides, other, batch_size) for other in range(1, factor)
        ]
        if first:
            done = beside(given)
            held, done = lax.optimization_barrier((held, done))
    piece = functools.reduce(jnp.add, [part.astype(F32) for part in held]).astype(BF16)
    for place in reversed(range(len(rounds))):
        factor, strides = rounds[place]
        rows, width = piece.shape
        held = [piece] + [
            swap_within(piece, strides, other, batch_size) for other in range(1, factor)
        ]
        if place == 0:
            return last_kernel(digits[0], held), done
        piece = pl.pallas_call(
            in_order_kernel,
            grid_spec=pltpu.PrefetchScalarGridSpec(
                num_scalar_prefetch=1,
                grid=(1,),
                in_specs=[whole((rows, width))] * factor,
                out_specs=whole((factor, rows, width)),
            ),
            out_shape=shape((factor, rows, width), BF16),
            compiler_params=pltpu.CompilerParams(vmem_limit_bytes=VMEM_LIMIT // 2),
            name="in_order",
        )(digits[place][None], *held).reshape(factor * rows, width)


def body(
    root_state, cond_table, block_gain, w_in, w_out, value_head, reward_head, small_head,
    unroll_len, actions, codes, policy_target, value_bins, reward_bins,
):
    tower_id = lax.axis_index("tower")
    other_id = 1 - tower_id
    tower_ref = tower_id.astype(jnp.int32)[None]
    steps, batch_rows = actions.shape
    blocks, width = block_gain.shape[1:]
    bins = value_head.shape[2]
    table_rows = cond_table.shape[0]
    rows = batch_rows // 2
    half = width // 2
    parts = lax.axis_size("batch")
    s = Sizes(steps, rows, blocks, width, bins, table_rows, parts)
    calls, wide = s.calls, s.wide

    root_mine = lax.dynamic_slice_in_dim(root_state, tower_id * rows, rows, 0)
    root_away = lax.dynamic_slice_in_dim(root_state, other_id * rows, rows, 0)
    root_got = swap(root_away, "tower", 1)
    in_own, out_own, gains_own = w_in[0], w_out[0], block_gain[0]
    value_own = value_head[0].T
    in_got = swap(in_own, "tower", 1)
    out_got = swap(out_own, "tower", 1)
    gains_got = swap(gains_own, "tower", 1)
    value_got = swap(value_own, "tower", 1)
    lengths = unroll_len.reshape(1, batch_rows)

    shape = jax.ShapeDtypeStruct
    params = pltpu.CompilerParams(vmem_limit_bytes=VMEM_LIMIT)
    products = steps * rows * (4 * blocks * width * width + 9 * width * wide)
    cost = pl.CostEstimate(flops=2 * products, bytes_accessed=40 * 2**20, transcendentals=0)
    mine = lambda *lead: pl.BlockSpec(
        lead + (rows,), lambda step, tower: (0,) * len(lead) + (tower[0],)
    )
    (
        lat, lat_own, lat_away, entry, after, slope, side, dlat, dlast, loss, head_grads,
    ) = pl.pallas_call(
        functools.partial(forward_kernel, s),
        grid_spec=pltpu.PrefetchScalarGridSpec(
            num_scalar_prefetch=1,
            grid=(steps,),
            in_specs=[
                whole((rows, half)),
                whole((rows, half)),
                mine(1),
                mine(steps),
                mine(steps),
                mine(steps),
                mine(steps, 2),
                mine(steps),
                whole((table_rows, width)),
                whole((blocks, width)),
                whole((blocks, width)),
                whole((blocks, width, width)),
                whole((blocks, width, width)),
                whole((blocks, width, width)),
                whole((blocks, width, width)),
                whole((bins, width)),
                whole((bins, width)),
                whole((bins, width)),
                whole((table_rows, width)),
            ],
            out_specs=[
                per_step(2, rows, width),
                per_step(rows, width),
                per_step(rows, width),
                per_step(calls, rows, width),
                per_step(calls, rows, width),
                per_step(calls, rows, width),
                per_step(calls + 2, rows, LANES),
                per_step(2, rows, width),
                whole((rows, width)),
                whole((8, rows)),
                whole((2, s.head_rows, width)),
            ],
            scratch_shapes=[
                pltpu.VMEM((rows, width), BF16),
                pltpu.VMEM((LANES, width), BF16),
                pltpu.VMEM((2, 8, width), F32),
                pltpu.VMEM((2, blocks, width, width), BF16),
                pltpu.VMEM((2, blocks, width, width), BF16),
                pltpu.VMEM((s.depth[0], width), BF16),
                pltpu.VMEM((s.depth[1], width), BF16),
                pltpu.VMEM((width, s.depth[0]), BF16),
                pltpu.VMEM((width, s.depth[1]), BF16),
                pltpu.VMEM((s.stack[0], width), F32),
                pltpu.VMEM((s.stack[1], width), F32),
                pltpu.VMEM((s.stack[0], rows), F32),
                pltpu.VMEM((s.stack[1], rows), F32),
                pltpu.VMEM((s.depth[0], rows), BF16),
                pltpu.VMEM((s.depth[1], rows), BF16),
                pltpu.VMEM((s.reward_at - s.sums_at, LANES), F32),
                pltpu.VMEM((s.reward_at - s.sums_at, width), F32),
            ],
        ),
        out_shape=[
            shape((steps, 2, rows, width), BF16),
            shape((steps, rows, width), BF16),
            shape((steps, rows, width), BF16),
            shape((steps, calls, rows, width), BF16),
            shape((steps, calls, rows, width), BF16),
            shape((steps, calls, rows, width), F32),
            shape((steps, calls + 2, rows, LANES), F32),
            shape((steps, 2, rows, width), F32),
            shape((rows, width), F32),
            shape((8, rows), F32),
            shape((2, s.head_rows, width), BF16),
        ],
        compiler_params=params,
        cost_estimate=cost,
        name="unroll_forward",
    )(
        tower_ref, root_mine, root_got, lengths, actions, codes, policy_target,
        jnp.swapaxes(value_bins, 0, 1), reward_bins, cond_table, gains_own, gains_got, in_own, in_got, out_own, out_got,
        value_own, value_got, reward_head.T, small_head.T,
    )
    descending = lambda *tail: pl.BlockSpec(
        (1,) + tail, lambda step, tower: (steps - 1 - step,) + (0,) * len(tail)
    )
    own, away, root_own, root_away = pl.pallas_call(
        functools.partial(backward_kernel, s),
        grid_spec=pltpu.PrefetchScalarGridSpec(
            num_scalar_prefetch=1,
            grid=(steps,),
            in_specs=[
                descending(2, rows, width),
                descending(calls, rows, width),
                descending(calls, rows, width),
                descending(calls, rows, width),
                descending(calls + 2, rows, LANES),
                descending(2, rows, width),
                whole((rows, width)),
                mine(steps),
                mine(steps),
                whole((blocks, width)),
                whole((blocks, width)),
                whole((blocks, width, width)),
                whole((blocks, width, width)),
                whole((blocks, width, width)),
                whole((blocks, width, width)),
                whole((2, s.head_rows, width)),
            ],
            out_specs=[
                whole((s.total, width)),
                whole((s.total, width)),
                whole((rows, half)),
                whole((rows, half)),
            ],
            scratch_shapes=[
                pltpu.VMEM((rows, width), F32),
                pltpu.VMEM((2, 16, width), F32),
                pltpu.VMEM((s.held, width), F32),
                pltpu.VMEM((2, calls, width, width), F32),
                pltpu.VMEM((2, 16, width), F32),
                pltpu.VMEM((2, 16, width), F32),
                pltpu.VMEM((2, blocks, width, width), BF16),
                pltpu.VMEM((2, blocks, width, width), BF16),
            ],
        ),
        out_shape=[
            shape((s.total, width), BF16),
            shape((s.total, width), BF16),
            shape((rows, half), BF16),
            shape((rows, half), BF16),
        ],
        compiler_params=params,
        cost_estimate=cost,
        name="unroll_backward",
    )(
        tower_ref, lat, entry, after, slope, side, dlat, dlast, actions, codes,
        gains_own, gains_got, in_own, in_got, out_own, out_got, head_grads,
    )
    got = swap(away, "tower", 1)

    def beside(given):
        lat_own, lat_away, loss, root_own, root_away = given
        lat_got = swap(lat_away, "tower", 1)
        loss_own = loss[0]
        loss_got = swap(loss_own, "tower", 1)
        root_got = swap(root_away, "tower", 1)

        latents, logits = pl.pallas_call(
            functools.partial(logits_kernel, s),
            grid_spec=pltpu.PrefetchScalarGridSpec(
                num_scalar_prefetch=1,
                grid=(steps,),
                in_specs=[per_step(rows, width), per_step(rows, width), whole((bins, width))],
                out_specs=[per_step(batch_rows, width), per_step(bins, batch_rows)],
            ),
            out_shape=[
                shape((steps, batch_rows, width), BF16),
                shape((steps, bins, batch_rows), BF16),
            ],
            compiler_params=params,
            cost_estimate=pl.CostEstimate(
                flops=2 * steps * batch_rows * width * wide, bytes_accessed=6 * 2**20, transcendentals=0
            ),
            name="latents_and_logits",
        )(tower_ref, lat_own, lat_got, value_own)

        def in_order(mine_value, got_value, axis):
            return jnp.where(
                tower_id == 0,
                jnp.concatenate([mine_value, got_value], axis=axis),
                jnp.concatenate([got_value, mine_value], axis=axis),
            )

        row_loss = in_order(loss_own, loss_got, 0)
        grad_root = in_order(root_own, root_got, 0).astype(F32)
        return latents, logits, row_loss, grad_root

    rounds = exchange_rounds(parts)

    def unpack(digit, held):
        scalars = jnp.stack([digit, tower_id]).astype(jnp.int32)
        shared_rows = s.shared_end - s.reward_at
        return pl.pallas_call(
            functools.partial(unpack_own_kernel, s),
            grid_spec=pltpu.PrefetchScalarGridSpec(
                num_scalar_prefetch=1,
                grid=(1,),
                in_specs=[whole(part.shape) for part in held],
                out_specs=[
                    whole((blocks, width, width)),
                    whole((blocks, width, width)),
                    whole((bins, 1, width)),
                    whole((blocks, 1, width)),
                    whole((blocks, 2, steps)),
                    whole((shared_rows, width)),
                ],
                scratch_shapes=[
                    pltpu.VMEM((s.total, width), BF16),
                    pltpu.VMEM((s.reward_at - s.sums_at, LANES), F32),
                ],
            ),
            out_shape=[
                shape((blocks, width, width), F32),
                shape((blocks, width, width), F32),
                shape((bins, 1, width), F32),
                shape((blocks, 1, width), F32),
                shape((blocks, 2, steps), F32),
                shape((shared_rows, width), BF16),
            ],
            compiler_params=params,
            name="unpack_own",
        )(scalars, *held)

    given = (lat_own, lat_away, loss, root_own, root_away)
    unpacked, done = exchange([own, got], rounds, parts, beside, given, unpack)
    grad_in, grad_out, value_t, gain_t, rms_t, shared = unpacked
    latents, logits, row_loss, grad_root = done
    shared_got = swap(shared, "tower", 1)
    reward_t, small_t, grad_cond = pl.pallas_call(
        functools.partial(unpack_shared_kernel, s),
        grid_spec=pltpu.PrefetchScalarGridSpec(
            num_scalar_prefetch=1,
            grid=(1,),
            in_specs=[whole(shared.shape), whole(shared.shape)],
            out_specs=[
                whole((bins, width)),
                whole((table_rows, width)),
                whole((table_rows, width)),
            ],
            scratch_shapes=[pltpu.VMEM((s.wide, width), F32)],
        ),
        out_shape=[
            shape((bins, width), F32),
            shape((table_rows, width), F32),
            shape((table_rows, width), F32),
        ],
        compiler_params=params,
        name="unpack_shared",
    )(tower_ref, shared, shared_got)
    layer_rms = jnp.transpose(rms_t, (2, 0, 1))[None]
    return (
        latents[None],
        jnp.swapaxes(logits, 1, 2)[None],
        row_loss,
        layer_rms,
        grad_root,
        grad_cond,
        jnp.swapaxes(gain_t, 0, 1),
        grad_in[None],
        grad_out[None],
        jnp.transpose(value_t, (1, 2, 0)),
        reward_t.T,
        small_t.T,
    )


def solution(mesh):
    placed = (
        P("batch", "tower"),
        P(),
        P("tower", None, None),
        P("tower", None, None, None),
        P("tower", None, None, None),
        P("tower", None, None),
        P(),
        P(),
        P("batch"),
        P(None, "batch"),
        P(None, "batch"),
        P(None, "batch"),
        P(None, None, "batch"),
        P(None, "batch"),
    )
    return jax.shard_map(
        body,
        mesh=mesh,
        in_specs=placed,
        out_specs=(
            P("tower", None, "batch", None),
            P("tower", None, "batch", None),
            P("batch"),
            P("tower", None, None, None),
            P("batch", "tower"),
            P(),
            P("tower", None, None),
            P("tower", None, None, None),
            P("tower", None, None, None),
            P("tower", None, None),
            P(),
            P(),
        ),
        check_vma=False,
    )
```

```python
import functools

import jax
import jax.numpy as jnp
from jax import lax
from jax.experimental import pallas as pl
from jax.experimental.pallas import tpu as pltpu
from jax.sharding import PartitionSpec as P

ACTIONS = 4
LANES = 128
MIB = 1024 * 1024
CHAIN_LIMIT = 20 * MIB
SMALL_LIMIT = 12 * MIB
epsilon = 1e-06
very_negative = -1e30
F32 = jnp.float32
BF16 = jnp.bfloat16


def natural(left, right):
    return lax.dot_general(left, right, (((1,), (0,)), ((), ())), preferred_element_type=F32)


def by_rows(left, right):
    return lax.dot_general(left, right, (((0,), (0,)), ((), ())), preferred_element_type=F32)


def by_lanes(left, right):
    return lax.dot_general(left, right, (((1,), (1,)), ((), ())), preferred_element_type=F32)


def round_up(value, unit):
    return (value + unit - 1) // unit * unit


def lane_sum(value):
    return jnp.sum(value, axis=-1, keepdims=True)


def inverse_rms(hidden):
    return lax.rsqrt(lane_sum(hidden * hidden) * (1.0 / hidden.shape[-1]) + epsilon)


def weave(*tasks):
    tasks = [(list(task)) for task in tasks]
    longest = max(len(task) for task in tasks)
    done = [0] * len(tasks)
    for turn in range(longest):
        for which, task in enumerate(tasks):
            until = (turn + 1) * len(task) // longest
            while done[which] < until:
                task[done[which]]()
                done[which] += 1


def cuts(length, unit=160):
    return [(start, min(start + unit, length)) for start in range(0, length, unit)]


class Sizes:
    def __init__(self, steps, rows, blocks, width, bins, table_rows, parts):
        self.steps, self.rows, self.blocks, self.width = steps, rows, blocks, width
        self.bins, self.table_rows, self.parts = bins, table_rows, parts
        self.calls = 2 * blocks
        self.wide = round_up(bins, 32)
        self.held = round_up(table_rows, 16)
        self.stack = (self.wide + self.held, 2 * self.wide + self.held)
        self.depth = tuple(round_up(rows_in, LANES) for rows_in in self.stack)
        half = self.wide // 2
        self.value_at = self.calls * width
        self.sums_at = self.value_at + self.wide
        self.kinds = 2 * self.calls
        self.gain_row = self.kinds + 1
        self.reward_at = self.sums_at + round_up(self.gain_row + blocks, 16)
        self.small_at = self.reward_at + half
        self.cond_at = self.small_at + self.held
        self.shared_end = self.cond_at + self.held
        self.total = round_up(self.shared_end, 16 * parts)
        self.head_rows = self.cond_at - self.value_at


def forward_kernel(
    sizes, tower_ref,
    root_own, root_got, lengths, actions, codes, policy, value_bins, reward_bins,
    table_in, gains_own, gains_got, in_own, in_got, out_own, out_got,
    value_own, value_got, reward_in, small_in,
    lat, lat_own, lat_away, entry, after, slope, side, dlat, dlast, loss, head_grads, in_turned, out_turned,
    state, identity, table, gains, w_in, w_out, heads0, heads1, flip0, flip1, acc0, acc1,
    logits0, logits1, cot0, cot1, sums, squares,
):
    s = sizes
    step = pl.program_id(0)
    tower_id = tower_ref[0]
    rows, width, wide = s.rows, s.width, s.wide

    @pl.when(step == 0)
    def _():
        first = tower_id == 0
        state[:, 0 : width // 2] = jnp.where(first, root_own[...], root_got[...])
        state[:, width // 2 : width] = jnp.where(first, root_got[...], root_own[...])
        for tower, w_first, w_second in (
            (tower_id, in_own, out_own),
            (1 - tower_id, in_got, out_got),
        ):
            w_in[pl.ds(tower * s.blocks, s.blocks)] = w_first[...]
            w_out[pl.ds(tower * s.blocks, s.blocks)] = w_second[...]
        gains[...] = jnp.zeros_like(gains)
        gains[tower_id, 0 : s.blocks, :] = gains_own[...].astype(F32)
        gains[1 - tower_id, 0 : s.blocks, :] = gains_got[...].astype(F32)
        table[...] = jnp.zeros_like(table)
        table[0 : s.table_rows, :] = table_in[...]
        heads0[...] = jnp.zeros_like(heads0)
        heads1[...] = jnp.zeros_like(heads1)
        heads0[0 : s.bins, :] = jnp.where(first, value_own[...], value_got[...])
        heads1[0 : s.bins, :] = jnp.where(first, value_got[...], value_own[...])
        heads1[wide : wide + s.bins, :] = reward_in[...]
        heads0[wide : wide + s.table_rows, :] = small_in[...]
        heads1[2 * wide : 2 * wide + s.table_rows, :] = small_in[...]
        down = lax.broadcasted_iota(jnp.int32, (width, width), 0)
        across = lax.broadcasted_iota(jnp.int32, (width, width), 1)
        identity[...] = jnp.where(down == across, 1.0, 0.0).astype(BF16)
        flip0[...] = by_lanes(identity[...], heads0[...]).astype(BF16)
        flip1[...] = by_lanes(identity[...], heads1[...]).astype(BF16)
        cot0[...] = jnp.zeros_like(cot0)
        cot1[...] = jnp.zeros_like(cot1)
        acc0[...] = jnp.zeros_like(acc0)
        acc1[...] = jnp.zeros_like(acc1)
        sums[...] = jnp.zeros_like(sums)
        squares[...] = jnp.zeros_like(squares)
        loss[...] = jnp.zeros_like(loss)

    earlier = jnp.maximum(step - 1, 0)
    live_now = (step < lengths[...]).astype(F32)
    live_before = ((step - 1 < lengths[...]) & (step > 0)).astype(F32)
    action_now = actions[pl.ds(step, 1), :]
    code_now = codes[pl.ds(step, 1), :]
    kinds = jnp.concatenate(
        [live_now, action_now.astype(F32), code_now.astype(F32), jnp.zeros((5, rows), F32)], axis=0
    )
    columns = kinds.T
    live = columns[:, 0:1]
    eights = lax.broadcasted_iota(jnp.int32, (8, rows), 0)

    def heads(tower, latent, live_row, at_step, put):
        weights, flip, logits, cot, acc = (
            (heads0, flip0, logits0, cot0, acc0)
            if tower == 0
            else (heads1, flip1, logits1, cot1, acc1)
        )
        pick = lambda kind: kind[pl.ds(at_step, 1), :]
        value_goal = value_bins[pl.ds(at_step, 1), tower, :]
        spans = [(0, wide, 0, s.bins, value_goal)]
        if tower == 1:
            spans.append((wide, wide, 0, s.bins, pick(reward_bins)))
            spans.append((2 * wide, s.held, 0, ACTIONS, pick(policy)))
        else:
            spans.append((wide, s.held, ACTIONS, s.table_rows, pick(codes) + ACTIONS))

        def make_logits():
            logits[...] = by_lanes(weights[0 : logits.shape[0], :], latent())

        def eight_rows(value):
            return value.reshape(-1, 8, rows)

        def mask(at, length, first, last):
            for start in range(0, length, 8):
                if start < first or start + 8 > last:
                    inside = (eights >= first - start) & (eights < last - start)
                    place = slice(at + start, at + start + 8)
                    logits[place, :] = jnp.where(inside, logits[place, :], very_negative)

        def find_top(at, start, stop, kept):
            top = jnp.max(eight_rows(logits[at + start : at + stop, :]), axis=0)
            kept["top"] = jnp.maximum(kept["top"], top) if "top" in kept else top

        def end_top(kept):
            kept["top"] = jnp.max(kept["top"], axis=0, keepdims=True)

        def make_terms(at, start, stop, goal, kept):
            place = slice(at + start, at + stop)
            value = logits[place, :]
            spot = lax.broadcasted_iota(jnp.int32, value.shape, 0)
            term = jnp.exp(value - kept["top"])
            logits[place, :] = term
            hit = spot == goal - start
            total = jnp.sum(eight_rows(term), axis=0)
            picked = jnp.sum(eight_rows(jnp.where(hit, value, 0.0)), axis=0)
            kept["total"] = kept["total"] + total if "total" in kept else total
            kept["picked"] = kept["picked"] + picked if "picked" in kept else picked

        def end_terms(kept):
            total = jnp.sum(kept["total"], axis=0, keepdims=True)
            picked = jnp.sum(kept["picked"], axis=0, keepdims=True)
            kept["scale"] = live_row / total
            loss[0:1, :] += live_row * (jnp.log(total) + kept["top"] - picked)

        def make_cotangent(at, start, stop, goal, kept):
            place = slice(at + start, at + stop)
            term = logits[place, :]
            spot = lax.broadcasted_iota(jnp.int32, term.shape, 0)
            hit = spot == goal - start
            cot[place, :] = (term * kept["scale"] - jnp.where(hit, live_row, 0.0)).astype(BF16)

        def make_grads():
            acc[...] += natural(cot[0 : acc.shape[0], :], latent())

        def make_latent():
            put(natural(flip[...], cot[...]).T)

        pieces = [make_logits]
        for at, length, first, last, goal in spans:
            kept = {}
            each = cuts(length)
            pieces.append(functools.partial(mask, at, length, first, last))
            pieces += [functools.partial(find_top, at, *cut, kept) for cut in each]
            pieces.append(functools.partial(end_top, kept))
            pieces += [functools.partial(make_terms, at, *cut, goal, kept) for cut in each]
            pieces.append(functools.partial(end_terms, kept))
            pieces += [functools.partial(make_cotangent, at, *cut, goal, kept) for cut in each]
        return pieces + [make_latent, make_grads]

    def tower_call(tower, x_in, code, done):
        kept = {}

        def begin():
            spot = lax.broadcasted_iota(jnp.int32, (rows, table.shape[0]), 1).astype(F32)
            onehot = jnp.where(spot == code, 1.0, 0.0).astype(BF16)
            kept["hidden"] = x_in().astype(F32) + natural(onehot, table[...])

        def scale_rows():
            row_squares = lane_sum(kept["hidden"] * kept["hidden"])
            return row_squares, lax.rsqrt(row_squares * (1.0 / width) + epsilon)

        def keep_squares(block, row_squares):
            place = 2 * (tower * s.blocks + block)
            total = jnp.sum(live * row_squares, axis=0, keepdims=True) * (1.0 / LANES)
            squares[place : place + 1, 0:LANES] = jnp.broadcast_to(total, (1, LANES))

        def into(block):
            place = tower * s.blocks + block
            gained = kept["hidden"] * gains[tower, block : block + 1, :]
            product = natural(gained.astype(BF16), w_in[place])
            row_squares, inv_scale = scale_rows()
            kept["u"] = product * inv_scale
            entry[0, place] = (gained * inv_scale).astype(BF16)
            side[0, place] = jnp.broadcast_to(inv_scale, (rows, LANES))
            if block > 0:
                keep_squares(block - 1, row_squares)

        def out_of(block):
            place = tower * s.blocks + block
            u = kept["u"]
            gate = 0.5 * jnp.tanh(0.5 * u) + 0.5
            after_rows = (u * gate).astype(BF16)
            branch = natural(after_rows, w_out[place])
            kept["hidden"] = kept["hidden"] + branch
            after[0, place] = after_rows
            slope[0, place] = gate * (1.0 + u * (1.0 - gate))
            spot = 2 * place + 1
            squares[spot : spot + 1, :] = jnp.sum(
                branch * branch * live, axis=0, keepdims=True
            )

        def finish():
            row_squares, inv_scale = scale_rows()
            side[0, s.calls + tower] = jnp.broadcast_to(inv_scale, (rows, LANES))
            latent = (kept["hidden"] * inv_scale).astype(BF16)
            lat[0, tower] = latent
            keep_squares(s.blocks - 1, row_squares)
            done(latent)

        pieces = [begin]
        for block in range(s.blocks):
            pieces += [functools.partial(into, block), functools.partial(out_of, block)]
        return pieces + [finish]

    found = {"s": state[...]}
    turn = jnp.minimum(step, s.calls - 1)

    def turn_weights(source, target):
        target[turn] = by_lanes(identity[...], source[turn]).astype(BF16)

    def put_state(value):
        dlat[0, 1] = value

    def put_after(value):
        dlat[0, 0] = value

    def put_last(value):
        dlast[...] = value

    chain = tower_call(0, lambda: found["s"], columns[:, 1:2], lambda y: found.update(a=y))
    chain += tower_call(
        1, lambda: found["a"], columns[:, 2:3] + ACTIONS, lambda y: found.update(n=y)
    )
    weave(
        chain,
        heads(1, lambda: found["s"], live_before, earlier, put_state)
        + heads(0, lambda: found["a"], live_now, step, put_after)
        + [
            functools.partial(turn_weights, w_in, in_turned),
            functools.partial(turn_weights, w_out, out_turned),
        ],
    )
    state[...] = found["n"]
    first = tower_id == 0
    lat_own[0] = jnp.where(first, found["a"], found["n"])
    lat_away[0] = jnp.where(first, found["n"], found["a"])
    total = jnp.sum(live, axis=0, keepdims=True) * (1.0 / LANES)
    squares[s.kinds : s.kinds + 1, 0:LANES] = jnp.broadcast_to(total, (1, LANES))
    at_lane = lax.broadcasted_iota(jnp.int32, sums.shape, 1) == step
    sums[...] = jnp.where(at_lane, lane_sum(squares[...]), sums[...])

    @pl.when(step == s.steps - 1)
    def _():
        for piece in heads(1, lambda: found["n"], live_now, step, put_last):
            piece()
        half = wide // 2
        head_grads[...] = jnp.zeros_like(head_grads)
        head_grads[0, 0:wide, :] = acc0[0:wide, :].astype(BF16)
        head_grads[1, 0:wide, :] = acc1[0:wide, :].astype(BF16)
        small = acc0[wide : wide + s.held, :] + acc1[2 * wide : 2 * wide + s.held, :]
        at = s.small_at - s.value_at
        head_grads[0, at : at + s.held, :] = small.astype(BF16)
        for tower in range(2):
            put = s.reward_at - s.value_at
            at = wide + tower * half
            head_grads[tower, put : put + half, :] = acc1[at : at + half, :].astype(BF16)
            head_grads[tower, wide : wide + sums.shape[0], 0:LANES] = sums[...].astype(BF16)


def backward_kernel(
    sizes, tower_ref,
    lat, entry, after, slope, side, dlat, dlast, actions, codes,
    gains_own, gains_got, w_in, w_out, head_grads,
    own, away, root_own, root_away,
    carry, gain_sum, cond_sum, grads, gains, inverse_gains,
):
    s = sizes
    turn = pl.program_id(0)
    step = s.steps - 1 - turn
    tower_id = tower_ref[0]
    blocks, width = s.blocks, s.width

    @pl.when(turn == 0)
    def _():
        gains[...] = jnp.ones_like(gains)
        gains[tower_id, 0:blocks, :] = gains_own[...].astype(F32)
        gains[1 - tower_id, 0:blocks, :] = gains_got[...].astype(F32)
        inverse_gains[...] = 1.0 / gains[...]
        carry[...] = dlast[...]
        grads[...] = jnp.zeros_like(grads)
        gain_sum[...] = jnp.zeros_like(gain_sum)
        cond_sum[...] = jnp.zeros_like(cond_sum)

    def over_lanes(column):
        return jnp.concatenate([column] * (width // LANES), axis=1)

    def tower_back(tower, d_latent, code):
        normed = lat[0, tower]
        normed_wide = normed.astype(F32)
        inv_scale = over_lanes(side[0, s.calls + tower])
        base = inv_scale * d_latent
        slant = inv_scale * (lane_sum(d_latent * normed_wide) * (1.0 / width))
        for block in reversed(range(blocks)):
            place = tower * blocks + block
            gain = gains[tower, block : block + 1, :]
            entry_rows = entry[0, place]
            entry_wide = entry_rows.astype(F32)
            inv_scale = over_lanes(side[0, place])
            both = natural(jnp.concatenate([normed, base.astype(BF16)], axis=0), w_out[place])
            d_after = both[s.rows :] - slant * both[: s.rows]
            d_hidden = base - slant * normed_wide
            d_before = (d_after * slope[0, place]).astype(BF16)
            d_entry = natural(d_before, w_in[place])
            grads[tower, blocks + block] += by_rows(after[0, place], d_hidden.astype(BF16))
            grads[tower, block] += by_rows(entry_rows, d_before)
            product = d_entry * entry_wide
            gain_sum[tower, block : block + 1, :] += jnp.sum(product, axis=0, keepdims=True)
            base = d_hidden + inv_scale * (d_entry * gain)
            slant = inv_scale * (lane_sum(product) * (1.0 / width))
            normed_wide = entry_wide * inverse_gains[tower, block : block + 1, :]
            normed = normed_wide.astype(BF16)
        d_hidden = base - slant * normed_wide
        spots = lax.broadcasted_iota(jnp.int32, (cond_sum.shape[0], d_hidden.shape[0]), 0)
        onehot = jnp.where(spots == code, 1.0, 0.0).astype(BF16)
        cond_sum[...] += natural(onehot, d_hidden.astype(BF16))
        return d_hidden

    d_after = tower_back(1, carry[...], codes[pl.ds(step, 1), :] + ACTIONS)
    d_state = tower_back(0, d_after + dlat[0, 0], actions[pl.ds(step, 1), :])
    carry[...] = d_state + dlat[0, 1]

    @pl.when(turn == s.steps - 1)
    def _():
        left = d_state[:, 0 : width // 2].astype(BF16)
        right = d_state[:, width // 2 : width].astype(BF16)
        root_own[...] = jnp.where(tower_id == 0, left, right)
        root_away[...] = jnp.where(tower_id == 0, right, left)
        gain_sum[...] = gain_sum[...] * inverse_gains[...]
        lines = lax.broadcasted_iota(jnp.int32, (s.reward_at - s.sums_at, width), 0)
        for target, which in ((own, tower_id), (away, 1 - tower_id)):
            for matrix in range(s.calls):
                at = matrix * width
                target[at : at + width, :] = grads[which, matrix].astype(BF16)
            target[s.value_at : s.cond_at, :] = head_grads[which]
            sums = head_grads[which, s.wide : s.wide + lines.shape[0], :].astype(F32)
            for block in range(blocks):
                gain = gain_sum[which, block : block + 1, :]
                sums = jnp.where(lines == s.gain_row + block, gain, sums)
            target[s.sums_at : s.reward_at, :] = sums.astype(BF16)
            here = jnp.where(which == 0, cond_sum[...], 0.0)
            target[s.cond_at : s.shared_end, :] = here.astype(BF16)
            if s.total > s.shared_end:
                target[s.shared_end :, :] = jnp.zeros((s.total - s.shared_end, width), BF16)


def logits_kernel(sizes, tower_ref, lat_own, lat_got, value_own, latents, logits):
    rows = sizes.rows
    tower_id = tower_ref[0]
    at_own = pl.ds(pl.multiple_of(tower_id * rows, rows), rows)
    at_got = pl.ds(pl.multiple_of((1 - tower_id) * rows, rows), rows)
    latents[0, at_own, :] = lat_own[0]
    latents[0, at_got, :] = lat_got[0]
    logits[0] = by_lanes(value_own[...], latents[0]).astype(BF16)


def add_and_split_kernel(count, digit_ref, *refs):
    inputs, outputs = refs[:count], refs[count:]
    digit = digit_ref[0]
    for other, target in enumerate(outputs):
        part = digit ^ other
        total = inputs[0][part].astype(F32)
        for source in inputs[1:]:
            total = total + source[part].astype(F32)
        target[...] = total.astype(BF16)


def in_order_kernel(digit_ref, *refs):
    digit = digit_ref[0]
    for other, source in enumerate(refs[:-1]):
        refs[-1][digit ^ other] = source[...]


def unpack_own_kernel(sizes, scalars, *refs):
    s = sizes
    factor = len(refs) - 7
    digit, tower_id = scalars[0], scalars[1]
    w_in, w_out, value, gain, rms, flat, held = refs[factor:]
    width = s.width
    length = refs[0].shape[0]
    for other, source in enumerate(refs[:factor]):
        at = pl.multiple_of((digit ^ other) * length, 16)
        flat[pl.ds(at, length), :] = source[...]
    for block in range(s.blocks):
        at = block * width
        w_in[block] = flat[at : at + width, :].astype(F32)
        at = (s.blocks + block) * width
        w_out[block] = flat[at : at + width, :].astype(F32)
    value[:, 0, :] = flat[s.value_at : s.sums_at, :].astype(F32)[0 : s.bins]
    sums = flat[s.sums_at : s.reward_at, :].astype(F32)
    for block in range(s.blocks):
        gain[block] = sums[s.gain_row + block : s.gain_row + block + 1, :]
    held[...] = sums[:, 0:LANES]
    count = jnp.maximum(held[s.kinds : s.kinds + 1, 0 : s.steps], 1.0)
    for block in range(s.blocks):
        for kind in range(2):
            spot = tower_id * s.calls + 2 * block + kind
            square = held[pl.ds(spot, 1), 0 : s.steps]
            rms[block, kind : kind + 1, :] = jnp.sqrt(jnp.maximum(square, 0.0) / (count * width))


def unpack_shared_kernel(sizes, tower_ref, mine, got, reward, small, cond, joined):
    s = sizes
    tower_id = tower_ref[0]
    half = s.wide // 2
    joined[pl.ds(pl.multiple_of(tower_id * half, 8), half), :] = mine[0:half, :].astype(F32)
    joined[pl.ds(pl.multiple_of((1 - tower_id) * half, 8), half), :] = got[0:half, :].astype(F32)
    reward[...] = joined[0 : s.bins, :]
    for target, at in ((small, s.small_at), (cond, s.cond_at)):
        rows = slice(at - s.reward_at, at - s.reward_at + s.held)
        target[...] = (mine[rows, :].astype(F32) + got[rows, :].astype(F32))[0 : s.table_rows]


def whole(shape):
    return pl.BlockSpec(shape, lambda step, tower: (0,) * len(shape))


def per_step(*tail):
    return pl.BlockSpec((1,) + tail, lambda step, tower: (step,) + (0,) * len(tail))


def swap(value, axis, mask):
    pairs = [(source, source ^ mask) for source in range(lax.axis_size(axis))]
    return lax.ppermute(value, axis, pairs)


AXES = ("tower", "batch")


def exchange_rounds(batch_size):
    factors, left = [], batch_size
    while left > 1:
        factors.append(4 if left % 4 == 0 else 2)
        left //= factors[-1]
    rounds, stride = [], 1
    for factor in factors:
        rounds.append((factor, stride))
        stride *= factor
    turned = rounds[::-1] if len(set(factors)) == 1 else rounds
    return [(one[0], (one[1], two[1])) for one, two in zip(rounds, turned)]


def swap_within(value, strides, other, batch_size):
    pairs = [
        (tower * batch_size + index, tower * batch_size + (index ^ (other * strides[tower])))
        for tower in range(2)
        for index in range(batch_size)
    ]
    return lax.ppermute(value, AXES, pairs)


def my_digit(factor, strides):
    stride = jnp.where(lax.axis_index("tower") == 0, strides[0], strides[1])
    return (lax.axis_index("batch") // stride) % factor


def exchange(value, rounds, batch_size, beside, given, last_kernel):
    shape = jax.ShapeDtypeStruct
    held = value
    digits = []
    for factor, strides in rounds:
        digit = my_digit(factor, strides)
        digits.append(digit)
        rows, width = held[0].shape
        rows = rows // factor
        split = pl.pallas_call(
            functools.partial(add_and_split_kernel, len(held)),
            grid_spec=pltpu.PrefetchScalarGridSpec(
                num_scalar_prefetch=1,
                grid=(1,),
                in_specs=[whole((factor, rows, width))] * len(held),
                out_specs=[whole((rows, width))] * factor,
            ),
            out_shape=[shape((rows, width), BF16)] * factor,
            compiler_params=pltpu.CompilerParams(vmem_limit_bytes=SMALL_LIMIT),
            name="add_and_split",
        )(digit[None], *[part.reshape(factor, rows, width) for part in held])
        first = len(digits) == 1
        if first:
            split, given = lax.optimization_barrier((split, given))
        held = [split[0]] + [
            swap_within(split[other], strides, other, batch_size) for other in range(1, factor)
        ]
        if first:
            done = beside(given)
            held, done = lax.optimization_barrier((held, done))
    piece = functools.reduce(jnp.add, [part.astype(F32) for part in held]).astype(BF16)
    for place in reversed(range(len(rounds))):
        factor, strides = rounds[place]
        rows, width = piece.shape
        held = [piece] + [
            swap_within(piece, strides, other, batch_size) for other in range(1, factor)
        ]
        if place == 0:
            return last_kernel(digits[0], held), done
        piece = pl.pallas_call(
            in_order_kernel,
            grid_spec=pltpu.PrefetchScalarGridSpec(
                num_scalar_prefetch=1,
                grid=(1,),
                in_specs=[whole((rows, width))] * factor,
                out_specs=whole((factor, rows, width)),
            ),
            out_shape=shape((factor, rows, width), BF16),
            compiler_params=pltpu.CompilerParams(vmem_limit_bytes=SMALL_LIMIT),
            name="in_order",
        )(digits[place][None], *held).reshape(factor * rows, width)


def body(
    root_state, cond_table, block_gain, w_in, w_out, value_head, reward_head, small_head,
    unroll_len, actions, codes, policy_target, value_bins, reward_bins,
):
    tower_id = lax.axis_index("tower")
    other_id = 1 - tower_id
    tower_ref = tower_id.astype(jnp.int32)[None]
    steps, batch_rows = actions.shape
    blocks, width = block_gain.shape[1:]
    bins = value_head.shape[2]
    table_rows = cond_table.shape[0]
    rows = batch_rows // 2
    half = width // 2
    parts = lax.axis_size("batch")
    s = Sizes(steps, rows, blocks, width, bins, table_rows, parts)
    calls, wide = s.calls, s.wide

    root_got = swap(root_state, "tower", 1)
    in_own, out_own, gains_own = w_in[0], w_out[0], block_gain[0]
    value_own = value_head[0].T
    in_got = swap(in_own, "tower", 1)
    out_got = swap(out_own, "tower", 1)
    gains_got = swap(gains_own, "tower", 1)
    value_got = swap(value_own, "tower", 1)
    lengths = unroll_len.reshape(1, batch_rows)

    shape = jax.ShapeDtypeStruct
    params = pltpu.CompilerParams(vmem_limit_bytes=CHAIN_LIMIT)
    small_params = pltpu.CompilerParams(vmem_limit_bytes=SMALL_LIMIT)
    products = steps * rows * (4 * blocks * width * width + 9 * width * wide)
    cost = pl.CostEstimate(flops=2 * products, bytes_accessed=40 * 2**20, transcendentals=0)
    mine = lambda *lead: pl.BlockSpec(
        lead + (rows,), lambda step, tower: (0,) * len(lead) + (tower[0],)
    )
    (
        lat, lat_own, lat_away, entry, after, slope, side, dlat, dlast, loss, head_grads,
        in_turned, out_turned,
    ) = pl.pallas_call(
        functools.partial(forward_kernel, s),
        grid_spec=pltpu.PrefetchScalarGridSpec(
            num_scalar_prefetch=1,
            grid=(steps,),
            in_specs=[
                pl.BlockSpec((rows, half), lambda step, tower: (tower[0], 0)),
                pl.BlockSpec((rows, half), lambda step, tower: (tower[0], 0)),
                mine(1),
                mine(steps),
                mine(steps),
                mine(steps),
                mine(steps, 2),
                mine(steps),
                whole((table_rows, width)),
                whole((blocks, width)),
                whole((blocks, width)),
                whole((blocks, width, width)),
                whole((blocks, width, width)),
                whole((blocks, width, width)),
                whole((blocks, width, width)),
                whole((bins, width)),
                whole((bins, width)),
                whole((bins, width)),
                whole((table_rows, width)),
            ],
            out_specs=[
                per_step(2, rows, width),
                per_step(rows, width),
                per_step(rows, width),
                per_step(calls, rows, width),
                per_step(calls, rows, width),
                per_step(calls, rows, width),
                per_step(calls + 2, rows, LANES),
                per_step(2, rows, width),
                whole((rows, width)),
                whole((8, rows)),
                whole((2, s.head_rows, width)),
                whole((calls, width, width)),
                whole((calls, width, width)),
            ],
            scratch_shapes=[
                pltpu.VMEM((rows, width), BF16),
                pltpu.VMEM((width, width), BF16),
                pltpu.VMEM((LANES, width), BF16),
                pltpu.VMEM((2, 8, width), F32),
                pltpu.VMEM((calls, width, width), BF16),
                pltpu.VMEM((calls, width, width), BF16),
                pltpu.VMEM((s.depth[0], width), BF16),
                pltpu.VMEM((s.depth[1], width), BF16),
                pltpu.VMEM((width, s.depth[0]), BF16),
                pltpu.VMEM((width, s.depth[1]), BF16),
                pltpu.VMEM((s.stack[0], width), F32),
                pltpu.VMEM((s.stack[1], width), F32),
                pltpu.VMEM((s.stack[0], rows), F32),
                pltpu.VMEM((s.stack[1], rows), F32),
                pltpu.VMEM((s.depth[0], rows), BF16),
                pltpu.VMEM((s.depth[1], rows), BF16),
                pltpu.VMEM((s.reward_at - s.sums_at, LANES), F32),
                pltpu.VMEM((s.reward_at - s.sums_at, width), F32),
            ],
        ),
        out_shape=[
            shape((steps, 2, rows, width), BF16),
            shape((steps, rows, width), BF16),
            shape((steps, rows, width), BF16),
            shape((steps, calls, rows, width), BF16),
            shape((steps, calls, rows, width), BF16),
            shape((steps, calls, rows, width), F32),
            shape((steps, calls + 2, rows, LANES), F32),
            shape((steps, 2, rows, width), F32),
            shape((rows, width), F32),
            shape((8, rows), F32),
            shape((2, s.head_rows, width), BF16),
            shape((calls, width, width), BF16),
            shape((calls, width, width), BF16),
        ],
        compiler_params=params,
        cost_estimate=cost,
        name="unroll_forward",
    )(
        tower_ref, root_state, root_got, lengths, actions, codes, policy_target,
        jnp.swapaxes(value_bins, 0, 1), reward_bins, cond_table, gains_own, gains_got, in_own, in_got, out_own, out_got,
        value_own, value_got, reward_head.T, small_head.T,
    )
    descending = lambda *tail: pl.BlockSpec(
        (1,) + tail, lambda step, tower: (steps - 1 - step,) + (0,) * len(tail)
    )
    own, away, root_own, root_away = pl.pallas_call(
        functools.partial(backward_kernel, s),
        grid_spec=pltpu.PrefetchScalarGridSpec(
            num_scalar_prefetch=1,
            grid=(steps,),
            in_specs=[
                descending(2, rows, width),
                descending(calls, rows, width),
                descending(calls, rows, width),
                descending(calls, rows, width),
                descending(calls + 2, rows, LANES),
                descending(2, rows, width),
                whole((rows, width)),
                mine(steps),
                mine(steps),
                whole((blocks, width)),
                whole((blocks, width)),
                whole((calls, width, width)),
                whole((calls, width, width)),
                whole((2, s.head_rows, width)),
            ],
            out_specs=[
                whole((s.total, width)),
                whole((s.total, width)),
                whole((rows, half)),
                whole((rows, half)),
            ],
            scratch_shapes=[
                pltpu.VMEM((rows, width), F32),
                pltpu.VMEM((2, 16, width), F32),
                pltpu.VMEM((s.held, width), F32),
                pltpu.VMEM((2, calls, width, width), F32),
                pltpu.VMEM((2, 16, width), F32),
                pltpu.VMEM((2, 16, width), F32),
            ],
        ),
        out_shape=[
            shape((s.total, width), BF16),
            shape((s.total, width), BF16),
            shape((rows, half), BF16),
            shape((rows, half), BF16),
        ],
        compiler_params=params,
        cost_estimate=cost,
        name="unroll_backward",
    )(
        tower_ref, lat, entry, after, slope, side, dlat, dlast, actions, codes,
        gains_own, gains_got, in_turned, out_turned, head_grads,
    )
    got = swap(away, "tower", 1)

    def beside(given):
        lat_own, lat_away, loss, root_own, root_away = given
        lat_got = swap(lat_away, "tower", 1)
        loss_own = loss[0]
        loss_got = swap(loss_own, "tower", 1)
        root_got = swap(root_away, "tower", 1)

        latents, logits = pl.pallas_call(
            functools.partial(logits_kernel, s),
            grid_spec=pltpu.PrefetchScalarGridSpec(
                num_scalar_prefetch=1,
                grid=(steps,),
                in_specs=[per_step(rows, width), per_step(rows, width), whole((bins, width))],
                out_specs=[per_step(batch_rows, width), per_step(bins, batch_rows)],
            ),
            out_shape=[
                shape((steps, batch_rows, width), BF16),
                shape((steps, bins, batch_rows), BF16),
            ],
            compiler_params=small_params,
            cost_estimate=pl.CostEstimate(
                flops=2 * steps * batch_rows * width * wide, bytes_accessed=6 * 2**20, transcendentals=0
            ),
            name="latents_and_logits",
        )(tower_ref, lat_own, lat_got, value_own)

        def in_order(mine_value, got_value, axis):
            return jnp.where(
                tower_id == 0,
                jnp.concatenate([mine_value, got_value], axis=axis),
                jnp.concatenate([got_value, mine_value], axis=axis),
            )

        row_loss = in_order(loss_own, loss_got, 0)
        grad_root = in_order(root_own, root_got, 0).astype(F32)
        return latents, logits, row_loss, grad_root

    rounds = exchange_rounds(parts)

    def unpack(digit, held):
        scalars = jnp.stack([digit, tower_id]).astype(jnp.int32)
        length = held[0].shape[0]
        block = s.reward_at // length
        at = s.reward_at - block * length
        parts_of = [part[at : at + s.shared_end - s.reward_at] for part in held]
        shared = parts_of[0]
        for other in range(1, len(held)):
            shared = jnp.where((digit ^ other) == block, parts_of[other], shared)
        shared_got = swap(shared, "tower", 1)
        return (shared, shared_got), pl.pallas_call(
            functools.partial(unpack_own_kernel, s),
            grid_spec=pltpu.PrefetchScalarGridSpec(
                num_scalar_prefetch=1,
                grid=(1,),
                in_specs=[whole(part.shape) for part in held],
                out_specs=[
                    whole((blocks, width, width)),
                    whole((blocks, width, width)),
                    whole((bins, 1, width)),
                    whole((blocks, 1, width)),
                    whole((blocks, 2, steps)),
                ],
                scratch_shapes=[
                    pltpu.VMEM((s.total, width), BF16),
                    pltpu.VMEM((s.reward_at - s.sums_at, LANES), F32),
                ],
            ),
            out_shape=[
                shape((blocks, width, width), F32),
                shape((blocks, width, width), F32),
                shape((bins, 1, width), F32),
                shape((blocks, 1, width), F32),
                shape((blocks, 2, steps), F32),
            ],
            compiler_params=small_params,
            name="unpack_own",
        )(scalars, *held)

    given = (lat_own, lat_away, loss, root_own, root_away)
    unpacked, done = exchange([own, got], rounds, parts, beside, given, unpack)
    (shared, shared_got), (grad_in, grad_out, value_t, gain_t, rms_t) = unpacked
    latents, logits, row_loss, grad_root = done
    reward_t, small_t, grad_cond = pl.pallas_call(
        functools.partial(unpack_shared_kernel, s),
        grid_spec=pltpu.PrefetchScalarGridSpec(
            num_scalar_prefetch=1,
            grid=(1,),
            in_specs=[whole(shared.shape), whole(shared.shape)],
            out_specs=[
                whole((bins, width)),
                whole((table_rows, width)),
                whole((table_rows, width)),
            ],
            scratch_shapes=[pltpu.VMEM((s.wide, width), F32)],
        ),
        out_shape=[
            shape((bins, width), F32),
            shape((table_rows, width), F32),
            shape((table_rows, width), F32),
        ],
        compiler_params=small_params,
        name="unpack_shared",
    )(tower_ref, shared, shared_got)
    layer_rms = jnp.transpose(rms_t, (2, 0, 1))[None]
    return (
        latents[None],
        jnp.swapaxes(logits, 1, 2)[None],
        row_loss,
        layer_rms,
        grad_root,
        grad_cond,
        jnp.swapaxes(gain_t, 0, 1),
        grad_in[None],
        grad_out[None],
        jnp.transpose(value_t, (1, 2, 0)),
        reward_t.T,
        small_t.T,
    )


def solution(mesh):
    placed = (
        P("batch", "tower"),
        P(),
        P("tower", None, None),
        P("tower", None, None, None),
        P("tower", None, None, None),
        P("tower", None, None),
        P(),
        P(),
        P("batch"),
        P(None, "batch"),
        P(None, "batch"),
        P(None, "batch"),
        P(None, None, "batch"),
        P(None, "batch"),
    )
    return jax.shard_map(
        body,
        mesh=mesh,
        in_specs=placed,
        out_specs=(
            P("tower", None, "batch", None),
            P("tower", None, "batch", None),
            P("batch"),
            P("tower", None, None, None),
            P("batch", "tower"),
            P(),
            P("tower", None, None),
            P("tower", None, None, None),
            P("tower", None, None, None),
            P("tower", None, None),
            P(),
            P(),
        ),
        check_vma=False,
    )
```

```python
import functools

import jax
import jax.numpy as jnp
from jax import lax
from jax.experimental import pallas as pl
from jax.experimental.pallas import tpu as pltpu
from jax.sharding import PartitionSpec as P

ACTIONS = 4
LANES = 128
MIB = 1024 * 1024
FORWARD_LIMIT = 20 * MIB
BACKWARD_LIMIT = 20 * MIB
SMALL_LIMIT = 12 * MIB
epsilon = 1e-06
very_negative = -1e30
F32 = jnp.float32
BF16 = jnp.bfloat16


def natural(left, right):
    return lax.dot_general(left, right, (((1,), (0,)), ((), ())), preferred_element_type=F32)


def by_rows(left, right):
    return lax.dot_general(left, right, (((0,), (0,)), ((), ())), preferred_element_type=F32)


def by_lanes(left, right):
    return lax.dot_general(left, right, (((1,), (1,)), ((), ())), preferred_element_type=F32)


def round_up(value, unit):
    return (value + unit - 1) // unit * unit


def lane_sum(value):
    return jnp.sum(value, axis=-1, keepdims=True)


def inverse_rms(hidden):
    return lax.rsqrt(lane_sum(hidden * hidden) * (1.0 / hidden.shape[-1]) + epsilon)


def weave(*tasks):
    tasks = [(list(task)) for task in tasks]
    longest = max(len(task) for task in tasks)
    done = [0] * len(tasks)
    for turn in range(longest):
        for which, task in enumerate(tasks):
            until = (turn + 1) * len(task) // longest
            while done[which] < until:
                task[done[which]]()
                done[which] += 1


def cuts(length, unit=160):
    return [(start, min(start + unit, length)) for start in range(0, length, unit)]


class Sizes:
    def __init__(self, steps, rows, blocks, width, bins, table_rows, parts):
        self.steps, self.rows, self.blocks, self.width = steps, rows, blocks, width
        self.bins, self.table_rows, self.parts = bins, table_rows, parts
        self.calls = 2 * blocks
        self.wide = round_up(bins, 32)
        self.held = round_up(table_rows, 16)
        self.stack = (self.wide + self.held, 2 * self.wide + self.held)
        self.depth = tuple(round_up(rows_in, LANES) for rows_in in self.stack)
        half = self.wide // 2
        self.value_at = self.calls * width
        self.sums_at = self.value_at + self.wide
        self.kinds = 2 * self.calls
        self.gain_row = self.kinds + 1
        self.reward_at = self.sums_at + round_up(self.gain_row + blocks, 16)
        self.small_at = self.reward_at + half
        self.cond_at = self.small_at + self.held
        self.shared_end = self.cond_at + self.held
        self.total = round_up(self.shared_end, 16 * parts)
        self.head_rows = self.cond_at - self.value_at


def forward_kernel(
    sizes, tower_ref,
    root_hbm, lengths_hbm, actions_hbm, codes_hbm, policy_hbm, value_bins_hbm, reward_bins_hbm,
    table_hbm, gains_hbm, in_hbm, out_hbm, value_hbm, reward_hbm, small_hbm,
    root_got, gains_got, in_got, out_got, value_got,
    lat, lat_own, lat_away, entry, after, slope, side, dlat, dlast, loss, head_grads, in_turned, out_turned, code_rows, gains,
    root_own, lengths, actions, codes, policy, value_bins, reward_bins,
    table_in, gains_own, in_own, out_own, value_own, reward_in, small_in, sems,
    state, identity, table, w_in, w_out, heads0, heads1, flip0, flip1, acc0, acc1,
    logits0, logits1, cot0, cot1, sums, squares,
):
    s = sizes
    step = pl.program_id(0)
    tower_id = tower_ref[0]
    rows, width, wide = s.rows, s.width, s.wide

    @pl.when(step == 0)
    def _():
        here = pl.ds(pl.multiple_of(tower_id * rows, rows), rows)
        moves = [
            (root_hbm.at[here], root_own),
            (lengths_hbm.at[:, here], lengths),
            (actions_hbm.at[:, here], actions),
            (codes_hbm.at[:, here], codes),
            (policy_hbm.at[:, here], policy),
            (value_bins_hbm.at[:, :, here], value_bins),
            (reward_bins_hbm.at[:, here], reward_bins),
            (table_hbm, table_in),
            (gains_hbm, gains_own),
            (in_hbm, in_own),
            (out_hbm, out_own),
            (value_hbm, value_own),
            (reward_hbm, reward_in),
            (small_hbm, small_in),
        ]
        moves = [
            pltpu.make_async_copy(source, target, sems.at[place])
            for place, (source, target) in enumerate(moves)
        ]
        for move in moves:
            move.start()
        for move in moves:
            move.wait()
        first = tower_id == 0
        code_rows[0] = actions[...]
        code_rows[1] = codes[...] + ACTIONS
        state[:, 0 : width // 2] = jnp.where(first, root_own[...], root_got[...])
        state[:, width // 2 : width] = jnp.where(first, root_got[...], root_own[...])
        for tower, w_first, w_second in (
            (tower_id, in_own, out_own),
            (1 - tower_id, in_got, out_got),
        ):
            w_in[pl.ds(tower * s.blocks, s.blocks)] = w_first[...]
            w_out[pl.ds(tower * s.blocks, s.blocks)] = w_second[...]
        gains[...] = jnp.zeros_like(gains)
        gains[tower_id, 0 : s.blocks, :] = gains_own[...].astype(F32)
        gains[1 - tower_id, 0 : s.blocks, :] = gains_got[...].astype(F32)
        table[...] = jnp.zeros_like(table)
        table[0 : s.table_rows, :] = table_in[...]
        heads0[...] = jnp.zeros_like(heads0)
        heads1[...] = jnp.zeros_like(heads1)
        heads0[0 : s.bins, :] = jnp.where(first, value_own[...], value_got[...])
        heads1[0 : s.bins, :] = jnp.where(first, value_got[...], value_own[...])
        heads1[wide : wide + s.bins, :] = reward_in[...]
        heads0[wide : wide + s.table_rows, :] = small_in[...]
        heads1[2 * wide : 2 * wide + s.table_rows, :] = small_in[...]
        down = lax.broadcasted_iota(jnp.int32, (width, width), 0)
        across = lax.broadcasted_iota(jnp.int32, (width, width), 1)
        identity[...] = jnp.where(down == across, 1.0, 0.0).astype(BF16)
        flip0[...] = by_lanes(identity[...], heads0[...]).astype(BF16)
        flip1[...] = by_lanes(identity[...], heads1[...]).astype(BF16)
        cot0[...] = jnp.zeros_like(cot0)
        cot1[...] = jnp.zeros_like(cot1)
        acc0[...] = jnp.zeros_like(acc0)
        acc1[...] = jnp.zeros_like(acc1)
        sums[...] = jnp.zeros_like(sums)
        squares[...] = jnp.zeros_like(squares)
        loss[...] = jnp.zeros_like(loss)

    earlier = jnp.maximum(step - 1, 0)
    live_now = (step < lengths[...]).astype(F32)
    live_before = ((step - 1 < lengths[...]) & (step > 0)).astype(F32)
    action_now = actions[pl.ds(step, 1), :]
    code_now = codes[pl.ds(step, 1), :]
    kinds = jnp.concatenate(
        [live_now, action_now.astype(F32), code_now.astype(F32), jnp.zeros((5, rows), F32)], axis=0
    )
    columns = kinds.T
    live = columns[:, 0:1]
    eights = lax.broadcasted_iota(jnp.int32, (8, rows), 0)

    def heads(tower, latent, live_row, at_step, put):
        weights, flip, logits, cot, acc = (
            (heads0, flip0, logits0, cot0, acc0)
            if tower == 0
            else (heads1, flip1, logits1, cot1, acc1)
        )
        pick = lambda kind: kind[pl.ds(at_step, 1), :]
        value_goal = value_bins[pl.ds(at_step, 1), tower, :]
        spans = [(0, wide, 0, s.bins, value_goal)]
        if tower == 1:
            spans.append((wide, wide, 0, s.bins, pick(reward_bins)))
            spans.append((2 * wide, s.held, 0, ACTIONS, pick(policy)))
        else:
            spans.append((wide, s.held, ACTIONS, s.table_rows, pick(codes) + ACTIONS))

        def make_logits():
            logits[...] = by_lanes(weights[0 : logits.shape[0], :], latent())

        def eight_rows(value):
            return value.reshape(-1, 8, rows)

        def mask(at, length, first, last):
            for start in range(0, length, 8):
                if start < first or start + 8 > last:
                    inside = (eights >= first - start) & (eights < last - start)
                    place = slice(at + start, at + start + 8)
                    logits[place, :] = jnp.where(inside, logits[place, :], very_negative)

        def find_top(at, start, stop, kept):
            top = jnp.max(eight_rows(logits[at + start : at + stop, :]), axis=0)
            kept["top"] = jnp.maximum(kept["top"], top) if "top" in kept else top

        def end_top(kept):
            kept["top"] = jnp.max(kept["top"], axis=0, keepdims=True)

        def make_terms(at, start, stop, goal, kept):
            place = slice(at + start, at + stop)
            value = logits[place, :]
            spot = lax.broadcasted_iota(jnp.int32, value.shape, 0)
            term = jnp.exp(value - kept["top"])
            logits[place, :] = term
            hit = spot == goal - start
            total = jnp.sum(eight_rows(term), axis=0)
            picked = jnp.sum(eight_rows(jnp.where(hit, value, 0.0)), axis=0)
            kept["total"] = kept["total"] + total if "total" in kept else total
            kept["picked"] = kept["picked"] + picked if "picked" in kept else picked

        def end_terms(kept):
            total = jnp.sum(kept["total"], axis=0, keepdims=True)
            picked = jnp.sum(kept["picked"], axis=0, keepdims=True)
            kept["scale"] = live_row / total
            loss[0:1, :] += live_row * (jnp.log(total) + kept["top"] - picked)

        def make_cotangent(at, start, stop, goal, kept):
            place = slice(at + start, at + stop)
            term = logits[place, :]
            spot = lax.broadcasted_iota(jnp.int32, term.shape, 0)
            hit = spot == goal - start
            cot[place, :] = (term * kept["scale"] - jnp.where(hit, live_row, 0.0)).astype(BF16)

        def make_grads():
            acc[...] += natural(cot[0 : acc.shape[0], :], latent())

        def make_latent():
            put(natural(flip[...], cot[...]).T)

        pieces = [make_logits]
        for at, length, first, last, goal in spans:
            kept = {}
            each = cuts(length)
            pieces.append(functools.partial(mask, at, length, first, last))
            pieces += [functools.partial(find_top, at, *cut, kept) for cut in each]
            pieces.append(functools.partial(end_top, kept))
            pieces += [functools.partial(make_terms, at, *cut, goal, kept) for cut in each]
            pieces.append(functools.partial(end_terms, kept))
            pieces += [functools.partial(make_cotangent, at, *cut, goal, kept) for cut in each]
        return pieces + [make_latent, make_grads]

    def tower_call(tower, x_in, code, done):
        kept = {}

        def begin():
            spot = lax.broadcasted_iota(jnp.int32, (rows, table.shape[0]), 1).astype(F32)
            onehot = jnp.where(spot == code, 1.0, 0.0).astype(BF16)
            kept["hidden"] = x_in().astype(F32) + natural(onehot, table[...])

        def scale_rows():
            row_squares = lane_sum(kept["hidden"] * kept["hidden"])
            return row_squares, lax.rsqrt(row_squares * (1.0 / width) + epsilon)

        def keep_squares(block, row_squares):
            place = 2 * (tower * s.blocks + block)
            total = jnp.sum(live * row_squares, axis=0, keepdims=True) * (1.0 / LANES)
            squares[place : place + 1, 0:LANES] = jnp.broadcast_to(total, (1, LANES))

        def into(block):
            place = tower * s.blocks + block
            gained = kept["hidden"] * gains[tower, block : block + 1, :]
            product = natural(gained.astype(BF16), w_in[place])
            row_squares, inv_scale = scale_rows()
            kept["u"] = product * inv_scale
            entry[0, place] = (gained * inv_scale).astype(BF16)
            side[0, place] = jnp.broadcast_to(inv_scale, (rows, LANES))
            if block > 0:
                keep_squares(block - 1, row_squares)

        def out_of(block):
            place = tower * s.blocks + block
            u = kept["u"]
            gate = 0.5 * jnp.tanh(0.5 * u) + 0.5
            after_rows = (u * gate).astype(BF16)
            branch = natural(after_rows, w_out[place])
            kept["hidden"] = kept["hidden"] + branch
            after[0, place] = after_rows
            slope[0, place] = gate * (1.0 + u * (1.0 - gate))
            spot = 2 * place + 1
            squares[spot : spot + 1, :] = jnp.sum(
                branch * branch * live, axis=0, keepdims=True
            )

        def finish():
            row_squares, inv_scale = scale_rows()
            side[0, s.calls + tower] = jnp.broadcast_to(inv_scale, (rows, LANES))
            latent = (kept["hidden"] * inv_scale).astype(BF16)
            lat[0, tower] = latent
            keep_squares(s.blocks - 1, row_squares)
            done(latent)

        pieces = [begin]
        for block in range(s.blocks):
            pieces += [functools.partial(into, block), functools.partial(out_of, block)]
        return pieces + [finish]

    found = {"s": state[...]}
    turn = jnp.minimum(step, s.calls - 1)

    def turn_weights(source, target):
        target[turn] = by_lanes(identity[...], source[turn]).astype(BF16)

    def put_state(value):
        dlat[0, 1] = value

    def put_after(value):
        dlat[0, 0] = value

    def put_last(value):
        dlast[...] = value

    chain = tower_call(0, lambda: found["s"], columns[:, 1:2], lambda y: found.update(a=y))
    chain += tower_call(
        1, lambda: found["a"], columns[:, 2:3] + ACTIONS, lambda y: found.update(n=y)
    )
    weave(
        chain,
        heads(1, lambda: found["s"], live_before, earlier, put_state)
        + heads(0, lambda: found["a"], live_now, step, put_after)
        + [
            functools.partial(turn_weights, w_in, in_turned),
            functools.partial(turn_weights, w_out, out_turned),
        ],
    )
    state[...] = found["n"]
    first = tower_id == 0
    lat_own[0] = jnp.where(first, found["a"], found["n"])
    lat_away[0] = jnp.where(first, found["n"], found["a"])
    total = jnp.sum(live, axis=0, keepdims=True) * (1.0 / LANES)
    squares[s.kinds : s.kinds + 1, 0:LANES] = jnp.broadcast_to(total, (1, LANES))
    at_lane = lax.broadcasted_iota(jnp.int32, sums.shape, 1) == step
    sums[...] = jnp.where(at_lane, lane_sum(squares[...]), sums[...])

    @pl.when(step == s.steps - 1)
    def _():
        for piece in heads(1, lambda: found["n"], live_now, step, put_last):
            piece()
        half = wide // 2
        head_grads[...] = jnp.zeros_like(head_grads)
        head_grads[0, 0:wide, :] = acc0[0:wide, :].astype(BF16)
        head_grads[1, 0:wide, :] = acc1[0:wide, :].astype(BF16)
        small = acc0[wide : wide + s.held, :] + acc1[2 * wide : 2 * wide + s.held, :]
        at = s.small_at - s.value_at
        head_grads[0, at : at + s.held, :] = small.astype(BF16)
        for tower in range(2):
            put = s.reward_at - s.value_at
            at = wide + tower * half
            head_grads[tower, put : put + half, :] = acc1[at : at + half, :].astype(BF16)
            head_grads[tower, wide : wide + sums.shape[0], 0:LANES] = sums[...].astype(BF16)


def backward_kernel(
    sizes, tower_ref,
    lat, entry, after, slope, side, dlat, dlast, code_rows, gains_in, w_in, w_out, head_grads,
    own, away, root_own, root_away,
    carry, gain_sum, cond_sum, grads, gains, inverse_gains,
):
    s = sizes
    turn = pl.program_id(0)
    step = s.steps - 1 - turn
    tower_id = tower_ref[0]
    blocks, width = s.blocks, s.width

    @pl.when(turn == 0)
    def _():
        gains[...] = jnp.ones_like(gains)
        gains[:, 0:blocks, :] = gains_in[:, 0:blocks, :]
        inverse_gains[...] = 1.0 / gains[...]
        carry[...] = dlast[...]
        grads[...] = jnp.zeros_like(grads)
        gain_sum[...] = jnp.zeros_like(gain_sum)
        cond_sum[...] = jnp.zeros_like(cond_sum)

    def over_lanes(column):
        return jnp.concatenate([column] * (width // LANES), axis=1)

    def tower_back(tower, d_latent, code):
        normed = lat[0, tower]
        normed_wide = normed.astype(F32)
        inv_scale = over_lanes(side[0, s.calls + tower])
        base = inv_scale * d_latent
        slant = inv_scale * (lane_sum(d_latent * normed_wide) * (1.0 / width))
        for block in reversed(range(blocks)):
            place = tower * blocks + block
            gain = gains[tower, block : block + 1, :]
            entry_rows = entry[0, place]
            entry_wide = entry_rows.astype(F32)
            inv_scale = over_lanes(side[0, place])
            both = natural(jnp.concatenate([normed, base.astype(BF16)], axis=0), w_out[place])
            d_after = both[s.rows :] - slant * both[: s.rows]
            d_hidden = base - slant * normed_wide
            d_before = (d_after * slope[0, place]).astype(BF16)
            d_entry = natural(d_before, w_in[place])
            grads[tower, blocks + block] += by_rows(after[0, place], d_hidden.astype(BF16))
            grads[tower, block] += by_rows(entry_rows, d_before)
            product = d_entry * entry_wide
            gain_sum[tower, block : block + 1, :] += jnp.sum(product, axis=0, keepdims=True)
            base = d_hidden + inv_scale * (d_entry * gain)
            slant = inv_scale * (lane_sum(product) * (1.0 / width))
            normed_wide = entry_wide * inverse_gains[tower, block : block + 1, :]
            normed = normed_wide.astype(BF16)
        d_hidden = base - slant * normed_wide
        spots = lax.broadcasted_iota(jnp.int32, (cond_sum.shape[0], d_hidden.shape[0]), 0)
        onehot = jnp.where(spots == code, 1.0, 0.0).astype(BF16)
        cond_sum[...] += natural(onehot, d_hidden.astype(BF16))
        return d_hidden

    d_after = tower_back(1, carry[...], code_rows[1, pl.ds(step, 1), :])
    d_state = tower_back(0, d_after + dlat[0, 0], code_rows[0, pl.ds(step, 1), :])
    carry[...] = d_state + dlat[0, 1]

    @pl.when(turn == s.steps - 1)
    def _():
        left = d_state[:, 0 : width // 2].astype(BF16)
        right = d_state[:, width // 2 : width].astype(BF16)
        root_own[...] = jnp.where(tower_id == 0, left, right)
        root_away[...] = jnp.where(tower_id == 0, right, left)
        gain_sum[...] = gain_sum[...] * inverse_gains[...]
        lines = lax.broadcasted_iota(jnp.int32, (s.reward_at - s.sums_at, width), 0)
        for target, which in ((own, tower_id), (away, 1 - tower_id)):
            for matrix in range(s.calls):
                at = matrix * width
                target[at : at + width, :] = grads[which, matrix].astype(BF16)
            target[s.value_at : s.cond_at, :] = head_grads[which]
            sums = head_grads[which, s.wide : s.wide + lines.shape[0], :].astype(F32)
            for block in range(blocks):
                gain = gain_sum[which, block : block + 1, :]
                sums = jnp.where(lines == s.gain_row + block, gain, sums)
            target[s.sums_at : s.reward_at, :] = sums.astype(BF16)
            here = jnp.where(which == 0, cond_sum[...], 0.0)
            target[s.cond_at : s.shared_end, :] = here.astype(BF16)
            if s.total > s.shared_end:
                target[s.shared_end :, :] = jnp.zeros((s.total - s.shared_end, width), BF16)


def logits_kernel(sizes, tower_ref, lat_own, lat_got, value_own, latents, logits):
    rows = sizes.rows
    tower_id = tower_ref[0]
    at_own = pl.ds(pl.multiple_of(tower_id * rows, rows), rows)
    at_got = pl.ds(pl.multiple_of((1 - tower_id) * rows, rows), rows)
    latents[0, at_own, :] = lat_own[0]
    latents[0, at_got, :] = lat_got[0]
    logits[0] = by_lanes(value_own[...], latents[0]).astype(BF16)


def add_and_split_kernel(count, digit_ref, *refs):
    inputs, outputs = refs[:count], refs[count:]
    digit = digit_ref[0]
    for other, target in enumerate(outputs):
        part = digit ^ other
        total = inputs[0][part].astype(F32)
        for source in inputs[1:]:
            total = total + source[part].astype(F32)
        target[...] = total.astype(BF16)


def in_order_kernel(digit_ref, *refs):
    digit = digit_ref[0]
    for other, source in enumerate(refs[:-1]):
        refs[-1][digit ^ other] = source[...]


def unpack_own_kernel(sizes, scalars, *refs):
    s = sizes
    factor = len(refs) - 7
    digit, tower_id = scalars[0], scalars[1]
    w_in, w_out, value, gain, rms, flat, held = refs[factor:]
    width = s.width
    length = refs[0].shape[0]
    for other, source in enumerate(refs[:factor]):
        at = pl.multiple_of((digit ^ other) * length, 16)
        flat[pl.ds(at, length), :] = source[...]
    for block in range(s.blocks):
        at = block * width
        w_in[block] = flat[at : at + width, :].astype(F32)
        at = (s.blocks + block) * width
        w_out[block] = flat[at : at + width, :].astype(F32)
    value[:, 0, :] = flat[s.value_at : s.sums_at, :].astype(F32)[0 : s.bins]
    sums = flat[s.sums_at : s.reward_at, :].astype(F32)
    for block in range(s.blocks):
        gain[block] = sums[s.gain_row + block : s.gain_row + block + 1, :]
    held[...] = sums[:, 0:LANES]
    count = jnp.maximum(held[s.kinds : s.kinds + 1, 0 : s.steps], 1.0)
    for block in range(s.blocks):
        for kind in range(2):
            spot = tower_id * s.calls + 2 * block + kind
            square = held[pl.ds(spot, 1), 0 : s.steps]
            rms[block, kind : kind + 1, :] = jnp.sqrt(jnp.maximum(square, 0.0) / (count * width))


def unpack_shared_kernel(sizes, tower_ref, mine, got, reward, small, cond, joined):
    s = sizes
    tower_id = tower_ref[0]
    half = s.wide // 2
    joined[pl.ds(pl.multiple_of(tower_id * half, 8), half), :] = mine[0:half, :].astype(F32)
    joined[pl.ds(pl.multiple_of((1 - tower_id) * half, 8), half), :] = got[0:half, :].astype(F32)
    reward[...] = joined[0 : s.bins, :]
    for target, at in ((small, s.small_at), (cond, s.cond_at)):
        rows = slice(at - s.reward_at, at - s.reward_at + s.held)
        target[...] = (mine[rows, :].astype(F32) + got[rows, :].astype(F32))[0 : s.table_rows]


def whole(shape):
    return pl.BlockSpec(shape, lambda step, tower: (0,) * len(shape))


def per_step(*tail):
    return pl.BlockSpec((1,) + tail, lambda step, tower: (step,) + (0,) * len(tail))


def swap(value, axis, mask):
    pairs = [(source, source ^ mask) for source in range(lax.axis_size(axis))]
    return lax.ppermute(value, axis, pairs)


AXES = ("tower", "batch")


def exchange_rounds(batch_size):
    factors, left = [], batch_size
    while left > 1:
        factors.append(4 if left % 4 == 0 else 2)
        left //= factors[-1]
    rounds, stride = [], 1
    for factor in factors:
        rounds.append((factor, stride))
        stride *= factor
    turned = rounds[::-1] if len(set(factors)) == 1 else rounds
    return [(one[0], (one[1], two[1])) for one, two in zip(rounds, turned)]


def swap_within(value, strides, other, batch_size):
    pairs = [
        (tower * batch_size + index, tower * batch_size + (index ^ (other * strides[tower])))
        for tower in range(2)
        for index in range(batch_size)
    ]
    return lax.ppermute(value, AXES, pairs)


def my_digit(factor, strides):
    stride = jnp.where(lax.axis_index("tower") == 0, strides[0], strides[1])
    return (lax.axis_index("batch") // stride) % factor


def exchange(value, rounds, batch_size, beside, given, last_kernel):
    shape = jax.ShapeDtypeStruct
    held = value
    digits = []
    for factor, strides in rounds:
        digit = my_digit(factor, strides)
        digits.append(digit)
        rows, width = held[0].shape
        rows = rows // factor
        split = pl.pallas_call(
            functools.partial(add_and_split_kernel, len(held)),
            grid_spec=pltpu.PrefetchScalarGridSpec(
                num_scalar_prefetch=1,
                grid=(1,),
                in_specs=[whole((factor, rows, width))] * len(held),
                out_specs=[whole((rows, width))] * factor,
            ),
            out_shape=[shape((rows, width), BF16)] * factor,
            compiler_params=pltpu.CompilerParams(vmem_limit_bytes=SMALL_LIMIT),
            name="add_and_split",
        )(digit[None], *[part.reshape(factor, rows, width) for part in held])
        first = len(digits) == 1
        if first:
            split, given = lax.optimization_barrier((split, given))
        held = [split[0]] + [
            swap_within(split[other], strides, other, batch_size) for other in range(1, factor)
        ]
        if first:
            done = beside(given)
            held, done = lax.optimization_barrier((held, done))
    piece = functools.reduce(jnp.add, [part.astype(F32) for part in held]).astype(BF16)
    for place in reversed(range(len(rounds))):
        factor, strides = rounds[place]
        rows, width = piece.shape
        held = [piece] + [
            swap_within(piece, strides, other, batch_size) for other in range(1, factor)
        ]
        if place == 0:
            return last_kernel(digits[0], held), done
        piece = pl.pallas_call(
            in_order_kernel,
            grid_spec=pltpu.PrefetchScalarGridSpec(
                num_scalar_prefetch=1,
                grid=(1,),
                in_specs=[whole((rows, width))] * factor,
                out_specs=whole((factor, rows, width)),
            ),
            out_shape=shape((factor, rows, width), BF16),
            compiler_params=pltpu.CompilerParams(vmem_limit_bytes=SMALL_LIMIT),
            name="in_order",
        )(digits[place][None], *held).reshape(factor * rows, width)


def body(
    root_state, cond_table, block_gain, w_in, w_out, value_head, reward_head, small_head,
    unroll_len, actions, codes, policy_target, value_bins, reward_bins,
):
    tower_id = lax.axis_index("tower")
    other_id = 1 - tower_id
    tower_ref = tower_id.astype(jnp.int32)[None]
    steps, batch_rows = actions.shape
    blocks, width = block_gain.shape[1:]
    bins = value_head.shape[2]
    table_rows = cond_table.shape[0]
    rows = batch_rows // 2
    half = width // 2
    parts = lax.axis_size("batch")
    s = Sizes(steps, rows, blocks, width, bins, table_rows, parts)
    calls, wide = s.calls, s.wide

    root_got = swap(root_state, "tower", 1)
    in_own, out_own, gains_own = w_in[0], w_out[0], block_gain[0]
    value_own = value_head[0].T
    in_got = swap(in_own, "tower", 1)
    out_got = swap(out_own, "tower", 1)
    gains_got = swap(gains_own, "tower", 1)
    value_got = swap(value_own, "tower", 1)
    lengths = unroll_len.reshape(1, batch_rows)

    shape = jax.ShapeDtypeStruct
    forward_params = pltpu.CompilerParams(vmem_limit_bytes=FORWARD_LIMIT)
    backward_params = pltpu.CompilerParams(vmem_limit_bytes=BACKWARD_LIMIT)
    small_params = pltpu.CompilerParams(vmem_limit_bytes=SMALL_LIMIT)
    products = steps * rows * (4 * blocks * width * width + 9 * width * wide)
    cost = pl.CostEstimate(flops=2 * products, bytes_accessed=40 * 2**20, transcendentals=0)
    (
        lat, lat_own, lat_away, entry, after, slope, side, dlat, dlast, loss, head_grads,
        in_turned, out_turned, code_rows, gains,
    ) = pl.pallas_call(
        functools.partial(forward_kernel, s),
        grid_spec=pltpu.PrefetchScalarGridSpec(
            num_scalar_prefetch=1,
            grid=(steps,),
            in_specs=[pl.BlockSpec(memory_space=pltpu.HBM)] * 14
            + [
                pl.BlockSpec((rows, half), lambda step, tower: (tower[0], 0)),
                whole((blocks, width)),
                whole((blocks, width, width)),
                whole((blocks, width, width)),
                whole((bins, width)),
            ],
            out_specs=[
                per_step(2, rows, width),
                per_step(rows, width),
                per_step(rows, width),
                per_step(calls, rows, width),
                per_step(calls, rows, width),
                per_step(calls, rows, width),
                per_step(calls + 2, rows, LANES),
                per_step(2, rows, width),
                whole((rows, width)),
                whole((8, rows)),
                whole((2, s.head_rows, width)),
                whole((calls, width, width)),
                whole((calls, width, width)),
                whole((2, steps, rows)),
                whole((2, 8, width)),
            ],
            scratch_shapes=[
                pltpu.VMEM((rows, half), BF16),
                pltpu.VMEM((1, rows), jnp.int32),
                pltpu.VMEM((steps, rows), jnp.int32),
                pltpu.VMEM((steps, rows), jnp.int32),
                pltpu.VMEM((steps, rows), jnp.int32),
                pltpu.VMEM((steps, 2, rows), jnp.int32),
                pltpu.VMEM((steps, rows), jnp.int32),
                pltpu.VMEM((table_rows, width), BF16),
                pltpu.VMEM((blocks, width), BF16),
                pltpu.VMEM((blocks, width, width), BF16),
                pltpu.VMEM((blocks, width, width), BF16),
                pltpu.VMEM((bins, width), BF16),
                pltpu.VMEM((bins, width), BF16),
                pltpu.VMEM((table_rows, width), BF16),
                pltpu.SemaphoreType.DMA((14,)),
                pltpu.VMEM((rows, width), BF16),
                pltpu.VMEM((width, width), BF16),
                pltpu.VMEM((LANES, width), BF16),
                pltpu.VMEM((calls, width, width), BF16),
                pltpu.VMEM((calls, width, width), BF16),
                pltpu.VMEM((s.depth[0], width), BF16),
                pltpu.VMEM((s.depth[1], width), BF16),
                pltpu.VMEM((width, s.depth[0]), BF16),
                pltpu.VMEM((width, s.depth[1]), BF16),
                pltpu.VMEM((s.stack[0], width), F32),
                pltpu.VMEM((s.stack[1], width), F32),
                pltpu.VMEM((s.stack[0], rows), F32),
                pltpu.VMEM((s.stack[1], rows), F32),
                pltpu.VMEM((s.depth[0], rows), BF16),
                pltpu.VMEM((s.depth[1], rows), BF16),
                pltpu.VMEM((s.reward_at - s.sums_at, LANES), F32),
                pltpu.VMEM((s.reward_at - s.sums_at, width), F32),
            ],
        ),
        out_shape=[
            shape((steps, 2, rows, width), BF16),
            shape((steps, rows, width), BF16),
            shape((steps, rows, width), BF16),
            shape((steps, calls, rows, width), BF16),
            shape((steps, calls, rows, width), BF16),
            shape((steps, calls, rows, width), F32),
            shape((steps, calls + 2, rows, LANES), F32),
            shape((steps, 2, rows, width), F32),
            shape((rows, width), F32),
            shape((8, rows), F32),
            shape((2, s.head_rows, width), BF16),
            shape((calls, width, width), BF16),
            shape((calls, width, width), BF16),
            shape((2, steps, rows), jnp.int32),
            shape((2, 8, width), F32),
        ],
        compiler_params=forward_params,
        cost_estimate=cost,
        name="unroll_forward",
    )(
        tower_ref,
        *[
            pltpu.with_memory_space_constraint(value, pltpu.HBM)
            for value in (
                root_state, lengths, actions, codes, policy_target,
                jnp.swapaxes(value_bins, 0, 1), reward_bins, cond_table, gains_own,
                in_own, out_own, value_own, reward_head.T, small_head.T,
            )
        ],
        root_got, gains_got, in_got, out_got, value_got,
    )

    descending = lambda *tail: pl.BlockSpec(
        (1,) + tail, lambda step, tower: (steps - 1 - step,) + (0,) * len(tail)
    )
    own, away, root_own, root_away = pl.pallas_call(
        functools.partial(backward_kernel, s),
        grid_spec=pltpu.PrefetchScalarGridSpec(
            num_scalar_prefetch=1,
            grid=(steps,),
            in_specs=[
                descending(2, rows, width),
                descending(calls, rows, width),
                descending(calls, rows, width),
                descending(calls, rows, width),
                descending(calls + 2, rows, LANES),
                descending(2, rows, width),
                whole((rows, width)),
                whole((2, steps, rows)),
                whole((2, 8, width)),
                whole((calls, width, width)),
                whole((calls, width, width)),
                whole((2, s.head_rows, width)),
            ],
            out_specs=[
                whole((s.total, width)),
                whole((s.total, width)),
                whole((rows, half)),
                whole((rows, half)),
            ],
            scratch_shapes=[
                pltpu.VMEM((rows, width), F32),
                pltpu.VMEM((2, 16, width), F32),
                pltpu.VMEM((s.held, width), F32),
                pltpu.VMEM((2, calls, width, width), F32),
                pltpu.VMEM((2, 16, width), F32),
                pltpu.VMEM((2, 16, width), F32),
            ],
        ),
        out_shape=[
            shape((s.total, width), BF16),
            shape((s.total, width), BF16),
            shape((rows, half), BF16),
            shape((rows, half), BF16),
        ],
        compiler_params=backward_params,
        cost_estimate=cost,
        name="unroll_backward",
    )(
        tower_ref, lat, entry, after, slope, side, dlat, dlast, code_rows, gains,
        in_turned, out_turned, head_grads,
    )
    got = swap(away, "tower", 1)

    def beside(given):
        lat_own, lat_away, loss, root_own, root_away = given
        lat_got = swap(lat_away, "tower", 1)
        loss_own = loss[0]
        loss_got = swap(loss_own, "tower", 1)
        root_got = swap(root_away, "tower", 1)

        latents, logits = pl.pallas_call(
            functools.partial(logits_kernel, s),
            grid_spec=pltpu.PrefetchScalarGridSpec(
                num_scalar_prefetch=1,
                grid=(steps,),
                in_specs=[per_step(rows, width), per_step(rows, width), whole((bins, width))],
                out_specs=[per_step(batch_rows, width), per_step(bins, batch_rows)],
            ),
            out_shape=[
                shape((steps, batch_rows, width), BF16),
                shape((steps, bins, batch_rows), BF16),
            ],
            compiler_params=small_params,
            cost_estimate=pl.CostEstimate(
                flops=2 * steps * batch_rows * width * wide, bytes_accessed=6 * 2**20, transcendentals=0
            ),
            name="latents_and_logits",
        )(tower_ref, lat_own, lat_got, value_own)

        def in_order(mine_value, got_value, axis):
            return jnp.where(
                tower_id == 0,
                jnp.concatenate([mine_value, got_value], axis=axis),
                jnp.concatenate([got_value, mine_value], axis=axis),
            )

        row_loss = in_order(loss_own, loss_got, 0)
        grad_root = in_order(root_own, root_got, 0).astype(F32)
        return latents, logits, row_loss, grad_root

    rounds = exchange_rounds(parts)

    def unpack(digit, held):
        scalars = jnp.stack([digit, tower_id]).astype(jnp.int32)
        length = held[0].shape[0]
        block = s.reward_at // length
        at = s.reward_at - block * length
        parts_of = [part[at : at + s.shared_end - s.reward_at] for part in held]
        shared = parts_of[0]
        for other in range(1, len(held)):
            shared = jnp.where((digit ^ other) == block, parts_of[other], shared)
        shared_got = swap(shared, "tower", 1)
        return (shared, shared_got), pl.pallas_call(
            functools.partial(unpack_own_kernel, s),
            grid_spec=pltpu.PrefetchScalarGridSpec(
                num_scalar_prefetch=1,
                grid=(1,),
                in_specs=[whole(part.shape) for part in held],
                out_specs=[
                    whole((blocks, width, width)),
                    whole((blocks, width, width)),
                    whole((bins, 1, width)),
                    whole((blocks, 1, width)),
                    whole((blocks, 2, steps)),
                ],
                scratch_shapes=[
                    pltpu.VMEM((s.total, width), BF16),
                    pltpu.VMEM((s.reward_at - s.sums_at, LANES), F32),
                ],
            ),
            out_shape=[
                shape((blocks, width, width), F32),
                shape((blocks, width, width), F32),
                shape((bins, 1, width), F32),
                shape((blocks, 1, width), F32),
                shape((blocks, 2, steps), F32),
            ],
            compiler_params=small_params,
            name="unpack_own",
        )(scalars, *held)

    given = (lat_own, lat_away, loss, root_own, root_away)
    unpacked, done = exchange([own, got], rounds, parts, beside, given, unpack)
    (shared, shared_got), (grad_in, grad_out, value_t, gain_t, rms_t) = unpacked
    latents, logits, row_loss, grad_root = done
    reward_t, small_t, grad_cond = pl.pallas_call(
        functools.partial(unpack_shared_kernel, s),
        grid_spec=pltpu.PrefetchScalarGridSpec(
            num_scalar_prefetch=1,
            grid=(1,),
            in_specs=[whole(shared.shape), whole(shared.shape)],
            out_specs=[
                whole((bins, width)),
                whole((table_rows, width)),
                whole((table_rows, width)),
            ],
            scratch_shapes=[pltpu.VMEM((s.wide, width), F32)],
        ),
        out_shape=[
            shape((bins, width), F32),
            shape((table_rows, width), F32),
            shape((table_rows, width), F32),
        ],
        compiler_params=small_params,
        name="unpack_shared",
    )(tower_ref, shared, shared_got)
    layer_rms = jnp.transpose(rms_t, (2, 0, 1))[None]
    return (
        latents[None],
        jnp.swapaxes(logits, 1, 2)[None],
        row_loss,
        layer_rms,
        grad_root,
        grad_cond,
        jnp.swapaxes(gain_t, 0, 1),
        grad_in[None],
        grad_out[None],
        jnp.transpose(value_t, (1, 2, 0)),
        reward_t.T,
        small_t.T,
    )


def solution(mesh):
    placed = (
        P("batch", "tower"),
        P(),
        P("tower", None, None),
        P("tower", None, None, None),
        P("tower", None, None, None),
        P("tower", None, None),
        P(),
        P(),
        P("batch"),
        P(None, "batch"),
        P(None, "batch"),
        P(None, "batch"),
        P(None, None, "batch"),
        P(None, "batch"),
    )
    return jax.shard_map(
        body,
        mesh=mesh,
        in_specs=placed,
        out_specs=(
            P("tower", None, "batch", None),
            P("tower", None, "batch", None),
            P("batch"),
            P("tower", None, None, None),
            P("batch", "tower"),
            P(),
            P("tower", None, None),
            P("tower", None, None, None),
            P("tower", None, None, None),
            P("tower", None, None),
            P(),
            P(),
        ),
        check_vma=False,
    )
```

```python
import functools

import jax
import jax.numpy as jnp
from jax import lax
from jax.experimental import pallas as pl
from jax.experimental.pallas import tpu as pltpu
from jax.sharding import PartitionSpec as P

ACTIONS = 4
LANES = 128
MIB = 1024 * 1024
FORWARD_LIMIT = 20 * MIB
BACKWARD_LIMIT = 20 * MIB
SMALL_LIMIT = 12 * MIB
epsilon = 1e-06
very_negative = -1e30
F32 = jnp.float32
BF16 = jnp.bfloat16


def natural(left, right):
    return lax.dot_general(left, right, (((1,), (0,)), ((), ())), preferred_element_type=F32)


def by_rows(left, right):
    return lax.dot_general(left, right, (((0,), (0,)), ((), ())), preferred_element_type=F32)


def by_lanes(left, right):
    return lax.dot_general(left, right, (((1,), (1,)), ((), ())), preferred_element_type=F32)


def round_up(value, unit):
    return (value + unit - 1) // unit * unit


def lane_sum(value):
    return jnp.sum(value, axis=-1, keepdims=True)


def inverse_rms(hidden):
    return lax.rsqrt(lane_sum(hidden * hidden) * (1.0 / hidden.shape[-1]) + epsilon)


def weave(*tasks):
    tasks = [(list(task)) for task in tasks]
    longest = max(len(task) for task in tasks)
    done = [0] * len(tasks)
    for turn in range(longest):
        for which, task in enumerate(tasks):
            until = (turn + 1) * len(task) // longest
            while done[which] < until:
                task[done[which]]()
                done[which] += 1


def cuts(length, unit=160):
    return [(start, min(start + unit, length)) for start in range(0, length, unit)]


class Sizes:
    def __init__(self, steps, rows, blocks, width, bins, table_rows, parts):
        self.steps, self.rows, self.blocks, self.width = steps, rows, blocks, width
        self.bins, self.table_rows, self.parts = bins, table_rows, parts
        self.calls = 2 * blocks
        self.pair = 2 if steps % 2 == 0 else 1
        self.wide = round_up(bins, 32)
        self.held = round_up(table_rows, 16)
        self.stack = (self.wide + self.held, 2 * self.wide + self.held)
        self.depth = tuple(round_up(rows_in, LANES) for rows_in in self.stack)
        half = self.wide // 2
        self.value_at = self.calls * width
        self.sums_at = self.value_at + self.wide
        self.kinds = 2 * self.calls
        self.gain_row = self.kinds + 1
        self.reward_at = self.sums_at + round_up(self.gain_row + blocks, 16)
        self.small_at = self.reward_at + half
        self.cond_at = self.small_at + self.held
        self.shared_end = self.cond_at + self.held
        self.total = round_up(self.shared_end, 16 * parts)
        self.head_rows = self.cond_at - self.value_at


def forward_kernel(
    sizes, tower_ref,
    root_hbm, lengths_hbm, actions_hbm, codes_hbm, policy_hbm, value_bins_hbm, reward_bins_hbm,
    table_hbm, gains_hbm, in_hbm, out_hbm, value_hbm, reward_hbm, small_hbm,
    root_got, gains_got, in_got, out_got, value_got,
    lat, lat_own, lat_away, entry, after, slope, side, dlat, dlast, loss, head_grads, turned, code_rows, gains,
    root_own, lengths, actions, codes, policy, value_bins, reward_bins,
    table_in, gains_own, in_own, out_own, value_own, reward_in, small_in, sems,
    state, past0, past1, identity, table, weights, heads0, heads1, flip0, flip1, acc0, acc1,
    logits0, logits1, cot0, cot1, sums, squares,
):
    s = sizes
    pair = s.pair
    turn = pl.program_id(0)
    first_step = turn * pair
    tower_id = tower_ref[0]
    rows, width, wide = s.rows, s.width, s.wide

    @pl.when(turn == 0)
    def _():
        here = pl.ds(pl.multiple_of(tower_id * rows, rows), rows)
        moves = [
            (root_hbm.at[here], root_own),
            (lengths_hbm.at[:, here], lengths),
            (actions_hbm.at[:, here], actions),
            (codes_hbm.at[:, here], codes),
            (policy_hbm.at[:, here], policy),
            (value_bins_hbm.at[:, :, here], value_bins),
            (reward_bins_hbm.at[:, here], reward_bins),
            (table_hbm, table_in),
            (gains_hbm, gains_own),
            (in_hbm, in_own),
            (out_hbm, out_own),
            (value_hbm, value_own),
            (reward_hbm, reward_in),
            (small_hbm, small_in),
        ]
        moves = [
            pltpu.make_async_copy(source, target, sems.at[place])
            for place, (source, target) in enumerate(moves)
        ]
        for move in moves:
            move.start()
        for move in moves:
            move.wait()
        first = tower_id == 0
        code_rows[0] = actions[...]
        code_rows[1] = codes[...] + ACTIONS
        state[:, 0 : width // 2] = jnp.where(first, root_own[...], root_got[...])
        state[:, width // 2 : width] = jnp.where(first, root_got[...], root_own[...])
        for tower, w_first, w_second in (
            (tower_id, in_own, out_own),
            (1 - tower_id, in_got, out_got),
        ):
            weights[pl.ds(tower * s.blocks, s.blocks)] = w_first[...]
            weights[pl.ds(s.calls + tower * s.blocks, s.blocks)] = w_second[...]
        gains[...] = jnp.zeros_like(gains)
        gains[tower_id, 0 : s.blocks, :] = gains_own[...].astype(F32)
        gains[1 - tower_id, 0 : s.blocks, :] = gains_got[...].astype(F32)
        table[...] = jnp.zeros_like(table)
        table[0 : s.table_rows, :] = table_in[...]
        heads0[...] = jnp.zeros_like(heads0)
        heads1[...] = jnp.zeros_like(heads1)
        heads0[0 : s.bins, :] = jnp.where(first, value_own[...], value_got[...])
        heads1[0 : s.bins, :] = jnp.where(first, value_got[...], value_own[...])
        heads1[wide : wide + s.bins, :] = reward_in[...]
        heads0[wide : wide + s.table_rows, :] = small_in[...]
        heads1[2 * wide : 2 * wide + s.table_rows, :] = small_in[...]
        down = lax.broadcasted_iota(jnp.int32, (width, width), 0)
        across = lax.broadcasted_iota(jnp.int32, (width, width), 1)
        identity[...] = jnp.where(down == across, 1.0, 0.0).astype(BF16)
        flip0[...] = by_lanes(identity[...], heads0[...]).astype(BF16)
        flip1[...] = by_lanes(identity[...], heads1[...]).astype(BF16)
        past0[...] = jnp.zeros_like(past0)
        past1[...] = jnp.zeros_like(past1)
        cot0[...] = jnp.zeros_like(cot0)
        cot1[...] = jnp.zeros_like(cot1)
        acc0[...] = jnp.zeros_like(acc0)
        acc1[...] = jnp.zeros_like(acc1)
        sums[...] = jnp.zeros_like(sums)
        squares[...] = jnp.zeros_like(squares)
        loss[...] = jnp.zeros_like(loss)

    eights = lax.broadcasted_iota(jnp.int32, (8, pair * rows), 0)
    before = jnp.maximum(first_step - pair, 0)

    def pair_row(kind, at_step, lead=()):
        return jnp.concatenate(
            [kind[(pl.ds(at_step + offset, 1),) + lead] for offset in range(pair)], axis=1
        )

    def live_rows(at_step):
        return jnp.concatenate(
            [(at_step + offset < lengths[...]).astype(F32) for offset in range(pair)], axis=1
        )

    kinds = []
    for offset in range(pair):
        step = first_step + offset
        kinds.append((step < lengths[...]).astype(F32))
        kinds.append(actions[pl.ds(step, 1), :].astype(F32))
        kinds.append((codes[pl.ds(step, 1), :] + ACTIONS).astype(F32))
    kinds.append(jnp.zeros((8 - len(kinds), rows), F32))
    columns = jnp.concatenate(kinds, axis=0).T

    def heads(tower, live_row, at_step, put):
        latent = past0 if tower == 0 else past1
        stack, flip, logits, cot, acc = (
            (heads0, flip0, logits0, cot0, acc0)
            if tower == 0
            else (heads1, flip1, logits1, cot1, acc1)
        )
        pick = lambda kind: pair_row(kind, at_step)
        value_goal = pair_row(value_bins, at_step, (tower,))
        spans = [(0, wide, 0, s.bins, value_goal)]
        if tower == 1:
            spans.append((wide, wide, 0, s.bins, pick(reward_bins)))
            spans.append((2 * wide, s.held, 0, ACTIONS, pick(policy)))
        else:
            spans.append((wide, s.held, ACTIONS, s.table_rows, pick(codes) + ACTIONS))

        def make_logits():
            logits[...] = by_lanes(stack[0 : logits.shape[0], :], latent[...])

        def eight_rows(value):
            return value.reshape(-1, 8, pair * rows)

        def mask(at, length, first, last):
            for start in range(0, length, 8):
                if start < first or start + 8 > last:
                    inside = (eights >= first - start) & (eights < last - start)
                    place = slice(at + start, at + start + 8)
                    logits[place, :] = jnp.where(inside, logits[place, :], very_negative)

        def find_top(at, start, stop, kept):
            top = jnp.max(eight_rows(logits[at + start : at + stop, :]), axis=0)
            kept["top"] = jnp.maximum(kept["top"], top) if "top" in kept else top

        def end_top(kept):
            kept["top"] = jnp.max(kept["top"], axis=0, keepdims=True)

        def make_terms(at, start, stop, goal, kept):
            place = slice(at + start, at + stop)
            value = logits[place, :]
            spot = lax.broadcasted_iota(jnp.int32, value.shape, 0)
            term = jnp.exp(value - kept["top"])
            logits[place, :] = term
            hit = spot == goal - start
            total = jnp.sum(eight_rows(term), axis=0)
            picked = jnp.sum(eight_rows(jnp.where(hit, value, 0.0)), axis=0)
            kept["total"] = kept["total"] + total if "total" in kept else total
            kept["picked"] = kept["picked"] + picked if "picked" in kept else picked

        def end_terms(kept):
            total = jnp.sum(kept["total"], axis=0, keepdims=True)
            picked = jnp.sum(kept["picked"], axis=0, keepdims=True)
            kept["scale"] = live_row / total
            row_loss = live_row * (jnp.log(total) + kept["top"] - picked)
            for offset in range(pair):
                loss[0:1, :] += row_loss[:, offset * rows : (offset + 1) * rows]

        def make_cotangent(at, start, stop, goal, kept):
            place = slice(at + start, at + stop)
            term = logits[place, :]
            spot = lax.broadcasted_iota(jnp.int32, term.shape, 0)
            hit = spot == goal - start
            cot[place, :] = (term * kept["scale"] - jnp.where(hit, live_row, 0.0)).astype(BF16)

        def make_grads():
            acc[...] += natural(cot[0 : acc.shape[0], :], latent[...])

        def make_latent():
            d_latent = natural(flip[...], cot[...]).T
            for offset in range(pair):
                put[offset, tower] = d_latent[offset * rows : (offset + 1) * rows]

        pieces = [make_logits]
        for at, length, first, last, goal in spans:
            kept = {}
            each = cuts(length)
            pieces.append(functools.partial(mask, at, length, first, last))
            pieces += [functools.partial(find_top, at, *cut, kept) for cut in each]
            pieces.append(functools.partial(end_top, kept))
            pieces += [functools.partial(make_terms, at, *cut, goal, kept) for cut in each]
            pieces.append(functools.partial(end_terms, kept))
            pieces += [functools.partial(make_cotangent, at, *cut, goal, kept) for cut in each]
        return pieces + [make_latent, make_grads]

    def tower_call(offset, tower, x_in, done):
        kept = {}
        live = columns[:, 3 * offset : 3 * offset + 1]
        code = columns[:, 3 * offset + 1 + tower : 3 * offset + 2 + tower]

        def begin():
            spot = lax.broadcasted_iota(jnp.int32, (rows, table.shape[0]), 1).astype(F32)
            onehot = jnp.where(spot == code, 1.0, 0.0).astype(BF16)
            kept["hidden"] = x_in().astype(F32) + natural(onehot, table[...])

        def scale_rows():
            row_squares = lane_sum(kept["hidden"] * kept["hidden"])
            return row_squares, lax.rsqrt(row_squares * (1.0 / width) + epsilon)

        def keep_squares(block, row_squares):
            place = 2 * (tower * s.blocks + block)
            total = jnp.sum(live * row_squares, axis=0, keepdims=True) * (1.0 / LANES)
            squares[offset, place : place + 1, 0:LANES] = jnp.broadcast_to(total, (1, LANES))

        def into(block):
            place = tower * s.blocks + block
            gained = kept["hidden"] * gains[tower, block : block + 1, :]
            product = natural(gained.astype(BF16), weights[place])
            row_squares, inv_scale = scale_rows()
            kept["u"] = product * inv_scale
            entry[offset, place] = (gained * inv_scale).astype(BF16)
            side[offset, place] = jnp.broadcast_to(inv_scale, (rows, LANES))
            if block > 0:
                keep_squares(block - 1, row_squares)

        def out_of(block):
            place = tower * s.blocks + block
            u = kept["u"]
            gate = 0.5 * jnp.tanh(0.5 * u) + 0.5
            after_rows = (u * gate).astype(BF16)
            branch = natural(after_rows, weights[s.calls + place])
            kept["hidden"] = kept["hidden"] + branch
            after[offset, place] = after_rows
            slope[offset, place] = gate * (1.0 + u * (1.0 - gate))
            spot = 2 * place + 1
            squares[offset, spot : spot + 1, :] = jnp.sum(
                branch * branch * live, axis=0, keepdims=True
            )

        def finish():
            row_squares, inv_scale = scale_rows()
            side[offset, s.calls + tower] = jnp.broadcast_to(inv_scale, (rows, LANES))
            latent = (kept["hidden"] * inv_scale).astype(BF16)
            lat[offset, tower] = latent
            keep_squares(s.blocks - 1, row_squares)
            if tower == 0:
                total = jnp.sum(live, axis=0, keepdims=True) * (1.0 / LANES)
                squares[offset, s.kinds : s.kinds + 1, 0:LANES] = jnp.broadcast_to(
                    total, (1, LANES)
                )
            done(latent)

        pieces = [begin]
        for block in range(s.blocks):
            pieces += [functools.partial(into, block), functools.partial(out_of, block)]
        return pieces + [finish]

    found = {(1, -1): state[...]}
    chain = []
    for offset in range(pair):
        for tower in range(2):
            source = (0, offset) if tower == 1 else (1, offset - 1)
            chain += tower_call(
                offset,
                tower,
                functools.partial(found.get, source),
                functools.partial(found.__setitem__, (tower, offset)),
            )

    turns = -(-2 * s.calls // (s.steps // pair))

    def turn_weights(which):
        matrix = jnp.minimum(turn * turns + which, 2 * s.calls - 1)
        turned[matrix] = by_lanes(identity[...], weights[matrix]).astype(BF16)

    live_before = jnp.where(turn > 0, live_rows(before), 0.0)
    weave(
        chain,
        heads(1, live_before, before, dlat)
        + heads(0, live_before, before, dlat)
        + [functools.partial(turn_weights, which) for which in range(turns)],
    )
    state[...] = found[1, pair - 1]
    first = tower_id == 0
    at_lane = lax.broadcasted_iota(jnp.int32, sums.shape, 1)
    for offset in range(pair):
        after_state, next_state = found[0, offset], found[1, offset]
        past0[offset * rows : (offset + 1) * rows, :] = after_state
        past1[offset * rows : (offset + 1) * rows, :] = next_state
        lat_own[offset] = jnp.where(first, after_state, next_state)
        lat_away[offset] = jnp.where(first, next_state, after_state)
        total = lane_sum(squares[offset])
        sums[...] = jnp.where(at_lane == first_step + offset, total, sums[...])

    @pl.when(turn == pl.num_programs(0) - 1)
    def _():
        live_now = live_rows(first_step)
        weave(heads(1, live_now, first_step, dlast), heads(0, live_now, first_step, dlast))
        half = wide // 2
        head_grads[...] = jnp.zeros_like(head_grads)
        head_grads[0, 0:wide, :] = acc0[0:wide, :].astype(BF16)
        head_grads[1, 0:wide, :] = acc1[0:wide, :].astype(BF16)
        small = acc0[wide : wide + s.held, :] + acc1[2 * wide : 2 * wide + s.held, :]
        at = s.small_at - s.value_at
        head_grads[0, at : at + s.held, :] = small.astype(BF16)
        for tower in range(2):
            put = s.reward_at - s.value_at
            at = wide + tower * half
            head_grads[tower, put : put + half, :] = acc1[at : at + half, :].astype(BF16)
            head_grads[tower, wide : wide + sums.shape[0], 0:LANES] = sums[...].astype(BF16)


def backward_kernel(
    sizes, tower_ref,
    lat, entry, after, slope, side, dlat, dlast, code_rows, gains_in, turned, head_grads,
    own, away, root_own, root_away,
    carry, gain_sum, cond_sum, grads, gains, inverse_gains, d_after_kept, d_before_kept,
    d_hidden_kept,
):
    s = sizes
    pair = s.pair
    turn = pl.program_id(0)
    first_step = s.steps - pair * (turn + 1)
    tower_id = tower_ref[0]
    blocks, width = s.blocks, s.width

    @pl.when(turn == 0)
    def _():
        gains[...] = jnp.ones_like(gains)
        gains[:, 0:blocks, :] = gains_in[:, 0:blocks, :]
        inverse_gains[...] = 1.0 / gains[...]
        carry[...] = jnp.zeros_like(carry)
        grads[...] = jnp.zeros_like(grads)
        gain_sum[...] = jnp.zeros_like(gain_sum)
        cond_sum[...] = jnp.zeros_like(cond_sum)

    def over_lanes(column):
        return jnp.concatenate([column] * (width // LANES), axis=1)

    def stacked(parts):
        return jnp.concatenate([parts[offset] for offset in range(pair)], axis=0)

    def add_grads(matrix, rows_of, place, kept, now):
        parts = [now] + [kept[offset, place] for offset in range(1, pair)]
        grads[matrix // s.calls, matrix % s.calls] += by_rows(
            stacked([rows_of[offset, place] for offset in range(pair)]), stacked(parts)
        )

    def tower_back(offset, tower, d_latent):
        normed = lat[offset, tower]
        normed_wide = normed.astype(F32)
        inv_scale = over_lanes(side[offset, s.calls + tower])
        base = inv_scale * d_latent
        slant = inv_scale * (lane_sum(d_latent * normed_wide) * (1.0 / width))
        for block in reversed(range(blocks)):
            place = tower * blocks + block
            gain = gains[tower, block : block + 1, :]
            entry_wide = entry[offset, place].astype(F32)
            inv_scale = over_lanes(side[offset, place])
            both = natural(
                jnp.concatenate([normed, base.astype(BF16)], axis=0), turned[s.calls + place]
            )
            d_after = both[s.rows :] - slant * both[: s.rows]
            d_hidden = base - slant * normed_wide
            d_branch = d_hidden.astype(BF16)
            d_before = (d_after * slope[offset, place]).astype(BF16)
            d_entry = natural(d_before, turned[place])
            if offset > 0:
                d_after_kept[offset, place] = d_branch
                d_before_kept[offset, place] = d_before
            else:
                matrix = tower * s.calls + block
                add_grads(matrix + blocks, after, place, d_after_kept, d_branch)
                add_grads(matrix, entry, place, d_before_kept, d_before)
            product = d_entry * entry_wide
            gain_sum[tower, block : block + 1, :] += jnp.sum(product, axis=0, keepdims=True)
            base = d_hidden + inv_scale * (d_entry * gain)
            slant = inv_scale * (lane_sum(product) * (1.0 / width))
            normed_wide = entry_wide * inverse_gains[tower, block : block + 1, :]
            normed = normed_wide.astype(BF16)
        d_hidden = base - slant * normed_wide
        if offset > 0:
            d_hidden_kept[offset, tower] = d_hidden.astype(BF16)
        else:
            code = jnp.concatenate(
                [code_rows[tower, pl.ds(first_step + each, 1), :] for each in range(pair)], axis=1
            )
            spots = lax.broadcasted_iota(jnp.int32, (cond_sum.shape[0], pair * s.rows), 0)
            onehot = jnp.where(spots == code, 1.0, 0.0).astype(BF16)
            parts = [d_hidden.astype(BF16)]
            parts += [d_hidden_kept[each, tower] for each in range(1, pair)]
            cond_sum[...] += natural(onehot, stacked(parts))
        return d_hidden

    def from_heads(offset, tower):
        return jnp.where(turn == 0, dlast[offset, tower], dlat[offset, tower])

    d_state = carry[...]
    for offset in reversed(range(pair)):
        d_after_state = tower_back(offset, 1, d_state + from_heads(offset, 1))
        d_state = tower_back(offset, 0, d_after_state + from_heads(offset, 0))
    carry[...] = d_state

    @pl.when(turn == pl.num_programs(0) - 1)
    def _():
        left = d_state[:, 0 : width // 2].astype(BF16)
        right = d_state[:, width // 2 : width].astype(BF16)
        root_own[...] = jnp.where(tower_id == 0, left, right)
        root_away[...] = jnp.where(tower_id == 0, right, left)
        gain_sum[...] = gain_sum[...] * inverse_gains[...]
        lines = lax.broadcasted_iota(jnp.int32, (s.reward_at - s.sums_at, width), 0)
        for target, which in ((own, tower_id), (away, 1 - tower_id)):
            for matrix in range(s.calls):
                at = matrix * width
                target[at : at + width, :] = grads[which, matrix].astype(BF16)
            target[s.value_at : s.cond_at, :] = head_grads[which]
            sums = head_grads[which, s.wide : s.wide + lines.shape[0], :].astype(F32)
            for block in range(blocks):
                gain = gain_sum[which, block : block + 1, :]
                sums = jnp.where(lines == s.gain_row + block, gain, sums)
            target[s.sums_at : s.reward_at, :] = sums.astype(BF16)
            here = jnp.where(which == 0, cond_sum[...], 0.0)
            target[s.cond_at : s.shared_end, :] = here.astype(BF16)
            if s.total > s.shared_end:
                target[s.shared_end :, :] = jnp.zeros((s.total - s.shared_end, width), BF16)


def logits_kernel(sizes, tower_ref, lat_own, lat_got, value_own, latents, logits):
    rows = sizes.rows
    tower_id = tower_ref[0]
    at_own = pl.ds(pl.multiple_of(tower_id * rows, rows), rows)
    at_got = pl.ds(pl.multiple_of((1 - tower_id) * rows, rows), rows)
    latents[0, at_own, :] = lat_own[0]
    latents[0, at_got, :] = lat_got[0]
    logits[0] = by_lanes(value_own[...], latents[0]).astype(BF16)


def add_and_split_kernel(count, digit_ref, *refs):
    inputs, outputs = refs[:count], refs[count:]
    digit = digit_ref[0]
    for other, target in enumerate(outputs):
        part = digit ^ other
        total = inputs[0][part].astype(F32)
        for source in inputs[1:]:
            total = total + source[part].astype(F32)
        target[...] = total.astype(BF16)


def in_order_kernel(digit_ref, *refs):
    digit = digit_ref[0]
    for other, source in enumerate(refs[:-1]):
        refs[-1][digit ^ other] = source[...]


def unpack_own_kernel(sizes, scalars, *refs):
    s = sizes
    factor = len(refs) - 7
    digit, tower_id = scalars[0], scalars[1]
    w_in, w_out, value, gain, rms, flat, held = refs[factor:]
    width = s.width
    length = refs[0].shape[0]
    for other, source in enumerate(refs[:factor]):
        at = pl.multiple_of((digit ^ other) * length, 16)
        flat[pl.ds(at, length), :] = source[...]
    for block in range(s.blocks):
        at = block * width
        w_in[block] = flat[at : at + width, :].astype(F32)
        at = (s.blocks + block) * width
        w_out[block] = flat[at : at + width, :].astype(F32)
    value[:, 0, :] = flat[s.value_at : s.sums_at, :].astype(F32)[0 : s.bins]
    sums = flat[s.sums_at : s.reward_at, :].astype(F32)
    for block in range(s.blocks):
        gain[block] = sums[s.gain_row + block : s.gain_row + block + 1, :]
    held[...] = sums[:, 0:LANES]
    count = jnp.maximum(held[s.kinds : s.kinds + 1, 0 : s.steps], 1.0)
    for block in range(s.blocks):
        for kind in range(2):
            spot = tower_id * s.calls + 2 * block + kind
            square = held[pl.ds(spot, 1), 0 : s.steps]
            rms[block, kind : kind + 1, :] = jnp.sqrt(jnp.maximum(square, 0.0) / (count * width))


def unpack_shared_kernel(sizes, tower_ref, mine, got, reward, small, cond, joined):
    s = sizes
    tower_id = tower_ref[0]
    half = s.wide // 2
    joined[pl.ds(pl.multiple_of(tower_id * half, 8), half), :] = mine[0:half, :].astype(F32)
    joined[pl.ds(pl.multiple_of((1 - tower_id) * half, 8), half), :] = got[0:half, :].astype(F32)
    reward[...] = joined[0 : s.bins, :]
    for target, at in ((small, s.small_at), (cond, s.cond_at)):
        rows = slice(at - s.reward_at, at - s.reward_at + s.held)
        target[...] = (mine[rows, :].astype(F32) + got[rows, :].astype(F32))[0 : s.table_rows]


def whole(shape):
    return pl.BlockSpec(shape, lambda step, tower: (0,) * len(shape))


def per_step(*tail):
    return pl.BlockSpec((1,) + tail, lambda step, tower: (step,) + (0,) * len(tail))


def swap(value, axis, mask):
    pairs = [(source, source ^ mask) for source in range(lax.axis_size(axis))]
    return lax.ppermute(value, axis, pairs)


AXES = ("tower", "batch")


def exchange_rounds(batch_size):
    factors, left = [], batch_size
    while left > 1:
        factors.append(4 if left % 4 == 0 else 2)
        left //= factors[-1]
    rounds, stride = [], 1
    for factor in factors:
        rounds.append((factor, stride))
        stride *= factor
    turned = rounds[::-1] if len(set(factors)) == 1 else rounds
    return [(one[0], (one[1], two[1])) for one, two in zip(rounds, turned)]


def swap_within(value, strides, other, batch_size):
    pairs = [
        (tower * batch_size + index, tower * batch_size + (index ^ (other * strides[tower])))
        for tower in range(2)
        for index in range(batch_size)
    ]
    return lax.ppermute(value, AXES, pairs)


def my_digit(factor, strides):
    stride = jnp.where(lax.axis_index("tower") == 0, strides[0], strides[1])
    return (lax.axis_index("batch") // stride) % factor


def exchange(value, rounds, batch_size, beside, given, last_kernel):
    shape = jax.ShapeDtypeStruct
    held = value
    digits = []
    for factor, strides in rounds:
        digit = my_digit(factor, strides)
        digits.append(digit)
        rows, width = held[0].shape
        rows = rows // factor
        split = pl.pallas_call(
            functools.partial(add_and_split_kernel, len(held)),
            grid_spec=pltpu.PrefetchScalarGridSpec(
                num_scalar_prefetch=1,
                grid=(1,),
                in_specs=[whole((factor, rows, width))] * len(held),
                out_specs=[whole((rows, width))] * factor,
            ),
            out_shape=[pltpu.HBM((rows, width), BF16)] * factor,
            compiler_params=pltpu.CompilerParams(vmem_limit_bytes=SMALL_LIMIT),
            name="add_and_split",
        )(digit[None], *[part.reshape(factor, rows, width) for part in held])
        first = len(digits) == 1
        if first:
            split, given = lax.optimization_barrier((split, given))
        held = [split[0]] + [
            swap_within(split[other], strides, other, batch_size) for other in range(1, factor)
        ]
        if first:
            done = beside(given)
            held, done = lax.optimization_barrier((held, done))
    piece = functools.reduce(jnp.add, [part.astype(F32) for part in held]).astype(BF16)
    for place in reversed(range(len(rounds))):
        factor, strides = rounds[place]
        rows, width = piece.shape
        held = [piece] + [
            swap_within(piece, strides, other, batch_size) for other in range(1, factor)
        ]
        if place == 0:
            return last_kernel(digits[0], held), done
        piece = pl.pallas_call(
            in_order_kernel,
            grid_spec=pltpu.PrefetchScalarGridSpec(
                num_scalar_prefetch=1,
                grid=(1,),
                in_specs=[whole((rows, width))] * factor,
                out_specs=whole((factor, rows, width)),
            ),
            out_shape=shape((factor, rows, width), BF16),
            compiler_params=pltpu.CompilerParams(vmem_limit_bytes=SMALL_LIMIT),
            name="in_order",
        )(digits[place][None], *held).reshape(factor * rows, width)


def body(
    root_state, cond_table, block_gain, w_in, w_out, value_head, reward_head, small_head,
    unroll_len, actions, codes, policy_target, value_bins, reward_bins,
):
    tower_id = lax.axis_index("tower")
    other_id = 1 - tower_id
    tower_ref = tower_id.astype(jnp.int32)[None]
    steps, batch_rows = actions.shape
    blocks, width = block_gain.shape[1:]
    bins = value_head.shape[2]
    table_rows = cond_table.shape[0]
    rows = batch_rows // 2
    half = width // 2
    parts = lax.axis_size("batch")
    s = Sizes(steps, rows, blocks, width, bins, table_rows, parts)
    calls, wide, pair = s.calls, s.wide, s.pair

    root_got = swap(root_state, "tower", 1)
    in_own, out_own, gains_own = w_in[0], w_out[0], block_gain[0]
    value_own = value_head[0].T
    in_got = swap(in_own, "tower", 1)
    out_got = swap(out_own, "tower", 1)
    gains_got = swap(gains_own, "tower", 1)
    value_got = swap(value_own, "tower", 1)
    lengths = unroll_len.reshape(1, batch_rows)

    shape = jax.ShapeDtypeStruct
    per_pair = lambda *tail: pl.BlockSpec(
        (pair,) + tail, lambda turn, tower: (turn,) + (0,) * len(tail)
    )
    forward_params = pltpu.CompilerParams(vmem_limit_bytes=FORWARD_LIMIT)
    backward_params = pltpu.CompilerParams(vmem_limit_bytes=BACKWARD_LIMIT)
    small_params = pltpu.CompilerParams(vmem_limit_bytes=SMALL_LIMIT)
    products = steps * rows * (4 * blocks * width * width + 9 * width * wide)
    cost = pl.CostEstimate(flops=2 * products, bytes_accessed=40 * 2**20, transcendentals=0)
    (
        lat, lat_own, lat_away, entry, after, slope, side, dlat, dlast, loss, head_grads,
        turned, code_rows, gains,
    ) = pl.pallas_call(
        functools.partial(forward_kernel, s),
        grid_spec=pltpu.PrefetchScalarGridSpec(
            num_scalar_prefetch=1,
            grid=(steps // pair,),
            in_specs=[pl.BlockSpec(memory_space=pltpu.HBM)] * 14
            + [
                pl.BlockSpec((rows, half), lambda step, tower: (tower[0], 0)),
                whole((blocks, width)),
                whole((blocks, width, width)),
                whole((blocks, width, width)),
                whole((bins, width)),
            ],
            out_specs=[
                per_pair(2, rows, width),
                per_pair(rows, width),
                per_pair(rows, width),
                per_pair(calls, rows, width),
                per_pair(calls, rows, width),
                per_pair(calls, rows, width),
                per_pair(calls + 2, rows, LANES),
                pl.BlockSpec(
                    (pair, 2, rows, width), lambda turn, tower: (jnp.maximum(turn - 1, 0), 0, 0, 0)
                ),
                whole((pair, 2, rows, width)),
                whole((8, rows)),
                whole((2, s.head_rows, width)),
                whole((2 * calls, width, width)),
                whole((2, steps, rows)),
                whole((2, 8, width)),
            ],
            scratch_shapes=[
                pltpu.VMEM((rows, half), BF16),
                pltpu.VMEM((1, rows), jnp.int32),
                pltpu.VMEM((steps, rows), jnp.int32),
                pltpu.VMEM((steps, rows), jnp.int32),
                pltpu.VMEM((steps, rows), jnp.int32),
                pltpu.VMEM((steps, 2, rows), jnp.int32),
                pltpu.VMEM((steps, rows), jnp.int32),
                pltpu.VMEM((table_rows, width), BF16),
                pltpu.VMEM((blocks, width), BF16),
                pltpu.VMEM((blocks, width, width), BF16),
                pltpu.VMEM((blocks, width, width), BF16),
                pltpu.VMEM((bins, width), BF16),
                pltpu.VMEM((bins, width), BF16),
                pltpu.VMEM((table_rows, width), BF16),
                pltpu.SemaphoreType.DMA((14,)),
                pltpu.VMEM((rows, width), BF16),
                pltpu.VMEM((pair * rows, width), BF16),
                pltpu.VMEM((pair * rows, width), BF16),
                pltpu.VMEM((width, width), BF16),
                pltpu.VMEM((LANES, width), BF16),
                pltpu.VMEM((2 * calls, width, width), BF16),
                pltpu.VMEM((s.depth[0], width), BF16),
                pltpu.VMEM((s.depth[1], width), BF16),
                pltpu.VMEM((width, s.depth[0]), BF16),
                pltpu.VMEM((width, s.depth[1]), BF16),
                pltpu.VMEM((s.stack[0], width), F32),
                pltpu.VMEM((s.stack[1], width), F32),
                pltpu.VMEM((s.stack[0], pair * rows), F32),
                pltpu.VMEM((s.stack[1], pair * rows), F32),
                pltpu.VMEM((s.depth[0], pair * rows), BF16),
                pltpu.VMEM((s.depth[1], pair * rows), BF16),
                pltpu.VMEM((s.reward_at - s.sums_at, LANES), F32),
                pltpu.VMEM((pair, s.reward_at - s.sums_at, width), F32),
            ],
        ),
        out_shape=[
            shape((steps, 2, rows, width), BF16),
            pltpu.HBM((steps, rows, width), BF16),
            pltpu.HBM((steps, rows, width), BF16),
            shape((steps, calls, rows, width), BF16),
            shape((steps, calls, rows, width), BF16),
            shape((steps, calls, rows, width), F32),
            shape((steps, calls + 2, rows, LANES), F32),
            shape((steps - pair, 2, rows, width), F32),
            shape((pair, 2, rows, width), F32),
            shape((8, rows), F32),
            shape((2, s.head_rows, width), BF16),
            shape((2 * calls, width, width), BF16),
            shape((2, steps, rows), jnp.int32),
            shape((2, 8, width), F32),
        ],
        compiler_params=forward_params,
        cost_estimate=cost,
        name="unroll_forward",
    )(
        tower_ref,
        *[
            pltpu.with_memory_space_constraint(value, pltpu.HBM)
            for value in (
                root_state, lengths, actions, codes, policy_target,
                jnp.swapaxes(value_bins, 0, 1), reward_bins, cond_table, gains_own,
                in_own, out_own, value_own, reward_head.T, small_head.T,
            )
        ],
        root_got, gains_got, in_got, out_got, value_got,
    )

    turns = steps // pair
    descending = lambda *tail: pl.BlockSpec(
        (pair,) + tail, lambda turn, tower: (turns - 1 - turn,) + (0,) * len(tail)
    )
    own, away, root_own, root_away = pl.pallas_call(
        functools.partial(backward_kernel, s),
        grid_spec=pltpu.PrefetchScalarGridSpec(
            num_scalar_prefetch=1,
            grid=(turns,),
            in_specs=[
                descending(2, rows, width),
                descending(calls, rows, width),
                descending(calls, rows, width),
                descending(calls, rows, width),
                descending(calls + 2, rows, LANES),
                pl.BlockSpec(
                    (pair, 2, rows, width),
                    lambda turn, tower: (jnp.minimum(turns - 1 - turn, turns - 2), 0, 0, 0),
                ),
                whole((pair, 2, rows, width)),
                whole((2, steps, rows)),
                whole((2, 8, width)),
                whole((2 * calls, width, width)),
                whole((2, s.head_rows, width)),
            ],
            out_specs=[
                whole((s.total, width)),
                whole((s.total, width)),
                whole((rows, half)),
                whole((rows, half)),
            ],
            scratch_shapes=[
                pltpu.VMEM((rows, width), F32),
                pltpu.VMEM((2, 16, width), F32),
                pltpu.VMEM((s.held, width), F32),
                pltpu.VMEM((2, calls, width, width), F32),
                pltpu.VMEM((2, 16, width), F32),
                pltpu.VMEM((2, 16, width), F32),
                pltpu.VMEM((pair, calls, rows, width), BF16),
                pltpu.VMEM((pair, calls, rows, width), BF16),
                pltpu.VMEM((pair, 2, rows, width), BF16),
            ],
        ),
        out_shape=[
            shape((s.total, width), BF16),
            shape((s.total, width), BF16),
            shape((rows, half), BF16),
            shape((rows, half), BF16),
        ],
        compiler_params=backward_params,
        cost_estimate=cost,
        name="unroll_backward",
    )(
        tower_ref, lat, entry, after, slope, side, dlat, dlast, code_rows, gains,
        turned, head_grads,
    )
    got = swap(away, "tower", 1)

    def beside(given):
        lat_own, lat_away, loss, root_own, root_away = given
        lat_got = swap(lat_away, "tower", 1)
        loss_own = loss[0]
        loss_got = swap(loss_own, "tower", 1)
        root_got = swap(root_away, "tower", 1)

        latents, logits = pl.pallas_call(
            functools.partial(logits_kernel, s),
            grid_spec=pltpu.PrefetchScalarGridSpec(
                num_scalar_prefetch=1,
                grid=(steps,),
                in_specs=[per_step(rows, width), per_step(rows, width), whole((bins, width))],
                out_specs=[per_step(batch_rows, width), per_step(bins, batch_rows)],
            ),
            out_shape=[
                shape((steps, batch_rows, width), BF16),
                shape((steps, bins, batch_rows), BF16),
            ],
            compiler_params=small_params,
            cost_estimate=pl.CostEstimate(
                flops=2 * steps * batch_rows * width * wide, bytes_accessed=6 * 2**20, transcendentals=0
            ),
            name="latents_and_logits",
        )(
            tower_ref,
            *[
                pltpu.with_memory_space_constraint(part, pltpu.HBM)
                for part in (lat_own, lat_got, value_own)
            ],
        )

        def in_order(mine_value, got_value, axis):
            return jnp.where(
                tower_id == 0,
                jnp.concatenate([mine_value, got_value], axis=axis),
                jnp.concatenate([got_value, mine_value], axis=axis),
            )

        row_loss = in_order(loss_own, loss_got, 0)
        grad_root = in_order(root_own, root_got, 0).astype(F32)
        return latents, logits, row_loss, grad_root

    rounds = exchange_rounds(parts)

    def unpack(digit, held):
        scalars = jnp.stack([digit, tower_id]).astype(jnp.int32)
        length = held[0].shape[0]
        block = s.reward_at // length
        at = s.reward_at - block * length
        parts_of = [part[at : at + s.shared_end - s.reward_at] for part in held]
        shared = parts_of[0]
        for other in range(1, len(held)):
            shared = jnp.where((digit ^ other) == block, parts_of[other], shared)
        shared_got = swap(shared, "tower", 1)
        return (shared, shared_got), pl.pallas_call(
            functools.partial(unpack_own_kernel, s),
            grid_spec=pltpu.PrefetchScalarGridSpec(
                num_scalar_prefetch=1,
                grid=(1,),
                in_specs=[whole(part.shape) for part in held],
                out_specs=[
                    whole((blocks, width, width)),
                    whole((blocks, width, width)),
                    whole((bins, 1, width)),
                    whole((blocks, 1, width)),
                    whole((blocks, 2, steps)),
                ],
                scratch_shapes=[
                    pltpu.VMEM((s.total, width), BF16),
                    pltpu.VMEM((s.reward_at - s.sums_at, LANES), F32),
                ],
            ),
            out_shape=[
                shape((blocks, width, width), F32),
                shape((blocks, width, width), F32),
                shape((bins, 1, width), F32),
                shape((blocks, 1, width), F32),
                shape((blocks, 2, steps), F32),
            ],
            compiler_params=small_params,
            name="unpack_own",
        )(scalars, *held)

    given = (lat_own, lat_away, loss, root_own, root_away)
    unpacked, done = exchange([own, got], rounds, parts, beside, given, unpack)
    (shared, shared_got), (grad_in, grad_out, value_t, gain_t, rms_t) = unpacked
    latents, logits, row_loss, grad_root = done
    reward_t, small_t, grad_cond = pl.pallas_call(
        functools.partial(unpack_shared_kernel, s),
        grid_spec=pltpu.PrefetchScalarGridSpec(
            num_scalar_prefetch=1,
            grid=(1,),
            in_specs=[whole(shared.shape), whole(shared.shape)],
            out_specs=[
                whole((bins, width)),
                whole((table_rows, width)),
                whole((table_rows, width)),
            ],
            scratch_shapes=[pltpu.VMEM((s.wide, width), F32)],
        ),
        out_shape=[
            shape((bins, width), F32),
            shape((table_rows, width), F32),
            shape((table_rows, width), F32),
        ],
        compiler_params=small_params,
        name="unpack_shared",
    )(tower_ref, shared, shared_got)
    layer_rms = jnp.transpose(rms_t, (2, 0, 1))[None]
    return (
        latents[None],
        jnp.swapaxes(logits, 1, 2)[None],
        row_loss,
        layer_rms,
        grad_root,
        grad_cond,
        jnp.swapaxes(gain_t, 0, 1),
        grad_in[None],
        grad_out[None],
        jnp.transpose(value_t, (1, 2, 0)),
        reward_t.T,
        small_t.T,
    )


def solution(mesh):
    placed = (
        P("batch", "tower"),
        P(),
        P("tower", None, None),
        P("tower", None, None, None),
        P("tower", None, None, None),
        P("tower", None, None),
        P(),
        P(),
        P("batch"),
        P(None, "batch"),
        P(None, "batch"),
        P(None, "batch"),
        P(None, None, "batch"),
        P(None, "batch"),
    )
    return jax.shard_map(
        body,
        mesh=mesh,
        in_specs=placed,
        out_specs=(
            P("tower", None, "batch", None),
            P("tower", None, "batch", None),
            P("batch"),
            P("tower", None, None, None),
            P("batch", "tower"),
            P(),
            P("tower", None, None),
            P("tower", None, None, None),
            P("tower", None, None, None),
            P("tower", None, None),
            P(),
            P(),
        ),
        check_vma=False,
    )
```

```python
import functools

import jax
import jax.numpy as jnp
from jax import lax
from jax.experimental import pallas as pl
from jax.experimental.pallas import tpu as pltpu
from jax.sharding import PartitionSpec as P

ACTIONS = 4
LANES = 128
MIB = 1024 * 1024
FORWARD_LIMIT = 20 * MIB
BACKWARD_LIMIT = 20 * MIB
SMALL_LIMIT = 12 * MIB
epsilon = 1e-06
very_negative = -1e30
F32 = jnp.float32
BF16 = jnp.bfloat16


def natural(left, right):
    return lax.dot_general(left, right, (((1,), (0,)), ((), ())), preferred_element_type=F32)


def by_rows(left, right):
    return lax.dot_general(left, right, (((0,), (0,)), ((), ())), preferred_element_type=F32)


def by_lanes(left, right):
    return lax.dot_general(left, right, (((1,), (1,)), ((), ())), preferred_element_type=F32)


def round_up(value, unit):
    return (value + unit - 1) // unit * unit


def lane_sum(value):
    return jnp.sum(value, axis=-1, keepdims=True)


def inverse_rms(hidden):
    return lax.rsqrt(lane_sum(hidden * hidden) * (1.0 / hidden.shape[-1]) + epsilon)


def weave(*tasks):
    tasks = [(list(task)) for task in tasks]
    longest = max(len(task) for task in tasks)
    done = [0] * len(tasks)
    for turn in range(longest):
        for which, task in enumerate(tasks):
            until = (turn + 1) * len(task) // longest
            while done[which] < until:
                task[done[which]]()
                done[which] += 1


def cuts(length, unit=160):
    return [(start, min(start + unit, length)) for start in range(0, length, unit)]


def round_factors(size):
    factors = []
    while size > 1:
        factors.append(4 if size % 4 == 0 else 2)
        size //= factors[-1]
    return factors


class Sizes:
    def __init__(self, steps, rows, blocks, width, bins, table_rows, parts):
        self.steps, self.rows, self.blocks, self.width = steps, rows, blocks, width
        self.bins, self.table_rows, self.parts = bins, table_rows, parts
        self.calls = 2 * blocks
        self.pair = 2 if steps % 2 == 0 else 1
        self.wide = round_up(bins, 32)
        self.held = round_up(table_rows, 16)
        self.stack = (self.wide + self.held, 2 * self.wide + self.held)
        self.depth = tuple(round_up(rows_in, LANES) for rows_in in self.stack)
        factor = round_factors(parts)[0]
        self.kinds = 2 * self.calls
        self.sums_at = self.wide
        self.reward_at = self.sums_at + round_up(self.kinds + 1, 16)
        self.small_at = self.reward_at + self.wide // 2
        self.head_end = self.small_at + self.held
        self.head_rows = round_up(self.head_end, 16 * parts)
        self.head_block = self.head_rows // factor
        self.gain_at = self.calls * width
        self.cond_at = self.gain_at + 16
        self.matrix_end = self.cond_at + self.held
        self.matrix_rows = round_up(self.matrix_end, 8 * parts)


def forward_kernel(
    sizes, tower_ref,
    root_hbm, lengths_hbm, actions_hbm, codes_hbm, policy_hbm, value_bins_hbm, reward_bins_hbm,
    table_hbm, gains_hbm, in_hbm, out_hbm, value_hbm, reward_hbm, small_hbm,
    root_got, gains_got, in_got, out_got, value_got,
    lat, lat_own, lat_away, entry, after, slope, side, dlat, dlast, loss, head_grads, turned, code_rows, gains,
    root_own, lengths, actions, codes, policy, value_bins, reward_bins,
    table_in, gains_own, in_own, out_own, value_own, reward_in, small_in, sems,
    state, past0, past1, identity, table, weights, heads0, heads1, flip0, flip1, acc0, acc1,
    logits0, logits1, cot0, cot1, sums, squares,
):
    s = sizes
    pair = s.pair
    turn = pl.program_id(0)
    first_step = turn * pair
    tower_id = tower_ref[0]
    rows, width, wide = s.rows, s.width, s.wide

    @pl.when(turn == 0)
    def _():
        here = pl.ds(pl.multiple_of(tower_id * rows, rows), rows)
        moves = [
            (root_hbm.at[here], root_own),
            (lengths_hbm.at[:, here], lengths),
            (actions_hbm.at[:, here], actions),
            (codes_hbm.at[:, here], codes),
            (policy_hbm.at[:, here], policy),
            (value_bins_hbm.at[:, :, here], value_bins),
            (reward_bins_hbm.at[:, here], reward_bins),
            (table_hbm, table_in),
            (gains_hbm, gains_own),
            (in_hbm, in_own),
            (out_hbm, out_own),
            (value_hbm, value_own),
            (reward_hbm, reward_in),
            (small_hbm, small_in),
        ]
        moves = [
            pltpu.make_async_copy(source, target, sems.at[place])
            for place, (source, target) in enumerate(moves)
        ]
        for move in moves:
            move.start()
        for move in moves:
            move.wait()
        first = tower_id == 0
        code_rows[0] = actions[...]
        code_rows[1] = codes[...] + ACTIONS
        state[:, 0 : width // 2] = jnp.where(first, root_own[...], root_got[...])
        state[:, width // 2 : width] = jnp.where(first, root_got[...], root_own[...])
        for tower, w_first, w_second in (
            (tower_id, in_own, out_own),
            (1 - tower_id, in_got, out_got),
        ):
            weights[pl.ds(tower * s.blocks, s.blocks)] = w_first[...]
            weights[pl.ds(s.calls + tower * s.blocks, s.blocks)] = w_second[...]
        gains[...] = jnp.zeros_like(gains)
        gains[tower_id, 0 : s.blocks, :] = gains_own[...].astype(F32)
        gains[1 - tower_id, 0 : s.blocks, :] = gains_got[...].astype(F32)
        table[...] = jnp.zeros_like(table)
        table[0 : s.table_rows, :] = table_in[...]
        heads0[...] = jnp.zeros_like(heads0)
        heads1[...] = jnp.zeros_like(heads1)
        heads0[0 : s.bins, :] = jnp.where(first, value_own[...], value_got[...])
        heads1[0 : s.bins, :] = jnp.where(first, value_got[...], value_own[...])
        heads1[wide : wide + s.bins, :] = reward_in[...]
        heads0[wide : wide + s.table_rows, :] = small_in[...]
        heads1[2 * wide : 2 * wide + s.table_rows, :] = small_in[...]
        down = lax.broadcasted_iota(jnp.int32, (width, width), 0)
        across = lax.broadcasted_iota(jnp.int32, (width, width), 1)
        identity[...] = jnp.where(down == across, 1.0, 0.0).astype(BF16)
        flip0[...] = by_lanes(identity[...], heads0[...]).astype(BF16)
        flip1[...] = by_lanes(identity[...], heads1[...]).astype(BF16)
        past0[...] = jnp.zeros_like(past0)
        past1[...] = jnp.zeros_like(past1)
        cot0[...] = jnp.zeros_like(cot0)
        cot1[...] = jnp.zeros_like(cot1)
        acc0[...] = jnp.zeros_like(acc0)
        acc1[...] = jnp.zeros_like(acc1)
        sums[...] = jnp.zeros_like(sums)
        squares[...] = jnp.zeros_like(squares)
        loss[...] = jnp.zeros_like(loss)

    eights = lax.broadcasted_iota(jnp.int32, (8, pair * rows), 0)
    before = jnp.maximum(first_step - pair, 0)

    def pair_row(kind, at_step, lead=()):
        return jnp.concatenate(
            [kind[(pl.ds(at_step + offset, 1),) + lead] for offset in range(pair)], axis=1
        )

    def live_rows(at_step):
        return jnp.concatenate(
            [(at_step + offset < lengths[...]).astype(F32) for offset in range(pair)], axis=1
        )

    kinds = []
    for offset in range(pair):
        step = first_step + offset
        kinds.append((step < lengths[...]).astype(F32))
        kinds.append(actions[pl.ds(step, 1), :].astype(F32))
        kinds.append((codes[pl.ds(step, 1), :] + ACTIONS).astype(F32))
    kinds.append(jnp.zeros((8 - len(kinds), rows), F32))
    columns = jnp.concatenate(kinds, axis=0).T

    def heads(tower, live_row, at_step, put):
        latent = past0 if tower == 0 else past1
        stack, flip, logits, cot, acc = (
            (heads0, flip0, logits0, cot0, acc0)
            if tower == 0
            else (heads1, flip1, logits1, cot1, acc1)
        )
        pick = lambda kind: pair_row(kind, at_step)
        value_goal = pair_row(value_bins, at_step, (tower,))
        spans = [(0, wide, 0, s.bins, value_goal)]
        if tower == 1:
            spans.append((wide, wide, 0, s.bins, pick(reward_bins)))
            spans.append((2 * wide, s.held, 0, ACTIONS, pick(policy)))
        else:
            spans.append((wide, s.held, ACTIONS, s.table_rows, pick(codes) + ACTIONS))

        def make_logits():
            logits[...] = by_lanes(stack[0 : logits.shape[0], :], latent[...])

        def eight_rows(value):
            return value.reshape(-1, 8, pair * rows)

        def mask(at, length, first, last):
            for start in range(0, length, 8):
                if start < first or start + 8 > last:
                    inside = (eights >= first - start) & (eights < last - start)
                    place = slice(at + start, at + start + 8)
                    logits[place, :] = jnp.where(inside, logits[place, :], very_negative)

        def find_top(at, start, stop, kept):
            top = jnp.max(eight_rows(logits[at + start : at + stop, :]), axis=0)
            kept["top"] = jnp.maximum(kept["top"], top) if "top" in kept else top

        def end_top(kept):
            kept["top"] = jnp.max(kept["top"], axis=0, keepdims=True)

        def make_terms(at, start, stop, goal, kept):
            place = slice(at + start, at + stop)
            value = logits[place, :]
            spot = lax.broadcasted_iota(jnp.int32, value.shape, 0)
            term = jnp.exp(value - kept["top"])
            logits[place, :] = term
            hit = spot == goal - start
            total = jnp.sum(eight_rows(term), axis=0)
            picked = jnp.sum(eight_rows(jnp.where(hit, value, 0.0)), axis=0)
            kept["total"] = kept["total"] + total if "total" in kept else total
            kept["picked"] = kept["picked"] + picked if "picked" in kept else picked

        def end_terms(kept):
            total = jnp.sum(kept["total"], axis=0, keepdims=True)
            picked = jnp.sum(kept["picked"], axis=0, keepdims=True)
            kept["scale"] = live_row / total
            row_loss = live_row * (jnp.log(total) + kept["top"] - picked)
            for offset in range(pair):
                loss[0:1, :] += row_loss[:, offset * rows : (offset + 1) * rows]

        def make_cotangent(at, start, stop, goal, kept):
            place = slice(at + start, at + stop)
            term = logits[place, :]
            spot = lax.broadcasted_iota(jnp.int32, term.shape, 0)
            hit = spot == goal - start
            cot[place, :] = (term * kept["scale"] - jnp.where(hit, live_row, 0.0)).astype(BF16)

        def make_grads():
            acc[...] += natural(cot[0 : acc.shape[0], :], latent[...])

        def make_latent():
            d_latent = natural(flip[...], cot[...]).T
            for offset in range(pair):
                put[offset, tower] = d_latent[offset * rows : (offset + 1) * rows]

        pieces = [make_logits]
        for at, length, first, last, goal in spans:
            kept = {}
            each = cuts(length)
            pieces.append(functools.partial(mask, at, length, first, last))
            pieces += [functools.partial(find_top, at, *cut, kept) for cut in each]
            pieces.append(functools.partial(end_top, kept))
            pieces += [functools.partial(make_terms, at, *cut, goal, kept) for cut in each]
            pieces.append(functools.partial(end_terms, kept))
            pieces += [functools.partial(make_cotangent, at, *cut, goal, kept) for cut in each]
        return pieces + [make_latent, make_grads]

    def tower_call(offset, tower, x_in, done):
        kept = {}
        live = columns[:, 3 * offset : 3 * offset + 1]
        code = columns[:, 3 * offset + 1 + tower : 3 * offset + 2 + tower]

        def begin():
            spot = lax.broadcasted_iota(jnp.int32, (rows, table.shape[0]), 1).astype(F32)
            onehot = jnp.where(spot == code, 1.0, 0.0).astype(BF16)
            kept["hidden"] = x_in().astype(F32) + natural(onehot, table[...])

        def scale_rows():
            row_squares = lane_sum(kept["hidden"] * kept["hidden"])
            return row_squares, lax.rsqrt(row_squares * (1.0 / width) + epsilon)

        def keep_squares(block, row_squares):
            place = 2 * (tower * s.blocks + block)
            total = jnp.sum(live * row_squares, axis=0, keepdims=True) * (1.0 / LANES)
            squares[offset, place : place + 1, 0:LANES] = jnp.broadcast_to(total, (1, LANES))

        def into(block):
            place = tower * s.blocks + block
            gained = kept["hidden"] * gains[tower, block : block + 1, :]
            product = natural(gained.astype(BF16), weights[place])
            row_squares, inv_scale = scale_rows()
            kept["u"] = product * inv_scale
            entry[offset, place] = (gained * inv_scale).astype(BF16)
            side[offset, place] = jnp.broadcast_to(inv_scale, (rows, LANES))
            if block > 0:
                keep_squares(block - 1, row_squares)

        def out_of(block):
            place = tower * s.blocks + block
            u = kept["u"]
            gate = 0.5 * jnp.tanh(0.5 * u) + 0.5
            after_rows = (u * gate).astype(BF16)
            branch = natural(after_rows, weights[s.calls + place])
            kept["hidden"] = kept["hidden"] + branch
            after[offset, place] = after_rows
            slope[offset, place] = gate * (1.0 + u * (1.0 - gate))
            spot = 2 * place + 1
            squares[offset, spot : spot + 1, :] = jnp.sum(
                branch * branch * live, axis=0, keepdims=True
            )

        def finish():
            row_squares, inv_scale = scale_rows()
            side[offset, s.calls + tower] = jnp.broadcast_to(inv_scale, (rows, LANES))
            latent = (kept["hidden"] * inv_scale).astype(BF16)
            lat[offset, tower] = latent
            keep_squares(s.blocks - 1, row_squares)
            if tower == 0:
                total = jnp.sum(live, axis=0, keepdims=True) * (1.0 / LANES)
                squares[offset, s.kinds : s.kinds + 1, 0:LANES] = jnp.broadcast_to(
                    total, (1, LANES)
                )
            done(latent)

        pieces = [begin]
        for block in range(s.blocks):
            pieces += [functools.partial(into, block), functools.partial(out_of, block)]
        return pieces + [finish]

    found = {(1, -1): state[...]}
    chain = []
    for offset in range(pair):
        for tower in range(2):
            source = (0, offset) if tower == 1 else (1, offset - 1)
            chain += tower_call(
                offset,
                tower,
                functools.partial(found.get, source),
                functools.partial(found.__setitem__, (tower, offset)),
            )

    turns = -(-2 * s.calls // (s.steps // pair))

    def turn_weights(which):
        matrix = jnp.minimum(turn * turns + which, 2 * s.calls - 1)
        turned[matrix] = by_lanes(identity[...], weights[matrix]).astype(BF16)

    live_before = jnp.where(turn > 0, live_rows(before), 0.0)
    weave(
        chain,
        heads(1, live_before, before, dlat)
        + heads(0, live_before, before, dlat)
        + [functools.partial(turn_weights, which) for which in range(turns)],
    )
    state[...] = found[1, pair - 1]
    first = tower_id == 0
    at_lane = lax.broadcasted_iota(jnp.int32, sums.shape, 1)
    for offset in range(pair):
        after_state, next_state = found[0, offset], found[1, offset]
        past0[offset * rows : (offset + 1) * rows, :] = after_state
        past1[offset * rows : (offset + 1) * rows, :] = next_state
        lat_own[offset] = jnp.where(first, after_state, next_state)
        lat_away[offset] = jnp.where(first, next_state, after_state)
        total = lane_sum(squares[offset])
        sums[...] = jnp.where(at_lane == first_step + offset, total, sums[...])

    @pl.when(turn == pl.num_programs(0) - 1)
    def _():
        live_now = live_rows(first_step)
        weave(heads(1, live_now, first_step, dlast), heads(0, live_now, first_step, dlast))
        half = wide // 2
        head_grads[...] = jnp.zeros_like(head_grads)

        def put(tower, at, value):
            done = 0
            while done < value.shape[0]:
                block, row = divmod(at + done, s.head_block)
                take = min(s.head_block - row, value.shape[0] - done)
                head_grads[block, tower, row : row + take, 0 : value.shape[1]] = value[
                    done : done + take
                ].astype(BF16)
                done += take

        put(0, 0, acc0[0:wide, :])
        put(1, 0, acc1[0:wide, :])
        put(0, s.small_at, acc0[wide : wide + s.held, :] + acc1[2 * wide : 2 * wide + s.held, :])
        for tower in range(2):
            at = wide + tower * half
            put(tower, s.reward_at, acc1[at : at + half, :])
            put(tower, s.sums_at, sums[...])


def backward_kernel(
    sizes, tower_ref,
    lat, entry, after, slope, side, dlat, dlast, code_rows, gains_in, turned,
    own, away, root_own, root_away,
    carry, gain_sum, cond_sum, grads, gains, inverse_gains, d_after_kept, d_before_kept,
    d_hidden_kept,
):
    s = sizes
    pair = s.pair
    turn = pl.program_id(0)
    first_step = s.steps - pair * (turn + 1)
    tower_id = tower_ref[0]
    blocks, width = s.blocks, s.width

    @pl.when(turn == 0)
    def _():
        gains[...] = jnp.ones_like(gains)
        gains[:, 0:blocks, :] = gains_in[:, 0:blocks, :]
        inverse_gains[...] = 1.0 / gains[...]
        carry[...] = jnp.zeros_like(carry)
        grads[...] = jnp.zeros_like(grads)
        gain_sum[...] = jnp.zeros_like(gain_sum)
        cond_sum[...] = jnp.zeros_like(cond_sum)

    def over_lanes(column):
        return jnp.concatenate([column] * (width // LANES), axis=1)

    def stacked(parts):
        return jnp.concatenate([parts[offset] for offset in range(pair)], axis=0)

    def add_grads(matrix, rows_of, place, kept, now):
        parts = [now] + [kept[offset, place] for offset in range(1, pair)]
        grads[matrix // s.calls, matrix % s.calls] += by_rows(
            stacked([rows_of[offset, place] for offset in range(pair)]), stacked(parts)
        )

    def tower_back(offset, tower, d_latent):
        normed = lat[offset, tower]
        normed_wide = normed.astype(F32)
        inv_scale = over_lanes(side[offset, s.calls + tower])
        base = inv_scale * d_latent
        slant = inv_scale * (lane_sum(d_latent * normed_wide) * (1.0 / width))
        for block in reversed(range(blocks)):
            place = tower * blocks + block
            gain = gains[tower, block : block + 1, :]
            entry_wide = entry[offset, place].astype(F32)
            inv_scale = over_lanes(side[offset, place])
            both = natural(
                jnp.concatenate([normed, base.astype(BF16)], axis=0), turned[s.calls + place]
            )
            d_after = both[s.rows :] - slant * both[: s.rows]
            d_hidden = base - slant * normed_wide
            d_branch = d_hidden.astype(BF16)
            d_before = (d_after * slope[offset, place]).astype(BF16)
            d_entry = natural(d_before, turned[place])
            if offset > 0:
                d_after_kept[offset, place] = d_branch
                d_before_kept[offset, place] = d_before
            else:
                matrix = tower * s.calls + block
                add_grads(matrix + blocks, after, place, d_after_kept, d_branch)
                add_grads(matrix, entry, place, d_before_kept, d_before)
            product = d_entry * entry_wide
            gain_sum[tower, block : block + 1, :] += jnp.sum(product, axis=0, keepdims=True)
            base = d_hidden + inv_scale * (d_entry * gain)
            slant = inv_scale * (lane_sum(product) * (1.0 / width))
            normed_wide = entry_wide * inverse_gains[tower, block : block + 1, :]
            normed = normed_wide.astype(BF16)
        d_hidden = base - slant * normed_wide
        if offset > 0:
            d_hidden_kept[offset, tower] = d_hidden.astype(BF16)
        else:
            code = jnp.concatenate(
                [code_rows[tower, pl.ds(first_step + each, 1), :] for each in range(pair)], axis=1
            )
            spots = lax.broadcasted_iota(jnp.int32, (cond_sum.shape[0], pair * s.rows), 0)
            onehot = jnp.where(spots == code, 1.0, 0.0).astype(BF16)
            parts = [d_hidden.astype(BF16)]
            parts += [d_hidden_kept[each, tower] for each in range(1, pair)]
            cond_sum[...] += natural(onehot, stacked(parts))
        return d_hidden

    def from_heads(offset, tower):
        return jnp.where(turn == 0, dlast[offset, tower], dlat[offset, tower])

    d_state = carry[...]
    for offset in reversed(range(pair)):
        d_after_state = tower_back(offset, 1, d_state + from_heads(offset, 1))
        d_state = tower_back(offset, 0, d_after_state + from_heads(offset, 0))
    carry[...] = d_state

    @pl.when(turn == pl.num_programs(0) - 1)
    def _():
        left = d_state[:, 0 : width // 2].astype(BF16)
        right = d_state[:, width // 2 : width].astype(BF16)
        root_own[...] = jnp.where(tower_id == 0, left, right)
        root_away[...] = jnp.where(tower_id == 0, right, left)
        gain_sum[...] = gain_sum[...] * inverse_gains[...]
        for target, which in ((own, tower_id), (away, 1 - tower_id)):
            for matrix in range(s.calls):
                at = matrix * width
                target[at : at + width, :] = grads[which, matrix].astype(BF16)
            target[s.gain_at : s.cond_at, :] = gain_sum[which].astype(BF16)
            here = jnp.where(which == 0, cond_sum[...], 0.0)
            target[s.cond_at : s.matrix_end, :] = here.astype(BF16)
            if s.matrix_rows > s.matrix_end:
                target[s.matrix_end :, :] = jnp.zeros((s.matrix_rows - s.matrix_end, width), BF16)


def logits_kernel(sizes, tower_ref, lat_own, lat_got, value_own, latents, logits):
    rows = sizes.rows
    tower_id = tower_ref[0]
    at_own = pl.ds(pl.multiple_of(tower_id * rows, rows), rows)
    at_got = pl.ds(pl.multiple_of((1 - tower_id) * rows, rows), rows)
    latents[0, at_own, :] = lat_own[0]
    latents[0, at_got, :] = lat_got[0]
    logits[0] = by_lanes(value_own[...], latents[0]).astype(BF16)


def add_and_split_kernel(count, digit_ref, *refs):
    inputs, outputs = refs[:count], refs[count:]
    digit = digit_ref[0]
    for other, target in enumerate(outputs):
        part = digit ^ other
        total = inputs[0][part].astype(F32)
        for source in inputs[1:]:
            total = total + source[part].astype(F32)
        target[...] = total.astype(BF16)


def in_order_kernel(digit_ref, *refs):
    digit = digit_ref[0]
    for other, source in enumerate(refs[:-1]):
        refs[-1][digit ^ other] = source[...]


def pick_and_add_kernel(tower_ref, mine, got, total):
    tower_id = tower_ref[0]
    total[...] = (mine[tower_id].astype(F32) + got[tower_id].astype(F32)).astype(BF16)


def unpack_matrices_kernel(sizes, scalars, *refs):
    s = sizes
    factor = len(refs) - 4
    digit = scalars[0]
    w_in, w_out, gain, flat = refs[factor:]
    width = s.width
    length = refs[0].shape[0]
    for other, source in enumerate(refs[:factor]):
        at = pl.multiple_of((digit ^ other) * length, 16)
        flat[pl.ds(at, length), :] = source[...]
    for block in range(s.blocks):
        at = block * width
        w_in[block] = flat[at : at + width, :].astype(F32)
        at = (s.blocks + block) * width
        w_out[block] = flat[at : at + width, :].astype(F32)
        gain[block] = flat[s.gain_at : s.cond_at, :].astype(F32)[block : block + 1]


def unpack_heads_kernel(
    sizes, tower_ref, heads, heads_got, cond_own, cond_got,
    value, rms, reward, small, cond, joined, held,
):
    s = sizes
    tower_id = tower_ref[0]
    half = s.wide // 2
    value[:, 0, :] = heads[0 : s.wide, :].astype(F32)[0 : s.bins]
    joined[pl.ds(pl.multiple_of(tower_id * half, 8), half), :] = heads[
        s.reward_at : s.small_at, :
    ].astype(F32)
    joined[pl.ds(pl.multiple_of((1 - tower_id) * half, 8), half), :] = heads_got[
        0:half, :
    ].astype(F32)
    reward[...] = joined[0 : s.bins, :]
    mine = heads[s.small_at : s.head_end, :].astype(F32)
    small[...] = (mine + heads_got[half : half + s.held, :].astype(F32))[0 : s.table_rows]
    cond[...] = (cond_own[...].astype(F32) + cond_got[...].astype(F32))[0 : s.table_rows]
    held[...] = heads[s.sums_at : s.reward_at, 0:LANES].astype(F32)
    count = jnp.maximum(held[s.kinds : s.kinds + 1, 0 : s.steps], 1.0)
    for block in range(s.blocks):
        for kind in range(2):
            spot = tower_id * s.calls + 2 * block + kind
            square = held[pl.ds(spot, 1), 0 : s.steps]
            rms[block, kind : kind + 1, :] = jnp.sqrt(jnp.maximum(square, 0.0) / (count * s.width))


def whole(shape):
    return pl.BlockSpec(shape, lambda step, tower: (0,) * len(shape))


def per_step(*tail):
    return pl.BlockSpec((1,) + tail, lambda step, tower: (step,) + (0,) * len(tail))


def swap(value, axis, mask):
    pairs = [(source, source ^ mask) for source in range(lax.axis_size(axis))]
    return lax.ppermute(value, axis, pairs)


AXES = ("tower", "batch")


def exchange_rounds(batch_size):
    factors = round_factors(batch_size)
    rounds, stride = [], 1
    for factor in factors:
        rounds.append((factor, stride))
        stride *= factor
    turned = rounds[::-1] if len(set(factors)) == 1 else rounds
    return [(one[0], (one[1], two[1])) for one, two in zip(rounds, turned)]


def swap_within(value, strides, other, batch_size):
    pairs = [
        (tower * batch_size + index, tower * batch_size + (index ^ (other * strides[tower])))
        for tower in range(2)
        for index in range(batch_size)
    ]
    return lax.ppermute(value, AXES, pairs)


def my_digit(factor, strides):
    stride = jnp.where(lax.axis_index("tower") == 0, strides[0], strides[1])
    return (lax.axis_index("batch") // stride) % factor


def batch_groups(factor, stride, batch_size):
    return [
        [base + stride * digit for digit in range(factor)]
        for base in range(batch_size)
        if (base // stride) % factor == 0
    ]


def exchange(value, rounds, batch_size, beside, given, last_kernel, other):
    shape = jax.ShapeDtypeStruct
    held = value
    digits = []
    for factor, strides in rounds:
        digit = my_digit(factor, strides)
        digits.append(digit)
        rows, width = held[0].shape
        rows = rows // factor
        split = pl.pallas_call(
            functools.partial(add_and_split_kernel, len(held)),
            grid_spec=pltpu.PrefetchScalarGridSpec(
                num_scalar_prefetch=1,
                grid=(1,),
                in_specs=[whole((factor, rows, width))] * len(held),
                out_specs=[whole((rows, width))] * factor,
            ),
            out_shape=[pltpu.HBM((rows, width), BF16)] * factor,
            compiler_params=pltpu.CompilerParams(vmem_limit_bytes=SMALL_LIMIT),
            name="add_and_split",
        )(digit[None], *[part.reshape(factor, rows, width) for part in held])
        first = len(digits) == 1
        if first:
            split, given = lax.optimization_barrier((split, given))
        held = [split[0]] + [
            swap_within(split[other], strides, other, batch_size) for other in range(1, factor)
        ]
        if first:
            done = beside(given)
            held, done = lax.optimization_barrier((held, done))
            other(held)
    piece = functools.reduce(jnp.add, [part.astype(F32) for part in held]).astype(BF16)
    for place in reversed(range(len(rounds))):
        factor, strides = rounds[place]
        rows, width = piece.shape
        held = [piece] + [
            swap_within(piece, strides, other, batch_size) for other in range(1, factor)
        ]
        if place == 0:
            return last_kernel(digits[0], held), done
        piece = pl.pallas_call(
            in_order_kernel,
            grid_spec=pltpu.PrefetchScalarGridSpec(
                num_scalar_prefetch=1,
                grid=(1,),
                in_specs=[whole((rows, width))] * factor,
                out_specs=whole((factor, rows, width)),
            ),
            out_shape=shape((factor, rows, width), BF16),
            compiler_params=pltpu.CompilerParams(vmem_limit_bytes=SMALL_LIMIT),
            name="in_order",
        )(digits[place][None], *held).reshape(factor * rows, width)
        other(piece)


def body(
    root_state, cond_table, block_gain, w_in, w_out, value_head, reward_head, small_head,
    unroll_len, actions, codes, policy_target, value_bins, reward_bins,
):
    tower_id = lax.axis_index("tower")
    other_id = 1 - tower_id
    tower_ref = tower_id.astype(jnp.int32)[None]
    steps, batch_rows = actions.shape
    blocks, width = block_gain.shape[1:]
    bins = value_head.shape[2]
    table_rows = cond_table.shape[0]
    rows = batch_rows // 2
    half = width // 2
    parts = lax.axis_size("batch")
    s = Sizes(steps, rows, blocks, width, bins, table_rows, parts)
    calls, wide, pair = s.calls, s.wide, s.pair

    root_got = swap(root_state, "tower", 1)
    in_own, out_own, gains_own = w_in[0], w_out[0], block_gain[0]
    value_own = value_head[0].T
    in_got = swap(in_own, "tower", 1)
    out_got = swap(out_own, "tower", 1)
    gains_got = swap(gains_own, "tower", 1)
    value_got = swap(value_own, "tower", 1)
    lengths = unroll_len.reshape(1, batch_rows)

    shape = jax.ShapeDtypeStruct
    per_pair = lambda *tail: pl.BlockSpec(
        (pair,) + tail, lambda turn, tower: (turn,) + (0,) * len(tail)
    )
    forward_params = pltpu.CompilerParams(vmem_limit_bytes=FORWARD_LIMIT)
    backward_params = pltpu.CompilerParams(vmem_limit_bytes=BACKWARD_LIMIT)
    small_params = pltpu.CompilerParams(vmem_limit_bytes=SMALL_LIMIT)
    products = steps * rows * (4 * blocks * width * width + 9 * width * wide)
    cost = pl.CostEstimate(flops=2 * products, bytes_accessed=40 * 2**20, transcendentals=0)
    (
        lat, lat_own, lat_away, entry, after, slope, side, dlat, dlast, loss, head_grads,
        turned, code_rows, gains,
    ) = pl.pallas_call(
        functools.partial(forward_kernel, s),
        grid_spec=pltpu.PrefetchScalarGridSpec(
            num_scalar_prefetch=1,
            grid=(steps // pair,),
            in_specs=[pl.BlockSpec(memory_space=pltpu.HBM)] * 14
            + [
                pl.BlockSpec((rows, half), lambda step, tower: (tower[0], 0)),
                whole((blocks, width)),
                whole((blocks, width, width)),
                whole((blocks, width, width)),
                whole((bins, width)),
            ],
            out_specs=[
                per_pair(2, rows, width),
                per_pair(rows, width),
                per_pair(rows, width),
                per_pair(calls, rows, width),
                per_pair(calls, rows, width),
                per_pair(calls, rows, width),
                per_pair(calls + 2, rows, LANES),
                pl.BlockSpec(
                    (pair, 2, rows, width), lambda turn, tower: (jnp.maximum(turn - 1, 0), 0, 0, 0)
                ),
                whole((pair, 2, rows, width)),
                whole((8, rows)),
                whole((s.head_rows // s.head_block, 2, s.head_block, width)),
                whole((2 * calls, width, width)),
                whole((2, steps, rows)),
                whole((2, 8, width)),
            ],
            scratch_shapes=[
                pltpu.VMEM((rows, half), BF16),
                pltpu.VMEM((1, rows), jnp.int32),
                pltpu.VMEM((steps, rows), jnp.int32),
                pltpu.VMEM((steps, rows), jnp.int32),
                pltpu.VMEM((steps, rows), jnp.int32),
                pltpu.VMEM((steps, 2, rows), jnp.int32),
                pltpu.VMEM((steps, rows), jnp.int32),
                pltpu.VMEM((table_rows, width), BF16),
                pltpu.VMEM((blocks, width), BF16),
                pltpu.VMEM((blocks, width, width), BF16),
                pltpu.VMEM((blocks, width, width), BF16),
                pltpu.VMEM((bins, width), BF16),
                pltpu.VMEM((bins, width), BF16),
                pltpu.VMEM((table_rows, width), BF16),
                pltpu.SemaphoreType.DMA((14,)),
                pltpu.VMEM((rows, width), BF16),
                pltpu.VMEM((pair * rows, width), BF16),
                pltpu.VMEM((pair * rows, width), BF16),
                pltpu.VMEM((width, width), BF16),
                pltpu.VMEM((LANES, width), BF16),
                pltpu.VMEM((2 * calls, width, width), BF16),
                pltpu.VMEM((s.depth[0], width), BF16),
                pltpu.VMEM((s.depth[1], width), BF16),
                pltpu.VMEM((width, s.depth[0]), BF16),
                pltpu.VMEM((width, s.depth[1]), BF16),
                pltpu.VMEM((s.stack[0], width), F32),
                pltpu.VMEM((s.stack[1], width), F32),
                pltpu.VMEM((s.stack[0], pair * rows), F32),
                pltpu.VMEM((s.stack[1], pair * rows), F32),
                pltpu.VMEM((s.depth[0], pair * rows), BF16),
                pltpu.VMEM((s.depth[1], pair * rows), BF16),
                pltpu.VMEM((s.reward_at - s.sums_at, LANES), F32),
                pltpu.VMEM((pair, s.reward_at - s.sums_at, width), F32),
            ],
        ),
        out_shape=[
            shape((steps, 2, rows, width), BF16),
            pltpu.HBM((steps, rows, width), BF16),
            pltpu.HBM((steps, rows, width), BF16),
            shape((steps, calls, rows, width), BF16),
            shape((steps, calls, rows, width), BF16),
            shape((steps, calls, rows, width), F32),
            shape((steps, calls + 2, rows, LANES), F32),
            shape((steps - pair, 2, rows, width), F32),
            shape((pair, 2, rows, width), F32),
            shape((8, rows), F32),
            shape((s.head_rows // s.head_block, 2, s.head_block, width), BF16),
            shape((2 * calls, width, width), BF16),
            shape((2, steps, rows), jnp.int32),
            shape((2, 8, width), F32),
        ],
        compiler_params=forward_params,
        cost_estimate=cost,
        name="unroll_forward",
    )(
        tower_ref,
        *[
            pltpu.with_memory_space_constraint(value, pltpu.HBM)
            for value in (
                root_state, lengths, actions, codes, policy_target,
                jnp.swapaxes(value_bins, 0, 1), reward_bins, cond_table, gains_own,
                in_own, out_own, value_own, reward_head.T, small_head.T,
            )
        ],
        root_got, gains_got, in_got, out_got, value_got,
    )

    factors = round_factors(parts)
    strides = [1]
    for factor in factors:
        strides.append(strides[-1] * factor)
    groups = [batch_groups(factor, stride, parts) for factor, stride in zip(factors, strides)]
    head_part = lax.psum_scatter(
        head_grads, "batch", scatter_dimension=0, axis_index_groups=groups[0]
    )

    turns = steps // pair
    descending = lambda *tail: pl.BlockSpec(
        (pair,) + tail, lambda turn, tower: (turns - 1 - turn,) + (0,) * len(tail)
    )
    own, away, root_own, root_away = pl.pallas_call(
        functools.partial(backward_kernel, s),
        grid_spec=pltpu.PrefetchScalarGridSpec(
            num_scalar_prefetch=1,
            grid=(turns,),
            in_specs=[
                descending(2, rows, width),
                descending(calls, rows, width),
                descending(calls, rows, width),
                descending(calls, rows, width),
                descending(calls + 2, rows, LANES),
                pl.BlockSpec(
                    (pair, 2, rows, width),
                    lambda turn, tower: (jnp.minimum(turns - 1 - turn, turns - 2), 0, 0, 0),
                ),
                whole((pair, 2, rows, width)),
                whole((2, steps, rows)),
                whole((2, 8, width)),
                whole((2 * calls, width, width)),
            ],
            out_specs=[
                whole((s.matrix_rows, width)),
                whole((s.matrix_rows, width)),
                whole((rows, half)),
                whole((rows, half)),
            ],
            scratch_shapes=[
                pltpu.VMEM((rows, width), F32),
                pltpu.VMEM((2, 16, width), F32),
                pltpu.VMEM((s.held, width), F32),
                pltpu.VMEM((2, calls, width, width), F32),
                pltpu.VMEM((2, 16, width), F32),
                pltpu.VMEM((2, 16, width), F32),
                pltpu.VMEM((pair, calls, rows, width), BF16),
                pltpu.VMEM((pair, calls, rows, width), BF16),
                pltpu.VMEM((pair, 2, rows, width), BF16),
            ],
        ),
        out_shape=[
            shape((s.matrix_rows, width), BF16),
            shape((s.matrix_rows, width), BF16),
            shape((rows, half), BF16),
            shape((rows, half), BF16),
        ],
        compiler_params=backward_params,
        cost_estimate=cost,
        name="unroll_backward",
    )(
        tower_ref, lat, entry, after, slope, side, dlat, dlast, code_rows, gains,
        turned,
    )
    got = swap(away, "tower", 1)

    def beside(given):
        lat_own, lat_away, loss, root_own, root_away = given
        lat_got = swap(lat_away, "tower", 1)
        loss_own = loss[0]
        loss_got = swap(loss_own, "tower", 1)
        root_got = swap(root_away, "tower", 1)

        latents, logits = pl.pallas_call(
            functools.partial(logits_kernel, s),
            grid_spec=pltpu.PrefetchScalarGridSpec(
                num_scalar_prefetch=1,
                grid=(steps,),
                in_specs=[per_step(rows, width), per_step(rows, width), whole((bins, width))],
                out_specs=[per_step(batch_rows, width), per_step(bins, batch_rows)],
            ),
            out_shape=[
                shape((steps, batch_rows, width), BF16),
                shape((steps, bins, batch_rows), BF16),
            ],
            compiler_params=small_params,
            cost_estimate=pl.CostEstimate(
                flops=2 * steps * batch_rows * width * wide, bytes_accessed=6 * 2**20, transcendentals=0
            ),
            name="latents_and_logits",
        )(
            tower_ref,
            *[
                pltpu.with_memory_space_constraint(part, pltpu.HBM)
                for part in (lat_own, lat_got, value_own)
            ],
        )

        def in_order(mine_value, got_value, axis):
            return jnp.where(
                tower_id == 0,
                jnp.concatenate([mine_value, got_value], axis=axis),
                jnp.concatenate([got_value, mine_value], axis=axis),
            )

        row_loss = in_order(loss_own, loss_got, 0)
        grad_root = in_order(root_own, root_got, 0).astype(F32)
        return latents, logits, row_loss, grad_root

    rounds = exchange_rounds(parts)

    def unpack(digit, held):
        length = held[0].shape[0]
        block = s.cond_at // length
        at = s.cond_at - block * length
        parts_of = [part[at : at + s.held] for part in held]
        cond_own = parts_of[0]
        for other in range(1, len(held)):
            cond_own = jnp.where((digit ^ other) == block, parts_of[other], cond_own)
        cond_got = swap(cond_own, "tower", 1)
        return (cond_own, cond_got), pl.pallas_call(
            functools.partial(unpack_matrices_kernel, s),
            grid_spec=pltpu.PrefetchScalarGridSpec(
                num_scalar_prefetch=1,
                grid=(1,),
                in_specs=[whole(part.shape) for part in held],
                out_specs=[
                    whole((blocks, width, width)),
                    whole((blocks, width, width)),
                    whole((blocks, 1, width)),
                ],
                scratch_shapes=[pltpu.VMEM((s.matrix_rows, width), BF16)],
            ),
            out_shape=[
                shape((blocks, width, width), F32),
                shape((blocks, width, width), F32),
                shape((blocks, 1, width), F32),
            ],
            compiler_params=small_params,
            name="unpack_matrices",
        )(digit[None], *held)

    head_got = swap(head_part, "tower", 1)
    head_part = pl.pallas_call(
        pick_and_add_kernel,
        grid_spec=pltpu.PrefetchScalarGridSpec(
            num_scalar_prefetch=1,
            grid=(1,),
            in_specs=[whole(head_part.shape)] * 2,
            out_specs=whole(head_part.shape[1:]),
        ),
        out_shape=shape(head_part.shape[1:], BF16),
        compiler_params=small_params,
        name="pick_and_add",
    )(tower_ref, head_part, head_got)
    def scatter(group, factor):
        return lambda value: lax.psum_scatter(
            value.reshape((factor, -1, width)), "batch", scatter_dimension=0,
            axis_index_groups=group,
        )

    def gather(group):
        return lambda value: lax.all_gather(value, "batch", axis_index_groups=group, tiled=True)

    transfers = [scatter(group, factor) for factor, group in zip(factors[1:], groups[1:])]
    transfers += [gather(group) for group in reversed(groups)]
    on_way = {"heads": transfers.pop(0)(head_part)}

    def other(anchor):
        if transfers:
            tied = lax.optimization_barrier((on_way["heads"], anchor))[0]
            on_way["heads"] = transfers.pop(0)(tied)

    given = (lat_own, lat_away, loss, root_own, root_away)
    unpacked, done = exchange([own, got], rounds, parts, beside, given, unpack, other)
    head_part = on_way["heads"]
    for transfer in transfers:
        head_part = transfer(head_part)
    heads_got = swap(head_part[s.reward_at : s.head_end], "tower", 1)
    (cond_own, cond_got), (grad_in, grad_out, gain_t) = unpacked
    latents, logits, row_loss, grad_root = done
    value_t, rms_t, reward_t, small_t, grad_cond = pl.pallas_call(
        functools.partial(unpack_heads_kernel, s),
        grid_spec=pltpu.PrefetchScalarGridSpec(
            num_scalar_prefetch=1,
            grid=(1,),
            in_specs=[
                whole(head_part.shape),
                whole(heads_got.shape),
                whole(cond_own.shape),
                whole(cond_got.shape),
            ],
            out_specs=[
                whole((bins, 1, width)),
                whole((blocks, 2, steps)),
                whole((bins, width)),
                whole((table_rows, width)),
                whole((table_rows, width)),
            ],
            scratch_shapes=[
                pltpu.VMEM((s.wide, width), F32),
                pltpu.VMEM((s.reward_at - s.sums_at, LANES), F32),
            ],
        ),
        out_shape=[
            shape((bins, 1, width), F32),
            shape((blocks, 2, steps), F32),
            shape((bins, width), F32),
            shape((table_rows, width), F32),
            shape((table_rows, width), F32),
        ],
        compiler_params=small_params,
        name="unpack_heads",
    )(tower_ref, head_part, heads_got, cond_own, cond_got)
    layer_rms = jnp.transpose(rms_t, (2, 0, 1))[None]
    return (
        latents[None],
        jnp.swapaxes(logits, 1, 2)[None],
        row_loss,
        layer_rms,
        grad_root,
        grad_cond,
        jnp.swapaxes(gain_t, 0, 1),
        grad_in[None],
        grad_out[None],
        jnp.transpose(value_t, (1, 2, 0)),
        reward_t.T,
        small_t.T,
    )


def solution(mesh):
    placed = (
        P("batch", "tower"),
        P(),
        P("tower", None, None),
        P("tower", None, None, None),
        P("tower", None, None, None),
        P("tower", None, None),
        P(),
        P(),
        P("batch"),
        P(None, "batch"),
        P(None, "batch"),
        P(None, "batch"),
        P(None, None, "batch"),
        P(None, "batch"),
    )
    return jax.shard_map(
        body,
        mesh=mesh,
        in_specs=placed,
        out_specs=(
            P("tower", None, "batch", None),
            P("tower", None, "batch", None),
            P("batch"),
            P("tower", None, None, None),
            P("batch", "tower"),
            P(),
            P("tower", None, None),
            P("tower", None, None, None),
            P("tower", None, None, None),
            P("tower", None, None),
            P(),
            P(),
        ),
        check_vma=False,
    )
```

```python
import functools

import jax
import jax.numpy as jnp
from jax import lax
from jax.experimental import pallas as pl
from jax.experimental.pallas import tpu as pltpu
from jax.sharding import PartitionSpec as P

ACTIONS = 4
LANES = 128
MIB = 1024 * 1024
GROUPS = 2
FORWARD_LIMIT = 20 * MIB
BACKWARD_LIMIT = 20 * MIB
SMALL_LIMIT = 12 * MIB
epsilon = 1e-06
very_negative = -1e30
F32 = jnp.float32
BF16 = jnp.bfloat16


def natural(left, right):
    return lax.dot_general(left, right, (((1,), (0,)), ((), ())), preferred_element_type=F32)


def by_rows(left, right):
    return lax.dot_general(left, right, (((0,), (0,)), ((), ())), preferred_element_type=F32)


def by_lanes(left, right):
    return lax.dot_general(left, right, (((1,), (1,)), ((), ())), preferred_element_type=F32)


def round_up(value, unit):
    return (value + unit - 1) // unit * unit


def lane_sum(value):
    return jnp.sum(value, axis=-1, keepdims=True)


def inverse_rms(hidden):
    return lax.rsqrt(lane_sum(hidden * hidden) * (1.0 / hidden.shape[-1]) + epsilon)


def weave(*tasks):
    tasks = [(list(task)) for task in tasks]
    longest = max(len(task) for task in tasks)
    done = [0] * len(tasks)
    for turn in range(longest):
        for which, task in enumerate(tasks):
            until = (turn + 1) * len(task) // longest
            while done[which] < until:
                task[done[which]]()
                done[which] += 1


def cuts(length, unit=160):
    return [(start, min(start + unit, length)) for start in range(0, length, unit)]


class Sizes:
    def __init__(self, steps, rows, blocks, width, bins, table_rows, parts):
        self.steps, self.rows, self.blocks, self.width = steps, rows, blocks, width
        self.bins, self.table_rows, self.parts = bins, table_rows, parts
        self.calls = 2 * blocks
        self.pair = 2 if steps % 2 == 0 else 1
        self.wide = round_up(bins, 32)
        self.held = round_up(table_rows, 16)
        self.stack = (self.wide + self.held, 2 * self.wide + self.held)
        self.depth = tuple(round_up(rows_in, LANES) for rows_in in self.stack)
        half = self.wide // 2
        self.value_at = self.calls * width
        self.sums_at = self.value_at + self.wide
        self.kinds = 2 * self.calls
        self.gain_row = self.kinds + 1
        self.reward_at = self.sums_at + round_up(self.gain_row + blocks, 16)
        self.small_at = self.reward_at + half
        self.cond_at = self.small_at + self.held
        self.shared_end = self.cond_at + self.held
        self.total = round_up(self.shared_end, 16 * parts)
        self.head_rows = self.cond_at - self.value_at


def forward_kernel(
    sizes, tower_ref,
    root_hbm, lengths_hbm, actions_hbm, codes_hbm, policy_hbm, value_bins_hbm, reward_bins_hbm,
    table_hbm, gains_hbm, in_hbm, out_hbm, value_hbm, reward_hbm, small_hbm,
    root_got, gains_got, in_got, out_got, value_got,
    lat, lat_own, lat_away, entry, after, slope, side, dlat, dlast, loss, head_grads, turned, code_rows, gains,
    root_own, lengths, actions, codes, policy, value_bins, reward_bins,
    table_in, gains_own, in_own, out_own, value_own, reward_in, small_in, sems,
    state, past0, past1, identity, table, weights, heads0, heads1, flip0, flip1, acc0, acc1,
    logits0, logits1, cot0, cot1, sums, squares,
):
    s = sizes
    pair = s.pair
    turn = pl.program_id(0)
    first_step = turn * pair
    tower_id = tower_ref[0]
    rows, width, wide = s.rows, s.width, s.wide

    @pl.when(turn == 0)
    def _():
        here = pl.ds(pl.multiple_of(tower_id * rows, rows), rows)
        moves = [
            (root_hbm.at[here], root_own),
            (lengths_hbm.at[:, here], lengths),
            (actions_hbm.at[:, here], actions),
            (codes_hbm.at[:, here], codes),
            (policy_hbm.at[:, here], policy),
            (value_bins_hbm.at[:, :, here], value_bins),
            (reward_bins_hbm.at[:, here], reward_bins),
            (table_hbm, table_in),
            (gains_hbm, gains_own),
            (in_hbm, in_own),
            (out_hbm, out_own),
            (value_hbm, value_own),
            (reward_hbm, reward_in),
            (small_hbm, small_in),
        ]
        moves = [
            pltpu.make_async_copy(source, target, sems.at[place])
            for place, (source, target) in enumerate(moves)
        ]
        for move in moves:
            move.start()
        for move in moves:
            move.wait()
        first = tower_id == 0
        code_rows[0] = actions[...]
        code_rows[1] = codes[...] + ACTIONS
        state[:, 0 : width // 2] = jnp.where(first, root_own[...], root_got[...])
        state[:, width // 2 : width] = jnp.where(first, root_got[...], root_own[...])
        for tower, w_first, w_second in (
            (tower_id, in_own, out_own),
            (1 - tower_id, in_got, out_got),
        ):
            weights[pl.ds(tower * s.blocks, s.blocks)] = w_first[...]
            weights[pl.ds(s.calls + tower * s.blocks, s.blocks)] = w_second[...]
        gains[...] = jnp.zeros_like(gains)
        gains[tower_id, 0 : s.blocks, :] = gains_own[...].astype(F32)
        gains[1 - tower_id, 0 : s.blocks, :] = gains_got[...].astype(F32)
        table[...] = jnp.zeros_like(table)
        table[0 : s.table_rows, :] = table_in[...]
        heads0[...] = jnp.zeros_like(heads0)
        heads1[...] = jnp.zeros_like(heads1)
        heads0[0 : s.bins, :] = jnp.where(first, value_own[...], value_got[...])
        heads1[0 : s.bins, :] = jnp.where(first, value_got[...], value_own[...])
        heads1[wide : wide + s.bins, :] = reward_in[...]
        heads0[wide : wide + s.table_rows, :] = small_in[...]
        heads1[2 * wide : 2 * wide + s.table_rows, :] = small_in[...]
        down = lax.broadcasted_iota(jnp.int32, (width, width), 0)
        across = lax.broadcasted_iota(jnp.int32, (width, width), 1)
        identity[...] = jnp.where(down == across, 1.0, 0.0).astype(BF16)
        flip0[...] = by_lanes(identity[...], heads0[...]).astype(BF16)
        flip1[...] = by_lanes(identity[...], heads1[...]).astype(BF16)
        past0[...] = jnp.zeros_like(past0)
        past1[...] = jnp.zeros_like(past1)
        cot0[...] = jnp.zeros_like(cot0)
        cot1[...] = jnp.zeros_like(cot1)
        acc0[...] = jnp.zeros_like(acc0)
        acc1[...] = jnp.zeros_like(acc1)
        sums[...] = jnp.zeros_like(sums)
        squares[...] = jnp.zeros_like(squares)
        loss[...] = jnp.zeros_like(loss)

    eights = lax.broadcasted_iota(jnp.int32, (8, pair * rows), 0)
    before = jnp.maximum(first_step - pair, 0)

    def pair_row(kind, at_step, lead=()):
        return jnp.concatenate(
            [kind[(pl.ds(at_step + offset, 1),) + lead] for offset in range(pair)], axis=1
        )

    def live_rows(at_step):
        return jnp.concatenate(
            [(at_step + offset < lengths[...]).astype(F32) for offset in range(pair)], axis=1
        )

    kinds = []
    for offset in range(pair):
        step = first_step + offset
        kinds.append((step < lengths[...]).astype(F32))
        kinds.append(actions[pl.ds(step, 1), :].astype(F32))
        kinds.append((codes[pl.ds(step, 1), :] + ACTIONS).astype(F32))
    kinds.append(jnp.zeros((8 - len(kinds), rows), F32))
    columns = jnp.concatenate(kinds, axis=0).T

    def heads(tower, live_row, at_step, put):
        latent = past0 if tower == 0 else past1
        stack, flip, logits, cot, acc = (
            (heads0, flip0, logits0, cot0, acc0)
            if tower == 0
            else (heads1, flip1, logits1, cot1, acc1)
        )
        pick = lambda kind: pair_row(kind, at_step)
        value_goal = pair_row(value_bins, at_step, (tower,))
        spans = [(0, wide, 0, s.bins, value_goal)]
        if tower == 1:
            spans.append((wide, wide, 0, s.bins, pick(reward_bins)))
            spans.append((2 * wide, s.held, 0, ACTIONS, pick(policy)))
        else:
            spans.append((wide, s.held, ACTIONS, s.table_rows, pick(codes) + ACTIONS))

        def make_logits():
            logits[...] = by_lanes(stack[0 : logits.shape[0], :], latent[...])

        def eight_rows(value):
            return value.reshape(-1, 8, pair * rows)

        def mask(at, length, first, last):
            for start in range(0, length, 8):
                if start < first or start + 8 > last:
                    inside = (eights >= first - start) & (eights < last - start)
                    place = slice(at + start, at + start + 8)
                    logits[place, :] = jnp.where(inside, logits[place, :], very_negative)

        def find_top(at, start, stop, kept):
            top = jnp.max(eight_rows(logits[at + start : at + stop, :]), axis=0)
            kept["top"] = jnp.maximum(kept["top"], top) if "top" in kept else top

        def end_top(kept):
            kept["top"] = jnp.max(kept["top"], axis=0, keepdims=True)

        def make_terms(at, start, stop, goal, kept):
            place = slice(at + start, at + stop)
            value = logits[place, :]
            spot = lax.broadcasted_iota(jnp.int32, value.shape, 0)
            term = jnp.exp(value - kept["top"])
            logits[place, :] = term
            hit = spot == goal - start
            total = jnp.sum(eight_rows(term), axis=0)
            picked = jnp.sum(eight_rows(jnp.where(hit, value, 0.0)), axis=0)
            kept["total"] = kept["total"] + total if "total" in kept else total
            kept["picked"] = kept["picked"] + picked if "picked" in kept else picked

        def end_terms(kept):
            total = jnp.sum(kept["total"], axis=0, keepdims=True)
            picked = jnp.sum(kept["picked"], axis=0, keepdims=True)
            kept["scale"] = live_row / total
            row_loss = live_row * (jnp.log(total) + kept["top"] - picked)
            for offset in range(pair):
                loss[0:1, :] += row_loss[:, offset * rows : (offset + 1) * rows]

        def make_cotangent(at, start, stop, goal, kept):
            place = slice(at + start, at + stop)
            term = logits[place, :]
            spot = lax.broadcasted_iota(jnp.int32, term.shape, 0)
            hit = spot == goal - start
            cot[place, :] = (term * kept["scale"] - jnp.where(hit, live_row, 0.0)).astype(BF16)

        def make_grads():
            acc[...] += natural(cot[0 : acc.shape[0], :], latent[...])

        def make_latent():
            d_latent = natural(flip[...], cot[...]).T
            for offset in range(pair):
                put[offset, tower] = d_latent[offset * rows : (offset + 1) * rows]

        pieces = [make_logits]
        for at, length, first, last, goal in spans:
            kept = {}
            each = cuts(length)
            pieces.append(functools.partial(mask, at, length, first, last))
            pieces += [functools.partial(find_top, at, *cut, kept) for cut in each]
            pieces.append(functools.partial(end_top, kept))
            pieces += [functools.partial(make_terms, at, *cut, goal, kept) for cut in each]
            pieces.append(functools.partial(end_terms, kept))
            pieces += [functools.partial(make_cotangent, at, *cut, goal, kept) for cut in each]
        return pieces + [make_latent, make_grads]

    def tower_call(offset, tower, x_in, done):
        kept = {}
        parts = {}

        def group_rows(group):
            size = rows // GROUPS
            return slice(group * size, (group + 1) * size)

        def columns_of(group):
            some = group_rows(group)
            live = columns[some, 3 * offset : 3 * offset + 1]
            return live, columns[some, 3 * offset + 1 + tower : 3 * offset + 2 + tower]

        def begin(group):
            some = group_rows(group)
            live, code = columns_of(group)
            spot = lax.broadcasted_iota(jnp.int32, (rows // GROUPS, table.shape[0]), 1)
            onehot = jnp.where(spot.astype(F32) == code, 1.0, 0.0).astype(BF16)
            kept[group] = x_in(group).astype(F32) + natural(onehot, table[...])

        def scale_rows(group):
            row_squares = lane_sum(kept[group] * kept[group])
            return row_squares, lax.rsqrt(row_squares * (1.0 / width) + epsilon)

        def add_up(name, group, value):
            parts[name] = value if group == 0 else parts[name] + value
            return parts[name] if group == GROUPS - 1 else None

        def keep_squares(group, block, row_squares):
            live, _ = columns_of(group)
            place = 2 * (tower * s.blocks + block)
            total = jnp.sum(live * row_squares, axis=0, keepdims=True) * (1.0 / LANES)
            total = add_up("stream", group, total)
            if total is not None:
                squares[offset, place : place + 1, 0:LANES] = jnp.broadcast_to(total, (1, LANES))

        def into(block, group):
            some = group_rows(group)
            place = tower * s.blocks + block
            gained = kept[group] * gains[tower, block : block + 1, :]
            product = natural(gained.astype(BF16), weights[place])
            row_squares, inv_scale = scale_rows(group)
            kept["u", group] = product * inv_scale
            entry[offset, place, some] = (gained * inv_scale).astype(BF16)
            side[offset, place, some] = jnp.broadcast_to(inv_scale, (rows // GROUPS, LANES))
            if block > 0:
                keep_squares(group, block - 1, row_squares)

        def out_of(block, group):
            some = group_rows(group)
            live, _ = columns_of(group)
            place = tower * s.blocks + block
            u = kept["u", group]
            gate = 0.5 * jnp.tanh(0.5 * u) + 0.5
            after_rows = (u * gate).astype(BF16)
            branch = natural(after_rows, weights[s.calls + place])
            kept[group] = kept[group] + branch
            after[offset, place, some] = after_rows
            slope[offset, place, some] = gate * (1.0 + u * (1.0 - gate))
            spot = 2 * place + 1
            total = add_up(
                "branch", group, jnp.sum(branch * branch * live, axis=0, keepdims=True)
            )
            if total is not None:
                squares[offset, spot : spot + 1, :] = total

        def finish(group):
            some = group_rows(group)
            live, _ = columns_of(group)
            row_squares, inv_scale = scale_rows(group)
            side[offset, s.calls + tower, some] = jnp.broadcast_to(
                inv_scale, (rows // GROUPS, LANES)
            )
            latent = (kept[group] * inv_scale).astype(BF16)
            lat[offset, tower, some] = latent
            keep_squares(group, s.blocks - 1, row_squares)
            if tower == 0:
                total = jnp.sum(live, axis=0, keepdims=True) * (1.0 / LANES)
                total = add_up("count", group, total)
                if total is not None:
                    squares[offset, s.kinds : s.kinds + 1, 0:LANES] = jnp.broadcast_to(
                        total, (1, LANES)
                    )
            done(group, latent)

        each = range(GROUPS)
        pieces = [functools.partial(begin, group) for group in each]
        for block in range(s.blocks):
            pieces += [functools.partial(into, block, group) for group in each]
            pieces += [functools.partial(out_of, block, group) for group in each]
        return pieces + [functools.partial(finish, group) for group in each]

    size = rows // GROUPS
    found = {
        (1, -1, group): state[group * size : (group + 1) * size, :] for group in range(GROUPS)
    }

    def get_latent(offset, tower, group):
        return found[tower, offset, group]

    def put_latent(offset, tower, group, value):
        found[tower, offset, group] = value

    chain = []
    for offset in range(pair):
        for tower in range(2):
            source = (offset, 0) if tower == 1 else (offset - 1, 1)
            chain += tower_call(
                offset,
                tower,
                functools.partial(get_latent, *source),
                functools.partial(put_latent, offset, tower),
            )

    turns = -(-2 * s.calls // (s.steps // pair))

    def turn_weights(which):
        matrix = jnp.minimum(turn * turns + which, 2 * s.calls - 1)
        turned[matrix] = by_lanes(identity[...], weights[matrix]).astype(BF16)

    live_before = jnp.where(turn > 0, live_rows(before), 0.0)
    weave(
        chain,
        heads(1, live_before, before, dlat)
        + heads(0, live_before, before, dlat)
        + [functools.partial(turn_weights, which) for which in range(turns)],
    )
    first = tower_id == 0
    at_lane = lax.broadcasted_iota(jnp.int32, sums.shape, 1)
    for offset in range(pair):
        for group in range(GROUPS):
            some = slice(group * size, (group + 1) * size)
            at = slice(offset * rows + group * size, offset * rows + (group + 1) * size)
            after_state, next_state = found[0, offset, group], found[1, offset, group]
            past0[at, :] = after_state
            past1[at, :] = next_state
            lat_own[offset, some] = jnp.where(first, after_state, next_state)
            lat_away[offset, some] = jnp.where(first, next_state, after_state)
            if offset == pair - 1:
                state[some, :] = next_state
        total = lane_sum(squares[offset])
        sums[...] = jnp.where(at_lane == first_step + offset, total, sums[...])

    @pl.when(turn == pl.num_programs(0) - 1)
    def _():
        live_now = live_rows(first_step)
        weave(heads(1, live_now, first_step, dlast), heads(0, live_now, first_step, dlast))
        half = wide // 2
        head_grads[...] = jnp.zeros_like(head_grads)
        head_grads[0, 0:wide, :] = acc0[0:wide, :].astype(BF16)
        head_grads[1, 0:wide, :] = acc1[0:wide, :].astype(BF16)
        small = acc0[wide : wide + s.held, :] + acc1[2 * wide : 2 * wide + s.held, :]
        at = s.small_at - s.value_at
        head_grads[0, at : at + s.held, :] = small.astype(BF16)
        for tower in range(2):
            put = s.reward_at - s.value_at
            at = wide + tower * half
            head_grads[tower, put : put + half, :] = acc1[at : at + half, :].astype(BF16)
            head_grads[tower, wide : wide + sums.shape[0], 0:LANES] = sums[...].astype(BF16)


def backward_kernel(
    sizes, tower_ref,
    lat, entry, after, slope, side, dlat, dlast, code_rows, gains_in, turned, head_grads,
    own, away, root_own, root_away,
    carry, gain_sum, cond_sum, grads, gains, inverse_gains, d_after_kept, d_before_kept,
    d_hidden_kept,
):
    s = sizes
    pair = s.pair
    turn = pl.program_id(0)
    first_step = s.steps - pair * (turn + 1)
    tower_id = tower_ref[0]
    blocks, width = s.blocks, s.width

    @pl.when(turn == 0)
    def _():
        gains[...] = jnp.ones_like(gains)
        gains[:, 0:blocks, :] = gains_in[:, 0:blocks, :]
        inverse_gains[...] = 1.0 / gains[...]
        carry[...] = jnp.zeros_like(carry)
        grads[...] = jnp.zeros_like(grads)
        gain_sum[...] = jnp.zeros_like(gain_sum)
        cond_sum[...] = jnp.zeros_like(cond_sum)

    def over_lanes(column):
        return jnp.concatenate([column] * (width // LANES), axis=1)

    def stacked(parts):
        return jnp.concatenate(parts, axis=0)

    size = s.rows // GROUPS
    each = range(GROUPS)

    def add_grads(matrix, rows_of, place, kept, now):
        later = [kept[offset, place] for offset in range(1, pair)]
        grads[matrix // s.calls, matrix % s.calls] += by_rows(
            stacked([rows_of[offset, place] for offset in range(pair)]), stacked(now + later)
        )

    def tower_back(offset, tower, d_latents):
        flow = []
        for group in each:
            some = slice(group * size, (group + 1) * size)
            normed = lat[offset, tower, some]
            normed_wide = normed.astype(F32)
            inv_scale = over_lanes(side[offset, s.calls + tower, some])
            base = inv_scale * d_latents[group]
            slant = inv_scale * (lane_sum(d_latents[group] * normed_wide) * (1.0 / width))
            flow.append((base, slant, normed, normed_wide))
        for block in reversed(range(blocks)):
            place = tower * blocks + block
            gain = gains[tower, block : block + 1, :]
            inverse_gain = inverse_gains[tower, block : block + 1, :]
            first = []
            for base, slant, normed, normed_wide in flow:
                both = natural(
                    jnp.concatenate([normed, base.astype(BF16)], axis=0), turned[s.calls + place]
                )
                first.append((both[size:] - slant * both[:size], base - slant * normed_wide))
            d_branch, d_before, flow, gain_part = [], [], [], None
            for group, (d_after, d_hidden) in enumerate(first):
                some = slice(group * size, (group + 1) * size)
                entry_wide = entry[offset, place, some].astype(F32)
                inv_scale = over_lanes(side[offset, place, some])
                d_branch.append(d_hidden.astype(BF16))
                d_before.append((d_after * slope[offset, place, some]).astype(BF16))
                d_entry = natural(d_before[-1], turned[place])
                product = d_entry * entry_wide
                part = jnp.sum(product, axis=0, keepdims=True)
                gain_part = part if gain_part is None else gain_part + part
                base = d_hidden + inv_scale * (d_entry * gain)
                slant = inv_scale * (lane_sum(product) * (1.0 / width))
                normed_wide = entry_wide * inverse_gain
                flow.append((base, slant, normed_wide.astype(BF16), normed_wide))
            gain_sum[tower, block : block + 1, :] += gain_part
            if offset > 0:
                for group in each:
                    some = slice(group * size, (group + 1) * size)
                    d_after_kept[offset, place, some] = d_branch[group]
                    d_before_kept[offset, place, some] = d_before[group]
            else:
                matrix = tower * s.calls + block
                add_grads(matrix + blocks, after, place, d_after_kept, d_branch)
                add_grads(matrix, entry, place, d_before_kept, d_before)
        d_hidden = [base - slant * normed_wide for base, slant, _, normed_wide in flow]
        if offset > 0:
            for group in each:
                some = slice(group * size, (group + 1) * size)
                d_hidden_kept[offset, tower, some] = d_hidden[group].astype(BF16)
        else:
            code = jnp.concatenate(
                [code_rows[tower, pl.ds(first_step + step, 1), :] for step in range(pair)], axis=1
            )
            spots = lax.broadcasted_iota(jnp.int32, (cond_sum.shape[0], pair * s.rows), 0)
            onehot = jnp.where(spots == code, 1.0, 0.0).astype(BF16)
            parts = [part.astype(BF16) for part in d_hidden]
            parts += [d_hidden_kept[step, tower] for step in range(1, pair)]
            cond_sum[...] += natural(onehot, stacked(parts))
        return d_hidden

    def from_heads(offset, tower, group):
        some = slice(group * size, (group + 1) * size)
        return jnp.where(turn == 0, dlast[offset, tower, some], dlat[offset, tower, some])

    d_states = [carry[group * size : (group + 1) * size, :] for group in each]
    for offset in reversed(range(pair)):
        for tower in (1, 0):
            d_states = tower_back(
                offset,
                tower,
                [part + from_heads(offset, tower, group) for group, part in enumerate(d_states)],
            )
    d_state = stacked(d_states)
    carry[...] = d_state

    @pl.when(turn == pl.num_programs(0) - 1)
    def _():
        left = d_state[:, 0 : width // 2].astype(BF16)
        right = d_state[:, width // 2 : width].astype(BF16)
        root_own[...] = jnp.where(tower_id == 0, left, right)
        root_away[...] = jnp.where(tower_id == 0, right, left)
        gain_sum[...] = gain_sum[...] * inverse_gains[...]
        lines = lax.broadcasted_iota(jnp.int32, (s.reward_at - s.sums_at, width), 0)
        for target, which in ((own, tower_id), (away, 1 - tower_id)):
            for matrix in range(s.calls):
                at = matrix * width
                target[at : at + width, :] = grads[which, matrix].astype(BF16)
            target[s.value_at : s.cond_at, :] = head_grads[which]
            sums = head_grads[which, s.wide : s.wide + lines.shape[0], :].astype(F32)
            for block in range(blocks):
                gain = gain_sum[which, block : block + 1, :]
                sums = jnp.where(lines == s.gain_row + block, gain, sums)
            target[s.sums_at : s.reward_at, :] = sums.astype(BF16)
            here = jnp.where(which == 0, cond_sum[...], 0.0)
            target[s.cond_at : s.shared_end, :] = here.astype(BF16)
            if s.total > s.shared_end:
                target[s.shared_end :, :] = jnp.zeros((s.total - s.shared_end, width), BF16)


def logits_kernel(sizes, tower_ref, lat_own, lat_got, value_own, latents, logits):
    rows = sizes.rows
    tower_id = tower_ref[0]
    at_own = pl.ds(pl.multiple_of(tower_id * rows, rows), rows)
    at_got = pl.ds(pl.multiple_of((1 - tower_id) * rows, rows), rows)
    for offset in range(sizes.pair):
        latents[offset, at_own, :] = lat_own[offset]
        latents[offset, at_got, :] = lat_got[offset]
        logits[offset] = by_lanes(value_own[...], latents[offset]).astype(BF16)


def add_and_split_kernel(count, digit_ref, *refs):
    inputs, outputs = refs[:count], refs[count:]
    digit = digit_ref[0]
    for other, target in enumerate(outputs):
        part = digit ^ other
        total = inputs[0][part].astype(F32)
        for source in inputs[1:]:
            total = total + source[part].astype(F32)
        target[...] = total.astype(BF16)


def unpack_own_kernel(sizes, scalars, *refs):
    s = sizes
    factor = len(refs) - 7
    digit, tower_id = scalars[0], scalars[1]
    w_in, w_out, value, gain, rms, flat, held = refs[factor:]
    width = s.width
    length = refs[0].shape[0]
    for other, source in enumerate(refs[:factor]):
        at = pl.multiple_of((digit ^ other) * length, 16)
        flat[pl.ds(at, length), :] = source[...]
    for block in range(s.blocks):
        at = block * width
        w_in[block] = flat[at : at + width, :].astype(F32)
        at = (s.blocks + block) * width
        w_out[block] = flat[at : at + width, :].astype(F32)
    value[:, 0, :] = flat[s.value_at : s.sums_at, :].astype(F32)[0 : s.bins]
    sums = flat[s.sums_at : s.reward_at, :].astype(F32)
    for block in range(s.blocks):
        gain[block] = sums[s.gain_row + block : s.gain_row + block + 1, :]
    held[...] = sums[:, 0:LANES]
    count = jnp.maximum(held[s.kinds : s.kinds + 1, 0 : s.steps], 1.0)
    for block in range(s.blocks):
        for kind in range(2):
            spot = tower_id * s.calls + 2 * block + kind
            square = held[pl.ds(spot, 1), 0 : s.steps]
            rms[block, kind : kind + 1, :] = jnp.sqrt(jnp.maximum(square, 0.0) / (count * width))


def unpack_shared_kernel(sizes, tower_ref, mine, got, reward, small, cond, joined):
    s = sizes
    tower_id = tower_ref[0]
    half = s.wide // 2
    joined[pl.ds(pl.multiple_of(tower_id * half, 8), half), :] = mine[0:half, :].astype(F32)
    joined[pl.ds(pl.multiple_of((1 - tower_id) * half, 8), half), :] = got[0:half, :].astype(F32)
    reward[...] = joined[0 : s.bins, :]
    for target, at in ((small, s.small_at), (cond, s.cond_at)):
        rows = slice(at - s.reward_at, at - s.reward_at + s.held)
        target[...] = (mine[rows, :].astype(F32) + got[rows, :].astype(F32))[0 : s.table_rows]


def whole(shape):
    return pl.BlockSpec(shape, lambda step, tower: (0,) * len(shape))


def swap(value, axis, mask):
    pairs = [(source, source ^ mask) for source in range(lax.axis_size(axis))]
    return lax.ppermute(value, axis, pairs)


AXES = ("tower", "batch")


def exchange_rounds(batch_size):
    factors, left = [], batch_size
    while left > 1:
        factors.append(4 if left % 4 == 0 else 2)
        left //= factors[-1]
    rounds, stride = [], 1
    for factor in factors:
        rounds.append((factor, stride))
        stride *= factor
    turned = rounds[::-1] if len(set(factors)) == 1 else rounds
    return [(one[0], (one[1], two[1])) for one, two in zip(rounds, turned)]


def swap_within(value, strides, other, batch_size):
    pairs = [
        (tower * batch_size + index, tower * batch_size + (index ^ (other * strides[tower])))
        for tower in range(2)
        for index in range(batch_size)
    ]
    return lax.ppermute(value, AXES, pairs)


def my_digit(factor, strides):
    stride = jnp.where(lax.axis_index("tower") == 0, strides[0], strides[1])
    return (lax.axis_index("batch") // stride) % factor


def add_kernel(*refs):
    total = refs[0][...].astype(F32)
    for source in refs[1:-1]:
        total = total + source[...].astype(F32)
    refs[-1][...] = total.astype(BF16)


def add_up(parts):
    return pl.pallas_call(
        add_kernel,
        out_shape=jax.ShapeDtypeStruct(parts[0].shape, BF16),
        compiler_params=pltpu.CompilerParams(vmem_limit_bytes=SMALL_LIMIT),
        name="add_up",
    )(*parts)


def exchange(value, rounds, batch_size, beside, given, last_kernel):
    factor, strides = rounds[0]
    digit = my_digit(factor, strides)
    rows, width = value[0].shape
    rows = rows // factor
    split = pl.pallas_call(
        functools.partial(add_and_split_kernel, len(value)),
        grid_spec=pltpu.PrefetchScalarGridSpec(
            num_scalar_prefetch=1,
            grid=(1,),
            in_specs=[whole((factor, rows, width))] * len(value),
            out_specs=[whole((rows, width))] * factor,
        ),
        out_shape=[pltpu.HBM((rows, width), BF16)] * factor,
        compiler_params=pltpu.CompilerParams(vmem_limit_bytes=SMALL_LIMIT),
        name="add_and_split",
    )(digit[None], *[part.reshape(factor, rows, width) for part in value])
    split, given = lax.optimization_barrier((split, given))
    held = [split[0]] + [
        swap_within(split[other], strides, other, batch_size) for other in range(1, factor)
    ]
    done = beside(given)
    held, done = lax.optimization_barrier((held, done))
    for size, steps in rounds[1:]:
        bit = 1
        while bit < size:
            block = add_up(held)
            held = [block, swap_within(block, steps, bit, batch_size)]
            bit *= 2
    block = add_up(held)
    held = [block] + [
        swap_within(block, strides, other, batch_size) for other in range(1, factor)
    ]
    return last_kernel(digit, held), done


def body(
    root_state, cond_table, block_gain, w_in, w_out, value_head, reward_head, small_head,
    unroll_len, actions, codes, policy_target, value_bins, reward_bins,
):
    tower_id = lax.axis_index("tower")
    other_id = 1 - tower_id
    tower_ref = tower_id.astype(jnp.int32)[None]
    steps, batch_rows = actions.shape
    blocks, width = block_gain.shape[1:]
    bins = value_head.shape[2]
    table_rows = cond_table.shape[0]
    rows = batch_rows // 2
    half = width // 2
    parts = lax.axis_size("batch")
    s = Sizes(steps, rows, blocks, width, bins, table_rows, parts)
    calls, wide, pair = s.calls, s.wide, s.pair

    root_got = swap(root_state, "tower", 1)
    in_own, out_own, gains_own = w_in[0], w_out[0], block_gain[0]
    value_own = value_head[0].T
    in_got = swap(in_own, "tower", 1)
    out_got = swap(out_own, "tower", 1)
    gains_got = swap(gains_own, "tower", 1)
    value_got = swap(value_own, "tower", 1)
    lengths = unroll_len.reshape(1, batch_rows)

    shape = jax.ShapeDtypeStruct
    per_pair = lambda *tail: pl.BlockSpec(
        (pair,) + tail, lambda turn, tower: (turn,) + (0,) * len(tail)
    )
    forward_params = pltpu.CompilerParams(vmem_limit_bytes=FORWARD_LIMIT)
    backward_params = pltpu.CompilerParams(vmem_limit_bytes=BACKWARD_LIMIT)
    small_params = pltpu.CompilerParams(vmem_limit_bytes=SMALL_LIMIT)
    products = steps * rows * (4 * blocks * width * width + 9 * width * wide)
    cost = pl.CostEstimate(flops=2 * products, bytes_accessed=40 * 2**20, transcendentals=0)
    (
        lat, lat_own, lat_away, entry, after, slope, side, dlat, dlast, loss, head_grads,
        turned, code_rows, gains,
    ) = pl.pallas_call(
        functools.partial(forward_kernel, s),
        grid_spec=pltpu.PrefetchScalarGridSpec(
            num_scalar_prefetch=1,
            grid=(steps // pair,),
            in_specs=[pl.BlockSpec(memory_space=pltpu.HBM)] * 14
            + [
                pl.BlockSpec((rows, half), lambda step, tower: (tower[0], 0)),
                whole((blocks, width)),
                whole((blocks, width, width)),
                whole((blocks, width, width)),
                whole((bins, width)),
            ],
            out_specs=[
                per_pair(2, rows, width),
                per_pair(rows, width),
                per_pair(rows, width),
                per_pair(calls, rows, width),
                per_pair(calls, rows, width),
                per_pair(calls, rows, width),
                per_pair(calls + 2, rows, LANES),
                pl.BlockSpec(
                    (pair, 2, rows, width), lambda turn, tower: (jnp.maximum(turn - 1, 0), 0, 0, 0)
                ),
                whole((pair, 2, rows, width)),
                whole((8, rows)),
                whole((2, s.head_rows, width)),
                whole((2 * calls, width, width)),
                whole((2, steps, rows)),
                whole((2, 8, width)),
            ],
            scratch_shapes=[
                pltpu.VMEM((rows, half), BF16),
                pltpu.VMEM((1, rows), jnp.int32),
                pltpu.VMEM((steps, rows), jnp.int32),
                pltpu.VMEM((steps, rows), jnp.int32),
                pltpu.VMEM((steps, rows), jnp.int32),
                pltpu.VMEM((steps, 2, rows), jnp.int32),
                pltpu.VMEM((steps, rows), jnp.int32),
                pltpu.VMEM((table_rows, width), BF16),
                pltpu.VMEM((blocks, width), BF16),
                pltpu.VMEM((blocks, width, width), BF16),
                pltpu.VMEM((blocks, width, width), BF16),
                pltpu.VMEM((bins, width), BF16),
                pltpu.VMEM((bins, width), BF16),
                pltpu.VMEM((table_rows, width), BF16),
                pltpu.SemaphoreType.DMA((14,)),
                pltpu.VMEM((rows, width), BF16),
                pltpu.VMEM((pair * rows, width), BF16),
                pltpu.VMEM((pair * rows, width), BF16),
                pltpu.VMEM((width, width), BF16),
                pltpu.VMEM((LANES, width), BF16),
                pltpu.VMEM((2 * calls, width, width), BF16),
                pltpu.VMEM((s.depth[0], width), BF16),
                pltpu.VMEM((s.depth[1], width), BF16),
                pltpu.VMEM((width, s.depth[0]), BF16),
                pltpu.VMEM((width, s.depth[1]), BF16),
                pltpu.VMEM((s.stack[0], width), F32),
                pltpu.VMEM((s.stack[1], width), F32),
                pltpu.VMEM((s.stack[0], pair * rows), F32),
                pltpu.VMEM((s.stack[1], pair * rows), F32),
                pltpu.VMEM((s.depth[0], pair * rows), BF16),
                pltpu.VMEM((s.depth[1], pair * rows), BF16),
                pltpu.VMEM((s.reward_at - s.sums_at, LANES), F32),
                pltpu.VMEM((pair, s.reward_at - s.sums_at, width), F32),
            ],
        ),
        out_shape=[
            shape((steps, 2, rows, width), BF16),
            pltpu.HBM((steps, rows, width), BF16),
            pltpu.HBM((steps, rows, width), BF16),
            shape((steps, calls, rows, width), BF16),
            shape((steps, calls, rows, width), BF16),
            shape((steps, calls, rows, width), F32),
            shape((steps, calls + 2, rows, LANES), F32),
            shape((steps - pair, 2, rows, width), F32),
            shape((pair, 2, rows, width), F32),
            shape((8, rows), F32),
            shape((2, s.head_rows, width), BF16),
            shape((2 * calls, width, width), BF16),
            shape((2, steps, rows), jnp.int32),
            shape((2, 8, width), F32),
        ],
        compiler_params=forward_params,
        cost_estimate=cost,
        name="unroll_forward",
    )(
        tower_ref,
        *[
            pltpu.with_memory_space_constraint(value, pltpu.HBM)
            for value in (
                root_state, lengths, actions, codes, policy_target,
                jnp.swapaxes(value_bins, 0, 1), reward_bins, cond_table, gains_own,
                in_own, out_own, value_own, reward_head.T, small_head.T,
            )
        ],
        root_got, gains_got, in_got, out_got, value_got,
    )

    turns = steps // pair
    descending = lambda *tail: pl.BlockSpec(
        (pair,) + tail, lambda turn, tower: (turns - 1 - turn,) + (0,) * len(tail)
    )
    own, away, root_own, root_away = pl.pallas_call(
        functools.partial(backward_kernel, s),
        grid_spec=pltpu.PrefetchScalarGridSpec(
            num_scalar_prefetch=1,
            grid=(turns,),
            in_specs=[
                descending(2, rows, width),
                descending(calls, rows, width),
                descending(calls, rows, width),
                descending(calls, rows, width),
                descending(calls + 2, rows, LANES),
                pl.BlockSpec(
                    (pair, 2, rows, width),
                    lambda turn, tower: (jnp.minimum(turns - 1 - turn, turns - 2), 0, 0, 0),
                ),
                whole((pair, 2, rows, width)),
                whole((2, steps, rows)),
                whole((2, 8, width)),
                whole((2 * calls, width, width)),
                whole((2, s.head_rows, width)),
            ],
            out_specs=[
                whole((s.total, width)),
                whole((s.total, width)),
                whole((rows, half)),
                whole((rows, half)),
            ],
            scratch_shapes=[
                pltpu.VMEM((rows, width), F32),
                pltpu.VMEM((2, 16, width), F32),
                pltpu.VMEM((s.held, width), F32),
                pltpu.VMEM((2, calls, width, width), F32),
                pltpu.VMEM((2, 16, width), F32),
                pltpu.VMEM((2, 16, width), F32),
                pltpu.VMEM((pair, calls, rows, width), BF16),
                pltpu.VMEM((pair, calls, rows, width), BF16),
                pltpu.VMEM((pair, 2, rows, width), BF16),
            ],
        ),
        out_shape=[
            shape((s.total, width), BF16),
            shape((s.total, width), BF16),
            shape((rows, half), BF16),
            shape((rows, half), BF16),
        ],
        compiler_params=backward_params,
        cost_estimate=cost,
        name="unroll_backward",
    )(
        tower_ref, lat, entry, after, slope, side, dlat, dlast, code_rows, gains,
        turned, head_grads,
    )
    got = swap(away, "tower", 1)

    def beside(given):
        lat_own, lat_away, loss, root_own, root_away = given
        lat_got = swap(lat_away, "tower", 1)
        loss_own = loss[0]
        loss_got = swap(loss_own, "tower", 1)
        root_got = swap(root_away, "tower", 1)

        latents, logits = pl.pallas_call(
            functools.partial(logits_kernel, s),
            grid_spec=pltpu.PrefetchScalarGridSpec(
                num_scalar_prefetch=1,
                grid=(steps // pair,),
                in_specs=[per_pair(rows, width), per_pair(rows, width), whole((bins, width))],
                out_specs=[per_pair(batch_rows, width), per_pair(bins, batch_rows)],
            ),
            out_shape=[
                shape((steps, batch_rows, width), BF16),
                shape((steps, bins, batch_rows), BF16),
            ],
            compiler_params=small_params,
            cost_estimate=pl.CostEstimate(
                flops=2 * steps * batch_rows * width * wide, bytes_accessed=6 * 2**20, transcendentals=0
            ),
            name="latents_and_logits",
        )(
            tower_ref,
            *[
                pltpu.with_memory_space_constraint(part, pltpu.HBM)
                for part in (lat_own, lat_got, value_own)
            ],
        )

        def in_order(mine_value, got_value, axis):
            return jnp.where(
                tower_id == 0,
                jnp.concatenate([mine_value, got_value], axis=axis),
                jnp.concatenate([got_value, mine_value], axis=axis),
            )

        row_loss = in_order(loss_own, loss_got, 0)
        grad_root = in_order(root_own, root_got, 0).astype(F32)
        return latents, logits, row_loss, grad_root

    rounds = exchange_rounds(parts)

    def unpack(digit, held):
        scalars = jnp.stack([digit, tower_id]).astype(jnp.int32)
        length = held[0].shape[0]
        block = s.reward_at // length
        at = s.reward_at - block * length
        parts_of = [part[at : at + s.shared_end - s.reward_at] for part in held]
        shared = parts_of[0]
        for other in range(1, len(held)):
            shared = jnp.where((digit ^ other) == block, parts_of[other], shared)
        shared_got = swap(shared, "tower", 1)
        return (shared, shared_got), pl.pallas_call(
            functools.partial(unpack_own_kernel, s),
            grid_spec=pltpu.PrefetchScalarGridSpec(
                num_scalar_prefetch=1,
                grid=(1,),
                in_specs=[whole(part.shape) for part in held],
                out_specs=[
                    whole((blocks, width, width)),
                    whole((blocks, width, width)),
                    whole((bins, 1, width)),
                    whole((blocks, 1, width)),
                    whole((blocks, 2, steps)),
                ],
                scratch_shapes=[
                    pltpu.VMEM((s.total, width), BF16),
                    pltpu.VMEM((s.reward_at - s.sums_at, LANES), F32),
                ],
            ),
            out_shape=[
                shape((blocks, width, width), F32),
                shape((blocks, width, width), F32),
                shape((bins, 1, width), F32),
                shape((blocks, 1, width), F32),
                shape((blocks, 2, steps), F32),
            ],
            compiler_params=small_params,
            name="unpack_own",
        )(scalars, *held)

    given = (lat_own, lat_away, loss, root_own, root_away)
    unpacked, done = exchange([own, got], rounds, parts, beside, given, unpack)
    (shared, shared_got), (grad_in, grad_out, value_t, gain_t, rms_t) = unpacked
    latents, logits, row_loss, grad_root = done
    reward_t, small_t, grad_cond = pl.pallas_call(
        functools.partial(unpack_shared_kernel, s),
        grid_spec=pltpu.PrefetchScalarGridSpec(
            num_scalar_prefetch=1,
            grid=(1,),
            in_specs=[whole(shared.shape), whole(shared.shape)],
            out_specs=[
                whole((bins, width)),
                whole((table_rows, width)),
                whole((table_rows, width)),
            ],
            scratch_shapes=[pltpu.VMEM((s.wide, width), F32)],
        ),
        out_shape=[
            shape((bins, width), F32),
            shape((table_rows, width), F32),
            shape((table_rows, width), F32),
        ],
        compiler_params=small_params,
        name="unpack_shared",
    )(tower_ref, shared, shared_got)
    layer_rms = jnp.transpose(rms_t, (2, 0, 1))[None]
    return (
        latents[None],
        jnp.swapaxes(logits, 1, 2)[None],
        row_loss,
        layer_rms,
        grad_root,
        grad_cond,
        jnp.swapaxes(gain_t, 0, 1),
        grad_in[None],
        grad_out[None],
        jnp.transpose(value_t, (1, 2, 0)),
        reward_t.T,
        small_t.T,
    )


def solution(mesh):
    placed = (
        P("batch", "tower"),
        P(),
        P("tower", None, None),
        P("tower", None, None, None),
        P("tower", None, None, None),
        P("tower", None, None),
        P(),
        P(),
        P("batch"),
        P(None, "batch"),
        P(None, "batch"),
        P(None, "batch"),
        P(None, None, "batch"),
        P(None, "batch"),
    )
    return jax.shard_map(
        body,
        mesh=mesh,
        in_specs=placed,
        out_specs=(
            P("tower", None, "batch", None),
            P("tower", None, "batch", None),
            P("batch"),
            P("tower", None, None, None),
            P("batch", "tower"),
            P(),
            P("tower", None, None),
            P("tower", None, None, None),
            P("tower", None, None, None),
            P("tower", None, None),
            P(),
            P(),
        ),
        check_vma=False,
    )
```

```python
import functools

import jax
import jax.numpy as jnp
from jax import lax
from jax.experimental import pallas as pl
from jax.experimental.pallas import tpu as pltpu
from jax.sharding import PartitionSpec as P

ACTIONS = 4
LANES = 128
MIB = 1024 * 1024
GROUPS = 1
FORWARD_LIMIT = 20 * MIB
BACKWARD_LIMIT = 20 * MIB
SMALL_LIMIT = 12 * MIB
epsilon = 1e-06
very_negative = -1e30
F32 = jnp.float32
BF16 = jnp.bfloat16


def natural(left, right):
    return lax.dot_general(left, right, (((1,), (0,)), ((), ())), preferred_element_type=F32)


def by_rows(left, right):
    return lax.dot_general(left, right, (((0,), (0,)), ((), ())), preferred_element_type=F32)


def by_lanes(left, right):
    return lax.dot_general(left, right, (((1,), (1,)), ((), ())), preferred_element_type=F32)


def round_up(value, unit):
    return (value + unit - 1) // unit * unit


def lane_sum(value):
    return jnp.sum(value, axis=-1, keepdims=True)


def inverse_rms(hidden):
    return lax.rsqrt(lane_sum(hidden * hidden) * (1.0 / hidden.shape[-1]) + epsilon)


def weave(*tasks):
    tasks = [(list(task)) for task in tasks]
    longest = max(len(task) for task in tasks)
    done = [0] * len(tasks)
    for turn in range(longest):
        for which, task in enumerate(tasks):
            until = (turn + 1) * len(task) // longest
            while done[which] < until:
                task[done[which]]()
                done[which] += 1


def cuts(length, unit=160):
    return [(start, min(start + unit, length)) for start in range(0, length, unit)]


def round_factors(size):
    factors = []
    while size > 1:
        factors.append(4 if size % 4 == 0 else 2)
        size //= factors[-1]
    return factors


class Sizes:
    def __init__(self, steps, rows, blocks, width, bins, table_rows, parts):
        self.steps, self.rows, self.blocks, self.width = steps, rows, blocks, width
        self.bins, self.table_rows, self.parts = bins, table_rows, parts
        self.calls = 2 * blocks
        self.pair = 2 if steps % 2 == 0 else 1
        self.wide = round_up(bins, 32)
        self.held = round_up(table_rows, 16)
        self.stack = (self.wide + self.held, 2 * self.wide + self.held)
        self.depth = tuple(round_up(rows_in, LANES) for rows_in in self.stack)
        half = self.wide // 2
        self.value_at = self.calls * width
        self.sums_at = self.value_at + self.wide
        self.kinds = 2 * self.calls
        self.gain_row = self.kinds + 1
        self.reward_at = self.sums_at + round_up(self.gain_row + blocks, 16)
        self.small_at = self.reward_at + half
        self.cond_at = self.small_at + self.held
        self.shared_end = self.cond_at + self.held
        self.factor = round_factors(parts)[0]
        unit = 16 * self.factor
        self.total = round_up(self.shared_end, unit)
        self.first_chunk = round_up(self.total * 2 // 3, unit)
        self.head_rows = self.cond_at - self.value_at


def forward_kernel(
    sizes, tower_ref,
    root_hbm, lengths_hbm, actions_hbm, codes_hbm, policy_hbm, value_bins_hbm, reward_bins_hbm,
    table_hbm, gains_hbm, in_hbm, out_hbm, value_hbm, reward_hbm, small_hbm,
    root_got, gains_got, in_got, out_got, value_got,
    lat, lat_own, lat_away, entry, after, slope, side, dlat, dlast, loss, head_grads, turned, code_rows, gains,
    root_own, lengths, actions, codes, policy, value_bins, reward_bins,
    table_in, gains_own, in_own, out_own, value_own, reward_in, small_in, sems,
    state, past0, past1, table, weights, heads0, heads1, acc0, acc1,
    logits0, logits1, cot0, cot1, sums, squares,
):
    s = sizes
    pair = s.pair
    turn = pl.program_id(0)
    first_step = turn * pair
    tower_id = tower_ref[0]
    rows, width, wide = s.rows, s.width, s.wide

    @pl.when(turn == 0)
    def _():
        here = pl.ds(pl.multiple_of(tower_id * rows, rows), rows)
        moves = [
            (root_hbm.at[here], root_own),
            (lengths_hbm.at[:, here], lengths),
            (actions_hbm.at[:, here], actions),
            (codes_hbm.at[:, here], codes),
            (policy_hbm.at[:, here], policy),
            (value_bins_hbm.at[:, :, here], value_bins),
            (reward_bins_hbm.at[:, here], reward_bins),
            (table_hbm, table_in),
            (gains_hbm, gains_own),
            (in_hbm, in_own),
            (out_hbm, out_own),
            (value_hbm, value_own),
            (reward_hbm, reward_in),
            (small_hbm, small_in),
        ]
        moves = [
            pltpu.make_async_copy(source, target, sems.at[place])
            for place, (source, target) in enumerate(moves)
        ]
        for move in moves:
            move.start()
        for move in moves:
            move.wait()
        first = tower_id == 0
        code_rows[0] = actions[...]
        code_rows[1] = codes[...] + ACTIONS
        state[:, 0 : width // 2] = jnp.where(first, root_own[...], root_got[...])
        state[:, width // 2 : width] = jnp.where(first, root_got[...], root_own[...])
        for tower, w_first, w_second in (
            (tower_id, in_own, out_own),
            (1 - tower_id, in_got, out_got),
        ):
            weights[pl.ds(tower * s.blocks, s.blocks)] = w_first[...]
            weights[pl.ds(s.calls + tower * s.blocks, s.blocks)] = w_second[...]
        gains[...] = jnp.zeros_like(gains)
        gains[tower_id, 0 : s.blocks, :] = gains_own[...].astype(F32)
        gains[1 - tower_id, 0 : s.blocks, :] = gains_got[...].astype(F32)
        table[...] = jnp.zeros_like(table)
        table[0 : s.table_rows, :] = table_in[...]
        heads0[...] = jnp.zeros_like(heads0)
        heads1[...] = jnp.zeros_like(heads1)
        heads0[0 : s.bins, :] = jnp.where(first, value_own[...], value_got[...])
        heads1[0 : s.bins, :] = jnp.where(first, value_got[...], value_own[...])
        heads1[wide : wide + s.bins, :] = reward_in[...]
        heads0[wide : wide + s.table_rows, :] = small_in[...]
        heads1[2 * wide : 2 * wide + s.table_rows, :] = small_in[...]
        past0[...] = jnp.zeros_like(past0)
        past1[...] = jnp.zeros_like(past1)
        cot0[...] = jnp.zeros_like(cot0)
        cot1[...] = jnp.zeros_like(cot1)
        acc0[...] = jnp.zeros_like(acc0)
        acc1[...] = jnp.zeros_like(acc1)
        sums[...] = jnp.zeros_like(sums)
        squares[...] = jnp.zeros_like(squares)
        loss[...] = jnp.zeros_like(loss)

    eights = lax.broadcasted_iota(jnp.int32, (8, pair * rows), 0)
    before = jnp.maximum(first_step - pair, 0)

    def pair_row(kind, at_step, lead=()):
        return jnp.concatenate(
            [kind[(pl.ds(at_step + offset, 1),) + lead] for offset in range(pair)], axis=1
        )

    def live_rows(at_step):
        return jnp.concatenate(
            [(at_step + offset < lengths[...]).astype(F32) for offset in range(pair)], axis=1
        )

    kinds = []
    for offset in range(pair):
        step = first_step + offset
        kinds.append((step < lengths[...]).astype(F32))
        kinds.append(actions[pl.ds(step, 1), :].astype(F32))
        kinds.append((codes[pl.ds(step, 1), :] + ACTIONS).astype(F32))
    kinds.append(jnp.zeros((8 - len(kinds), rows), F32))
    columns = jnp.concatenate(kinds, axis=0).T

    def heads(tower, live_row, at_step, put):
        latent = past0 if tower == 0 else past1
        stack, logits, cot, acc = (
            (heads0, logits0, cot0, acc0) if tower == 0 else (heads1, logits1, cot1, acc1)
        )
        pick = lambda kind: pair_row(kind, at_step)
        value_goal = pair_row(value_bins, at_step, (tower,))
        spans = [(0, wide, 0, s.bins, value_goal)]
        if tower == 1:
            spans.append((wide, wide, 0, s.bins, pick(reward_bins)))
            spans.append((2 * wide, s.held, 0, ACTIONS, pick(policy)))
        else:
            spans.append((wide, s.held, ACTIONS, s.table_rows, pick(codes) + ACTIONS))

        def make_logits():
            logits[...] = by_lanes(stack[0 : logits.shape[0], :], latent[...])

        def eight_rows(value):
            return value.reshape(-1, 8, pair * rows)

        def mask(at, length, first, last):
            for start in range(0, length, 8):
                if start < first or start + 8 > last:
                    inside = (eights >= first - start) & (eights < last - start)
                    place = slice(at + start, at + start + 8)
                    logits[place, :] = jnp.where(inside, logits[place, :], very_negative)

        def find_top(at, start, stop, kept):
            top = jnp.max(eight_rows(logits[at + start : at + stop, :]), axis=0)
            kept["top"] = jnp.maximum(kept["top"], top) if "top" in kept else top

        def end_top(kept):
            kept["top"] = jnp.max(kept["top"], axis=0, keepdims=True)

        def make_terms(at, start, stop, goal, kept):
            place = slice(at + start, at + stop)
            value = logits[place, :]
            spot = lax.broadcasted_iota(jnp.int32, value.shape, 0)
            term = jnp.exp(value - kept["top"])
            logits[place, :] = term
            hit = spot == goal - start
            total = jnp.sum(eight_rows(term), axis=0)
            picked = jnp.sum(eight_rows(jnp.where(hit, value, 0.0)), axis=0)
            kept["total"] = kept["total"] + total if "total" in kept else total
            kept["picked"] = kept["picked"] + picked if "picked" in kept else picked

        def end_terms(kept):
            total = jnp.sum(kept["total"], axis=0, keepdims=True)
            picked = jnp.sum(kept["picked"], axis=0, keepdims=True)
            kept["scale"] = live_row / total
            row_loss = live_row * (jnp.log(total) + kept["top"] - picked)
            for offset in range(pair):
                loss[0:1, :] += row_loss[:, offset * rows : (offset + 1) * rows]

        def make_cotangent(at, start, stop, goal, kept):
            place = slice(at + start, at + stop)
            term = logits[place, :]
            spot = lax.broadcasted_iota(jnp.int32, term.shape, 0)
            hit = spot == goal - start
            cot[place, :] = (term * kept["scale"] - jnp.where(hit, live_row, 0.0)).astype(BF16)

        def make_grads():
            acc[...] += natural(cot[0 : acc.shape[0], :], latent[...])

        def make_latent():
            d_latent = by_rows(cot[...], stack[...])
            for offset in range(pair):
                put[offset, tower] = d_latent[offset * rows : (offset + 1) * rows]

        pieces = [make_logits]
        for at, length, first, last, goal in spans:
            kept = {}
            each = cuts(length)
            pieces.append(functools.partial(mask, at, length, first, last))
            pieces += [functools.partial(find_top, at, *cut, kept) for cut in each]
            pieces.append(functools.partial(end_top, kept))
            pieces += [functools.partial(make_terms, at, *cut, goal, kept) for cut in each]
            pieces.append(functools.partial(end_terms, kept))
            pieces += [functools.partial(make_cotangent, at, *cut, goal, kept) for cut in each]
        return pieces + [make_latent, make_grads]

    def tower_call(offset, tower, x_in, done):
        kept = {}
        parts = {}

        def group_rows(group):
            size = rows // GROUPS
            return slice(group * size, (group + 1) * size)

        def columns_of(group):
            some = group_rows(group)
            live = columns[some, 3 * offset : 3 * offset + 1]
            return live, columns[some, 3 * offset + 1 + tower : 3 * offset + 2 + tower]

        def begin(group):
            some = group_rows(group)
            live, code = columns_of(group)
            spot = lax.broadcasted_iota(jnp.int32, (rows // GROUPS, table.shape[0]), 1)
            onehot = jnp.where(spot.astype(F32) == code, 1.0, 0.0).astype(BF16)
            kept[group] = x_in(group).astype(F32) + natural(onehot, table[...])

        def scale_rows(group):
            row_squares = lane_sum(kept[group] * kept[group])
            return row_squares, lax.rsqrt(row_squares * (1.0 / width) + epsilon)

        def add_up(name, group, value):
            parts[name] = value if group == 0 else parts[name] + value
            return parts[name] if group == GROUPS - 1 else None

        def keep_squares(group, block, row_squares):
            live, _ = columns_of(group)
            place = 2 * (tower * s.blocks + block)
            total = jnp.sum(live * row_squares, axis=0, keepdims=True) * (1.0 / LANES)
            total = add_up("stream", group, total)
            if total is not None:
                squares[offset, place : place + 1, 0:LANES] = jnp.broadcast_to(total, (1, LANES))

        def into(block, group):
            some = group_rows(group)
            place = tower * s.blocks + block
            gained = kept[group] * gains[tower, block : block + 1, :]
            product = natural(gained.astype(BF16), weights[place])
            row_squares, inv_scale = scale_rows(group)
            kept["u", group] = product * inv_scale
            entry[offset, place, some] = (gained * inv_scale).astype(BF16)
            side[offset, place, some] = jnp.broadcast_to(inv_scale, (rows // GROUPS, LANES))
            if block > 0:
                keep_squares(group, block - 1, row_squares)

        def out_of(block, group):
            some = group_rows(group)
            live, _ = columns_of(group)
            place = tower * s.blocks + block
            u = kept["u", group]
            gate = 0.5 * jnp.tanh(0.5 * u) + 0.5
            after_rows = (u * gate).astype(BF16)
            branch = natural(after_rows, weights[s.calls + place])
            kept[group] = kept[group] + branch
            after[offset, place, some] = after_rows
            slope[offset, place, some] = gate * (1.0 + u * (1.0 - gate))
            spot = 2 * place + 1
            total = add_up(
                "branch", group, jnp.sum(branch * branch * live, axis=0, keepdims=True)
            )
            if total is not None:
                squares[offset, spot : spot + 1, :] = total

        def finish(group):
            some = group_rows(group)
            live, _ = columns_of(group)
            row_squares, inv_scale = scale_rows(group)
            side[offset, s.calls + tower, some] = jnp.broadcast_to(
                inv_scale, (rows // GROUPS, LANES)
            )
            latent = (kept[group] * inv_scale).astype(BF16)
            lat[offset, tower, some] = latent
            keep_squares(group, s.blocks - 1, row_squares)
            if tower == 0:
                total = jnp.sum(live, axis=0, keepdims=True) * (1.0 / LANES)
                total = add_up("count", group, total)
                if total is not None:
                    squares[offset, s.kinds : s.kinds + 1, 0:LANES] = jnp.broadcast_to(
                        total, (1, LANES)
                    )
            done(group, latent)

        each = range(GROUPS)
        pieces = [functools.partial(begin, group) for group in each]
        for block in range(s.blocks):
            pieces += [functools.partial(into, block, group) for group in each]
            pieces += [functools.partial(out_of, block, group) for group in each]
        return pieces + [functools.partial(finish, group) for group in each]

    size = rows // GROUPS
    found = {
        (1, -1, group): state[group * size : (group + 1) * size, :] for group in range(GROUPS)
    }

    def get_latent(offset, tower, group):
        return found[tower, offset, group]

    def put_latent(offset, tower, group, value):
        found[tower, offset, group] = value

    chain = []
    for offset in range(pair):
        for tower in range(2):
            source = (offset, 0) if tower == 1 else (offset - 1, 1)
            chain += tower_call(
                offset,
                tower,
                functools.partial(get_latent, *source),
                functools.partial(put_latent, offset, tower),
            )

    turns = -(-2 * s.calls // (s.steps // pair))

    def turn_weights(which):
        matrix = jnp.minimum(turn * turns + which, 2 * s.calls - 1)
        turned[matrix] = weights[matrix].T

    live_before = jnp.where(turn > 0, live_rows(before), 0.0)
    weave(
        chain,
        heads(1, live_before, before, dlat)
        + heads(0, live_before, before, dlat)
        + [functools.partial(turn_weights, which) for which in range(turns)],
    )
    first = tower_id == 0
    at_lane = lax.broadcasted_iota(jnp.int32, sums.shape, 1)
    for offset in range(pair):
        for group in range(GROUPS):
            some = slice(group * size, (group + 1) * size)
            at = slice(offset * rows + group * size, offset * rows + (group + 1) * size)
            after_state, next_state = found[0, offset, group], found[1, offset, group]
            past0[at, :] = after_state
            past1[at, :] = next_state
            lat_own[offset, some] = jnp.where(first, after_state, next_state)
            lat_away[offset, some] = jnp.where(first, next_state, after_state)
            if offset == pair - 1:
                state[some, :] = next_state
        total = lane_sum(squares[offset])
        sums[...] = jnp.where(at_lane == first_step + offset, total, sums[...])

    @pl.when(turn == pl.num_programs(0) - 1)
    def _():
        live_now = live_rows(first_step)
        weave(heads(1, live_now, first_step, dlast), heads(0, live_now, first_step, dlast))
        half = wide // 2
        head_grads[...] = jnp.zeros_like(head_grads)
        head_grads[0, 0:wide, :] = acc0[0:wide, :].astype(BF16)
        head_grads[1, 0:wide, :] = acc1[0:wide, :].astype(BF16)
        small = acc0[wide : wide + s.held, :] + acc1[2 * wide : 2 * wide + s.held, :]
        at = s.small_at - s.value_at
        head_grads[0, at : at + s.held, :] = small.astype(BF16)
        for tower in range(2):
            put = s.reward_at - s.value_at
            at = wide + tower * half
            head_grads[tower, put : put + half, :] = acc1[at : at + half, :].astype(BF16)
            head_grads[tower, wide : wide + sums.shape[0], 0:LANES] = sums[...].astype(BF16)


def backward_kernel(
    sizes, tower_ref,
    lat, entry, after, slope, side, dlat, dlast, code_rows, gains_in, turned, head_grads,
    own, away, root_own, root_away,
    carry, gain_sum, cond_sum, grads, gains, inverse_gains, d_after_kept, d_before_kept,
    d_hidden_kept,
):
    s = sizes
    pair = s.pair
    turn = pl.program_id(0)
    first_step = s.steps - pair * (turn + 1)
    tower_id = tower_ref[0]
    blocks, width = s.blocks, s.width

    @pl.when(turn == 0)
    def _():
        gains[...] = jnp.ones_like(gains)
        gains[:, 0:blocks, :] = gains_in[:, 0:blocks, :]
        inverse_gains[...] = 1.0 / gains[...]
        carry[...] = jnp.zeros_like(carry)
        grads[...] = jnp.zeros_like(grads)
        gain_sum[...] = jnp.zeros_like(gain_sum)
        cond_sum[...] = jnp.zeros_like(cond_sum)

    def over_lanes(column):
        return jnp.concatenate([column] * (width // LANES), axis=1)

    def stacked(parts):
        return jnp.concatenate(parts, axis=0)

    size = s.rows // GROUPS
    each = range(GROUPS)

    def add_grads(matrix, rows_of, place, kept, now):
        later = [kept[offset, place] for offset in range(1, pair)]
        grads[matrix // s.calls, matrix % s.calls] += by_rows(
            stacked([rows_of[offset, place] for offset in range(pair)]), stacked(now + later)
        )

    def tower_back(offset, tower, d_latents):
        flow = []
        for group in each:
            some = slice(group * size, (group + 1) * size)
            normed = lat[offset, tower, some]
            normed_wide = normed.astype(F32)
            inv_scale = over_lanes(side[offset, s.calls + tower, some])
            base = inv_scale * d_latents[group]
            slant = inv_scale * (lane_sum(d_latents[group] * normed_wide) * (1.0 / width))
            flow.append((base, slant, normed, normed_wide))
        for block in reversed(range(blocks)):
            place = tower * blocks + block
            gain = gains[tower, block : block + 1, :]
            inverse_gain = inverse_gains[tower, block : block + 1, :]
            first = []
            for base, slant, normed, normed_wide in flow:
                both = natural(
                    jnp.concatenate([normed, base.astype(BF16)], axis=0), turned[s.calls + place]
                )
                first.append((both[size:] - slant * both[:size], base - slant * normed_wide))
            d_branch, d_before, flow, gain_part = [], [], [], None
            for group, (d_after, d_hidden) in enumerate(first):
                some = slice(group * size, (group + 1) * size)
                entry_wide = entry[offset, place, some].astype(F32)
                inv_scale = over_lanes(side[offset, place, some])
                d_branch.append(d_hidden.astype(BF16))
                d_before.append((d_after * slope[offset, place, some]).astype(BF16))
                d_entry = natural(d_before[-1], turned[place])
                product = d_entry * entry_wide
                part = jnp.sum(product, axis=0, keepdims=True)
                gain_part = part if gain_part is None else gain_part + part
                base = d_hidden + inv_scale * (d_entry * gain)
                slant = inv_scale * (lane_sum(product) * (1.0 / width))
                normed_wide = entry_wide * inverse_gain
                flow.append((base, slant, normed_wide.astype(BF16), normed_wide))
            gain_sum[tower, block : block + 1, :] += gain_part
            if offset > 0:
                for group in each:
                    some = slice(group * size, (group + 1) * size)
                    d_after_kept[offset, place, some] = d_branch[group]
                    d_before_kept[offset, place, some] = d_before[group]
            else:
                matrix = tower * s.calls + block
                add_grads(matrix + blocks, after, place, d_after_kept, d_branch)
                add_grads(matrix, entry, place, d_before_kept, d_before)
        d_hidden = [base - slant * normed_wide for base, slant, _, normed_wide in flow]
        if offset > 0:
            for group in each:
                some = slice(group * size, (group + 1) * size)
                d_hidden_kept[offset, tower, some] = d_hidden[group].astype(BF16)
        else:
            code = jnp.concatenate(
                [code_rows[tower, pl.ds(first_step + step, 1), :] for step in range(pair)], axis=1
            )
            spots = lax.broadcasted_iota(jnp.int32, (cond_sum.shape[0], pair * s.rows), 0)
            onehot = jnp.where(spots == code, 1.0, 0.0).astype(BF16)
            parts = [part.astype(BF16) for part in d_hidden]
            parts += [d_hidden_kept[step, tower] for step in range(1, pair)]
            cond_sum[...] += natural(onehot, stacked(parts))
        return d_hidden

    def from_heads(offset, tower, group):
        some = slice(group * size, (group + 1) * size)
        return jnp.where(turn == 0, dlast[offset, tower, some], dlat[offset, tower, some])

    d_states = [carry[group * size : (group + 1) * size, :] for group in each]
    for offset in reversed(range(pair)):
        for tower in (1, 0):
            d_states = tower_back(
                offset,
                tower,
                [part + from_heads(offset, tower, group) for group, part in enumerate(d_states)],
            )
    d_state = stacked(d_states)
    carry[...] = d_state

    @pl.when(turn == pl.num_programs(0) - 1)
    def _():
        left = d_state[:, 0 : width // 2].astype(BF16)
        right = d_state[:, width // 2 : width].astype(BF16)
        root_own[...] = jnp.where(tower_id == 0, left, right)
        root_away[...] = jnp.where(tower_id == 0, right, left)
        gain_sum[...] = gain_sum[...] * inverse_gains[...]
        lines = lax.broadcasted_iota(jnp.int32, (s.reward_at - s.sums_at, width), 0)
        for target, which in ((own, tower_id), (away, 1 - tower_id)):
            for matrix in range(s.calls):
                at = matrix * width
                target[at : at + width, :] = grads[which, matrix].astype(BF16)
            target[s.value_at : s.cond_at, :] = head_grads[which]
            sums = head_grads[which, s.wide : s.wide + lines.shape[0], :].astype(F32)
            for block in range(blocks):
                gain = gain_sum[which, block : block + 1, :]
                sums = jnp.where(lines == s.gain_row + block, gain, sums)
            target[s.sums_at : s.reward_at, :] = sums.astype(BF16)
            here = jnp.where(which == 0, cond_sum[...], 0.0)
            target[s.cond_at : s.shared_end, :] = here.astype(BF16)
            if s.total > s.shared_end:
                target[s.shared_end :, :] = jnp.zeros((s.total - s.shared_end, width), BF16)


def logits_kernel(sizes, tower_ref, lat_own, lat_got, value_own, latents, logits):
    rows = sizes.rows
    tower_id = tower_ref[0]
    at_own = pl.ds(pl.multiple_of(tower_id * rows, rows), rows)
    at_got = pl.ds(pl.multiple_of((1 - tower_id) * rows, rows), rows)
    for offset in range(sizes.pair):
        latents[offset, at_own, :] = lat_own[offset]
        latents[offset, at_got, :] = lat_got[offset]
        logits[offset] = by_lanes(value_own[...], latents[offset]).astype(BF16)


def add_and_split_kernel(sizes, digits_ref, mine, got, *outputs):
    s = sizes
    start = 0
    for chunk, stop in enumerate((s.first_chunk, s.total)):
        digit = digits_ref[chunk]
        length = (stop - start) // s.factor
        for other in range(s.factor):
            at = pl.ds(pl.multiple_of(start + (digit ^ other) * length, 16), length)
            total = mine[at, :].astype(F32) + got[at, :].astype(F32)
            outputs[chunk * s.factor + other][...] = total.astype(BF16)
        start = stop


def unpack_own_kernel(sizes, scalars, *refs):
    s = sizes
    blocks_in = refs[: 2 * s.factor]
    tower_id = scalars[2]
    w_in, w_out, value, gain, rms, flat, held = refs[2 * s.factor :]
    width = s.width
    for place, source in enumerate(blocks_in):
        chunk, other = divmod(place, s.factor)
        length = source.shape[0]
        start = chunk * s.first_chunk
        at = pl.multiple_of(start + (scalars[chunk] ^ other) * length, 16)
        flat[pl.ds(at, length), :] = source[...]
    for block in range(s.blocks):
        at = block * width
        w_in[block] = flat[at : at + width, :].astype(F32)
        at = (s.blocks + block) * width
        w_out[block] = flat[at : at + width, :].astype(F32)
    value[:, 0, :] = flat[s.value_at : s.sums_at, :].astype(F32)[0 : s.bins]
    sums = flat[s.sums_at : s.reward_at, :].astype(F32)
    for block in range(s.blocks):
        gain[block] = sums[s.gain_row + block : s.gain_row + block + 1, :]
    held[...] = sums[:, 0:LANES]
    count = jnp.maximum(held[s.kinds : s.kinds + 1, 0 : s.steps], 1.0)
    for block in range(s.blocks):
        for kind in range(2):
            spot = tower_id * s.calls + 2 * block + kind
            square = held[pl.ds(spot, 1), 0 : s.steps]
            rms[block, kind : kind + 1, :] = jnp.sqrt(jnp.maximum(square, 0.0) / (count * width))


def unpack_shared_kernel(sizes, tower_ref, mine, got, reward, small, cond, joined):
    s = sizes
    tower_id = tower_ref[0]
    half = s.wide // 2
    joined[pl.ds(pl.multiple_of(tower_id * half, 8), half), :] = mine[0:half, :].astype(F32)
    joined[pl.ds(pl.multiple_of((1 - tower_id) * half, 8), half), :] = got[0:half, :].astype(F32)
    reward[...] = joined[0 : s.bins, :]
    for target, at in ((small, s.small_at), (cond, s.cond_at)):
        rows = slice(at - s.reward_at, at - s.reward_at + s.held)
        target[...] = (mine[rows, :].astype(F32) + got[rows, :].astype(F32))[0 : s.table_rows]


def whole(shape):
    return pl.BlockSpec(shape, lambda step, tower: (0,) * len(shape))


def swap(value, axis, mask):
    pairs = [(source, source ^ mask) for source in range(lax.axis_size(axis))]
    return lax.ppermute(value, axis, pairs)


AXES = ("tower", "batch")


def exchange_rounds(batch_size):
    factors = round_factors(batch_size)
    rounds, stride = [], 1
    for factor in factors:
        rounds.append((factor, stride))
        stride *= factor
    turned = rounds[::-1] if len(set(factors)) == 1 else rounds
    return [
        [(one[0], (one[1], two[1])) for one, two in zip(rounds, second)]
        for second in (turned, rounds)
    ]


def swap_within(value, strides, other, batch_size):
    pairs = [
        (tower * batch_size + index, tower * batch_size + (index ^ (other * strides[tower])))
        for tower in range(2)
        for index in range(batch_size)
    ]
    return lax.ppermute(value, AXES, pairs)


def my_digit(factor, strides):
    stride = jnp.where(lax.axis_index("tower") == 0, strides[0], strides[1])
    return (lax.axis_index("batch") // stride) % factor


def add_kernel(counts, *refs):
    targets = refs[sum(counts) :]
    place = 0
    for count, target in zip(counts, targets):
        total = refs[place][...].astype(F32)
        for source in refs[place + 1 : place + count]:
            total = total + source[...].astype(F32)
        target[...] = total.astype(BF16)
        place += count


def add_up(chunks):
    return pl.pallas_call(
        functools.partial(add_kernel, [len(parts) for parts in chunks]),
        out_shape=[jax.ShapeDtypeStruct(parts[0].shape, BF16) for parts in chunks],
        compiler_params=pltpu.CompilerParams(vmem_limit_bytes=SMALL_LIMIT),
        name="add_up",
    )(*[part for parts in chunks for part in parts])


def exchange(sizes, own, got, rounds, batch_size, beside, given, last_kernel):
    s = sizes
    factor = s.factor
    lengths = (s.first_chunk // factor, (s.total - s.first_chunk) // factor)
    digits = jnp.stack([my_digit(factor, steps[0][1]) for steps in rounds]).astype(jnp.int32)
    split = pl.pallas_call(
        functools.partial(add_and_split_kernel, s),
        grid_spec=pltpu.PrefetchScalarGridSpec(
            num_scalar_prefetch=1,
            grid=(1,),
            in_specs=[whole(own.shape)] * 2,
            out_specs=[whole((length, s.width)) for length in lengths for _ in range(factor)],
        ),
        out_shape=[
            (jax.ShapeDtypeStruct if other == 0 else pltpu.HBM)((length, s.width), BF16)
            for length in lengths
            for other in range(factor)
        ],
        compiler_params=pltpu.CompilerParams(vmem_limit_bytes=SMALL_LIMIT),
        name="add_and_split",
    )(digits, own, got)
    chunks = [split[:factor], split[factor:]]

    def outer(blocks, chunk):
        _, strides = rounds[chunk][0]
        return [
            swap_within(blocks[other], strides, other, batch_size) for other in range(1, factor)
        ]

    chunks = [[blocks[0]] + outer(blocks, chunk) for chunk, blocks in enumerate(chunks)]
    sums = add_up(chunks)
    done = None
    for place in range(1, len(rounds[0])):
        bit = 1
        while bit < rounds[0][place][0]:
            if done is None:
                sums, given = lax.optimization_barrier((sums, given))
            held = [
                [block, swap_within(block, rounds[chunk][place][1], bit, batch_size)]
                for chunk, block in enumerate(sums)
            ]
            if done is None:
                done = beside(given)
                held, done = lax.optimization_barrier((held, done))
            sums = add_up(held)
            bit *= 2
    if done is None:
        done = beside(given)
    held = [[block] + outer([block] * factor, chunk) for chunk, block in enumerate(sums)]
    return last_kernel(digits, held), done


def body(
    root_state, cond_table, block_gain, w_in, w_out, value_head, reward_head, small_head,
    unroll_len, actions, codes, policy_target, value_bins, reward_bins,
):
    tower_id = lax.axis_index("tower")
    other_id = 1 - tower_id
    tower_ref = tower_id.astype(jnp.int32)[None]
    steps, batch_rows = actions.shape
    blocks, width = block_gain.shape[1:]
    bins = value_head.shape[2]
    table_rows = cond_table.shape[0]
    rows = batch_rows // 2
    half = width // 2
    parts = lax.axis_size("batch")
    s = Sizes(steps, rows, blocks, width, bins, table_rows, parts)
    calls, wide, pair = s.calls, s.wide, s.pair

    root_got = swap(root_state, "tower", 1)
    in_own, out_own, gains_own = w_in[0], w_out[0], block_gain[0]
    value_own = value_head[0].T
    in_got = swap(in_own, "tower", 1)
    out_got = swap(out_own, "tower", 1)
    gains_got = swap(gains_own, "tower", 1)
    value_got = swap(value_own, "tower", 1)
    lengths = unroll_len.reshape(1, batch_rows)

    shape = jax.ShapeDtypeStruct
    per_pair = lambda *tail: pl.BlockSpec(
        (pair,) + tail, lambda turn, tower: (turn,) + (0,) * len(tail)
    )
    forward_params = pltpu.CompilerParams(vmem_limit_bytes=FORWARD_LIMIT)
    backward_params = pltpu.CompilerParams(vmem_limit_bytes=BACKWARD_LIMIT)
    small_params = pltpu.CompilerParams(vmem_limit_bytes=SMALL_LIMIT)
    products = steps * rows * (4 * blocks * width * width + 9 * width * wide)
    cost = pl.CostEstimate(flops=2 * products, bytes_accessed=40 * 2**20, transcendentals=0)
    (
        lat, lat_own, lat_away, entry, after, slope, side, dlat, dlast, loss, head_grads,
        turned, code_rows, gains,
    ) = pl.pallas_call(
        functools.partial(forward_kernel, s),
        grid_spec=pltpu.PrefetchScalarGridSpec(
            num_scalar_prefetch=1,
            grid=(steps // pair,),
            in_specs=[pl.BlockSpec(memory_space=pltpu.HBM)] * 14
            + [
                pl.BlockSpec((rows, half), lambda step, tower: (tower[0], 0)),
                whole((blocks, width)),
                whole((blocks, width, width)),
                whole((blocks, width, width)),
                whole((bins, width)),
            ],
            out_specs=[
                per_pair(2, rows, width),
                per_pair(rows, width),
                per_pair(rows, width),
                per_pair(calls, rows, width),
                per_pair(calls, rows, width),
                per_pair(calls, rows, width),
                per_pair(calls + 2, rows, LANES),
                pl.BlockSpec(
                    (pair, 2, rows, width), lambda turn, tower: (jnp.maximum(turn - 1, 0), 0, 0, 0)
                ),
                whole((pair, 2, rows, width)),
                whole((8, rows)),
                whole((2, s.head_rows, width)),
                whole((2 * calls, width, width)),
                whole((2, steps, rows)),
                whole((2, 8, width)),
            ],
            scratch_shapes=[
                pltpu.VMEM((rows, half), BF16),
                pltpu.VMEM((1, rows), jnp.int32),
                pltpu.VMEM((steps, rows), jnp.int32),
                pltpu.VMEM((steps, rows), jnp.int32),
                pltpu.VMEM((steps, rows), jnp.int32),
                pltpu.VMEM((steps, 2, rows), jnp.int32),
                pltpu.VMEM((steps, rows), jnp.int32),
                pltpu.VMEM((table_rows, width), BF16),
                pltpu.VMEM((blocks, width), BF16),
                pltpu.VMEM((blocks, width, width), BF16),
                pltpu.VMEM((blocks, width, width), BF16),
                pltpu.VMEM((bins, width), BF16),
                pltpu.VMEM((bins, width), BF16),
                pltpu.VMEM((table_rows, width), BF16),
                pltpu.SemaphoreType.DMA((14,)),
                pltpu.VMEM((rows, width), BF16),
                pltpu.VMEM((pair * rows, width), BF16),
                pltpu.VMEM((pair * rows, width), BF16),
                pltpu.VMEM((LANES, width), BF16),
                pltpu.VMEM((2 * calls, width, width), BF16),
                pltpu.VMEM((s.depth[0], width), BF16),
                pltpu.VMEM((s.depth[1], width), BF16),
                pltpu.VMEM((s.stack[0], width), F32),
                pltpu.VMEM((s.stack[1], width), F32),
                pltpu.VMEM((s.stack[0], pair * rows), F32),
                pltpu.VMEM((s.stack[1], pair * rows), F32),
                pltpu.VMEM((s.depth[0], pair * rows), BF16),
                pltpu.VMEM((s.depth[1], pair * rows), BF16),
                pltpu.VMEM((s.reward_at - s.sums_at, LANES), F32),
                pltpu.VMEM((pair, s.reward_at - s.sums_at, width), F32),
            ],
        ),
        out_shape=[
            shape((steps, 2, rows, width), BF16),
            pltpu.HBM((steps, rows, width), BF16),
            pltpu.HBM((steps, rows, width), BF16),
            shape((steps, calls, rows, width), BF16),
            shape((steps, calls, rows, width), BF16),
            shape((steps, calls, rows, width), F32),
            shape((steps, calls + 2, rows, LANES), F32),
            shape((steps - pair, 2, rows, width), F32),
            shape((pair, 2, rows, width), F32),
            shape((8, rows), F32),
            shape((2, s.head_rows, width), BF16),
            shape((2 * calls, width, width), BF16),
            shape((2, steps, rows), jnp.int32),
            shape((2, 8, width), F32),
        ],
        compiler_params=forward_params,
        cost_estimate=cost,
        name="unroll_forward",
    )(
        tower_ref,
        *[
            pltpu.with_memory_space_constraint(value, pltpu.HBM)
            for value in (
                root_state, lengths, actions, codes, policy_target,
                jnp.swapaxes(value_bins, 0, 1), reward_bins, cond_table, gains_own,
                in_own, out_own, value_own, reward_head.T, small_head.T,
            )
        ],
        root_got, gains_got, in_got, out_got, value_got,
    )

    turns = steps // pair
    descending = lambda *tail: pl.BlockSpec(
        (pair,) + tail, lambda turn, tower: (turns - 1 - turn,) + (0,) * len(tail)
    )
    own, away, root_own, root_away = pl.pallas_call(
        functools.partial(backward_kernel, s),
        grid_spec=pltpu.PrefetchScalarGridSpec(
            num_scalar_prefetch=1,
            grid=(turns,),
            in_specs=[
                descending(2, rows, width),
                descending(calls, rows, width),
                descending(calls, rows, width),
                descending(calls, rows, width),
                descending(calls + 2, rows, LANES),
                pl.BlockSpec(
                    (pair, 2, rows, width),
                    lambda turn, tower: (jnp.minimum(turns - 1 - turn, turns - 2), 0, 0, 0),
                ),
                whole((pair, 2, rows, width)),
                whole((2, steps, rows)),
                whole((2, 8, width)),
                whole((2 * calls, width, width)),
                whole((2, s.head_rows, width)),
            ],
            out_specs=[
                whole((s.total, width)),
                whole((s.total, width)),
                whole((rows, half)),
                whole((rows, half)),
            ],
            scratch_shapes=[
                pltpu.VMEM((rows, width), F32),
                pltpu.VMEM((2, 16, width), F32),
                pltpu.VMEM((s.held, width), F32),
                pltpu.VMEM((2, calls, width, width), F32),
                pltpu.VMEM((2, 16, width), F32),
                pltpu.VMEM((2, 16, width), F32),
                pltpu.VMEM((pair, calls, rows, width), BF16),
                pltpu.VMEM((pair, calls, rows, width), BF16),
                pltpu.VMEM((pair, 2, rows, width), BF16),
            ],
        ),
        out_shape=[
            shape((s.total, width), BF16),
            shape((s.total, width), BF16),
            shape((rows, half), BF16),
            shape((rows, half), BF16),
        ],
        compiler_params=backward_params,
        cost_estimate=cost,
        name="unroll_backward",
    )(
        tower_ref, lat, entry, after, slope, side, dlat, dlast, code_rows, gains,
        turned, head_grads,
    )
    got = swap(away, "tower", 1)

    def beside(given):
        lat_own, lat_away, loss, root_own, root_away = given
        lat_got = swap(lat_away, "tower", 1)
        loss_own = loss[0]
        loss_got = swap(loss_own, "tower", 1)
        root_got = swap(root_away, "tower", 1)

        latents, logits = pl.pallas_call(
            functools.partial(logits_kernel, s),
            grid_spec=pltpu.PrefetchScalarGridSpec(
                num_scalar_prefetch=1,
                grid=(steps // pair,),
                in_specs=[per_pair(rows, width), per_pair(rows, width), whole((bins, width))],
                out_specs=[per_pair(batch_rows, width), per_pair(bins, batch_rows)],
            ),
            out_shape=[
                shape((steps, batch_rows, width), BF16),
                shape((steps, bins, batch_rows), BF16),
            ],
            compiler_params=small_params,
            cost_estimate=pl.CostEstimate(
                flops=2 * steps * batch_rows * width * wide, bytes_accessed=6 * 2**20, transcendentals=0
            ),
            name="latents_and_logits",
        )(
            tower_ref,
            *[
                pltpu.with_memory_space_constraint(part, pltpu.HBM)
                for part in (lat_own, lat_got, value_own)
            ],
        )

        def in_order(mine_value, got_value, axis):
            return jnp.where(
                tower_id == 0,
                jnp.concatenate([mine_value, got_value], axis=axis),
                jnp.concatenate([got_value, mine_value], axis=axis),
            )

        row_loss = in_order(loss_own, loss_got, 0)
        grad_root = in_order(root_own, root_got, 0).astype(F32)
        return latents, logits, row_loss, grad_root

    rounds = exchange_rounds(parts)

    def unpack(digits, held):
        scalars = jnp.concatenate([digits, tower_ref])
        length = held[1][0].shape[0]
        start = s.reward_at - s.first_chunk
        stop = s.shared_end - s.first_chunk
        covered = []
        for block in range(start // length, -(-stop // length)):
            chosen = held[1][0]
            for other in range(1, s.factor):
                chosen = jnp.where((digits[1] ^ other) == block, held[1][other], chosen)
            covered.append(chosen)
        at = start - start // length * length
        shared = jnp.concatenate(covered, axis=0)[at : at + stop - start]
        shared_got = swap(shared, "tower", 1)
        held = held[0] + held[1]
        return (shared, shared_got), pl.pallas_call(
            functools.partial(unpack_own_kernel, s),
            grid_spec=pltpu.PrefetchScalarGridSpec(
                num_scalar_prefetch=1,
                grid=(1,),
                in_specs=[whole(part.shape) for part in held],
                out_specs=[
                    whole((blocks, width, width)),
                    whole((blocks, width, width)),
                    whole((bins, 1, width)),
                    whole((blocks, 1, width)),
                    whole((blocks, 2, steps)),
                ],
                scratch_shapes=[
                    pltpu.VMEM((s.total, width), BF16),
                    pltpu.VMEM((s.reward_at - s.sums_at, LANES), F32),
                ],
            ),
            out_shape=[
                shape((blocks, width, width), F32),
                shape((blocks, width, width), F32),
                shape((bins, 1, width), F32),
                shape((blocks, 1, width), F32),
                shape((blocks, 2, steps), F32),
            ],
            compiler_params=small_params,
            name="unpack_own",
        )(scalars, *held)

    given = (lat_own, lat_away, loss, root_own, root_away)
    unpacked, done = exchange(s, own, got, rounds, parts, beside, given, unpack)
    (shared, shared_got), (grad_in, grad_out, value_t, gain_t, rms_t) = unpacked
    latents, logits, row_loss, grad_root = done
    reward_t, small_t, grad_cond = pl.pallas_call(
        functools.partial(unpack_shared_kernel, s),
        grid_spec=pltpu.PrefetchScalarGridSpec(
            num_scalar_prefetch=1,
            grid=(1,),
            in_specs=[whole(shared.shape), whole(shared.shape)],
            out_specs=[
                whole((bins, width)),
                whole((table_rows, width)),
                whole((table_rows, width)),
            ],
            scratch_shapes=[pltpu.VMEM((s.wide, width), F32)],
        ),
        out_shape=[
            shape((bins, width), F32),
            shape((table_rows, width), F32),
            shape((table_rows, width), F32),
        ],
        compiler_params=small_params,
        name="unpack_shared",
    )(tower_ref, shared, shared_got)
    layer_rms = jnp.transpose(rms_t, (2, 0, 1))[None]
    return (
        latents[None],
        jnp.swapaxes(logits, 1, 2)[None],
        row_loss,
        layer_rms,
        grad_root,
        grad_cond,
        jnp.swapaxes(gain_t, 0, 1),
        grad_in[None],
        grad_out[None],
        jnp.transpose(value_t, (1, 2, 0)),
        reward_t.T,
        small_t.T,
    )


def solution(mesh):
    placed = (
        P("batch", "tower"),
        P(),
        P("tower", None, None),
        P("tower", None, None, None),
        P("tower", None, None, None),
        P("tower", None, None),
        P(),
        P(),
        P("batch"),
        P(None, "batch"),
        P(None, "batch"),
        P(None, "batch"),
        P(None, None, "batch"),
        P(None, "batch"),
    )
    return jax.shard_map(
        body,
        mesh=mesh,
        in_specs=placed,
        out_specs=(
            P("tower", None, "batch", None),
            P("tower", None, "batch", None),
            P("batch"),
            P("tower", None, None, None),
            P("batch", "tower"),
            P(),
            P("tower", None, None),
            P("tower", None, None, None),
            P("tower", None, None, None),
            P("tower", None, None),
            P(),
            P(),
        ),
        check_vma=False,
    )
```

```python
import functools

import jax
import jax.numpy as jnp
from jax import lax
from jax.experimental import pallas as pl
from jax.experimental.pallas import tpu as pltpu
from jax.sharding import PartitionSpec as P

ACTIONS = 4
LANES = 128
MIB = 1024 * 1024
GROUPS = 1
FORWARD_LIMIT = 20 * MIB
BACKWARD_LIMIT = 20 * MIB
SMALL_LIMIT = 12 * MIB
epsilon = 1e-06
very_negative = -1e30
F32 = jnp.float32
BF16 = jnp.bfloat16


def natural(left, right):
    return lax.dot_general(left, right, (((1,), (0,)), ((), ())), preferred_element_type=F32)


def by_rows(left, right):
    return lax.dot_general(left, right, (((0,), (0,)), ((), ())), preferred_element_type=F32)


def by_lanes(left, right):
    return lax.dot_general(left, right, (((1,), (1,)), ((), ())), preferred_element_type=F32)


def round_up(value, unit):
    return (value + unit - 1) // unit * unit


def lane_sum(value):
    return jnp.sum(value, axis=-1, keepdims=True)


def inverse_rms(hidden):
    return lax.rsqrt(lane_sum(hidden * hidden) * (1.0 / hidden.shape[-1]) + epsilon)


def alternate(one, two):
    merged, taken = [], 0
    for place, item in enumerate(one):
        merged.append(item)
        until = (place + 1) * len(two) // len(one)
        merged += two[taken:until]
        taken = until
    return merged


def weave(*tasks):
    tasks = [(list(task)) for task in tasks]
    longest = max(len(task) for task in tasks)
    done = [0] * len(tasks)
    for turn in range(longest):
        for which, task in enumerate(tasks):
            until = (turn + 1) * len(task) // longest
            while done[which] < until:
                task[done[which]]()
                done[which] += 1


def cuts(length, unit=64):
    return [(start, min(start + unit, length)) for start in range(0, length, unit)]


class Sizes:
    def __init__(self, steps, rows, blocks, width, bins, table_rows, parts):
        self.steps, self.rows, self.blocks, self.width = steps, rows, blocks, width
        self.bins, self.table_rows, self.parts = bins, table_rows, parts
        self.calls = 2 * blocks
        self.pair = 2 if steps % 2 == 0 else 1
        self.wide = round_up(bins, 32)
        self.held = round_up(table_rows, 16)
        self.stack = (self.wide + self.held, 2 * self.wide + self.held)
        self.depth = tuple(round_up(rows_in, LANES) for rows_in in self.stack)
        half = self.wide // 2
        self.value_at = self.calls * width
        self.sums_at = self.value_at + self.wide
        self.kinds = 2 * self.calls
        self.gain_row = self.kinds + 1
        self.reward_at = self.sums_at + round_up(self.gain_row + blocks, 16)
        self.small_at = self.reward_at + half
        self.cond_at = self.small_at + self.held
        self.shared_end = self.cond_at + self.held
        self.total = round_up(self.shared_end, 16 * parts)
        self.head_rows = self.cond_at - self.value_at


def forward_kernel(
    sizes, tower_ref,
    root_hbm, lengths_hbm, actions_hbm, codes_hbm, policy_hbm, value_bins_hbm, reward_bins_hbm,
    table_hbm, gains_hbm, in_hbm, out_hbm, value_hbm, reward_hbm, small_hbm,
    root_any, in_got, out_got, value_any, gains_got,
    lat, lat_own, lat_away, entry, after, slope, side, dlat, dlast, loss, head_grads, turned, code_rows, gains,
    root_own, root_got, lengths, actions, codes, policy, value_bins, reward_bins,
    table_in, gains_own, value_own, value_got, reward_in, small_in, sems,
    state, past0, past1, table, weights, heads0, heads1, acc0, acc1,
    logits0, logits1, cot0, cot1, sums, squares,
):
    s = sizes
    pair = s.pair
    turn = pl.program_id(0)
    first_step = turn * pair
    tower_id = tower_ref[0]
    rows, width, wide = s.rows, s.width, s.wide

    @pl.when(turn == 0)
    def _():
        here = pl.ds(pl.multiple_of(tower_id * rows, rows), rows)

        def matrices(kind, tower):
            return weights.at[pl.ds(kind * s.calls + tower * s.blocks, s.blocks)]

        moves = [
            (in_hbm, matrices(0, tower_id)),
            (out_hbm, matrices(1, tower_id)),
            (in_got, matrices(0, 1 - tower_id)),
            (out_got, matrices(1, 1 - tower_id)),
            (value_hbm, value_own),
            (value_any, value_got),
            (reward_hbm, reward_in),
            (small_hbm, small_in),
            (table_hbm, table_in),
            (gains_hbm, gains_own),
            (root_hbm.at[here], root_own),
            (root_any.at[here], root_got),
            (actions_hbm.at[:, here], actions),
            (codes_hbm.at[:, here], codes),
            (lengths_hbm.at[:, here], lengths),
            (policy_hbm.at[:, here], policy),
            (value_bins_hbm.at[:, :, here], value_bins),
            (reward_bins_hbm.at[:, here], reward_bins),
        ]
        moves = [
            pltpu.make_async_copy(source, target, sems.at[place])
            for place, (source, target) in enumerate(moves)
        ]
        for move in moves:
            move.start()
        for target in (
            gains, table, heads0, heads1, past0, past1, cot0, cot1, acc0, acc1, sums, squares, loss
        ):
            target[...] = jnp.zeros_like(target)
        for move in moves:
            move.wait()
        first = tower_id == 0
        code_rows[0] = actions[...]
        code_rows[1] = codes[...] + ACTIONS
        state[:, 0 : width // 2] = jnp.where(first, root_own[...], root_got[...])
        state[:, width // 2 : width] = jnp.where(first, root_got[...], root_own[...])
        gains[tower_id, 0 : s.blocks, :] = gains_own[...].astype(F32)
        gains[1 - tower_id, 0 : s.blocks, :] = gains_got[...].astype(F32)
        table[0 : s.table_rows, :] = table_in[...]
        heads0[0 : s.bins, :] = jnp.where(first, value_own[...], value_got[...])
        heads1[0 : s.bins, :] = jnp.where(first, value_got[...], value_own[...])
        heads1[wide : wide + s.bins, :] = reward_in[...]
        heads0[wide : wide + s.table_rows, :] = small_in[...]
        heads1[2 * wide : 2 * wide + s.table_rows, :] = small_in[...]

    eights = lax.broadcasted_iota(jnp.int32, (8, pair * rows), 0)
    before = jnp.maximum(first_step - pair, 0)

    def pair_row(kind, at_step, lead=()):
        return jnp.concatenate(
            [kind[(pl.ds(at_step + offset, 1),) + lead] for offset in range(pair)], axis=1
        )

    def live_rows(at_step):
        return jnp.concatenate(
            [(at_step + offset < lengths[...]).astype(F32) for offset in range(pair)], axis=1
        )

    kinds = []
    for offset in range(pair):
        step = first_step + offset
        kinds.append((step < lengths[...]).astype(F32))
        kinds.append(actions[pl.ds(step, 1), :].astype(F32))
        kinds.append((codes[pl.ds(step, 1), :] + ACTIONS).astype(F32))
    kinds.append(jnp.zeros((8 - len(kinds), rows), F32))
    columns = jnp.concatenate(kinds, axis=0).T

    def heads(tower, live_row, at_step, put):
        latent = past0 if tower == 0 else past1
        stack, logits, cot, acc = (
            (heads0, logits0, cot0, acc0) if tower == 0 else (heads1, logits1, cot1, acc1)
        )
        pick = lambda kind: pair_row(kind, at_step)
        value_goal = pair_row(value_bins, at_step, (tower,))
        spans = [(0, wide, 0, s.bins, value_goal)]
        if tower == 1:
            spans.append((wide, wide, 0, s.bins, pick(reward_bins)))
            spans.append((2 * wide, s.held, 0, ACTIONS, pick(policy)))
        else:
            spans.append((wide, s.held, ACTIONS, s.table_rows, pick(codes) + ACTIONS))

        def make_logits():
            logits[...] = by_lanes(stack[0 : logits.shape[0], :], latent[...])

        def eight_rows(value):
            return value.reshape(-1, 8, pair * rows)

        def mask(at, length, first, last):
            for start in range(0, length, 8):
                if start < first or start + 8 > last:
                    inside = (eights >= first - start) & (eights < last - start)
                    place = slice(at + start, at + start + 8)
                    logits[place, :] = jnp.where(inside, logits[place, :], very_negative)

        def find_top(at, start, stop, kept):
            top = jnp.max(eight_rows(logits[at + start : at + stop, :]), axis=0)
            kept["top"] = jnp.maximum(kept["top"], top) if "top" in kept else top

        def end_top(kept):
            kept["top"] = jnp.max(kept["top"], axis=0, keepdims=True)

        def make_terms(at, start, stop, goal, kept):
            place = slice(at + start, at + stop)
            value = logits[place, :]
            spot = lax.broadcasted_iota(jnp.int32, value.shape, 0)
            term = jnp.exp(value - kept["top"])
            logits[place, :] = term
            hit = spot == goal - start
            total = jnp.sum(eight_rows(term), axis=0)
            picked = jnp.sum(eight_rows(jnp.where(hit, value, 0.0)), axis=0)
            kept["total"] = kept["total"] + total if "total" in kept else total
            kept["picked"] = kept["picked"] + picked if "picked" in kept else picked

        def end_terms(kept):
            total = jnp.sum(kept["total"], axis=0, keepdims=True)
            picked = jnp.sum(kept["picked"], axis=0, keepdims=True)
            kept["scale"] = live_row / total
            row_loss = live_row * (jnp.log(total) + kept["top"] - picked)
            for offset in range(pair):
                loss[0:1, :] += row_loss[:, offset * rows : (offset + 1) * rows]

        def make_cotangent(at, start, stop, goal, kept):
            place = slice(at + start, at + stop)
            term = logits[place, :]
            spot = lax.broadcasted_iota(jnp.int32, term.shape, 0)
            hit = spot == goal - start
            cot[place, :] = (term * kept["scale"] - jnp.where(hit, live_row, 0.0)).astype(BF16)

        def make_grads():
            acc[...] += natural(cot[0 : acc.shape[0], :], latent[...])

        def make_latent():
            d_latent = by_rows(cot[...], stack[...])
            for offset in range(pair):
                put[offset, tower] = d_latent[offset * rows : (offset + 1) * rows]

        pieces = [make_logits]
        for at, length, first, last, goal in spans:
            kept = {}
            each = cuts(length)
            pieces.append(functools.partial(mask, at, length, first, last))
            pieces += [functools.partial(find_top, at, *cut, kept) for cut in each]
            pieces.append(functools.partial(end_top, kept))
            pieces += [functools.partial(make_terms, at, *cut, goal, kept) for cut in each]
            pieces.append(functools.partial(end_terms, kept))
            pieces += [functools.partial(make_cotangent, at, *cut, goal, kept) for cut in each]
        return pieces + [make_latent, make_grads]

    def tower_call(offset, tower, x_in, done):
        kept = {}
        parts = {}

        def group_rows(group):
            size = rows // GROUPS
            return slice(group * size, (group + 1) * size)

        def columns_of(group):
            some = group_rows(group)
            live = columns[some, 3 * offset : 3 * offset + 1]
            return live, columns[some, 3 * offset + 1 + tower : 3 * offset + 2 + tower]

        def begin(group):
            some = group_rows(group)
            live, code = columns_of(group)
            spot = lax.broadcasted_iota(jnp.int32, (rows // GROUPS, table.shape[0]), 1)
            onehot = jnp.where(spot.astype(F32) == code, 1.0, 0.0).astype(BF16)
            kept[group] = x_in(group).astype(F32) + natural(onehot, table[...])

        def scale_rows(group):
            row_squares = lane_sum(kept[group] * kept[group])
            return row_squares, lax.rsqrt(row_squares * (1.0 / width) + epsilon)

        def add_up(name, group, value):
            parts[name] = value if group == 0 else parts[name] + value
            return parts[name] if group == GROUPS - 1 else None

        def keep_squares(group, block, row_squares):
            live, _ = columns_of(group)
            place = 2 * (tower * s.blocks + block)
            total = jnp.sum(live * row_squares, axis=0, keepdims=True) * (1.0 / LANES)
            total = add_up("stream", group, total)
            if total is not None:
                squares[offset, place : place + 1, 0:LANES] = jnp.broadcast_to(total, (1, LANES))

        def into(block, group):
            some = group_rows(group)
            place = tower * s.blocks + block
            gained = kept[group] * gains[tower, block : block + 1, :]
            product = natural(gained.astype(BF16), weights[place])
            row_squares, inv_scale = scale_rows(group)
            kept["u", group] = product * inv_scale
            entry[offset, place, some] = (gained * inv_scale).astype(BF16)
            side[offset, place, some] = jnp.broadcast_to(inv_scale, (rows // GROUPS, LANES))
            if block > 0:
                keep_squares(group, block - 1, row_squares)

        def out_of(block, group):
            some = group_rows(group)
            live, _ = columns_of(group)
            place = tower * s.blocks + block
            u = kept["u", group]
            gate = 0.5 * jnp.tanh(0.5 * u) + 0.5
            after_rows = (u * gate).astype(BF16)
            branch = natural(after_rows, weights[s.calls + place])
            kept[group] = kept[group] + branch
            after[offset, place, some] = after_rows
            slope[offset, place, some] = gate * (1.0 + u * (1.0 - gate))
            spot = 2 * place + 1
            total = add_up(
                "branch", group, jnp.sum(branch * branch * live, axis=0, keepdims=True)
            )
            if total is not None:
                squares[offset, spot : spot + 1, :] = total

        def finish(group):
            some = group_rows(group)
            live, _ = columns_of(group)
            row_squares, inv_scale = scale_rows(group)
            side[offset, s.calls + tower, some] = jnp.broadcast_to(
                inv_scale, (rows // GROUPS, LANES)
            )
            latent = (kept[group] * inv_scale).astype(BF16)
            lat[offset, tower, some] = latent
            keep_squares(group, s.blocks - 1, row_squares)
            if tower == 0:
                total = jnp.sum(live, axis=0, keepdims=True) * (1.0 / LANES)
                total = add_up("count", group, total)
                if total is not None:
                    squares[offset, s.kinds : s.kinds + 1, 0:LANES] = jnp.broadcast_to(
                        total, (1, LANES)
                    )
            done(group, latent)

        each = range(GROUPS)
        pieces = [functools.partial(begin, group) for group in each]
        for block in range(s.blocks):
            pieces += [functools.partial(into, block, group) for group in each]
            pieces += [functools.partial(out_of, block, group) for group in each]
        return pieces + [functools.partial(finish, group) for group in each]

    size = rows // GROUPS
    found = {
        (1, -1, group): state[group * size : (group + 1) * size, :] for group in range(GROUPS)
    }

    def get_latent(offset, tower, group):
        return found[tower, offset, group]

    def put_latent(offset, tower, group, value):
        found[tower, offset, group] = value

    chain = []
    for offset in range(pair):
        for tower in range(2):
            source = (offset, 0) if tower == 1 else (offset - 1, 1)
            chain += tower_call(
                offset,
                tower,
                functools.partial(get_latent, *source),
                functools.partial(put_latent, offset, tower),
            )

    turns = -(-2 * s.calls // (s.steps // pair))

    def turn_weights(which):
        matrix = jnp.minimum(turn * turns + which, 2 * s.calls - 1)
        turned[matrix] = weights[matrix].T

    live_before = jnp.where(turn > 0, live_rows(before), 0.0)
    weave(
        chain,
        alternate(heads(1, live_before, before, dlat), heads(0, live_before, before, dlat))
        + [functools.partial(turn_weights, which) for which in range(turns)],
    )
    first = tower_id == 0
    at_lane = lax.broadcasted_iota(jnp.int32, sums.shape, 1)
    for offset in range(pair):
        for group in range(GROUPS):
            some = slice(group * size, (group + 1) * size)
            at = slice(offset * rows + group * size, offset * rows + (group + 1) * size)
            after_state, next_state = found[0, offset, group], found[1, offset, group]
            past0[at, :] = after_state
            past1[at, :] = next_state
            lat_own[offset, some] = jnp.where(first, after_state, next_state)
            lat_away[offset, some] = jnp.where(first, next_state, after_state)
            if offset == pair - 1:
                state[some, :] = next_state
        total = lane_sum(squares[offset])
        sums[...] = jnp.where(at_lane == first_step + offset, total, sums[...])

    @pl.when(turn == pl.num_programs(0) - 1)
    def _():
        live_now = live_rows(first_step)
        weave(heads(1, live_now, first_step, dlast), heads(0, live_now, first_step, dlast))
        half = wide // 2
        head_grads[...] = jnp.zeros_like(head_grads)
        head_grads[0, 0:wide, :] = acc0[0:wide, :].astype(BF16)
        head_grads[1, 0:wide, :] = acc1[0:wide, :].astype(BF16)
        small = acc0[wide : wide + s.held, :] + acc1[2 * wide : 2 * wide + s.held, :]
        at = s.small_at - s.value_at
        head_grads[0, at : at + s.held, :] = small.astype(BF16)
        for tower in range(2):
            put = s.reward_at - s.value_at
            at = wide + tower * half
            head_grads[tower, put : put + half, :] = acc1[at : at + half, :].astype(BF16)
            head_grads[tower, wide : wide + sums.shape[0], 0:LANES] = sums[...].astype(BF16)


def backward_kernel(
    sizes, tower_ref,
    lat, entry, after, slope, side, dlat, dlast, code_rows, gains_in, turned, head_grads,
    own, away, root_own, root_away,
    carry, gain_sum, cond_sum, grads, gains, inverse_gains, d_after_kept, d_before_kept,
    d_hidden_kept,
):
    s = sizes
    pair = s.pair
    turn = pl.program_id(0)
    first_step = s.steps - pair * (turn + 1)
    tower_id = tower_ref[0]
    blocks, width = s.blocks, s.width

    @pl.when(turn == 0)
    def _():
        gains[...] = jnp.ones_like(gains)
        gains[:, 0:blocks, :] = gains_in[:, 0:blocks, :]
        inverse_gains[...] = 1.0 / gains[...]
        carry[...] = jnp.zeros_like(carry)
        grads[...] = jnp.zeros_like(grads)
        gain_sum[...] = jnp.zeros_like(gain_sum)
        cond_sum[...] = jnp.zeros_like(cond_sum)

    def over_lanes(column):
        return jnp.concatenate([column] * (width // LANES), axis=1)

    def stacked(parts):
        return jnp.concatenate(parts, axis=0)

    size = s.rows // GROUPS
    each = range(GROUPS)

    def add_grads(matrix, rows_of, place, kept, now):
        later = [kept[offset, place] for offset in range(1, pair)]
        grads[matrix // s.calls, matrix % s.calls] += by_rows(
            stacked([rows_of[offset, place] for offset in range(pair)]), stacked(now + later)
        )

    def tower_back(offset, tower, d_latents):
        flow = []
        for group in each:
            some = slice(group * size, (group + 1) * size)
            normed = lat[offset, tower, some]
            normed_wide = normed.astype(F32)
            inv_scale = over_lanes(side[offset, s.calls + tower, some])
            base = inv_scale * d_latents[group]
            slant = inv_scale * (lane_sum(d_latents[group] * normed_wide) * (1.0 / width))
            flow.append((base, slant, normed, normed_wide))
        for block in reversed(range(blocks)):
            place = tower * blocks + block
            gain = gains[tower, block : block + 1, :]
            inverse_gain = inverse_gains[tower, block : block + 1, :]
            first = []
            for base, slant, normed, normed_wide in flow:
                both = natural(
                    jnp.concatenate([normed, base.astype(BF16)], axis=0), turned[s.calls + place]
                )
                first.append((both[size:] - slant * both[:size], base - slant * normed_wide))
            d_branch, d_before, flow, gain_part = [], [], [], None
            for group, (d_after, d_hidden) in enumerate(first):
                some = slice(group * size, (group + 1) * size)
                entry_wide = entry[offset, place, some].astype(F32)
                inv_scale = over_lanes(side[offset, place, some])
                d_branch.append(d_hidden.astype(BF16))
                d_before.append((d_after * slope[offset, place, some]).astype(BF16))
                d_entry = natural(d_before[-1], turned[place])
                product = d_entry * entry_wide
                part = jnp.sum(product, axis=0, keepdims=True)
                gain_part = part if gain_part is None else gain_part + part
                base = d_hidden + inv_scale * (d_entry * gain)
                slant = inv_scale * (lane_sum(product) * (1.0 / width))
                normed_wide = entry_wide * inverse_gain
                flow.append((base, slant, normed_wide.astype(BF16), normed_wide))
            gain_sum[tower, block : block + 1, :] += gain_part
            if offset > 0:
                for group in each:
                    some = slice(group * size, (group + 1) * size)
                    d_after_kept[offset, place, some] = d_branch[group]
                    d_before_kept[offset, place, some] = d_before[group]
            else:
                matrix = tower * s.calls + block
                add_grads(matrix + blocks, after, place, d_after_kept, d_branch)
                add_grads(matrix, entry, place, d_before_kept, d_before)
        d_hidden = [base - slant * normed_wide for base, slant, _, normed_wide in flow]
        if offset > 0:
            for group in each:
                some = slice(group * size, (group + 1) * size)
                d_hidden_kept[offset, tower, some] = d_hidden[group].astype(BF16)
        else:
            code = jnp.concatenate(
                [code_rows[tower, pl.ds(first_step + step, 1), :] for step in range(pair)], axis=1
            )
            spots = lax.broadcasted_iota(jnp.int32, (cond_sum.shape[0], pair * s.rows), 0)
            onehot = jnp.where(spots == code, 1.0, 0.0).astype(BF16)
            parts = [part.astype(BF16) for part in d_hidden]
            parts += [d_hidden_kept[step, tower] for step in range(1, pair)]
            cond_sum[...] += natural(onehot, stacked(parts))
        return d_hidden

    def from_heads(offset, tower, group):
        some = slice(group * size, (group + 1) * size)
        return jnp.where(turn == 0, dlast[offset, tower, some], dlat[offset, tower, some])

    d_states = [carry[group * size : (group + 1) * size, :] for group in each]
    for offset in reversed(range(pair)):
        for tower in (1, 0):
            d_states = tower_back(
                offset,
                tower,
                [part + from_heads(offset, tower, group) for group, part in enumerate(d_states)],
            )
    d_state = stacked(d_states)
    carry[...] = d_state

    @pl.when(turn == pl.num_programs(0) - 1)
    def _():
        left = d_state[:, 0 : width // 2].astype(BF16)
        right = d_state[:, width // 2 : width].astype(BF16)
        root_own[...] = jnp.where(tower_id == 0, left, right)
        root_away[...] = jnp.where(tower_id == 0, right, left)
        gain_sum[...] = gain_sum[...] * inverse_gains[...]
        lines = lax.broadcasted_iota(jnp.int32, (s.reward_at - s.sums_at, width), 0)
        for target, which in ((own, tower_id), (away, 1 - tower_id)):
            for matrix in range(s.calls):
                at = matrix * width
                target[at : at + width, :] = grads[which, matrix].astype(BF16)
            target[s.value_at : s.cond_at, :] = head_grads[which]
            sums = head_grads[which, s.wide : s.wide + lines.shape[0], :].astype(F32)
            for block in range(blocks):
                gain = gain_sum[which, block : block + 1, :]
                sums = jnp.where(lines == s.gain_row + block, gain, sums)
            target[s.sums_at : s.reward_at, :] = sums.astype(BF16)
            here = jnp.where(which == 0, cond_sum[...], 0.0)
            target[s.cond_at : s.shared_end, :] = here.astype(BF16)
            if s.total > s.shared_end:
                target[s.shared_end :, :] = jnp.zeros((s.total - s.shared_end, width), BF16)


def logits_kernel(sizes, tower_ref, lat_own, lat_got, value_own, latents, logits):
    rows = sizes.rows
    tower_id = tower_ref[0]
    at_own = pl.ds(pl.multiple_of(tower_id * rows, rows), rows)
    at_got = pl.ds(pl.multiple_of((1 - tower_id) * rows, rows), rows)
    for offset in range(sizes.pair):
        latents[offset, at_own, :] = lat_own[offset]
        latents[offset, at_got, :] = lat_got[offset]
        logits[offset] = by_lanes(value_own[...], latents[offset]).astype(BF16)


def add_and_split_kernel(count, digit_ref, *refs):
    inputs, outputs = refs[:count], refs[count:]
    digit = digit_ref[0]
    for other, target in enumerate(outputs):
        part = digit ^ other
        total = inputs[0][part].astype(F32)
        for source in inputs[1:]:
            total = total + source[part].astype(F32)
        target[...] = total.astype(BF16)


def unpack_own_kernel(sizes, scalars, *refs):
    s = sizes
    factor = len(refs) - 7
    digit, tower_id = scalars[0], scalars[1]
    w_in, w_out, value, gain, rms, flat, held = refs[factor:]
    width = s.width
    length = refs[0].shape[0]
    for other, source in enumerate(refs[:factor]):
        at = pl.multiple_of((digit ^ other) * length, 16)
        flat[pl.ds(at, length), :] = source[...]
    for block in range(s.blocks):
        at = block * width
        w_in[block] = flat[at : at + width, :].astype(F32)
        at = (s.blocks + block) * width
        w_out[block] = flat[at : at + width, :].astype(F32)
    value[:, 0, :] = flat[s.value_at : s.sums_at, :].astype(F32)[0 : s.bins]
    sums = flat[s.sums_at : s.reward_at, :].astype(F32)
    for block in range(s.blocks):
        gain[block] = sums[s.gain_row + block : s.gain_row + block + 1, :]
    held[...] = sums[:, 0:LANES]
    count = jnp.maximum(held[s.kinds : s.kinds + 1, 0 : s.steps], 1.0)
    for block in range(s.blocks):
        for kind in range(2):
            spot = tower_id * s.calls + 2 * block + kind
            square = held[pl.ds(spot, 1), 0 : s.steps]
            rms[block, kind : kind + 1, :] = jnp.sqrt(jnp.maximum(square, 0.0) / (count * width))


def unpack_shared_kernel(sizes, tower_ref, mine, got, reward, small, cond, joined):
    s = sizes
    tower_id = tower_ref[0]
    half = s.wide // 2
    joined[pl.ds(pl.multiple_of(tower_id * half, 8), half), :] = mine[0:half, :].astype(F32)
    joined[pl.ds(pl.multiple_of((1 - tower_id) * half, 8), half), :] = got[0:half, :].astype(F32)
    reward[...] = joined[0 : s.bins, :]
    for target, at in ((small, s.small_at), (cond, s.cond_at)):
        rows = slice(at - s.reward_at, at - s.reward_at + s.held)
        target[...] = (mine[rows, :].astype(F32) + got[rows, :].astype(F32))[0 : s.table_rows]


def whole(shape):
    return pl.BlockSpec(shape, lambda step, tower: (0,) * len(shape))


def swap(value, axis, mask):
    pairs = [(source, source ^ mask) for source in range(lax.axis_size(axis))]
    return lax.ppermute(value, axis, pairs)


AXES = ("tower", "batch")


def exchange_rounds(batch_size):
    factors, left = [], batch_size
    while left > 1:
        factors.append(4 if left % 4 == 0 else 2)
        left //= factors[-1]
    rounds, stride = [], 1
    for factor in factors:
        rounds.append((factor, stride))
        stride *= factor
    turned = rounds[::-1] if len(set(factors)) == 1 else rounds
    return [(one[0], (one[1], two[1])) for one, two in zip(rounds, turned)]


def swap_within(value, strides, other, batch_size):
    pairs = [
        (tower * batch_size + index, tower * batch_size + (index ^ (other * strides[tower])))
        for tower in range(2)
        for index in range(batch_size)
    ]
    return lax.ppermute(value, AXES, pairs)


def my_digit(factor, strides):
    stride = jnp.where(lax.axis_index("tower") == 0, strides[0], strides[1])
    return (lax.axis_index("batch") // stride) % factor


def add_kernel(*refs):
    total = refs[0][...].astype(F32)
    for source in refs[1:-1]:
        total = total + source[...].astype(F32)
    refs[-1][...] = total.astype(BF16)


def add_up(parts):
    return pl.pallas_call(
        add_kernel,
        out_shape=jax.ShapeDtypeStruct(parts[0].shape, BF16),
        compiler_params=pltpu.CompilerParams(vmem_limit_bytes=SMALL_LIMIT),
        name="add_up",
    )(*parts)


def exchange(value, rounds, batch_size, beside, given, last_kernel):
    factor, strides = rounds[0]
    digit = my_digit(factor, strides)
    rows, width = value[0].shape
    rows = rows // factor
    split = pl.pallas_call(
        functools.partial(add_and_split_kernel, len(value)),
        grid_spec=pltpu.PrefetchScalarGridSpec(
            num_scalar_prefetch=1,
            grid=(1,),
            in_specs=[whole((factor, rows, width))] * len(value),
            out_specs=[whole((rows, width))] * factor,
        ),
        out_shape=[pltpu.HBM((rows, width), BF16)] * factor,
        compiler_params=pltpu.CompilerParams(vmem_limit_bytes=SMALL_LIMIT),
        name="add_and_split",
    )(digit[None], *[part.reshape(factor, rows, width) for part in value])
    split, given = lax.optimization_barrier((split, given))
    held = [split[0]] + [
        swap_within(split[other], strides, other, batch_size) for other in range(1, factor)
    ]
    done = beside(given)
    held, done = lax.optimization_barrier((held, done))
    for size, steps in rounds[1:]:
        bit = 1
        while bit < size:
            block = add_up(held)
            held = [block, swap_within(block, steps, bit, batch_size)]
            bit *= 2
    block = add_up(held)
    held = [block] + [
        swap_within(block, strides, other, batch_size) for other in range(1, factor)
    ]
    return last_kernel(digit, held), done


def body(
    root_state, cond_table, block_gain, w_in, w_out, value_head, reward_head, small_head,
    unroll_len, actions, codes, policy_target, value_bins, reward_bins,
):
    tower_id = lax.axis_index("tower")
    other_id = 1 - tower_id
    tower_ref = tower_id.astype(jnp.int32)[None]
    steps, batch_rows = actions.shape
    blocks, width = block_gain.shape[1:]
    bins = value_head.shape[2]
    table_rows = cond_table.shape[0]
    rows = batch_rows // 2
    half = width // 2
    parts = lax.axis_size("batch")
    s = Sizes(steps, rows, blocks, width, bins, table_rows, parts)
    calls, wide, pair = s.calls, s.wide, s.pair

    root_got = swap(root_state, "tower", 1)
    in_own, out_own, gains_own = w_in[0], w_out[0], block_gain[0]
    value_own = value_head[0].T
    in_got = swap(in_own, "tower", 1)
    out_got = swap(out_own, "tower", 1)
    gains_got = swap(gains_own, "tower", 1)
    value_got = swap(value_own, "tower", 1)
    lengths = unroll_len.reshape(1, batch_rows)

    shape = jax.ShapeDtypeStruct
    per_pair = lambda *tail: pl.BlockSpec(
        (pair,) + tail, lambda turn, tower: (turn,) + (0,) * len(tail)
    )
    forward_params = pltpu.CompilerParams(vmem_limit_bytes=FORWARD_LIMIT)
    backward_params = pltpu.CompilerParams(vmem_limit_bytes=BACKWARD_LIMIT)
    small_params = pltpu.CompilerParams(vmem_limit_bytes=SMALL_LIMIT)
    products = steps * rows * (4 * blocks * width * width + 9 * width * wide)
    cost = pl.CostEstimate(flops=2 * products, bytes_accessed=40 * 2**20, transcendentals=0)
    (
        lat, lat_own, lat_away, entry, after, slope, side, dlat, dlast, loss, head_grads,
        turned, code_rows, gains,
    ) = pl.pallas_call(
        functools.partial(forward_kernel, s),
        grid_spec=pltpu.PrefetchScalarGridSpec(
            num_scalar_prefetch=1,
            grid=(steps // pair,),
            in_specs=[pl.BlockSpec(memory_space=pltpu.HBM)] * 14
            + [pl.BlockSpec(memory_space=pl.ANY)] * 4
            + [whole((blocks, width))],
            out_specs=[
                per_pair(2, rows, width),
                per_pair(rows, width),
                per_pair(rows, width),
                per_pair(calls, rows, width),
                per_pair(calls, rows, width),
                per_pair(calls, rows, width),
                per_pair(calls + 2, rows, LANES),
                pl.BlockSpec(
                    (pair, 2, rows, width), lambda turn, tower: (jnp.maximum(turn - 1, 0), 0, 0, 0)
                ),
                whole((pair, 2, rows, width)),
                whole((8, rows)),
                whole((2, s.head_rows, width)),
                whole((2 * calls, width, width)),
                whole((2, steps, rows)),
                whole((2, 8, width)),
            ],
            scratch_shapes=[
                pltpu.VMEM((rows, half), BF16),
                pltpu.VMEM((rows, half), BF16),
                pltpu.VMEM((1, rows), jnp.int32),
                pltpu.VMEM((steps, rows), jnp.int32),
                pltpu.VMEM((steps, rows), jnp.int32),
                pltpu.VMEM((steps, rows), jnp.int32),
                pltpu.VMEM((steps, 2, rows), jnp.int32),
                pltpu.VMEM((steps, rows), jnp.int32),
                pltpu.VMEM((table_rows, width), BF16),
                pltpu.VMEM((blocks, width), BF16),
                pltpu.VMEM((bins, width), BF16),
                pltpu.VMEM((bins, width), BF16),
                pltpu.VMEM((bins, width), BF16),
                pltpu.VMEM((table_rows, width), BF16),
                pltpu.SemaphoreType.DMA((18,)),
                pltpu.VMEM((rows, width), BF16),
                pltpu.VMEM((pair * rows, width), BF16),
                pltpu.VMEM((pair * rows, width), BF16),
                pltpu.VMEM((LANES, width), BF16),
                pltpu.VMEM((2 * calls, width, width), BF16),
                pltpu.VMEM((s.depth[0], width), BF16),
                pltpu.VMEM((s.depth[1], width), BF16),
                pltpu.VMEM((s.stack[0], width), F32),
                pltpu.VMEM((s.stack[1], width), F32),
                pltpu.VMEM((s.stack[0], pair * rows), F32),
                pltpu.VMEM((s.stack[1], pair * rows), F32),
                pltpu.VMEM((s.depth[0], pair * rows), BF16),
                pltpu.VMEM((s.depth[1], pair * rows), BF16),
                pltpu.VMEM((s.reward_at - s.sums_at, LANES), F32),
                pltpu.VMEM((pair, s.reward_at - s.sums_at, width), F32),
            ],
        ),
        out_shape=[
            shape((steps, 2, rows, width), BF16),
            pltpu.HBM((steps, rows, width), BF16),
            pltpu.HBM((steps, rows, width), BF16),
            shape((steps, calls, rows, width), BF16),
            shape((steps, calls, rows, width), BF16),
            shape((steps, calls, rows, width), F32),
            shape((steps, calls + 2, rows, LANES), F32),
            shape((steps - pair, 2, rows, width), F32),
            shape((pair, 2, rows, width), F32),
            shape((8, rows), F32),
            shape((2, s.head_rows, width), BF16),
            shape((2 * calls, width, width), BF16),
            shape((2, steps, rows), jnp.int32),
            shape((2, 8, width), F32),
        ],
        compiler_params=forward_params,
        cost_estimate=cost,
        name="unroll_forward",
    )(
        tower_ref,
        *[
            pltpu.with_memory_space_constraint(value, pltpu.HBM)
            for value in (
                root_state, lengths, actions, codes, policy_target,
                jnp.swapaxes(value_bins, 0, 1), reward_bins, cond_table, gains_own,
                in_own, out_own, value_own, reward_head.T, small_head.T,
            )
        ],
        root_got, in_got, out_got, value_got, gains_got,
    )

    turns = steps // pair
    descending = lambda *tail: pl.BlockSpec(
        (pair,) + tail, lambda turn, tower: (turns - 1 - turn,) + (0,) * len(tail)
    )
    own, away, root_own, root_away = pl.pallas_call(
        functools.partial(backward_kernel, s),
        grid_spec=pltpu.PrefetchScalarGridSpec(
            num_scalar_prefetch=1,
            grid=(turns,),
            in_specs=[
                descending(2, rows, width),
                descending(calls, rows, width),
                descending(calls, rows, width),
                descending(calls, rows, width),
                descending(calls + 2, rows, LANES),
                pl.BlockSpec(
                    (pair, 2, rows, width),
                    lambda turn, tower: (jnp.minimum(turns - 1 - turn, turns - 2), 0, 0, 0),
                ),
                whole((pair, 2, rows, width)),
                whole((2, steps, rows)),
                whole((2, 8, width)),
                whole((2 * calls, width, width)),
                whole((2, s.head_rows, width)),
            ],
            out_specs=[
                whole((s.total, width)),
                whole((s.total, width)),
                whole((rows, half)),
                whole((rows, half)),
            ],
            scratch_shapes=[
                pltpu.VMEM((rows, width), F32),
                pltpu.VMEM((2, 16, width), F32),
                pltpu.VMEM((s.held, width), F32),
                pltpu.VMEM((2, calls, width, width), F32),
                pltpu.VMEM((2, 16, width), F32),
                pltpu.VMEM((2, 16, width), F32),
                pltpu.VMEM((pair, calls, rows, width), BF16),
                pltpu.VMEM((pair, calls, rows, width), BF16),
                pltpu.VMEM((pair, 2, rows, width), BF16),
            ],
        ),
        out_shape=[
            shape((s.total, width), BF16),
            shape((s.total, width), BF16),
            shape((rows, half), BF16),
            shape((rows, half), BF16),
        ],
        compiler_params=backward_params,
        cost_estimate=cost,
        name="unroll_backward",
    )(
        tower_ref, lat, entry, after, slope, side, dlat, dlast, code_rows, gains,
        turned, head_grads,
    )
    got = swap(away, "tower", 1)

    def beside(given):
        lat_own, lat_away, loss, root_own, root_away = given
        lat_got = swap(lat_away, "tower", 1)
        loss_own = loss[0]
        loss_got = swap(loss_own, "tower", 1)
        root_got = swap(root_away, "tower", 1)

        latents, logits = pl.pallas_call(
            functools.partial(logits_kernel, s),
            grid_spec=pltpu.PrefetchScalarGridSpec(
                num_scalar_prefetch=1,
                grid=(steps // pair,),
                in_specs=[per_pair(rows, width), per_pair(rows, width), whole((bins, width))],
                out_specs=[per_pair(batch_rows, width), per_pair(bins, batch_rows)],
            ),
            out_shape=[
                shape((steps, batch_rows, width), BF16),
                shape((steps, bins, batch_rows), BF16),
            ],
            compiler_params=small_params,
            cost_estimate=pl.CostEstimate(
                flops=2 * steps * batch_rows * width * wide, bytes_accessed=6 * 2**20, transcendentals=0
            ),
            name="latents_and_logits",
        )(
            tower_ref,
            *[
                pltpu.with_memory_space_constraint(part, pltpu.HBM)
                for part in (lat_own, lat_got, value_own)
            ],
        )

        def in_order(mine_value, got_value, axis):
            return jnp.where(
                tower_id == 0,
                jnp.concatenate([mine_value, got_value], axis=axis),
                jnp.concatenate([got_value, mine_value], axis=axis),
            )

        row_loss = in_order(loss_own, loss_got, 0)
        grad_root = in_order(root_own, root_got, 0).astype(F32)
        return latents, logits, row_loss, grad_root

    rounds = exchange_rounds(parts)

    def unpack(digit, held):
        scalars = jnp.stack([digit, tower_id]).astype(jnp.int32)
        length = held[0].shape[0]
        block = s.reward_at // length
        at = s.reward_at - block * length
        parts_of = [part[at : at + s.shared_end - s.reward_at] for part in held]
        shared = parts_of[0]
        for other in range(1, len(held)):
            shared = jnp.where((digit ^ other) == block, parts_of[other], shared)
        shared_got = swap(shared, "tower", 1)
        return (shared, shared_got), pl.pallas_call(
            functools.partial(unpack_own_kernel, s),
            grid_spec=pltpu.PrefetchScalarGridSpec(
                num_scalar_prefetch=1,
                grid=(1,),
                in_specs=[whole(part.shape) for part in held],
                out_specs=[
                    whole((blocks, width, width)),
                    whole((blocks, width, width)),
                    whole((bins, 1, width)),
                    whole((blocks, 1, width)),
                    whole((blocks, 2, steps)),
                ],
                scratch_shapes=[
                    pltpu.VMEM((s.total, width), BF16),
                    pltpu.VMEM((s.reward_at - s.sums_at, LANES), F32),
                ],
            ),
            out_shape=[
                shape((blocks, width, width), F32),
                shape((blocks, width, width), F32),
                shape((bins, 1, width), F32),
                shape((blocks, 1, width), F32),
                shape((blocks, 2, steps), F32),
            ],
            compiler_params=small_params,
            name="unpack_own",
        )(scalars, *held)

    given = (lat_own, lat_away, loss, root_own, root_away)
    unpacked, done = exchange([own, got], rounds, parts, beside, given, unpack)
    (shared, shared_got), (grad_in, grad_out, value_t, gain_t, rms_t) = unpacked
    latents, logits, row_loss, grad_root = done
    reward_t, small_t, grad_cond = pl.pallas_call(
        functools.partial(unpack_shared_kernel, s),
        grid_spec=pltpu.PrefetchScalarGridSpec(
            num_scalar_prefetch=1,
            grid=(1,),
            in_specs=[whole(shared.shape), whole(shared.shape)],
            out_specs=[
                whole((bins, width)),
                whole((table_rows, width)),
                whole((table_rows, width)),
            ],
            scratch_shapes=[pltpu.VMEM((s.wide, width), F32)],
        ),
        out_shape=[
            shape((bins, width), F32),
            shape((table_rows, width), F32),
            shape((table_rows, width), F32),
        ],
        compiler_params=small_params,
        name="unpack_shared",
    )(tower_ref, shared, shared_got)
    layer_rms = jnp.transpose(rms_t, (2, 0, 1))[None]
    return (
        latents[None],
        jnp.swapaxes(logits, 1, 2)[None],
        row_loss,
        layer_rms,
        grad_root,
        grad_cond,
        jnp.swapaxes(gain_t, 0, 1),
        grad_in[None],
        grad_out[None],
        jnp.transpose(value_t, (1, 2, 0)),
        reward_t.T,
        small_t.T,
    )


def solution(mesh):
    placed = (
        P("batch", "tower"),
        P(),
        P("tower", None, None),
        P("tower", None, None, None),
        P("tower", None, None, None),
        P("tower", None, None),
        P(),
        P(),
        P("batch"),
        P(None, "batch"),
        P(None, "batch"),
        P(None, "batch"),
        P(None, None, "batch"),
        P(None, "batch"),
    )
    return jax.shard_map(
        body,
        mesh=mesh,
        in_specs=placed,
        out_specs=(
            P("tower", None, "batch", None),
            P("tower", None, "batch", None),
            P("batch"),
            P("tower", None, None, None),
            P("batch", "tower"),
            P(),
            P("tower", None, None),
            P("tower", None, None, None),
            P("tower", None, None, None),
            P("tower", None, None),
            P(),
            P(),
        ),
        check_vma=False,
    )
```

```python
import functools

import jax
import jax.numpy as jnp
from jax import lax
from jax.experimental import pallas as pl
from jax.experimental.pallas import tpu as pltpu
from jax.sharding import PartitionSpec as P

ACTIONS = 4
LANES = 128
MIB = 1024 * 1024
FORWARD_LIMIT = 20 * MIB
BACKWARD_LIMIT = 20 * MIB
SMALL_LIMIT = 12 * MIB
epsilon = 1e-06
very_negative = -1e30
F32 = jnp.float32
BF16 = jnp.bfloat16


def natural(left, right):
    return lax.dot_general(left, right, (((1,), (0,)), ((), ())), preferred_element_type=F32)


def by_rows(left, right):
    return lax.dot_general(left, right, (((0,), (0,)), ((), ())), preferred_element_type=F32)


def by_lanes(left, right):
    return lax.dot_general(left, right, (((1,), (1,)), ((), ())), preferred_element_type=F32)


def round_up(value, unit):
    return (value + unit - 1) // unit * unit


def lane_sum(value):
    return jnp.sum(value, axis=-1, keepdims=True)


def inverse_rms(hidden):
    return lax.rsqrt(lane_sum(hidden * hidden) * (1.0 / hidden.shape[-1]) + epsilon)


def weave(*tasks):
    tasks = [(list(task)) for task in tasks]
    longest = max(len(task) for task in tasks)
    done = [0] * len(tasks)
    for turn in range(longest):
        for which, task in enumerate(tasks):
            until = (turn + 1) * len(task) // longest
            while done[which] < until:
                task[done[which]]()
                done[which] += 1


def cuts(length, unit=160):
    return [(start, min(start + unit, length)) for start in range(0, length, unit)]


class Sizes:
    def __init__(self, steps, rows, blocks, width, bins, table_rows, parts):
        self.steps, self.rows, self.blocks, self.width = steps, rows, blocks, width
        self.bins, self.table_rows, self.parts = bins, table_rows, parts
        self.calls = 2 * blocks
        self.pair = 2 if steps % 2 == 0 else 1
        self.wide = round_up(bins, 32)
        self.held = round_up(table_rows, 16)
        self.stack = (self.wide + self.held, 2 * self.wide + self.held)
        self.depth = tuple(round_up(rows_in, LANES) for rows_in in self.stack)
        half = self.wide // 2
        self.value_at = self.calls * width
        self.sums_at = self.value_at + self.wide
        self.kinds = 2 * self.calls
        self.gain_row = self.kinds + 1
        self.reward_at = self.sums_at + round_up(self.gain_row + blocks, 16)
        self.small_at = self.reward_at + half
        self.cond_at = self.small_at + self.held
        self.shared_end = self.cond_at + self.held
        self.total = round_up(self.shared_end, 16 * parts)
        self.head_rows = self.cond_at - self.value_at


def forward_kernel(
    sizes, tower_ref,
    root_hbm, lengths_hbm, actions_hbm, codes_hbm, policy_hbm, value_bins_hbm, reward_bins_hbm,
    table_hbm, gains_hbm, in_hbm, out_hbm, value_hbm, reward_hbm, small_hbm,
    root_any, in_got, out_got, value_any, gains_got,
    lat, lat_own, lat_away, entry, after, slope, side, dlat, dlast, loss, head_grads, turned, code_rows, gains,
    root_own, root_got, lengths, actions, codes, policy, value_bins, reward_bins,
    table_in, gains_own, value_own, value_got, reward_in, small_in, sems,
    state, past0, past1, table, weights, heads0, heads1, acc0, acc1,
    logits0, logits1, cot0, cot1, sums, squares,
):
    s = sizes
    pair = s.pair
    turn = pl.program_id(0)
    first_step = turn * pair
    tower_id = tower_ref[0]
    rows, width, wide = s.rows, s.width, s.wide

    @pl.when(turn == 0)
    def _():
        here = pl.ds(pl.multiple_of(tower_id * rows, rows), rows)

        def matrices(kind, tower):
            return weights.at[pl.ds(kind * s.calls + tower * s.blocks, s.blocks)]

        moves = [
            (in_hbm, matrices(0, tower_id)),
            (out_hbm, matrices(1, tower_id)),
            (in_got, matrices(0, 1 - tower_id)),
            (out_got, matrices(1, 1 - tower_id)),
            (value_hbm, value_own),
            (value_any, value_got),
            (reward_hbm, reward_in),
            (small_hbm, small_in),
            (table_hbm, table_in),
            (gains_hbm, gains_own),
            (root_hbm.at[here], root_own),
            (root_any.at[here], root_got),
            (actions_hbm.at[:, here], actions),
            (codes_hbm.at[:, here], codes),
            (lengths_hbm.at[:, here], lengths),
            (policy_hbm.at[:, here], policy),
            (value_bins_hbm.at[:, :, here], value_bins),
            (reward_bins_hbm.at[:, here], reward_bins),
        ]
        moves = [
            pltpu.make_async_copy(source, target, sems.at[place])
            for place, (source, target) in enumerate(moves)
        ]
        for move in moves:
            move.start()
        for target in (
            gains, table, heads0, heads1, past0, past1, cot0, cot1, acc0, acc1, sums, squares, loss
        ):
            target[...] = jnp.zeros_like(target)
        for move in moves:
            move.wait()
        first = tower_id == 0
        code_rows[0] = actions[...]
        code_rows[1] = codes[...] + ACTIONS
        state[:, 0 : width // 2] = jnp.where(first, root_own[...], root_got[...])
        state[:, width // 2 : width] = jnp.where(first, root_got[...], root_own[...])
        gains[tower_id, 0 : s.blocks, :] = gains_own[...].astype(F32)
        gains[1 - tower_id, 0 : s.blocks, :] = gains_got[...].astype(F32)
        table[0 : s.table_rows, :] = table_in[...]
        heads0[0 : s.bins, :] = jnp.where(first, value_own[...], value_got[...])
        heads1[0 : s.bins, :] = jnp.where(first, value_got[...], value_own[...])
        heads1[wide : wide + s.bins, :] = reward_in[...]
        heads0[wide : wide + s.table_rows, :] = small_in[...]
        heads1[2 * wide : 2 * wide + s.table_rows, :] = small_in[...]

    eights = lax.broadcasted_iota(jnp.int32, (8, pair * rows), 0)
    before = jnp.maximum(first_step - pair, 0)

    def pair_row(kind, at_step, lead=()):
        return jnp.concatenate(
            [kind[(pl.ds(at_step + offset, 1),) + lead] for offset in range(pair)], axis=1
        )

    def live_rows(at_step):
        return jnp.concatenate(
            [(at_step + offset < lengths[...]).astype(F32) for offset in range(pair)], axis=1
        )

    kinds = []
    for offset in range(pair):
        step = first_step + offset
        kinds.append((step < lengths[...]).astype(F32))
        kinds.append(actions[pl.ds(step, 1), :].astype(F32))
        kinds.append((codes[pl.ds(step, 1), :] + ACTIONS).astype(F32))
    kinds.append(jnp.zeros((8 - len(kinds), rows), F32))
    columns = jnp.concatenate(kinds, axis=0).T

    def heads(tower, live_row, at_step, put):
        latent = past0 if tower == 0 else past1
        stack, logits, cot, acc = (
            (heads0, logits0, cot0, acc0) if tower == 0 else (heads1, logits1, cot1, acc1)
        )
        pick = lambda kind: pair_row(kind, at_step)
        value_goal = pair_row(value_bins, at_step, (tower,))
        spans = [(0, wide, 0, s.bins, value_goal)]
        if tower == 1:
            spans.append((wide, wide, 0, s.bins, pick(reward_bins)))
            spans.append((2 * wide, s.held, 0, ACTIONS, pick(policy)))
        else:
            spans.append((wide, s.held, ACTIONS, s.table_rows, pick(codes) + ACTIONS))

        def make_logits(start, stop):
            logits[start:stop, :] = by_lanes(stack[start:stop, :], latent[...])

        def eight_rows(value):
            return value.reshape(-1, 8, pair * rows)

        def mask(at, length, first, last):
            for start in range(0, length, 8):
                if start < first or start + 8 > last:
                    inside = (eights >= first - start) & (eights < last - start)
                    place = slice(at + start, at + start + 8)
                    logits[place, :] = jnp.where(inside, logits[place, :], very_negative)

        def find_top(at, start, stop, kept):
            top = jnp.max(eight_rows(logits[at + start : at + stop, :]), axis=0)
            kept["top"] = jnp.maximum(kept["top"], top) if "top" in kept else top

        def end_top(kept):
            kept["top"] = jnp.max(kept["top"], axis=0, keepdims=True)

        def make_terms(at, start, stop, goal, kept):
            place = slice(at + start, at + stop)
            value = logits[place, :]
            spot = lax.broadcasted_iota(jnp.int32, value.shape, 0)
            term = jnp.exp(value - kept["top"])
            logits[place, :] = term
            hit = spot == goal - start
            total = jnp.sum(eight_rows(term), axis=0)
            picked = jnp.sum(eight_rows(jnp.where(hit, value, 0.0)), axis=0)
            kept["total"] = kept["total"] + total if "total" in kept else total
            kept["picked"] = kept["picked"] + picked if "picked" in kept else picked

        def end_terms(kept):
            total = jnp.sum(kept["total"], axis=0, keepdims=True)
            picked = jnp.sum(kept["picked"], axis=0, keepdims=True)
            kept["scale"] = live_row / total
            row_loss = live_row * (jnp.log(total) + kept["top"] - picked)
            for offset in range(pair):
                loss[0:1, :] += row_loss[:, offset * rows : (offset + 1) * rows]

        def make_cotangent(at, start, stop, goal, kept):
            place = slice(at + start, at + stop)
            term = logits[place, :]
            spot = lax.broadcasted_iota(jnp.int32, term.shape, 0)
            hit = spot == goal - start
            cot[place, :] = (term * kept["scale"] - jnp.where(hit, live_row, 0.0)).astype(BF16)

        def make_grads(start, stop):
            acc[start:stop, :] += natural(cot[start:stop, :], latent[...])

        def make_latent():
            d_latent = by_rows(cot[...], stack[...])
            for offset in range(pair):
                put[offset, tower] = d_latent[offset * rows : (offset + 1) * rows]

        large = cuts(acc.shape[0], 320)
        pieces = [functools.partial(make_logits, *cut) for cut in large]
        for at, length, first, last, goal in spans:
            kept = {}
            each = cuts(length)
            pieces.append(functools.partial(mask, at, length, first, last))
            pieces += [functools.partial(find_top, at, *cut, kept) for cut in each]
            pieces.append(functools.partial(end_top, kept))
            pieces += [functools.partial(make_terms, at, *cut, goal, kept) for cut in each]
            pieces.append(functools.partial(end_terms, kept))
            pieces += [functools.partial(make_cotangent, at, *cut, goal, kept) for cut in each]
        return pieces + [make_latent] + [functools.partial(make_grads, *cut) for cut in large]

    def columns_of(offset, tower):
        live = columns[:, 3 * offset : 3 * offset + 1]
        return live, columns[:, 3 * offset + 1 + tower : 3 * offset + 2 + tower]

    def embedding(offset, tower):
        _, code = columns_of(offset, tower)
        spot = lax.broadcasted_iota(jnp.int32, (rows, table.shape[0]), 1)
        onehot = jnp.where(spot.astype(F32) == code, 1.0, 0.0).astype(BF16)
        return natural(onehot, table[...])

    def tower_call(offset, tower, chain):
        live, _ = columns_of(offset, tower)

        def scale_rows():
            row_squares = lane_sum(chain["hidden"] * chain["hidden"])
            return row_squares, lax.rsqrt(row_squares * (1.0 / width) + epsilon)

        def keep_squares(block, row_squares):
            place = 2 * (tower * s.blocks + block)
            total = jnp.sum(live * row_squares, axis=0, keepdims=True) * (1.0 / LANES)
            squares[offset, place : place + 1, 0:LANES] = jnp.broadcast_to(total, (1, LANES))

        def end_block(block):
            branch = chain["product"]
            chain["hidden"] = chain["hidden"] + branch
            return branch

        def keep_branch(block, branch):
            spot = 2 * (tower * s.blocks + block) + 1
            squares[offset, spot : spot + 1, :] = jnp.sum(
                branch * branch * live, axis=0, keepdims=True
            )

        def into(block):
            place = tower * s.blocks + block
            if block > 0:
                branch = end_block(block - 1)
            gained = chain["hidden"] * gains[tower, block : block + 1, :]
            chain["product"] = natural(gained.astype(BF16), weights[place])
            row_squares, inv_scale = scale_rows()
            chain["scale"] = inv_scale
            entry[offset, place] = (gained * inv_scale).astype(BF16)
            side[offset, place] = jnp.broadcast_to(inv_scale, (rows, LANES))
            if block > 0:
                keep_squares(block - 1, row_squares)
                keep_branch(block - 1, branch)

        def out_of(block):
            place = tower * s.blocks + block
            u = chain["product"] * chain["scale"]
            gate = 0.5 * jnp.tanh(0.5 * u) + 0.5
            after_rows = (u * gate).astype(BF16)
            chain["product"] = natural(after_rows, weights[s.calls + place])
            after[offset, place] = after_rows
            slope[offset, place] = gate * (1.0 + u * (1.0 - gate))

        def finish():
            branch = end_block(s.blocks - 1)
            row_squares, inv_scale = scale_rows()
            latent = (chain["hidden"] * inv_scale).astype(BF16)
            chain[offset, tower] = latent
            following = (offset, 1) if tower == 0 else (offset + 1, 0)
            if following in chain:
                chain["hidden"] = latent.astype(F32) + chain[following]

            def keep():
                side[offset, s.calls + tower] = jnp.broadcast_to(inv_scale, (rows, LANES))
                lat[offset, tower] = latent
                keep_squares(s.blocks - 1, row_squares)
                keep_branch(s.blocks - 1, branch)
                if tower == 0:
                    total = jnp.sum(live, axis=0, keepdims=True) * (1.0 / LANES)
                    squares[offset, s.kinds : s.kinds + 1, 0:LANES] = jnp.broadcast_to(
                        total, (1, LANES)
                    )

            return keep

        pieces = []
        for block in range(s.blocks):
            pieces += [functools.partial(into, block), functools.partial(out_of, block)]
        return pieces, finish

    chain = {
        (offset, tower): embedding(offset, tower) for offset in range(pair) for tower in range(2)
    }
    chain["hidden"] = state[...].astype(F32) + chain[0, 0]
    pieces = []
    keeps = []

    def begin_next(finish, into):
        keeps.append(finish())
        into()
        keeps.pop()()

    ending = None
    for offset in range(pair):
        for tower in range(2):
            calls, finish = tower_call(offset, tower, chain)
            if ending is not None:
                calls[0] = functools.partial(begin_next, ending, calls[0])
            pieces += calls
            ending = finish
    pieces.append(lambda: ending()())

    turns = -(-2 * s.calls // (s.steps // pair))

    def turn_weights(which):
        matrix = jnp.minimum(turn * turns + which, 2 * s.calls - 1)
        turned[matrix] = weights[matrix].T

    live_before = jnp.where(turn > 0, live_rows(before), 0.0)
    weave(
        pieces,
        heads(1, live_before, before, dlat)
        + heads(0, live_before, before, dlat)
        + [functools.partial(turn_weights, which) for which in range(turns)],
    )
    first = tower_id == 0
    at_lane = lax.broadcasted_iota(jnp.int32, sums.shape, 1)
    for offset in range(pair):
        at = slice(offset * rows, (offset + 1) * rows)
        after_state, next_state = chain[offset, 0], chain[offset, 1]
        past0[at, :] = after_state
        past1[at, :] = next_state
        lat_own[offset] = jnp.where(first, after_state, next_state)
        lat_away[offset] = jnp.where(first, next_state, after_state)
        if offset == pair - 1:
            state[...] = next_state
        total = lane_sum(squares[offset])
        sums[...] = jnp.where(at_lane == first_step + offset, total, sums[...])

    @pl.when(turn == pl.num_programs(0) - 1)
    def _():
        live_now = live_rows(first_step)
        weave(heads(1, live_now, first_step, dlast), heads(0, live_now, first_step, dlast))
        half = wide // 2
        head_grads[...] = jnp.zeros_like(head_grads)
        head_grads[0, 0:wide, :] = acc0[0:wide, :].astype(BF16)
        head_grads[1, 0:wide, :] = acc1[0:wide, :].astype(BF16)
        small = acc0[wide : wide + s.held, :] + acc1[2 * wide : 2 * wide + s.held, :]
        at = s.small_at - s.value_at
        head_grads[0, at : at + s.held, :] = small.astype(BF16)
        for tower in range(2):
            put = s.reward_at - s.value_at
            at = wide + tower * half
            head_grads[tower, put : put + half, :] = acc1[at : at + half, :].astype(BF16)
            head_grads[tower, wide : wide + sums.shape[0], 0:LANES] = sums[...].astype(BF16)


def backward_kernel(
    sizes, tower_ref,
    lat, entry, after, slope, side, dlat, dlast, code_rows, gains_in, turned, head_grads,
    own, away, root_own, root_away,
    carry, gain_sum, cond_sum, grads, gains, inverse_gains, d_after_kept, d_before_kept,
    d_hidden_kept,
):
    s = sizes
    pair = s.pair
    turn = pl.program_id(0)
    first_step = s.steps - pair * (turn + 1)
    tower_id = tower_ref[0]
    blocks, width = s.blocks, s.width

    @pl.when(turn == 0)
    def _():
        gains[...] = jnp.ones_like(gains)
        gains[:, 0:blocks, :] = gains_in[:, 0:blocks, :]
        inverse_gains[...] = 1.0 / gains[...]
        carry[...] = jnp.zeros_like(carry)
        grads[...] = jnp.zeros_like(grads)
        gain_sum[...] = jnp.zeros_like(gain_sum)
        cond_sum[...] = jnp.zeros_like(cond_sum)

    def over_lanes(column):
        return jnp.concatenate([column] * (width // LANES), axis=1)

    def stacked(parts):
        return jnp.concatenate(parts, axis=0)

    def add_grads(matrix, rows_of, place, kept, now):
        later = [kept[offset, place] for offset in range(1, pair)]
        grads[matrix // s.calls, matrix % s.calls] += by_rows(
            stacked([rows_of[offset, place] for offset in range(pair)]), stacked([now] + later)
        )

    def add_cond(offset, tower, d_hidden):
        if offset > 0:
            d_hidden_kept[offset, tower] = d_hidden.astype(BF16)
            return
        code = jnp.concatenate(
            [code_rows[tower, pl.ds(first_step + step, 1), :] for step in range(pair)], axis=1
        )
        spots = lax.broadcasted_iota(jnp.int32, (cond_sum.shape[0], pair * s.rows), 0)
        onehot = jnp.where(spots == code, 1.0, 0.0).astype(BF16)
        parts = [d_hidden.astype(BF16)]
        parts += [d_hidden_kept[step, tower] for step in range(1, pair)]
        cond_sum[...] += natural(onehot, stacked(parts))

    behind = []

    def catch_up():
        while behind:
            behind.pop(0)()

    def tower_back(offset, tower, d_latent):
        normed = lat[offset, tower]
        normed_wide = normed.astype(F32)
        inv_scale = over_lanes(side[offset, s.calls + tower])
        base = inv_scale * d_latent
        slant = inv_scale * (lane_sum(d_latent * normed_wide) * (1.0 / width))
        for block in reversed(range(blocks)):
            place = tower * blocks + block
            matrix = tower * s.calls + block
            both = natural(
                jnp.concatenate([normed, base.astype(BF16)], axis=0), turned[s.calls + place]
            )
            d_hidden = base - slant * normed_wide
            d_branch = d_hidden.astype(BF16)
            entry_wide = entry[offset, place].astype(F32)
            inv_scale = over_lanes(side[offset, place])
            catch_up()
            d_after = both[s.rows :] - slant * both[: s.rows]
            d_before = (d_after * slope[offset, place]).astype(BF16)
            d_entry = natural(d_before, turned[place])
            if offset > 0:
                d_after_kept[offset, place] = d_branch
                d_before_kept[offset, place] = d_before
            else:
                add_grads(matrix + blocks, after, place, d_after_kept, d_branch)
                behind.append(
                    functools.partial(add_grads, matrix, entry, place, d_before_kept, d_before)
                )
            gain = gains[tower, block : block + 1, :]
            normed_wide = entry_wide * inverse_gains[tower, block : block + 1, :]
            normed = normed_wide.astype(BF16)
            product = d_entry * entry_wide
            base = d_hidden + inv_scale * (d_entry * gain)
            slant = inv_scale * (lane_sum(product) * (1.0 / width))

            def add_gain(tower=tower, block=block, product=product):
                gain_sum[tower, block : block + 1, :] += jnp.sum(product, axis=0, keepdims=True)

            behind.append(add_gain)
        d_hidden = base - slant * normed_wide
        behind.append(functools.partial(add_cond, offset, tower, d_hidden))
        return d_hidden

    def from_heads(offset, tower):
        return jnp.where(turn == 0, dlast[offset, tower], dlat[offset, tower])

    d_state = carry[...]
    for offset in reversed(range(pair)):
        for tower in (1, 0):
            d_state = tower_back(offset, tower, d_state + from_heads(offset, tower))
    catch_up()
    carry[...] = d_state

    @pl.when(turn == pl.num_programs(0) - 1)
    def _():
        left = d_state[:, 0 : width // 2].astype(BF16)
        right = d_state[:, width // 2 : width].astype(BF16)
        root_own[...] = jnp.where(tower_id == 0, left, right)
        root_away[...] = jnp.where(tower_id == 0, right, left)
        gain_sum[...] = gain_sum[...] * inverse_gains[...]
        lines = lax.broadcasted_iota(jnp.int32, (s.reward_at - s.sums_at, width), 0)
        for target, which in ((own, tower_id), (away, 1 - tower_id)):
            for matrix in range(s.calls):
                at = matrix * width
                target[at : at + width, :] = grads[which, matrix].astype(BF16)
            target[s.value_at : s.cond_at, :] = head_grads[which]
            sums = head_grads[which, s.wide : s.wide + lines.shape[0], :].astype(F32)
            for block in range(blocks):
                gain = gain_sum[which, block : block + 1, :]
                sums = jnp.where(lines == s.gain_row + block, gain, sums)
            target[s.sums_at : s.reward_at, :] = sums.astype(BF16)
            here = jnp.where(which == 0, cond_sum[...], 0.0)
            target[s.cond_at : s.shared_end, :] = here.astype(BF16)
            if s.total > s.shared_end:
                target[s.shared_end :, :] = jnp.zeros((s.total - s.shared_end, width), BF16)


def logits_kernel(sizes, tower_ref, lat_own, lat_got, value_own, latents, logits):
    rows = sizes.rows
    tower_id = tower_ref[0]
    at_own = pl.ds(pl.multiple_of(tower_id * rows, rows), rows)
    at_got = pl.ds(pl.multiple_of((1 - tower_id) * rows, rows), rows)
    for offset in range(sizes.pair):
        latents[offset, at_own, :] = lat_own[offset]
        latents[offset, at_got, :] = lat_got[offset]
        logits[offset] = by_lanes(value_own[...], latents[offset]).astype(BF16)


def add_and_split_kernel(count, digit_ref, *refs):
    inputs, outputs = refs[:count], refs[count:]
    digit = digit_ref[0]
    for other, target in enumerate(outputs):
        part = digit ^ other
        total = inputs[0][part].astype(F32)
        for source in inputs[1:]:
            total = total + source[part].astype(F32)
        target[...] = total.astype(BF16)


def unpack_own_kernel(sizes, scalars, *refs):
    s = sizes
    factor = len(refs) - 7
    digit, tower_id = scalars[0], scalars[1]
    w_in, w_out, value, gain, rms, flat, held = refs[factor:]
    width = s.width
    length = refs[0].shape[0]
    for other, source in enumerate(refs[:factor]):
        at = pl.multiple_of((digit ^ other) * length, 16)
        flat[pl.ds(at, length), :] = source[...]
    for block in range(s.blocks):
        at = block * width
        w_in[block] = flat[at : at + width, :].astype(F32)
        at = (s.blocks + block) * width
        w_out[block] = flat[at : at + width, :].astype(F32)
    value[:, 0, :] = flat[s.value_at : s.sums_at, :].astype(F32)[0 : s.bins]
    sums = flat[s.sums_at : s.reward_at, :].astype(F32)
    for block in range(s.blocks):
        gain[block] = sums[s.gain_row + block : s.gain_row + block + 1, :]
    held[...] = sums[:, 0:LANES]
    count = jnp.maximum(held[s.kinds : s.kinds + 1, 0 : s.steps], 1.0)
    for block in range(s.blocks):
        for kind in range(2):
            spot = tower_id * s.calls + 2 * block + kind
            square = held[pl.ds(spot, 1), 0 : s.steps]
            rms[block, kind : kind + 1, :] = jnp.sqrt(jnp.maximum(square, 0.0) / (count * width))


def unpack_shared_kernel(sizes, tower_ref, mine, got, reward, small, cond, joined):
    s = sizes
    tower_id = tower_ref[0]
    half = s.wide // 2
    joined[pl.ds(pl.multiple_of(tower_id * half, 8), half), :] = mine[0:half, :].astype(F32)
    joined[pl.ds(pl.multiple_of((1 - tower_id) * half, 8), half), :] = got[0:half, :].astype(F32)
    reward[...] = joined[0 : s.bins, :]
    for target, at in ((small, s.small_at), (cond, s.cond_at)):
        rows = slice(at - s.reward_at, at - s.reward_at + s.held)
        target[...] = (mine[rows, :].astype(F32) + got[rows, :].astype(F32))[0 : s.table_rows]


def whole(shape):
    return pl.BlockSpec(shape, lambda step, tower: (0,) * len(shape))


def swap(value, axis, mask):
    pairs = [(source, source ^ mask) for source in range(lax.axis_size(axis))]
    return lax.ppermute(value, axis, pairs)


AXES = ("tower", "batch")


def exchange_rounds(batch_size):
    factors, left = [], batch_size
    while left > 1:
        factors.append(4 if left % 4 == 0 else 2)
        left //= factors[-1]
    rounds, stride = [], 1
    for factor in factors:
        rounds.append((factor, stride))
        stride *= factor
    turned = rounds[::-1] if len(set(factors)) == 1 else rounds
    return [(one[0], (one[1], two[1])) for one, two in zip(rounds, turned)]


def swap_within(value, strides, other, batch_size):
    pairs = [
        (tower * batch_size + index, tower * batch_size + (index ^ (other * strides[tower])))
        for tower in range(2)
        for index in range(batch_size)
    ]
    return lax.ppermute(value, AXES, pairs)


def my_digit(factor, strides):
    stride = jnp.where(lax.axis_index("tower") == 0, strides[0], strides[1])
    return (lax.axis_index("batch") // stride) % factor


def add_kernel(*refs):
    total = refs[0][...].astype(F32)
    for source in refs[1:-1]:
        total = total + source[...].astype(F32)
    refs[-1][...] = total.astype(BF16)


def add_up(parts):
    return pl.pallas_call(
        add_kernel,
        out_shape=jax.ShapeDtypeStruct(parts[0].shape, BF16),
        compiler_params=pltpu.CompilerParams(vmem_limit_bytes=SMALL_LIMIT),
        name="add_up",
    )(*parts)


def exchange(value, rounds, batch_size, beside, given, last_kernel):
    factor, strides = rounds[0]
    digit = my_digit(factor, strides)
    rows, width = value[0].shape
    rows = rows // factor
    split = pl.pallas_call(
        functools.partial(add_and_split_kernel, len(value)),
        grid_spec=pltpu.PrefetchScalarGridSpec(
            num_scalar_prefetch=1,
            grid=(1,),
            in_specs=[whole((factor, rows, width))] * len(value),
            out_specs=[whole((rows, width))] * factor,
        ),
        out_shape=[pltpu.HBM((rows, width), BF16)] * factor,
        compiler_params=pltpu.CompilerParams(vmem_limit_bytes=SMALL_LIMIT),
        name="add_and_split",
    )(digit[None], *[part.reshape(factor, rows, width) for part in value])
    split, given = lax.optimization_barrier((split, given))
    held = [split[0]] + [
        swap_within(split[other], strides, other, batch_size) for other in range(1, factor)
    ]
    done = beside(given)
    held, done = lax.optimization_barrier((held, done))
    for size, steps in rounds[1:]:
        bit = 1
        while bit < size:
            block = add_up(held)
            held = [block, swap_within(block, steps, bit, batch_size)]
            bit *= 2
    block = add_up(held)
    held = [block] + [
        swap_within(block, strides, other, batch_size) for other in range(1, factor)
    ]
    return last_kernel(digit, held), done


def body(
    root_state, cond_table, block_gain, w_in, w_out, value_head, reward_head, small_head,
    unroll_len, actions, codes, policy_target, value_bins, reward_bins,
):
    tower_id = lax.axis_index("tower")
    other_id = 1 - tower_id
    tower_ref = tower_id.astype(jnp.int32)[None]
    steps, batch_rows = actions.shape
    blocks, width = block_gain.shape[1:]
    bins = value_head.shape[2]
    table_rows = cond_table.shape[0]
    rows = batch_rows // 2
    half = width // 2
    parts = lax.axis_size("batch")
    s = Sizes(steps, rows, blocks, width, bins, table_rows, parts)
    calls, wide, pair = s.calls, s.wide, s.pair

    root_got = swap(root_state, "tower", 1)
    in_own, out_own, gains_own = w_in[0], w_out[0], block_gain[0]
    value_own = value_head[0].T
    in_got = swap(in_own, "tower", 1)
    out_got = swap(out_own, "tower", 1)
    gains_got = swap(gains_own, "tower", 1)
    value_got = swap(value_own, "tower", 1)
    lengths = unroll_len.reshape(1, batch_rows)

    shape = jax.ShapeDtypeStruct
    per_pair = lambda *tail: pl.BlockSpec(
        (pair,) + tail, lambda turn, tower: (turn,) + (0,) * len(tail)
    )
    forward_params = pltpu.CompilerParams(vmem_limit_bytes=FORWARD_LIMIT)
    backward_params = pltpu.CompilerParams(vmem_limit_bytes=BACKWARD_LIMIT)
    small_params = pltpu.CompilerParams(vmem_limit_bytes=SMALL_LIMIT)
    products = steps * rows * (4 * blocks * width * width + 9 * width * wide)
    cost = pl.CostEstimate(flops=2 * products, bytes_accessed=40 * 2**20, transcendentals=0)
    (
        lat, lat_own, lat_away, entry, after, slope, side, dlat, dlast, loss, head_grads,
        turned, code_rows, gains,
    ) = pl.pallas_call(
        functools.partial(forward_kernel, s),
        grid_spec=pltpu.PrefetchScalarGridSpec(
            num_scalar_prefetch=1,
            grid=(steps // pair,),
            in_specs=[pl.BlockSpec(memory_space=pltpu.HBM)] * 14
            + [pl.BlockSpec(memory_space=pl.ANY)] * 4
            + [whole((blocks, width))],
            out_specs=[
                per_pair(2, rows, width),
                per_pair(rows, width),
                per_pair(rows, width),
                per_pair(calls, rows, width),
                per_pair(calls, rows, width),
                per_pair(calls, rows, width),
                per_pair(calls + 2, rows, LANES),
                pl.BlockSpec(
                    (pair, 2, rows, width), lambda turn, tower: (jnp.maximum(turn - 1, 0), 0, 0, 0)
                ),
                whole((pair, 2, rows, width)),
                whole((8, rows)),
                whole((2, s.head_rows, width)),
                whole((2 * calls, width, width)),
                whole((2, steps, rows)),
                whole((2, 8, width)),
            ],
            scratch_shapes=[
                pltpu.VMEM((rows, half), BF16),
                pltpu.VMEM((rows, half), BF16),
                pltpu.VMEM((1, rows), jnp.int32),
                pltpu.VMEM((steps, rows), jnp.int32),
                pltpu.VMEM((steps, rows), jnp.int32),
                pltpu.VMEM((steps, rows), jnp.int32),
                pltpu.VMEM((steps, 2, rows), jnp.int32),
                pltpu.VMEM((steps, rows), jnp.int32),
                pltpu.VMEM((table_rows, width), BF16),
                pltpu.VMEM((blocks, width), BF16),
                pltpu.VMEM((bins, width), BF16),
                pltpu.VMEM((bins, width), BF16),
                pltpu.VMEM((bins, width), BF16),
                pltpu.VMEM((table_rows, width), BF16),
                pltpu.SemaphoreType.DMA((18,)),
                pltpu.VMEM((rows, width), BF16),
                pltpu.VMEM((pair * rows, width), BF16),
                pltpu.VMEM((pair * rows, width), BF16),
                pltpu.VMEM((LANES, width), BF16),
                pltpu.VMEM((2 * calls, width, width), BF16),
                pltpu.VMEM((s.depth[0], width), BF16),
                pltpu.VMEM((s.depth[1], width), BF16),
                pltpu.VMEM((s.stack[0], width), F32),
                pltpu.VMEM((s.stack[1], width), F32),
                pltpu.VMEM((s.stack[0], pair * rows), F32),
                pltpu.VMEM((s.stack[1], pair * rows), F32),
                pltpu.VMEM((s.depth[0], pair * rows), BF16),
                pltpu.VMEM((s.depth[1], pair * rows), BF16),
                pltpu.VMEM((s.reward_at - s.sums_at, LANES), F32),
                pltpu.VMEM((pair, s.reward_at - s.sums_at, width), F32),
            ],
        ),
        out_shape=[
            shape((steps, 2, rows, width), BF16),
            pltpu.HBM((steps, rows, width), BF16),
            pltpu.HBM((steps, rows, width), BF16),
            shape((steps, calls, rows, width), BF16),
            shape((steps, calls, rows, width), BF16),
            shape((steps, calls, rows, width), F32),
            shape((steps, calls + 2, rows, LANES), F32),
            shape((steps - pair, 2, rows, width), F32),
            shape((pair, 2, rows, width), F32),
            shape((8, rows), F32),
            shape((2, s.head_rows, width), BF16),
            shape((2 * calls, width, width), BF16),
            shape((2, steps, rows), jnp.int32),
            shape((2, 8, width), F32),
        ],
        compiler_params=forward_params,
        cost_estimate=cost,
        name="unroll_forward",
    )(
        tower_ref,
        *[
            pltpu.with_memory_space_constraint(value, pltpu.HBM)
            for value in (
                root_state, lengths, actions, codes, policy_target,
                jnp.swapaxes(value_bins, 0, 1), reward_bins, cond_table, gains_own,
                in_own, out_own, value_own, reward_head.T, small_head.T,
            )
        ],
        root_got, in_got, out_got, value_got, gains_got,
    )

    turns = steps // pair
    descending = lambda *tail: pl.BlockSpec(
        (pair,) + tail, lambda turn, tower: (turns - 1 - turn,) + (0,) * len(tail)
    )
    own, away, root_own, root_away = pl.pallas_call(
        functools.partial(backward_kernel, s),
        grid_spec=pltpu.PrefetchScalarGridSpec(
            num_scalar_prefetch=1,
            grid=(turns,),
            in_specs=[
                descending(2, rows, width),
                descending(calls, rows, width),
                descending(calls, rows, width),
                descending(calls, rows, width),
                descending(calls + 2, rows, LANES),
                pl.BlockSpec(
                    (pair, 2, rows, width),
                    lambda turn, tower: (jnp.minimum(turns - 1 - turn, turns - 2), 0, 0, 0),
                ),
                whole((pair, 2, rows, width)),
                whole((2, steps, rows)),
                whole((2, 8, width)),
                whole((2 * calls, width, width)),
                whole((2, s.head_rows, width)),
            ],
            out_specs=[
                whole((s.total, width)),
                whole((s.total, width)),
                whole((rows, half)),
                whole((rows, half)),
            ],
            scratch_shapes=[
                pltpu.VMEM((rows, width), F32),
                pltpu.VMEM((2, 16, width), F32),
                pltpu.VMEM((s.held, width), F32),
                pltpu.VMEM((2, calls, width, width), F32),
                pltpu.VMEM((2, 16, width), F32),
                pltpu.VMEM((2, 16, width), F32),
                pltpu.VMEM((pair, calls, rows, width), BF16),
                pltpu.VMEM((pair, calls, rows, width), BF16),
                pltpu.VMEM((pair, 2, rows, width), BF16),
            ],
        ),
        out_shape=[
            shape((s.total, width), BF16),
            shape((s.total, width), BF16),
            shape((rows, half), BF16),
            shape((rows, half), BF16),
        ],
        compiler_params=backward_params,
        cost_estimate=cost,
        name="unroll_backward",
    )(
        tower_ref, lat, entry, after, slope, side, dlat, dlast, code_rows, gains,
        turned, head_grads,
    )
    got = swap(away, "tower", 1)

    def beside(given):
        lat_own, lat_away, loss, root_own, root_away = given
        lat_got = swap(lat_away, "tower", 1)
        loss_own = loss[0]
        loss_got = swap(loss_own, "tower", 1)
        root_got = swap(root_away, "tower", 1)

        latents, logits = pl.pallas_call(
            functools.partial(logits_kernel, s),
            grid_spec=pltpu.PrefetchScalarGridSpec(
                num_scalar_prefetch=1,
                grid=(steps // pair,),
                in_specs=[per_pair(rows, width), per_pair(rows, width), whole((bins, width))],
                out_specs=[per_pair(batch_rows, width), per_pair(bins, batch_rows)],
            ),
            out_shape=[
                shape((steps, batch_rows, width), BF16),
                shape((steps, bins, batch_rows), BF16),
            ],
            compiler_params=small_params,
            cost_estimate=pl.CostEstimate(
                flops=2 * steps * batch_rows * width * wide, bytes_accessed=6 * 2**20, transcendentals=0
            ),
            name="latents_and_logits",
        )(
            tower_ref,
            *[
                pltpu.with_memory_space_constraint(part, pltpu.HBM)
                for part in (lat_own, lat_got, value_own)
            ],
        )

        def in_order(mine_value, got_value, axis):
            return jnp.where(
                tower_id == 0,
                jnp.concatenate([mine_value, got_value], axis=axis),
                jnp.concatenate([got_value, mine_value], axis=axis),
            )

        row_loss = in_order(loss_own, loss_got, 0)
        grad_root = in_order(root_own, root_got, 0).astype(F32)
        return latents, logits, row_loss, grad_root

    rounds = exchange_rounds(parts)

    def unpack(digit, held):
        scalars = jnp.stack([digit, tower_id]).astype(jnp.int32)
        length = held[0].shape[0]
        block = s.reward_at // length
        at = s.reward_at - block * length
        parts_of = [part[at : at + s.shared_end - s.reward_at] for part in held]
        shared = parts_of[0]
        for other in range(1, len(held)):
            shared = jnp.where((digit ^ other) == block, parts_of[other], shared)
        shared_got = swap(shared, "tower", 1)
        return (shared, shared_got), pl.pallas_call(
            functools.partial(unpack_own_kernel, s),
            grid_spec=pltpu.PrefetchScalarGridSpec(
                num_scalar_prefetch=1,
                grid=(1,),
                in_specs=[whole(part.shape) for part in held],
                out_specs=[
                    whole((blocks, width, width)),
                    whole((blocks, width, width)),
                    whole((bins, 1, width)),
                    whole((blocks, 1, width)),
                    whole((blocks, 2, steps)),
                ],
                scratch_shapes=[
                    pltpu.VMEM((s.total, width), BF16),
                    pltpu.VMEM((s.reward_at - s.sums_at, LANES), F32),
                ],
            ),
            out_shape=[
                shape((blocks, width, width), F32),
                shape((blocks, width, width), F32),
                shape((bins, 1, width), F32),
                shape((blocks, 1, width), F32),
                shape((blocks, 2, steps), F32),
            ],
            compiler_params=small_params,
            name="unpack_own",
        )(scalars, *held)

    given = (lat_own, lat_away, loss, root_own, root_away)
    unpacked, done = exchange([own, got], rounds, parts, beside, given, unpack)
    (shared, shared_got), (grad_in, grad_out, value_t, gain_t, rms_t) = unpacked
    latents, logits, row_loss, grad_root = done
    reward_t, small_t, grad_cond = pl.pallas_call(
        functools.partial(unpack_shared_kernel, s),
        grid_spec=pltpu.PrefetchScalarGridSpec(
            num_scalar_prefetch=1,
            grid=(1,),
            in_specs=[whole(shared.shape), whole(shared.shape)],
            out_specs=[
                whole((bins, width)),
                whole((table_rows, width)),
                whole((table_rows, width)),
            ],
            scratch_shapes=[pltpu.VMEM((s.wide, width), F32)],
        ),
        out_shape=[
            shape((bins, width), F32),
            shape((table_rows, width), F32),
            shape((table_rows, width), F32),
        ],
        compiler_params=small_params,
        name="unpack_shared",
    )(tower_ref, shared, shared_got)
    layer_rms = jnp.transpose(rms_t, (2, 0, 1))[None]
    return (
        latents[None],
        jnp.swapaxes(logits, 1, 2)[None],
        row_loss,
        layer_rms,
        grad_root,
        grad_cond,
        jnp.swapaxes(gain_t, 0, 1),
        grad_in[None],
        grad_out[None],
        jnp.transpose(value_t, (1, 2, 0)),
        reward_t.T,
        small_t.T,
    )


def solution(mesh):
    placed = (
        P("batch", "tower"),
        P(),
        P("tower", None, None),
        P("tower", None, None, None),
        P("tower", None, None, None),
        P("tower", None, None),
        P(),
        P(),
        P("batch"),
        P(None, "batch"),
        P(None, "batch"),
        P(None, "batch"),
        P(None, None, "batch"),
        P(None, "batch"),
    )
    return jax.shard_map(
        body,
        mesh=mesh,
        in_specs=placed,
        out_specs=(
            P("tower", None, "batch", None),
            P("tower", None, "batch", None),
            P("batch"),
            P("tower", None, None, None),
            P("batch", "tower"),
            P(),
            P("tower", None, None),
            P("tower", None, None, None),
            P("tower", None, None, None),
            P("tower", None, None),
            P(),
            P(),
        ),
        check_vma=False,
    )
```

```python
import functools

import jax
import jax.numpy as jnp
from jax import lax
from jax.experimental import pallas as pl
from jax.experimental.pallas import tpu as pltpu
from jax.sharding import PartitionSpec as P

ACTIONS = 4
LANES = 128
MIB = 1024 * 1024
UNROLL_LIMIT = 46 * MIB
SMALL_LIMIT = 12 * MIB
epsilon = 1e-06
very_negative = -1e30
F32 = jnp.float32
BF16 = jnp.bfloat16


def natural(left, right):
    return lax.dot_general(left, right, (((1,), (0,)), ((), ())), preferred_element_type=F32)


def by_rows(left, right):
    return lax.dot_general(left, right, (((0,), (0,)), ((), ())), preferred_element_type=F32)


def by_lanes(left, right):
    return lax.dot_general(left, right, (((1,), (1,)), ((), ())), preferred_element_type=F32)


def round_up(value, unit):
    return (value + unit - 1) // unit * unit


def lane_sum(value):
    return jnp.sum(value, axis=-1, keepdims=True)


def inverse_rms(hidden):
    return lax.rsqrt(lane_sum(hidden * hidden) * (1.0 / hidden.shape[-1]) + epsilon)


def weave(*tasks):
    tasks = [(list(task)) for task in tasks]
    longest = max(len(task) for task in tasks)
    done = [0] * len(tasks)
    for turn in range(longest):
        for which, task in enumerate(tasks):
            until = (turn + 1) * len(task) // longest
            while done[which] < until:
                task[done[which]]()
                done[which] += 1


def cuts(length, unit=160):
    return [(start, min(start + unit, length)) for start in range(0, length, unit)]


class Sizes:
    def __init__(self, steps, rows, blocks, width, bins, table_rows, parts):
        self.steps, self.rows, self.blocks, self.width = steps, rows, blocks, width
        self.bins, self.table_rows, self.parts = bins, table_rows, parts
        self.calls = 2 * blocks
        self.pair = 2 if steps % 2 == 0 else 1
        self.wide = round_up(bins, 32)
        self.held = round_up(table_rows, 16)
        self.stack = (self.wide + self.held, 2 * self.wide + self.held)
        self.depth = tuple(round_up(rows_in, LANES) for rows_in in self.stack)
        half = self.wide // 2
        self.value_at = self.calls * width
        self.sums_at = self.value_at + self.wide
        self.kinds = 2 * self.calls
        self.gain_row = self.kinds + 1
        self.reward_at = self.sums_at + round_up(self.gain_row + blocks, 16)
        self.small_at = self.reward_at + half
        self.cond_at = self.small_at + self.held
        self.shared_end = self.cond_at + self.held
        self.total = round_up(self.shared_end, 16 * parts)
        self.head_rows = self.cond_at - self.value_at


def unroll_kernel(
    sizes, tower_ref,
    root_hbm, lengths_hbm, actions_hbm, codes_hbm, policy_hbm, value_bins_hbm, reward_bins_hbm,
    table_hbm, gains_hbm, in_hbm, out_hbm, value_hbm, reward_hbm, small_hbm,
    root_any, in_got, out_got, value_any, gains_got,
    lat_own, lat_away, loss, own, away, root_own_grad, root_away_grad,
    lat, entry, after, slope, side, dlat, turned, gains,
    root_own, root_got, lengths, actions, codes, policy, value_bins, reward_bins,
    table_in, gains_own, value_own, value_got, reward_in, small_in, sems,
    state, past0, past1, table, weights, heads0, heads1, acc0, acc1,
    logits0, logits1, cot0, cot1, sums, squares,
    carry, gain_sum, cond_sum, grads, inverse_gains, d_after_kept, d_before_kept, d_hidden_kept,
):
    turn = pl.program_id(0)
    turns = sizes.steps // sizes.pair

    @pl.when(turn < turns)
    def _():
        forward_turn(
            sizes, turn, tower_ref,
            root_hbm, lengths_hbm, actions_hbm, codes_hbm, policy_hbm, value_bins_hbm,
            reward_bins_hbm, table_hbm, gains_hbm, in_hbm, out_hbm, value_hbm, reward_hbm,
            small_hbm, root_any, in_got, out_got, value_any, gains_got,
            lat, lat_own, lat_away, entry, after, slope, side, dlat, loss, turned, gains,
            root_own, root_got, lengths, actions, codes, policy, value_bins, reward_bins,
            table_in, gains_own, value_own, value_got, reward_in, small_in, sems,
            state, past0, past1, table, weights, heads0, heads1, acc0, acc1,
            logits0, logits1, cot0, cot1, sums, squares,
        )

    @pl.when(turn >= turns)
    def _():
        backward_turn(
            sizes, turn - turns, tower_ref,
            lat, entry, after, slope, side, dlat, actions, codes, turned, acc0, acc1, sums,
            own, away, root_own_grad, root_away_grad,
            carry, gain_sum, cond_sum, grads, gains, inverse_gains, d_after_kept, d_before_kept,
            d_hidden_kept,
        )


def forward_turn(
    sizes, turn, tower_ref,
    root_hbm, lengths_hbm, actions_hbm, codes_hbm, policy_hbm, value_bins_hbm, reward_bins_hbm,
    table_hbm, gains_hbm, in_hbm, out_hbm, value_hbm, reward_hbm, small_hbm,
    root_any, in_got, out_got, value_any, gains_got,
    lat, lat_own, lat_away, entry, after, slope, side, dlat, loss, turned, gains,
    root_own, root_got, lengths, actions, codes, policy, value_bins, reward_bins,
    table_in, gains_own, value_own, value_got, reward_in, small_in, sems,
    state, past0, past1, table, weights, heads0, heads1, acc0, acc1,
    logits0, logits1, cot0, cot1, sums, squares,
):
    s = sizes
    pair = s.pair
    first_step = turn * pair
    tower_id = tower_ref[0]
    rows, width, wide = s.rows, s.width, s.wide

    @pl.when(turn == 0)
    def _():
        here = pl.ds(pl.multiple_of(tower_id * rows, rows), rows)

        def matrices(kind, tower):
            return weights.at[pl.ds(kind * s.calls + tower * s.blocks, s.blocks)]

        moves = [
            (in_hbm, matrices(0, tower_id)),
            (out_hbm, matrices(1, tower_id)),
            (in_got, matrices(0, 1 - tower_id)),
            (out_got, matrices(1, 1 - tower_id)),
            (value_hbm, value_own),
            (value_any, value_got),
            (reward_hbm, reward_in),
            (small_hbm, small_in),
            (table_hbm, table_in),
            (gains_hbm, gains_own),
            (root_hbm.at[here], root_own),
            (root_any.at[here], root_got),
            (actions_hbm.at[:, here], actions),
            (codes_hbm.at[:, here], codes),
            (lengths_hbm.at[:, here], lengths),
            (policy_hbm.at[:, here], policy),
            (value_bins_hbm.at[:, :, here], value_bins),
            (reward_bins_hbm.at[:, here], reward_bins),
        ]
        moves = [
            pltpu.make_async_copy(source, target, sems.at[place])
            for place, (source, target) in enumerate(moves)
        ]
        for move in moves:
            move.start()
        gains[...] = jnp.ones_like(gains)
        for target in (
            table, heads0, heads1, past0, past1, cot0, cot1, acc0, acc1, sums, squares, loss
        ):
            target[...] = jnp.zeros_like(target)
        for move in moves:
            move.wait()
        first = tower_id == 0
        state[:, 0 : width // 2] = jnp.where(first, root_own[...], root_got[...])
        state[:, width // 2 : width] = jnp.where(first, root_got[...], root_own[...])
        gains[tower_id, 0 : s.blocks, :] = gains_own[...].astype(F32)
        gains[1 - tower_id, 0 : s.blocks, :] = gains_got[...].astype(F32)
        table[0 : s.table_rows, :] = table_in[...]
        heads0[0 : s.bins, :] = jnp.where(first, value_own[...], value_got[...])
        heads1[0 : s.bins, :] = jnp.where(first, value_got[...], value_own[...])
        heads1[wide : wide + s.bins, :] = reward_in[...]
        heads0[wide : wide + s.table_rows, :] = small_in[...]
        heads1[2 * wide : 2 * wide + s.table_rows, :] = small_in[...]

    eights = lax.broadcasted_iota(jnp.int32, (8, pair * rows), 0)
    before = jnp.maximum(first_step - pair, 0)

    def pair_row(kind, at_step, lead=()):
        return jnp.concatenate(
            [kind[(pl.ds(at_step + offset, 1),) + lead] for offset in range(pair)], axis=1
        )

    def live_rows(at_step):
        return jnp.concatenate(
            [(at_step + offset < lengths[...]).astype(F32) for offset in range(pair)], axis=1
        )

    kinds = []
    for offset in range(pair):
        step = first_step + offset
        kinds.append((step < lengths[...]).astype(F32))
        kinds.append(actions[pl.ds(step, 1), :].astype(F32))
        kinds.append((codes[pl.ds(step, 1), :] + ACTIONS).astype(F32))
    kinds.append(jnp.zeros((8 - len(kinds), rows), F32))
    columns = jnp.concatenate(kinds, axis=0).T

    def heads(tower, live_row, at_step, put):
        latent = past0 if tower == 0 else past1
        stack, logits, cot, acc = (
            (heads0, logits0, cot0, acc0) if tower == 0 else (heads1, logits1, cot1, acc1)
        )
        pick = lambda kind: pair_row(kind, at_step)
        value_goal = pair_row(value_bins, at_step, (tower,))
        spans = [(0, wide, 0, s.bins, value_goal)]
        if tower == 1:
            spans.append((wide, wide, 0, s.bins, pick(reward_bins)))
            spans.append((2 * wide, s.held, 0, ACTIONS, pick(policy)))
        else:
            spans.append((wide, s.held, ACTIONS, s.table_rows, pick(codes) + ACTIONS))

        def make_logits(start, stop):
            logits[start:stop, :] = by_lanes(stack[start:stop, :], latent[...])

        def eight_rows(value):
            return value.reshape(-1, 8, pair * rows)

        def mask(at, length, first, last):
            for start in range(0, length, 8):
                if start < first or start + 8 > last:
                    inside = (eights >= first - start) & (eights < last - start)
                    place = slice(at + start, at + start + 8)
                    logits[place, :] = jnp.where(inside, logits[place, :], very_negative)

        def find_top(at, start, stop, kept):
            top = jnp.max(eight_rows(logits[at + start : at + stop, :]), axis=0)
            kept["top"] = jnp.maximum(kept["top"], top) if "top" in kept else top

        def end_top(kept):
            kept["top"] = jnp.max(kept["top"], axis=0, keepdims=True)

        def make_terms(at, start, stop, goal, kept):
            place = slice(at + start, at + stop)
            value = logits[place, :]
            spot = lax.broadcasted_iota(jnp.int32, value.shape, 0)
            term = jnp.exp(value - kept["top"])
            logits[place, :] = term
            hit = spot == goal - start
            total = jnp.sum(eight_rows(term), axis=0)
            picked = jnp.sum(eight_rows(jnp.where(hit, value, 0.0)), axis=0)
            kept["total"] = kept["total"] + total if "total" in kept else total
            kept["picked"] = kept["picked"] + picked if "picked" in kept else picked

        def end_terms(kept):
            total = jnp.sum(kept["total"], axis=0, keepdims=True)
            picked = jnp.sum(kept["picked"], axis=0, keepdims=True)
            kept["scale"] = live_row / total
            row_loss = live_row * (jnp.log(total) + kept["top"] - picked)
            for offset in range(pair):
                loss[0:1, :] += row_loss[:, offset * rows : (offset + 1) * rows]

        def make_cotangent(at, start, stop, goal, kept):
            place = slice(at + start, at + stop)
            term = logits[place, :]
            spot = lax.broadcasted_iota(jnp.int32, term.shape, 0)
            hit = spot == goal - start
            cot[place, :] = (term * kept["scale"] - jnp.where(hit, live_row, 0.0)).astype(BF16)

        def make_grads(start, stop):
            acc[start:stop, :] += natural(cot[start:stop, :], latent[...])

        def make_latent():
            d_latent = by_rows(cot[...], stack[...])
            for offset in range(pair):
                put[at_step + offset, tower] = d_latent[offset * rows : (offset + 1) * rows]

        large = cuts(acc.shape[0], 320)
        pieces = [functools.partial(make_logits, *cut) for cut in large]
        for at, length, first, last, goal in spans:
            kept = {}
            each = cuts(length)
            pieces.append(functools.partial(mask, at, length, first, last))
            pieces += [functools.partial(find_top, at, *cut, kept) for cut in each]
            pieces.append(functools.partial(end_top, kept))
            pieces += [functools.partial(make_terms, at, *cut, goal, kept) for cut in each]
            pieces.append(functools.partial(end_terms, kept))
            pieces += [functools.partial(make_cotangent, at, *cut, goal, kept) for cut in each]
        return pieces + [make_latent] + [functools.partial(make_grads, *cut) for cut in large]

    def columns_of(offset, tower):
        live = columns[:, 3 * offset : 3 * offset + 1]
        return live, columns[:, 3 * offset + 1 + tower : 3 * offset + 2 + tower]

    def embedding(offset, tower):
        _, code = columns_of(offset, tower)
        spot = lax.broadcasted_iota(jnp.int32, (rows, table.shape[0]), 1)
        onehot = jnp.where(spot.astype(F32) == code, 1.0, 0.0).astype(BF16)
        return natural(onehot, table[...])

    def tower_call(offset, tower, chain):
        live, _ = columns_of(offset, tower)

        def scale_rows():
            row_squares = lane_sum(chain["hidden"] * chain["hidden"])
            return row_squares, lax.rsqrt(row_squares * (1.0 / width) + epsilon)

        def keep_squares(block, row_squares):
            place = 2 * (tower * s.blocks + block)
            total = jnp.sum(live * row_squares, axis=0, keepdims=True) * (1.0 / LANES)
            squares[offset, place : place + 1, 0:LANES] = jnp.broadcast_to(total, (1, LANES))

        def end_block(block):
            branch = chain["product"]
            chain["hidden"] = chain["hidden"] + branch
            return branch

        def keep_branch(block, branch):
            spot = 2 * (tower * s.blocks + block) + 1
            squares[offset, spot : spot + 1, :] = jnp.sum(
                branch * branch * live, axis=0, keepdims=True
            )

        def into(block):
            place = tower * s.blocks + block
            if block > 0:
                branch = end_block(block - 1)
            gained = chain["hidden"] * gains[tower, block : block + 1, :]
            chain["product"] = natural(gained.astype(BF16), weights[place])
            row_squares, inv_scale = scale_rows()
            chain["scale"] = inv_scale
            entry[first_step + offset, place] = (gained * inv_scale).astype(BF16)
            side[first_step + offset, place] = jnp.broadcast_to(inv_scale, (rows, LANES))
            if block > 0:
                keep_squares(block - 1, row_squares)
                keep_branch(block - 1, branch)

        def out_of(block):
            place = tower * s.blocks + block
            u = chain["product"] * chain["scale"]
            gate = 0.5 * jnp.tanh(0.5 * u) + 0.5
            after_rows = (u * gate).astype(BF16)
            chain["product"] = natural(after_rows, weights[s.calls + place])
            after[first_step + offset, place] = after_rows
            slope[first_step + offset, place] = gate * (1.0 + u * (1.0 - gate))

        def finish():
            branch = end_block(s.blocks - 1)
            row_squares, inv_scale = scale_rows()
            latent = (chain["hidden"] * inv_scale).astype(BF16)
            chain[offset, tower] = latent
            following = (offset, 1) if tower == 0 else (offset + 1, 0)
            if following in chain:
                chain["hidden"] = latent.astype(F32) + chain[following]

            def keep():
                side[first_step + offset, s.calls + tower] = jnp.broadcast_to(inv_scale, (rows, LANES))
                lat[first_step + offset, tower] = latent
                keep_squares(s.blocks - 1, row_squares)
                keep_branch(s.blocks - 1, branch)
                if tower == 0:
                    total = jnp.sum(live, axis=0, keepdims=True) * (1.0 / LANES)
                    squares[offset, s.kinds : s.kinds + 1, 0:LANES] = jnp.broadcast_to(
                        total, (1, LANES)
                    )

            return keep

        pieces = []
        for block in range(s.blocks):
            pieces += [functools.partial(into, block), functools.partial(out_of, block)]
        return pieces, finish

    chain = {
        (offset, tower): embedding(offset, tower) for offset in range(pair) for tower in range(2)
    }
    chain["hidden"] = state[...].astype(F32) + chain[0, 0]
    pieces = []
    keeps = []

    def begin_next(finish, into):
        keeps.append(finish())
        into()
        keeps.pop()()

    ending = None
    for offset in range(pair):
        for tower in range(2):
            calls, finish = tower_call(offset, tower, chain)
            if ending is not None:
                calls[0] = functools.partial(begin_next, ending, calls[0])
            pieces += calls
            ending = finish
    pieces.append(lambda: ending()())

    turns = -(-2 * s.calls // (s.steps // pair))

    def turn_weights(which):
        matrix = jnp.minimum(turn * turns + which, 2 * s.calls - 1)
        turned[matrix] = weights[matrix].T

    live_before = jnp.where(turn > 0, live_rows(before), 0.0)
    weave(
        pieces,
        heads(1, live_before, before, dlat)
        + heads(0, live_before, before, dlat)
        + [functools.partial(turn_weights, which) for which in range(turns)],
    )
    first = tower_id == 0
    at_lane = lax.broadcasted_iota(jnp.int32, sums.shape, 1)
    for offset in range(pair):
        at = slice(offset * rows, (offset + 1) * rows)
        after_state, next_state = chain[offset, 0], chain[offset, 1]
        past0[at, :] = after_state
        past1[at, :] = next_state
        lat_own[offset] = jnp.where(first, after_state, next_state)
        lat_away[offset] = jnp.where(first, next_state, after_state)
        if offset == pair - 1:
            state[...] = next_state
        total = lane_sum(squares[offset])
        sums[...] = jnp.where(at_lane == first_step + offset, total, sums[...])

    @pl.when(turn == s.steps // pair - 1)
    def _():
        live_now = live_rows(first_step)
        weave(heads(1, live_now, first_step, dlat), heads(0, live_now, first_step, dlat))


def backward_turn(
    sizes, turn, tower_ref,
    lat, entry, after, slope, side, dlat, actions, codes, turned, acc0, acc1, sums,
    own, away, root_own, root_away,
    carry, gain_sum, cond_sum, grads, gains, inverse_gains, d_after_kept, d_before_kept,
    d_hidden_kept,
):
    s = sizes
    pair = s.pair
    first_step = s.steps - pair * (turn + 1)
    tower_id = tower_ref[0]
    blocks, width = s.blocks, s.width

    @pl.when(turn == 0)
    def _():
        inverse_gains[...] = 1.0 / gains[...]
        carry[...] = jnp.zeros_like(carry)
        grads[...] = jnp.zeros_like(grads)
        gain_sum[...] = jnp.zeros_like(gain_sum)
        cond_sum[...] = jnp.zeros_like(cond_sum)

    def over_lanes(column):
        return jnp.concatenate([column] * (width // LANES), axis=1)

    def stacked(parts):
        return jnp.concatenate(parts, axis=0)

    def add_grads(matrix, rows_of, place, kept, now):
        later = [kept[offset, place] for offset in range(1, pair)]
        grads[matrix // s.calls, matrix % s.calls] += by_rows(
            stacked([rows_of[first_step + offset, place] for offset in range(pair)]), stacked([now] + later)
        )

    def add_cond(offset, tower, d_hidden):
        if offset > 0:
            d_hidden_kept[offset, tower] = d_hidden.astype(BF16)
            return
        codes_of, shift = (actions, 0) if tower == 0 else (codes, ACTIONS)
        code = jnp.concatenate(
            [codes_of[pl.ds(first_step + step, 1), :] + shift for step in range(pair)], axis=1
        )
        spots = lax.broadcasted_iota(jnp.int32, (cond_sum.shape[0], pair * s.rows), 0)
        onehot = jnp.where(spots == code, 1.0, 0.0).astype(BF16)
        parts = [d_hidden.astype(BF16)]
        parts += [d_hidden_kept[step, tower] for step in range(1, pair)]
        cond_sum[...] += natural(onehot, stacked(parts))

    behind = []

    def catch_up():
        while behind:
            behind.pop(0)()

    def tower_back(offset, tower, d_latent):
        normed = lat[first_step + offset, tower]
        normed_wide = normed.astype(F32)
        inv_scale = over_lanes(side[first_step + offset, s.calls + tower])
        base = inv_scale * d_latent
        slant = inv_scale * (lane_sum(d_latent * normed_wide) * (1.0 / width))
        for block in reversed(range(blocks)):
            place = tower * blocks + block
            matrix = tower * s.calls + block
            both = natural(
                jnp.concatenate([normed, base.astype(BF16)], axis=0), turned[s.calls + place]
            )
            d_hidden = base - slant * normed_wide
            d_branch = d_hidden.astype(BF16)
            entry_wide = entry[first_step + offset, place].astype(F32)
            inv_scale = over_lanes(side[first_step + offset, place])
            catch_up()
            d_after = both[s.rows :] - slant * both[: s.rows]
            d_before = (d_after * slope[first_step + offset, place]).astype(BF16)
            d_entry = natural(d_before, turned[place])
            if offset > 0:
                d_after_kept[offset, place] = d_branch
                d_before_kept[offset, place] = d_before
            else:
                add_grads(matrix + blocks, after, place, d_after_kept, d_branch)
                behind.append(
                    functools.partial(add_grads, matrix, entry, place, d_before_kept, d_before)
                )
            gain = gains[tower, block : block + 1, :]
            normed_wide = entry_wide * inverse_gains[tower, block : block + 1, :]
            normed = normed_wide.astype(BF16)
            product = d_entry * entry_wide
            base = d_hidden + inv_scale * (d_entry * gain)
            slant = inv_scale * (lane_sum(product) * (1.0 / width))

            def add_gain(tower=tower, block=block, product=product):
                gain_sum[tower, block : block + 1, :] += jnp.sum(product, axis=0, keepdims=True)

            behind.append(add_gain)
        d_hidden = base - slant * normed_wide
        behind.append(functools.partial(add_cond, offset, tower, d_hidden))
        return d_hidden

    def from_heads(offset, tower):
        return jnp.where(turn == 0, dlast[offset, tower], dlat[first_step + offset, tower])

    d_state = carry[...]
    for offset in reversed(range(pair)):
        for tower in (1, 0):
            d_state = tower_back(offset, tower, d_state + dlat[first_step + offset, tower])
    catch_up()
    carry[...] = d_state

    @pl.when(turn == s.steps // pair - 1)
    def _():
        left = d_state[:, 0 : width // 2].astype(BF16)
        right = d_state[:, width // 2 : width].astype(BF16)
        root_own[...] = jnp.where(tower_id == 0, left, right)
        root_away[...] = jnp.where(tower_id == 0, right, left)
        gain_sum[...] = gain_sum[...] * inverse_gains[...]
        wide, half = s.wide, s.wide // 2
        lines = lax.broadcasted_iota(jnp.int32, sums.shape, 0)
        small = acc0[wide : wide + s.held, :] + acc1[2 * wide : 2 * wide + s.held, :]
        for target, which in ((own, tower_id), (away, 1 - tower_id)):
            first = which == 0
            for matrix in range(s.calls):
                at = matrix * width
                target[at : at + width, :] = grads[which, matrix].astype(BF16)
            for start, stop in cuts(wide):
                value = jnp.where(first, acc0[start:stop, :], acc1[start:stop, :])
                target[s.value_at + start : s.value_at + stop, :] = value.astype(BF16)
            for start, stop in cuts(half):
                reward = jnp.where(
                    first,
                    acc1[wide + start : wide + stop, :],
                    acc1[wide + half + start : wide + half + stop, :],
                )
                target[s.reward_at + start : s.reward_at + stop, :] = reward.astype(BF16)
            here = jnp.where(first, small, 0.0)
            target[s.small_at : s.small_at + s.held, :] = here.astype(BF16)
            here = jnp.where(first, cond_sum[...], 0.0)
            target[s.cond_at : s.shared_end, :] = here.astype(BF16)
            kept = sums[...]
            for block in range(blocks):
                gain = gain_sum[which, block : block + 1, 0:LANES]
                kept = jnp.where(lines == s.gain_row + block, gain, kept)
            target[s.sums_at : s.reward_at, 0:LANES] = kept.astype(BF16)
            kept = jnp.zeros_like(kept)
            for block in range(blocks):
                gain = gain_sum[which, block : block + 1, LANES:]
                kept = jnp.where(lines == s.gain_row + block, gain, kept)
            target[s.sums_at : s.reward_at, LANES:] = kept.astype(BF16)
            if s.total > s.shared_end:
                target[s.shared_end :, :] = jnp.zeros((s.total - s.shared_end, width), BF16)


def logits_kernel(sizes, tower_ref, lat_own, lat_got, value_own, latents, logits):
    rows = sizes.rows
    tower_id = tower_ref[0]
    at_own = pl.ds(pl.multiple_of(tower_id * rows, rows), rows)
    at_got = pl.ds(pl.multiple_of((1 - tower_id) * rows, rows), rows)
    for offset in range(sizes.pair):
        latents[offset, at_own, :] = lat_own[offset]
        latents[offset, at_got, :] = lat_got[offset]
        logits[offset] = by_lanes(value_own[...], latents[offset]).astype(BF16)


def add_and_split_kernel(count, digit_ref, *refs):
    inputs, outputs = refs[:count], refs[count:]
    digit = digit_ref[0]
    for other, target in enumerate(outputs):
        part = digit ^ other
        total = inputs[0][part].astype(F32)
        for source in inputs[1:]:
            total = total + source[part].astype(F32)
        target[...] = total.astype(BF16)


def unpack_own_kernel(sizes, scalars, *refs):
    s = sizes
    factor = len(refs) - 7
    digit, tower_id = scalars[0], scalars[1]
    w_in, w_out, value, gain, rms, flat, held = refs[factor:]
    width = s.width
    length = refs[0].shape[0]
    for other, source in enumerate(refs[:factor]):
        at = pl.multiple_of((digit ^ other) * length, 16)
        flat[pl.ds(at, length), :] = source[...]
    for block in range(s.blocks):
        at = block * width
        w_in[block] = flat[at : at + width, :].astype(F32)
        at = (s.blocks + block) * width
        w_out[block] = flat[at : at + width, :].astype(F32)
    value[:, 0, :] = flat[s.value_at : s.sums_at, :].astype(F32)[0 : s.bins]
    sums = flat[s.sums_at : s.reward_at, :].astype(F32)
    for block in range(s.blocks):
        gain[block] = sums[s.gain_row + block : s.gain_row + block + 1, :]
    held[...] = sums[:, 0:LANES]
    count = jnp.maximum(held[s.kinds : s.kinds + 1, 0 : s.steps], 1.0)
    for block in range(s.blocks):
        for kind in range(2):
            spot = tower_id * s.calls + 2 * block + kind
            square = held[pl.ds(spot, 1), 0 : s.steps]
            rms[block, kind : kind + 1, :] = jnp.sqrt(jnp.maximum(square, 0.0) / (count * width))


def unpack_shared_kernel(sizes, tower_ref, mine, got, reward, small, cond, joined):
    s = sizes
    tower_id = tower_ref[0]
    half = s.wide // 2
    joined[pl.ds(pl.multiple_of(tower_id * half, 8), half), :] = mine[0:half, :].astype(F32)
    joined[pl.ds(pl.multiple_of((1 - tower_id) * half, 8), half), :] = got[0:half, :].astype(F32)
    reward[...] = joined[0 : s.bins, :]
    for target, at in ((small, s.small_at), (cond, s.cond_at)):
        rows = slice(at - s.reward_at, at - s.reward_at + s.held)
        target[...] = (mine[rows, :].astype(F32) + got[rows, :].astype(F32))[0 : s.table_rows]


def whole(shape):
    return pl.BlockSpec(shape, lambda step, tower: (0,) * len(shape))


def swap(value, axis, mask):
    pairs = [(source, source ^ mask) for source in range(lax.axis_size(axis))]
    return lax.ppermute(value, axis, pairs)


AXES = ("tower", "batch")


def exchange_rounds(batch_size):
    factors, left = [], batch_size
    while left > 1:
        factors.append(4 if left % 4 == 0 else 2)
        left //= factors[-1]
    rounds, stride = [], 1
    for factor in factors:
        rounds.append((factor, stride))
        stride *= factor
    turned = rounds[::-1] if len(set(factors)) == 1 else rounds
    return [(one[0], (one[1], two[1])) for one, two in zip(rounds, turned)]


def swap_within(value, strides, other, batch_size):
    pairs = [
        (tower * batch_size + index, tower * batch_size + (index ^ (other * strides[tower])))
        for tower in range(2)
        for index in range(batch_size)
    ]
    return lax.ppermute(value, AXES, pairs)


def my_digit(factor, strides):
    stride = jnp.where(lax.axis_index("tower") == 0, strides[0], strides[1])
    return (lax.axis_index("batch") // stride) % factor


def add_kernel(*refs):
    total = refs[0][...].astype(F32)
    for source in refs[1:-1]:
        total = total + source[...].astype(F32)
    refs[-1][...] = total.astype(BF16)


def add_up(parts):
    return pl.pallas_call(
        add_kernel,
        out_shape=jax.ShapeDtypeStruct(parts[0].shape, BF16),
        compiler_params=pltpu.CompilerParams(vmem_limit_bytes=SMALL_LIMIT),
        name="add_up",
    )(*parts)


def exchange(value, rounds, batch_size, beside, given, last_kernel):
    factor, strides = rounds[0]
    digit = my_digit(factor, strides)
    rows, width = value[0].shape
    rows = rows // factor
    split = pl.pallas_call(
        functools.partial(add_and_split_kernel, len(value)),
        grid_spec=pltpu.PrefetchScalarGridSpec(
            num_scalar_prefetch=1,
            grid=(1,),
            in_specs=[whole((factor, rows, width))] * len(value),
            out_specs=[whole((rows, width))] * factor,
        ),
        out_shape=[pltpu.HBM((rows, width), BF16)] * factor,
        compiler_params=pltpu.CompilerParams(vmem_limit_bytes=SMALL_LIMIT),
        name="add_and_split",
    )(digit[None], *[part.reshape(factor, rows, width) for part in value])
    split, given = lax.optimization_barrier((split, given))
    held = [split[0]] + [
        swap_within(split[other], strides, other, batch_size) for other in range(1, factor)
    ]
    done = beside(given)
    held, done = lax.optimization_barrier((held, done))
    for size, steps in rounds[1:]:
        bit = 1
        while bit < size:
            block = add_up(held)
            held = [block, swap_within(block, steps, bit, batch_size)]
            bit *= 2
    block = add_up(held)
    held = [block] + [
        swap_within(block, strides, other, batch_size) for other in range(1, factor)
    ]
    return last_kernel(digit, held), done


def body(
    root_state, cond_table, block_gain, w_in, w_out, value_head, reward_head, small_head,
    unroll_len, actions, codes, policy_target, value_bins, reward_bins,
):
    tower_id = lax.axis_index("tower")
    other_id = 1 - tower_id
    tower_ref = tower_id.astype(jnp.int32)[None]
    steps, batch_rows = actions.shape
    blocks, width = block_gain.shape[1:]
    bins = value_head.shape[2]
    table_rows = cond_table.shape[0]
    rows = batch_rows // 2
    half = width // 2
    parts = lax.axis_size("batch")
    s = Sizes(steps, rows, blocks, width, bins, table_rows, parts)
    calls, wide, pair = s.calls, s.wide, s.pair

    root_got = swap(root_state, "tower", 1)
    in_own, out_own, gains_own = w_in[0], w_out[0], block_gain[0]
    value_own = value_head[0].T
    in_got = swap(in_own, "tower", 1)
    out_got = swap(out_own, "tower", 1)
    gains_got = swap(gains_own, "tower", 1)
    value_got = swap(value_own, "tower", 1)
    lengths = unroll_len.reshape(1, batch_rows)

    shape = jax.ShapeDtypeStruct
    per_pair = lambda *tail: pl.BlockSpec(
        (pair,) + tail, lambda turn, tower: (turn,) + (0,) * len(tail)
    )
    unroll_params = pltpu.CompilerParams(vmem_limit_bytes=UNROLL_LIMIT)
    small_params = pltpu.CompilerParams(vmem_limit_bytes=SMALL_LIMIT)
    products = steps * rows * (4 * blocks * width * width + 9 * width * wide)
    cost = pl.CostEstimate(flops=2 * products, bytes_accessed=40 * 2**20, transcendentals=0)
    turns = steps // pair
    paired = pl.BlockSpec(
        (pair, rows, width), lambda turn, tower: (jnp.minimum(turn, turns - 1), 0, 0)
    )
    lat_own, lat_away, loss, own, away, root_own, root_away = pl.pallas_call(
        functools.partial(unroll_kernel, s),
        grid_spec=pltpu.PrefetchScalarGridSpec(
            num_scalar_prefetch=1,
            grid=(2 * turns,),
            in_specs=[pl.BlockSpec(memory_space=pltpu.HBM)] * 14
            + [pl.BlockSpec(memory_space=pl.ANY)] * 4
            + [whole((blocks, width))],
            out_specs=[
                paired,
                paired,
                whole((8, rows)),
                whole((s.total, width)),
                whole((s.total, width)),
                whole((rows, half)),
                whole((rows, half)),
            ],
            scratch_shapes=[
                pltpu.VMEM((steps, 2, rows, width), BF16),
                pltpu.VMEM((steps, calls, rows, width), BF16),
                pltpu.VMEM((steps, calls, rows, width), BF16),
                pltpu.VMEM((steps, calls, rows, width), F32),
                pltpu.VMEM((steps, calls + 2, rows, LANES), F32),
                pltpu.VMEM((steps, 2, rows, width), F32),
                pltpu.VMEM((2 * calls, width, width), BF16),
                pltpu.VMEM((2, 16, width), F32),
                pltpu.VMEM((rows, half), BF16),
                pltpu.VMEM((rows, half), BF16),
                pltpu.VMEM((1, rows), jnp.int32),
                pltpu.VMEM((steps, rows), jnp.int32),
                pltpu.VMEM((steps, rows), jnp.int32),
                pltpu.VMEM((steps, rows), jnp.int32),
                pltpu.VMEM((steps, 2, rows), jnp.int32),
                pltpu.VMEM((steps, rows), jnp.int32),
                pltpu.VMEM((table_rows, width), BF16),
                pltpu.VMEM((blocks, width), BF16),
                pltpu.VMEM((bins, width), BF16),
                pltpu.VMEM((bins, width), BF16),
                pltpu.VMEM((bins, width), BF16),
                pltpu.VMEM((table_rows, width), BF16),
                pltpu.SemaphoreType.DMA((18,)),
                pltpu.VMEM((rows, width), BF16),
                pltpu.VMEM((pair * rows, width), BF16),
                pltpu.VMEM((pair * rows, width), BF16),
                pltpu.VMEM((LANES, width), BF16),
                pltpu.VMEM((2 * calls, width, width), BF16),
                pltpu.VMEM((s.depth[0], width), BF16),
                pltpu.VMEM((s.depth[1], width), BF16),
                pltpu.VMEM((s.stack[0], width), F32),
                pltpu.VMEM((s.stack[1], width), F32),
                pltpu.VMEM((s.stack[0], pair * rows), F32),
                pltpu.VMEM((s.stack[1], pair * rows), F32),
                pltpu.VMEM((s.depth[0], pair * rows), BF16),
                pltpu.VMEM((s.depth[1], pair * rows), BF16),
                pltpu.VMEM((s.reward_at - s.sums_at, LANES), F32),
                pltpu.VMEM((pair, s.reward_at - s.sums_at, width), F32),
                pltpu.VMEM((rows, width), F32),
                pltpu.VMEM((2, 16, width), F32),
                pltpu.VMEM((s.held, width), F32),
                pltpu.VMEM((2, calls, width, width), F32),
                pltpu.VMEM((2, 16, width), F32),
                pltpu.VMEM((pair, calls, rows, width), BF16),
                pltpu.VMEM((pair, calls, rows, width), BF16),
                pltpu.VMEM((pair, 2, rows, width), BF16),
            ],
        ),
        out_shape=[
            pltpu.HBM((steps, rows, width), BF16),
            pltpu.HBM((steps, rows, width), BF16),
            shape((8, rows), F32),
            shape((s.total, width), BF16),
            shape((s.total, width), BF16),
            shape((rows, half), BF16),
            shape((rows, half), BF16),
        ],
        compiler_params=unroll_params,
        cost_estimate=cost,
        name="unroll",
    )(
        tower_ref,
        *[
            pltpu.with_memory_space_constraint(value, pltpu.HBM)
            for value in (
                root_state, lengths, actions, codes, policy_target,
                jnp.swapaxes(value_bins, 0, 1), reward_bins, cond_table, gains_own,
                in_own, out_own, value_own, reward_head.T, small_head.T,
            )
        ],
        root_got, in_got, out_got, value_got, gains_got,
    )
    got = swap(away, "tower", 1)

    def beside(given):
        lat_own, lat_away, loss, root_own, root_away = given
        lat_got = swap(lat_away, "tower", 1)
        loss_own = loss[0]
        loss_got = swap(loss_own, "tower", 1)
        root_got = swap(root_away, "tower", 1)

        latents, logits = pl.pallas_call(
            functools.partial(logits_kernel, s),
            grid_spec=pltpu.PrefetchScalarGridSpec(
                num_scalar_prefetch=1,
                grid=(steps // pair,),
                in_specs=[per_pair(rows, width), per_pair(rows, width), whole((bins, width))],
                out_specs=[per_pair(batch_rows, width), per_pair(bins, batch_rows)],
            ),
            out_shape=[
                shape((steps, batch_rows, width), BF16),
                shape((steps, bins, batch_rows), BF16),
            ],
            compiler_params=small_params,
            cost_estimate=pl.CostEstimate(
                flops=2 * steps * batch_rows * width * wide, bytes_accessed=6 * 2**20, transcendentals=0
            ),
            name="latents_and_logits",
        )(
            tower_ref,
            *[
                pltpu.with_memory_space_constraint(part, pltpu.HBM)
                for part in (lat_own, lat_got, value_own)
            ],
        )

        def in_order(mine_value, got_value, axis):
            return jnp.where(
                tower_id == 0,
                jnp.concatenate([mine_value, got_value], axis=axis),
                jnp.concatenate([got_value, mine_value], axis=axis),
            )

        row_loss = in_order(loss_own, loss_got, 0)
        grad_root = in_order(root_own, root_got, 0).astype(F32)
        return latents, logits, row_loss, grad_root

    rounds = exchange_rounds(parts)

    def unpack(digit, held):
        scalars = jnp.stack([digit, tower_id]).astype(jnp.int32)
        length = held[0].shape[0]
        block = s.reward_at // length
        at = s.reward_at - block * length
        parts_of = [part[at : at + s.shared_end - s.reward_at] for part in held]
        shared = parts_of[0]
        for other in range(1, len(held)):
            shared = jnp.where((digit ^ other) == block, parts_of[other], shared)
        shared_got = swap(shared, "tower", 1)
        return (shared, shared_got), pl.pallas_call(
            functools.partial(unpack_own_kernel, s),
            grid_spec=pltpu.PrefetchScalarGridSpec(
                num_scalar_prefetch=1,
                grid=(1,),
                in_specs=[whole(part.shape) for part in held],
                out_specs=[
                    whole((blocks, width, width)),
                    whole((blocks, width, width)),
                    whole((bins, 1, width)),
                    whole((blocks, 1, width)),
                    whole((blocks, 2, steps)),
                ],
                scratch_shapes=[
                    pltpu.VMEM((s.total, width), BF16),
                    pltpu.VMEM((s.reward_at - s.sums_at, LANES), F32),
                ],
            ),
            out_shape=[
                shape((blocks, width, width), F32),
                shape((blocks, width, width), F32),
                shape((bins, 1, width), F32),
                shape((blocks, 1, width), F32),
                shape((blocks, 2, steps), F32),
            ],
            compiler_params=small_params,
            name="unpack_own",
        )(scalars, *held)

    given = (lat_own, lat_away, loss, root_own, root_away)
    unpacked, done = exchange([own, got], rounds, parts, beside, given, unpack)
    (shared, shared_got), (grad_in, grad_out, value_t, gain_t, rms_t) = unpacked
    latents, logits, row_loss, grad_root = done
    reward_t, small_t, grad_cond = pl.pallas_call(
        functools.partial(unpack_shared_kernel, s),
        grid_spec=pltpu.PrefetchScalarGridSpec(
            num_scalar_prefetch=1,
            grid=(1,),
            in_specs=[whole(shared.shape), whole(shared.shape)],
            out_specs=[
                whole((bins, width)),
                whole((table_rows, width)),
                whole((table_rows, width)),
            ],
            scratch_shapes=[pltpu.VMEM((s.wide, width), F32)],
        ),
        out_shape=[
            shape((bins, width), F32),
            shape((table_rows, width), F32),
            shape((table_rows, width), F32),
        ],
        compiler_params=small_params,
        name="unpack_shared",
    )(tower_ref, shared, shared_got)
    layer_rms = jnp.transpose(rms_t, (2, 0, 1))[None]
    return (
        latents[None],
        jnp.swapaxes(logits, 1, 2)[None],
        row_loss,
        layer_rms,
        grad_root,
        grad_cond,
        jnp.swapaxes(gain_t, 0, 1),
        grad_in[None],
        grad_out[None],
        jnp.transpose(value_t, (1, 2, 0)),
        reward_t.T,
        small_t.T,
    )


def solution(mesh):
    placed = (
        P("batch", "tower"),
        P(),
        P("tower", None, None),
        P("tower", None, None, None),
        P("tower", None, None, None),
        P("tower", None, None),
        P(),
        P(),
        P("batch"),
        P(None, "batch"),
        P(None, "batch"),
        P(None, "batch"),
        P(None, None, "batch"),
        P(None, "batch"),
    )
    return jax.shard_map(
        body,
        mesh=mesh,
        in_specs=placed,
        out_specs=(
            P("tower", None, "batch", None),
            P("tower", None, "batch", None),
            P("batch"),
            P("tower", None, None, None),
            P("batch", "tower"),
            P(),
            P("tower", None, None),
            P("tower", None, None, None),
            P("tower", None, None, None),
            P("tower", None, None),
            P(),
            P(),
        ),
        check_vma=False,
    )
```

```python
import functools

import jax
import jax.numpy as jnp
from jax import lax
from jax.experimental import pallas as pl
from jax.experimental.pallas import tpu as pltpu
from jax.sharding import PartitionSpec as P

ACTIONS = 4
LANES = 128
MIB = 1024 * 1024
UNROLL_LIMIT = 58 * MIB
SMALL_LIMIT = 12 * MIB
epsilon = 1e-06
very_negative = -1e30
F32 = jnp.float32
BF16 = jnp.bfloat16


def natural(left, right):
    return lax.dot_general(left, right, (((1,), (0,)), ((), ())), preferred_element_type=F32)


def by_rows(left, right):
    return lax.dot_general(left, right, (((0,), (0,)), ((), ())), preferred_element_type=F32)


def by_lanes(left, right):
    return lax.dot_general(left, right, (((1,), (1,)), ((), ())), preferred_element_type=F32)


def round_up(value, unit):
    return (value + unit - 1) // unit * unit


def lane_sum(value):
    return jnp.sum(value, axis=-1, keepdims=True)


def inverse_rms(hidden):
    return lax.rsqrt(lane_sum(hidden * hidden) * (1.0 / hidden.shape[-1]) + epsilon)


def weave(*tasks):
    tasks = [(list(task)) for task in tasks]
    longest = max(len(task) for task in tasks)
    done = [0] * len(tasks)
    for turn in range(longest):
        for which, task in enumerate(tasks):
            until = (turn + 1) * len(task) // longest
            while done[which] < until:
                task[done[which]]()
                done[which] += 1


def cuts(length, unit=160):
    return [(start, min(start + unit, length)) for start in range(0, length, unit)]


class Sizes:
    def __init__(self, steps, rows, blocks, width, bins, table_rows, parts):
        self.steps, self.rows, self.blocks, self.width = steps, rows, blocks, width
        self.bins, self.table_rows, self.parts = bins, table_rows, parts
        self.calls = 2 * blocks
        self.pair = 2 if steps % 2 == 0 else 1
        self.wide = round_up(bins, 32)
        self.held = round_up(table_rows, 16)
        self.stack = (self.wide + self.held, 2 * self.wide + self.held)
        self.depth = tuple(round_up(rows_in, LANES) for rows_in in self.stack)
        half = self.wide // 2
        self.value_at = self.calls * width
        self.sums_at = self.value_at + self.wide
        self.kinds = 2 * self.calls
        self.gain_row = self.kinds + 1
        self.reward_at = self.sums_at + round_up(self.gain_row + blocks, 16)
        self.small_at = self.reward_at + half
        self.cond_at = self.small_at + self.held
        self.shared_end = self.cond_at + self.held
        self.total = round_up(self.shared_end, 16 * parts)
        self.head_rows = self.cond_at - self.value_at


def unroll_kernel(
    sizes, tower_ref,
    root_hbm, lengths_hbm, actions_hbm, codes_hbm, policy_hbm, value_bins_hbm, reward_bins_hbm,
    table_hbm, gains_hbm, in_hbm, out_hbm, value_hbm, reward_hbm, small_hbm,
    root_any, in_got, out_got, value_any, gains_got,
    lat_own, lat_away, loss, own, away, root_own_grad, root_away_grad,
    lat, entry, after, slope, side, dlat, turned, gains,
    root_own, root_got, lengths, actions, codes, policy, value_bins, reward_bins,
    table_in, gains_own, value_own, value_got, reward_in, small_in, sems,
    state, past0, past1, table, weights, heads0, heads1, acc0, acc1,
    logits0, logits1, cot0, cot1, sums, squares,
    carry, gain_sum, cond_sum, grads, inverse_gains, d_after_kept, d_before_kept, d_hidden_kept,
):
    turns = sizes.steps // sizes.pair
    for turn in range(turns):
        forward_turn(
            sizes, turn, tower_ref,
            root_hbm, lengths_hbm, actions_hbm, codes_hbm, policy_hbm, value_bins_hbm,
            reward_bins_hbm, table_hbm, gains_hbm, in_hbm, out_hbm, value_hbm, reward_hbm,
            small_hbm, root_any, in_got, out_got, value_any, gains_got,
            lat, lat_own, lat_away, entry, after, slope, side, dlat, loss, turned, gains,
            root_own, root_got, lengths, actions, codes, policy, value_bins, reward_bins,
            table_in, gains_own, value_own, value_got, reward_in, small_in, sems,
            state, past0, past1, table, weights, heads0, heads1, acc0, acc1,
            logits0, logits1, cot0, cot1, sums, squares,
        )
    for turn in range(turns):
        backward_turn(
            sizes, turn, tower_ref,
            lat, entry, after, slope, side, dlat, actions, codes, turned, acc0, acc1, sums,
            own, away, root_own_grad, root_away_grad,
            carry, gain_sum, cond_sum, grads, gains, inverse_gains, d_after_kept, d_before_kept,
            d_hidden_kept,
        )


def forward_turn(
    sizes, turn, tower_ref,
    root_hbm, lengths_hbm, actions_hbm, codes_hbm, policy_hbm, value_bins_hbm, reward_bins_hbm,
    table_hbm, gains_hbm, in_hbm, out_hbm, value_hbm, reward_hbm, small_hbm,
    root_any, in_got, out_got, value_any, gains_got,
    lat, lat_own, lat_away, entry, after, slope, side, dlat, loss, turned, gains,
    root_own, root_got, lengths, actions, codes, policy, value_bins, reward_bins,
    table_in, gains_own, value_own, value_got, reward_in, small_in, sems,
    state, past0, past1, table, weights, heads0, heads1, acc0, acc1,
    logits0, logits1, cot0, cot1, sums, squares,
):
    s = sizes
    pair = s.pair
    first_step = turn * pair
    tower_id = tower_ref[0]
    rows, width, wide = s.rows, s.width, s.wide

    if turn == 0:
        here = pl.ds(pl.multiple_of(tower_id * rows, rows), rows)

        def matrices(kind, tower):
            return weights.at[pl.ds(kind * s.calls + tower * s.blocks, s.blocks)]

        moves = [
            (in_hbm, matrices(0, tower_id)),
            (out_hbm, matrices(1, tower_id)),
            (in_got, matrices(0, 1 - tower_id)),
            (out_got, matrices(1, 1 - tower_id)),
            (value_hbm, value_own),
            (value_any, value_got),
            (reward_hbm, reward_in),
            (small_hbm, small_in),
            (table_hbm, table_in),
            (gains_hbm, gains_own),
            (root_hbm.at[here], root_own),
            (root_any.at[here], root_got),
            (actions_hbm.at[:, here], actions),
            (codes_hbm.at[:, here], codes),
            (lengths_hbm.at[:, here], lengths),
            (policy_hbm.at[:, here], policy),
            (value_bins_hbm.at[:, :, here], value_bins),
            (reward_bins_hbm.at[:, here], reward_bins),
        ]
        moves = [
            pltpu.make_async_copy(source, target, sems.at[place])
            for place, (source, target) in enumerate(moves)
        ]
        for move in moves:
            move.start()
        gains[...] = jnp.ones_like(gains)
        for target in (
            table, heads0, heads1, past0, past1, cot0, cot1, acc0, acc1, sums, squares, loss
        ):
            target[...] = jnp.zeros_like(target)
        for move in moves:
            move.wait()
        first = tower_id == 0
        state[:, 0 : width // 2] = jnp.where(first, root_own[...], root_got[...])
        state[:, width // 2 : width] = jnp.where(first, root_got[...], root_own[...])
        gains[tower_id, 0 : s.blocks, :] = gains_own[...].astype(F32)
        gains[1 - tower_id, 0 : s.blocks, :] = gains_got[...].astype(F32)
        table[0 : s.table_rows, :] = table_in[...]
        heads0[0 : s.bins, :] = jnp.where(first, value_own[...], value_got[...])
        heads1[0 : s.bins, :] = jnp.where(first, value_got[...], value_own[...])
        heads1[wide : wide + s.bins, :] = reward_in[...]
        heads0[wide : wide + s.table_rows, :] = small_in[...]
        heads1[2 * wide : 2 * wide + s.table_rows, :] = small_in[...]

    eights = lax.broadcasted_iota(jnp.int32, (8, pair * rows), 0)
    before = first_step - pair

    def pair_row(kind, at_step, lead=()):
        return jnp.concatenate(
            [kind[(slice(at_step + offset, at_step + offset + 1),) + lead] for offset in range(pair)],
            axis=1,
        )

    def live_rows(at_step):
        return jnp.concatenate(
            [(at_step + offset < lengths[...]).astype(F32) for offset in range(pair)], axis=1
        )

    kinds = []
    for offset in range(pair):
        step = first_step + offset
        kinds.append((step < lengths[...]).astype(F32))
        kinds.append(actions[step : step + 1, :].astype(F32))
        kinds.append((codes[step : step + 1, :] + ACTIONS).astype(F32))
    kinds.append(jnp.zeros((8 - len(kinds), rows), F32))
    columns = jnp.concatenate(kinds, axis=0).T

    def heads(tower, live_row, at_step, put):
        latent = past0 if tower == 0 else past1
        stack, logits, cot, acc = (
            (heads0, logits0, cot0, acc0) if tower == 0 else (heads1, logits1, cot1, acc1)
        )
        pick = lambda kind: pair_row(kind, at_step)
        value_goal = pair_row(value_bins, at_step, (tower,))
        spans = [(0, wide, 0, s.bins, value_goal)]
        if tower == 1:
            spans.append((wide, wide, 0, s.bins, pick(reward_bins)))
            spans.append((2 * wide, s.held, 0, ACTIONS, pick(policy)))
        else:
            spans.append((wide, s.held, ACTIONS, s.table_rows, pick(codes) + ACTIONS))

        def make_logits(start, stop):
            logits[start:stop, :] = by_lanes(stack[start:stop, :], latent[...])

        def eight_rows(value):
            return value.reshape(-1, 8, pair * rows)

        def mask(at, length, first, last):
            for start in range(0, length, 8):
                if start < first or start + 8 > last:
                    inside = (eights >= first - start) & (eights < last - start)
                    place = slice(at + start, at + start + 8)
                    logits[place, :] = jnp.where(inside, logits[place, :], very_negative)

        def find_top(at, start, stop, kept):
            top = jnp.max(eight_rows(logits[at + start : at + stop, :]), axis=0)
            kept["top"] = jnp.maximum(kept["top"], top) if "top" in kept else top

        def end_top(kept):
            kept["top"] = jnp.max(kept["top"], axis=0, keepdims=True)

        def make_terms(at, start, stop, goal, kept):
            place = slice(at + start, at + stop)
            value = logits[place, :]
            spot = lax.broadcasted_iota(jnp.int32, value.shape, 0)
            term = jnp.exp(value - kept["top"])
            logits[place, :] = term
            hit = spot == goal - start
            total = jnp.sum(eight_rows(term), axis=0)
            picked = jnp.sum(eight_rows(jnp.where(hit, value, 0.0)), axis=0)
            kept["total"] = kept["total"] + total if "total" in kept else total
            kept["picked"] = kept["picked"] + picked if "picked" in kept else picked

        def end_terms(kept):
            total = jnp.sum(kept["total"], axis=0, keepdims=True)
            picked = jnp.sum(kept["picked"], axis=0, keepdims=True)
            kept["scale"] = live_row / total
            row_loss = live_row * (jnp.log(total) + kept["top"] - picked)
            for offset in range(pair):
                loss[0:1, :] += row_loss[:, offset * rows : (offset + 1) * rows]

        def make_cotangent(at, start, stop, goal, kept):
            place = slice(at + start, at + stop)
            term = logits[place, :]
            spot = lax.broadcasted_iota(jnp.int32, term.shape, 0)
            hit = spot == goal - start
            cot[place, :] = (term * kept["scale"] - jnp.where(hit, live_row, 0.0)).astype(BF16)

        def make_grads(start, stop):
            acc[start:stop, :] += natural(cot[start:stop, :], latent[...])

        def make_latent():
            d_latent = by_rows(cot[...], stack[...])
            for offset in range(pair):
                put[at_step + offset, tower] = d_latent[offset * rows : (offset + 1) * rows]

        large = cuts(acc.shape[0], 320)
        pieces = [functools.partial(make_logits, *cut) for cut in large]
        for at, length, first, last, goal in spans:
            kept = {}
            each = cuts(length)
            pieces.append(functools.partial(mask, at, length, first, last))
            pieces += [functools.partial(find_top, at, *cut, kept) for cut in each]
            pieces.append(functools.partial(end_top, kept))
            pieces += [functools.partial(make_terms, at, *cut, goal, kept) for cut in each]
            pieces.append(functools.partial(end_terms, kept))
            pieces += [functools.partial(make_cotangent, at, *cut, goal, kept) for cut in each]
        return pieces + [make_latent] + [functools.partial(make_grads, *cut) for cut in large]

    def columns_of(offset, tower):
        live = columns[:, 3 * offset : 3 * offset + 1]
        return live, columns[:, 3 * offset + 1 + tower : 3 * offset + 2 + tower]

    def embedding(offset, tower):
        _, code = columns_of(offset, tower)
        spot = lax.broadcasted_iota(jnp.int32, (rows, table.shape[0]), 1)
        onehot = jnp.where(spot.astype(F32) == code, 1.0, 0.0).astype(BF16)
        return natural(onehot, table[...])

    def tower_call(offset, tower, chain):
        live, _ = columns_of(offset, tower)

        def scale_rows():
            row_squares = lane_sum(chain["hidden"] * chain["hidden"])
            return row_squares, lax.rsqrt(row_squares * (1.0 / width) + epsilon)

        def keep_squares(block, row_squares):
            place = 2 * (tower * s.blocks + block)
            total = jnp.sum(live * row_squares, axis=0, keepdims=True) * (1.0 / LANES)
            squares[first_step + offset, place : place + 1, 0:LANES] = jnp.broadcast_to(total, (1, LANES))

        def end_block(block):
            branch = chain["product"]
            chain["hidden"] = chain["hidden"] + branch
            return branch

        def keep_branch(block, branch):
            spot = 2 * (tower * s.blocks + block) + 1
            squares[first_step + offset, spot : spot + 1, :] = jnp.sum(
                branch * branch * live, axis=0, keepdims=True
            )

        def into(block):
            place = tower * s.blocks + block
            if block > 0:
                branch = end_block(block - 1)
            gained = chain["hidden"] * gains[tower, block : block + 1, :]
            chain["product"] = natural(gained.astype(BF16), weights[place])
            row_squares, inv_scale = scale_rows()
            chain["scale"] = inv_scale
            entry[first_step + offset, place] = (gained * inv_scale).astype(BF16)
            side[first_step + offset, place] = jnp.broadcast_to(inv_scale, (rows, LANES))
            if block > 0:
                keep_squares(block - 1, row_squares)
                keep_branch(block - 1, branch)

        def out_of(block):
            place = tower * s.blocks + block
            u = chain["product"] * chain["scale"]
            gate = 0.5 * jnp.tanh(0.5 * u) + 0.5
            after_rows = (u * gate).astype(BF16)
            chain["product"] = natural(after_rows, weights[s.calls + place])
            after[first_step + offset, place] = after_rows
            slope[first_step + offset, place] = (gate * (1.0 + u * (1.0 - gate))).astype(BF16)

        def finish():
            branch = end_block(s.blocks - 1)
            row_squares, inv_scale = scale_rows()
            latent = (chain["hidden"] * inv_scale).astype(BF16)
            chain[offset, tower] = latent
            following = (offset, 1) if tower == 0 else (offset + 1, 0)
            if following in chain:
                chain["hidden"] = latent.astype(F32) + chain[following]

            def keep():
                side[first_step + offset, s.calls + tower] = jnp.broadcast_to(inv_scale, (rows, LANES))
                lat[first_step + offset, tower] = latent
                keep_squares(s.blocks - 1, row_squares)
                keep_branch(s.blocks - 1, branch)
                if tower == 0:
                    total = jnp.sum(live, axis=0, keepdims=True) * (1.0 / LANES)
                    squares[first_step + offset, s.kinds : s.kinds + 1, 0:LANES] = jnp.broadcast_to(
                        total, (1, LANES)
                    )

            return keep

        pieces = []
        for block in range(s.blocks):
            pieces += [functools.partial(into, block), functools.partial(out_of, block)]
        return pieces, finish

    chain = {
        (offset, tower): embedding(offset, tower) for offset in range(pair) for tower in range(2)
    }
    chain["hidden"] = state[...].astype(F32) + chain[0, 0]
    pieces = []
    keeps = []

    def begin_next(finish, into):
        keeps.append(finish())
        into()
        keeps.pop()()

    ending = None
    for offset in range(pair):
        for tower in range(2):
            calls, finish = tower_call(offset, tower, chain)
            if ending is not None:
                calls[0] = functools.partial(begin_next, ending, calls[0])
            pieces += calls
            ending = finish
    pieces.append(lambda: ending()())

    turns = -(-2 * s.calls // (s.steps // pair))

    def turn_weights(matrix):
        turned[matrix] = weights[matrix].T

    beside = []
    if turn > 0:
        live_before = live_rows(before)
        beside += heads(1, live_before, before, dlat) + heads(0, live_before, before, dlat)
    matrices_now = range(turn * turns, min((turn + 1) * turns, 2 * s.calls))
    beside += [functools.partial(turn_weights, matrix) for matrix in matrices_now]
    weave(pieces, beside)
    first = tower_id == 0
    at_lane = lax.broadcasted_iota(jnp.int32, sums.shape, 1)
    for offset in range(pair):
        at = slice(offset * rows, (offset + 1) * rows)
        after_state, next_state = chain[offset, 0], chain[offset, 1]
        past0[at, :] = after_state
        past1[at, :] = next_state
        lat_own[first_step + offset] = jnp.where(first, after_state, next_state)
        lat_away[first_step + offset] = jnp.where(first, next_state, after_state)
        if offset == pair - 1:
            state[...] = next_state
        total = lane_sum(squares[first_step + offset])
        sums[...] = jnp.where(at_lane == first_step + offset, total, sums[...])

    if turn == s.steps // pair - 1:
        live_now = live_rows(first_step)
        for piece in heads(1, live_now, first_step, dlat) + heads(0, live_now, first_step, dlat):
            piece()


def backward_turn(
    sizes, turn, tower_ref,
    lat, entry, after, slope, side, dlat, actions, codes, turned, acc0, acc1, sums,
    own, away, root_own, root_away,
    carry, gain_sum, cond_sum, grads, gains, inverse_gains, d_after_kept, d_before_kept,
    d_hidden_kept,
):
    s = sizes
    pair = s.pair
    first_step = s.steps - pair * (turn + 1)
    tower_id = tower_ref[0]
    blocks, width = s.blocks, s.width

    if turn == 0:
        inverse_gains[...] = 1.0 / gains[...]
        carry[...] = jnp.zeros_like(carry)
        grads[...] = jnp.zeros_like(grads)
        gain_sum[...] = jnp.zeros_like(gain_sum)
        cond_sum[...] = jnp.zeros_like(cond_sum)

    def over_lanes(column):
        return jnp.concatenate([column] * (width // LANES), axis=1)

    def stacked(parts):
        return jnp.concatenate(parts, axis=0)

    def add_grads(matrix, rows_of, place, kept, now):
        later = [kept[offset, place] for offset in range(1, pair)]
        grads[matrix // s.calls, matrix % s.calls] += by_rows(
            stacked([rows_of[first_step + offset, place] for offset in range(pair)]), stacked([now] + later)
        )

    def add_cond(offset, tower, d_hidden):
        if offset > 0:
            d_hidden_kept[offset, tower] = d_hidden.astype(BF16)
            return
        codes_of, shift = (actions, 0) if tower == 0 else (codes, ACTIONS)
        code = jnp.concatenate(
            [
                codes_of[first_step + step : first_step + step + 1, :] + shift
                for step in range(pair)
            ],
            axis=1,
        )
        spots = lax.broadcasted_iota(jnp.int32, (cond_sum.shape[0], pair * s.rows), 0)
        onehot = jnp.where(spots == code, 1.0, 0.0).astype(BF16)
        parts = [d_hidden.astype(BF16)]
        parts += [d_hidden_kept[step, tower] for step in range(1, pair)]
        cond_sum[...] += natural(onehot, stacked(parts))

    behind = []

    def catch_up():
        while behind:
            behind.pop(0)()

    def tower_back(offset, tower, d_latent):
        normed = lat[first_step + offset, tower]
        normed_wide = normed.astype(F32)
        inv_scale = over_lanes(side[first_step + offset, s.calls + tower])
        base = inv_scale * d_latent
        slant = inv_scale * (lane_sum(d_latent * normed_wide) * (1.0 / width))
        for block in reversed(range(blocks)):
            place = tower * blocks + block
            matrix = tower * s.calls + block
            both = natural(
                jnp.concatenate([normed, base.astype(BF16)], axis=0), turned[s.calls + place]
            )
            d_hidden = base - slant * normed_wide
            d_branch = d_hidden.astype(BF16)
            entry_wide = entry[first_step + offset, place].astype(F32)
            inv_scale = over_lanes(side[first_step + offset, place])
            catch_up()
            d_after = both[s.rows :] - slant * both[: s.rows]
            d_before = (d_after * slope[first_step + offset, place].astype(F32)).astype(BF16)
            d_entry = natural(d_before, turned[place])
            if offset > 0:
                d_after_kept[offset, place] = d_branch
                d_before_kept[offset, place] = d_before
            else:
                add_grads(matrix + blocks, after, place, d_after_kept, d_branch)
                behind.append(
                    functools.partial(add_grads, matrix, entry, place, d_before_kept, d_before)
                )
            gain = gains[tower, block : block + 1, :]
            normed_wide = entry_wide * inverse_gains[tower, block : block + 1, :]
            normed = normed_wide.astype(BF16)
            product = d_entry * entry_wide
            base = d_hidden + inv_scale * (d_entry * gain)
            slant = inv_scale * (lane_sum(product) * (1.0 / width))

            def add_gain(tower=tower, block=block, product=product):
                gain_sum[tower, block : block + 1, :] += jnp.sum(product, axis=0, keepdims=True)

            behind.append(add_gain)
        d_hidden = base - slant * normed_wide
        behind.append(functools.partial(add_cond, offset, tower, d_hidden))
        return d_hidden

    def from_heads(offset, tower):
        return jnp.where(turn == 0, dlast[offset, tower], dlat[first_step + offset, tower])

    d_state = carry[...]
    for offset in reversed(range(pair)):
        for tower in (1, 0):
            d_state = tower_back(offset, tower, d_state + dlat[first_step + offset, tower])
    catch_up()
    carry[...] = d_state

    if turn == s.steps // pair - 1:
        left = d_state[:, 0 : width // 2].astype(BF16)
        right = d_state[:, width // 2 : width].astype(BF16)
        root_own[...] = jnp.where(tower_id == 0, left, right)
        root_away[...] = jnp.where(tower_id == 0, right, left)
        gain_sum[...] = gain_sum[...] * inverse_gains[...]
        wide, half = s.wide, s.wide // 2
        lines = lax.broadcasted_iota(jnp.int32, sums.shape, 0)
        small = acc0[wide : wide + s.held, :] + acc1[2 * wide : 2 * wide + s.held, :]
        for target, which in ((own, tower_id), (away, 1 - tower_id)):
            first = which == 0
            for matrix in range(s.calls):
                at = matrix * width
                target[at : at + width, :] = grads[which, matrix].astype(BF16)
            for start, stop in cuts(wide):
                value = jnp.where(first, acc0[start:stop, :], acc1[start:stop, :])
                target[s.value_at + start : s.value_at + stop, :] = value.astype(BF16)
            for start, stop in cuts(half):
                reward = jnp.where(
                    first,
                    acc1[wide + start : wide + stop, :],
                    acc1[wide + half + start : wide + half + stop, :],
                )
                target[s.reward_at + start : s.reward_at + stop, :] = reward.astype(BF16)
            here = jnp.where(first, small, 0.0)
            target[s.small_at : s.small_at + s.held, :] = here.astype(BF16)
            here = jnp.where(first, cond_sum[...], 0.0)
            target[s.cond_at : s.shared_end, :] = here.astype(BF16)
            kept = sums[...]
            for block in range(blocks):
                gain = gain_sum[which, block : block + 1, 0:LANES]
                kept = jnp.where(lines == s.gain_row + block, gain, kept)
            target[s.sums_at : s.reward_at, 0:LANES] = kept.astype(BF16)
            kept = jnp.zeros_like(kept)
            for block in range(blocks):
                gain = gain_sum[which, block : block + 1, LANES:]
                kept = jnp.where(lines == s.gain_row + block, gain, kept)
            target[s.sums_at : s.reward_at, LANES:] = kept.astype(BF16)
            if s.total > s.shared_end:
                target[s.shared_end :, :] = jnp.zeros((s.total - s.shared_end, width), BF16)


def logits_kernel(sizes, tower_ref, lat_own, lat_got, value_own, latents, logits):
    rows = sizes.rows
    tower_id = tower_ref[0]
    at_own = pl.ds(pl.multiple_of(tower_id * rows, rows), rows)
    at_got = pl.ds(pl.multiple_of((1 - tower_id) * rows, rows), rows)
    for offset in range(sizes.pair):
        latents[offset, at_own, :] = lat_own[offset]
        latents[offset, at_got, :] = lat_got[offset]
        logits[offset] = by_lanes(value_own[...], latents[offset]).astype(BF16)


def add_and_split_kernel(count, digit_ref, *refs):
    inputs, outputs = refs[:count], refs[count:]
    digit = digit_ref[0]
    for other, target in enumerate(outputs):
        part = digit ^ other
        total = inputs[0][part].astype(F32)
        for source in inputs[1:]:
            total = total + source[part].astype(F32)
        target[...] = total.astype(BF16)


def unpack_own_kernel(sizes, scalars, *refs):
    s = sizes
    factor = len(refs) - 7
    digit, tower_id = scalars[0], scalars[1]
    w_in, w_out, value, gain, rms, flat, held = refs[factor:]
    width = s.width
    length = refs[0].shape[0]
    for other, source in enumerate(refs[:factor]):
        at = pl.multiple_of((digit ^ other) * length, 16)
        flat[pl.ds(at, length), :] = source[...]
    for block in range(s.blocks):
        at = block * width
        w_in[block] = flat[at : at + width, :].astype(F32)
        at = (s.blocks + block) * width
        w_out[block] = flat[at : at + width, :].astype(F32)
    value[:, 0, :] = flat[s.value_at : s.sums_at, :].astype(F32)[0 : s.bins]
    sums = flat[s.sums_at : s.reward_at, :].astype(F32)
    for block in range(s.blocks):
        gain[block] = sums[s.gain_row + block : s.gain_row + block + 1, :]
    held[...] = sums[:, 0:LANES]
    count = jnp.maximum(held[s.kinds : s.kinds + 1, 0 : s.steps], 1.0)
    for block in range(s.blocks):
        for kind in range(2):
            spot = tower_id * s.calls + 2 * block + kind
            square = held[pl.ds(spot, 1), 0 : s.steps]
            rms[block, kind : kind + 1, :] = jnp.sqrt(jnp.maximum(square, 0.0) / (count * width))


def unpack_shared_kernel(sizes, tower_ref, mine, got, reward, small, cond, joined):
    s = sizes
    tower_id = tower_ref[0]
    half = s.wide // 2
    joined[pl.ds(pl.multiple_of(tower_id * half, 8), half), :] = mine[0:half, :].astype(F32)
    joined[pl.ds(pl.multiple_of((1 - tower_id) * half, 8), half), :] = got[0:half, :].astype(F32)
    reward[...] = joined[0 : s.bins, :]
    for target, at in ((small, s.small_at), (cond, s.cond_at)):
        rows = slice(at - s.reward_at, at - s.reward_at + s.held)
        target[...] = (mine[rows, :].astype(F32) + got[rows, :].astype(F32))[0 : s.table_rows]


def whole(shape):
    return pl.BlockSpec(shape, lambda step, tower: (0,) * len(shape))


def swap(value, axis, mask):
    pairs = [(source, source ^ mask) for source in range(lax.axis_size(axis))]
    return lax.ppermute(value, axis, pairs)


AXES = ("tower", "batch")


def exchange_rounds(batch_size):
    factors, left = [], batch_size
    while left > 1:
        factors.append(4 if left % 4 == 0 else 2)
        left //= factors[-1]
    rounds, stride = [], 1
    for factor in factors:
        rounds.append((factor, stride))
        stride *= factor
    turned = rounds[::-1] if len(set(factors)) == 1 else rounds
    return [(one[0], (one[1], two[1])) for one, two in zip(rounds, turned)]


def swap_within(value, strides, other, batch_size):
    pairs = [
        (tower * batch_size + index, tower * batch_size + (index ^ (other * strides[tower])))
        for tower in range(2)
        for index in range(batch_size)
    ]
    return lax.ppermute(value, AXES, pairs)


def my_digit(factor, strides):
    stride = jnp.where(lax.axis_index("tower") == 0, strides[0], strides[1])
    return (lax.axis_index("batch") // stride) % factor


def add_kernel(*refs):
    total = refs[0][...].astype(F32)
    for source in refs[1:-1]:
        total = total + source[...].astype(F32)
    refs[-1][...] = total.astype(BF16)


def add_up(parts):
    return pl.pallas_call(
        add_kernel,
        out_shape=jax.ShapeDtypeStruct(parts[0].shape, BF16),
        compiler_params=pltpu.CompilerParams(vmem_limit_bytes=SMALL_LIMIT),
        name="add_up",
    )(*parts)


def exchange(value, rounds, batch_size, beside, given, last_kernel):
    factor, strides = rounds[0]
    digit = my_digit(factor, strides)
    rows, width = value[0].shape
    rows = rows // factor
    split = pl.pallas_call(
        functools.partial(add_and_split_kernel, len(value)),
        grid_spec=pltpu.PrefetchScalarGridSpec(
            num_scalar_prefetch=1,
            grid=(1,),
            in_specs=[whole((factor, rows, width))] * len(value),
            out_specs=[whole((rows, width))] * factor,
        ),
        out_shape=[pltpu.HBM((rows, width), BF16)] * factor,
        compiler_params=pltpu.CompilerParams(vmem_limit_bytes=SMALL_LIMIT),
        name="add_and_split",
    )(digit[None], *[part.reshape(factor, rows, width) for part in value])
    split, given = lax.optimization_barrier((split, given))
    held = [split[0]] + [
        swap_within(split[other], strides, other, batch_size) for other in range(1, factor)
    ]
    done = beside(given)
    held, done = lax.optimization_barrier((held, done))
    for size, steps in rounds[1:]:
        bit = 1
        while bit < size:
            block = add_up(held)
            held = [block, swap_within(block, steps, bit, batch_size)]
            bit *= 2
    block = add_up(held)
    held = [block] + [
        swap_within(block, strides, other, batch_size) for other in range(1, factor)
    ]
    return last_kernel(digit, held), done


def body(
    root_state, cond_table, block_gain, w_in, w_out, value_head, reward_head, small_head,
    unroll_len, actions, codes, policy_target, value_bins, reward_bins,
):
    tower_id = lax.axis_index("tower")
    other_id = 1 - tower_id
    tower_ref = tower_id.astype(jnp.int32)[None]
    steps, batch_rows = actions.shape
    blocks, width = block_gain.shape[1:]
    bins = value_head.shape[2]
    table_rows = cond_table.shape[0]
    rows = batch_rows // 2
    half = width // 2
    parts = lax.axis_size("batch")
    s = Sizes(steps, rows, blocks, width, bins, table_rows, parts)
    calls, wide, pair = s.calls, s.wide, s.pair

    root_got = swap(root_state, "tower", 1)
    in_own, out_own, gains_own = w_in[0], w_out[0], block_gain[0]
    value_own = value_head[0].T
    in_got = swap(in_own, "tower", 1)
    out_got = swap(out_own, "tower", 1)
    gains_got = swap(gains_own, "tower", 1)
    value_got = swap(value_own, "tower", 1)
    lengths = unroll_len.reshape(1, batch_rows)

    shape = jax.ShapeDtypeStruct
    per_pair = lambda *tail: pl.BlockSpec(
        (pair,) + tail, lambda turn, tower: (turn,) + (0,) * len(tail)
    )
    unroll_params = pltpu.CompilerParams(vmem_limit_bytes=UNROLL_LIMIT)
    small_params = pltpu.CompilerParams(vmem_limit_bytes=SMALL_LIMIT)
    products = steps * rows * (4 * blocks * width * width + 9 * width * wide)
    cost = pl.CostEstimate(flops=2 * products, bytes_accessed=40 * 2**20, transcendentals=0)
    lat_own, lat_away, loss, own, away, root_own, root_away = pl.pallas_call(
        functools.partial(unroll_kernel, s),
        grid_spec=pltpu.PrefetchScalarGridSpec(
            num_scalar_prefetch=1,
            grid=(1,),
            in_specs=[pl.BlockSpec(memory_space=pltpu.HBM)] * 14
            + [pl.BlockSpec(memory_space=pl.ANY)] * 4
            + [whole((blocks, width))],
            out_specs=[
                whole((steps, rows, width)),
                whole((steps, rows, width)),
                whole((8, rows)),
                whole((s.total, width)),
                whole((s.total, width)),
                whole((rows, half)),
                whole((rows, half)),
            ],
            scratch_shapes=[
                pltpu.VMEM((steps, 2, rows, width), BF16),
                pltpu.VMEM((steps, calls, rows, width), BF16),
                pltpu.VMEM((steps, calls, rows, width), BF16),
                pltpu.VMEM((steps, calls, rows, width), BF16),
                pltpu.VMEM((steps, calls + 2, rows, LANES), F32),
                pltpu.VMEM((steps, 2, rows, width), F32),
                pltpu.VMEM((2 * calls, width, width), BF16),
                pltpu.VMEM((2, 16, width), F32),
                pltpu.VMEM((rows, half), BF16),
                pltpu.VMEM((rows, half), BF16),
                pltpu.VMEM((1, rows), jnp.int32),
                pltpu.VMEM((steps, rows), jnp.int32),
                pltpu.VMEM((steps, rows), jnp.int32),
                pltpu.VMEM((steps, rows), jnp.int32),
                pltpu.VMEM((steps, 2, rows), jnp.int32),
                pltpu.VMEM((steps, rows), jnp.int32),
                pltpu.VMEM((table_rows, width), BF16),
                pltpu.VMEM((blocks, width), BF16),
                pltpu.VMEM((bins, width), BF16),
                pltpu.VMEM((bins, width), BF16),
                pltpu.VMEM((bins, width), BF16),
                pltpu.VMEM((table_rows, width), BF16),
                pltpu.SemaphoreType.DMA((18,)),
                pltpu.VMEM((rows, width), BF16),
                pltpu.VMEM((pair * rows, width), BF16),
                pltpu.VMEM((pair * rows, width), BF16),
                pltpu.VMEM((LANES, width), BF16),
                pltpu.VMEM((2 * calls, width, width), BF16),
                pltpu.VMEM((s.depth[0], width), BF16),
                pltpu.VMEM((s.depth[1], width), BF16),
                pltpu.VMEM((s.stack[0], width), F32),
                pltpu.VMEM((s.stack[1], width), F32),
                pltpu.VMEM((s.stack[0], pair * rows), F32),
                pltpu.VMEM((s.stack[1], pair * rows), F32),
                pltpu.VMEM((s.depth[0], pair * rows), BF16),
                pltpu.VMEM((s.depth[1], pair * rows), BF16),
                pltpu.VMEM((s.reward_at - s.sums_at, LANES), F32),
                pltpu.VMEM((steps, s.reward_at - s.sums_at, width), F32),
                pltpu.VMEM((rows, width), F32),
                pltpu.VMEM((2, 16, width), F32),
                pltpu.VMEM((s.held, width), F32),
                pltpu.VMEM((2, calls, width, width), F32),
                pltpu.VMEM((2, 16, width), F32),
                pltpu.VMEM((pair, calls, rows, width), BF16),
                pltpu.VMEM((pair, calls, rows, width), BF16),
                pltpu.VMEM((pair, 2, rows, width), BF16),
            ],
        ),
        out_shape=[
            pltpu.HBM((steps, rows, width), BF16),
            pltpu.HBM((steps, rows, width), BF16),
            shape((8, rows), F32),
            shape((s.total, width), BF16),
            shape((s.total, width), BF16),
            shape((rows, half), BF16),
            shape((rows, half), BF16),
        ],
        compiler_params=unroll_params,
        cost_estimate=cost,
        name="unroll",
    )(
        tower_ref,
        *[
            pltpu.with_memory_space_constraint(value, pltpu.HBM)
            for value in (
                root_state, lengths, actions, codes, policy_target,
                jnp.swapaxes(value_bins, 0, 1), reward_bins, cond_table, gains_own,
                in_own, out_own, value_own, reward_head.T, small_head.T,
            )
        ],
        root_got, in_got, out_got, value_got, gains_got,
    )
    got = swap(away, "tower", 1)

    def beside(given):
        lat_own, lat_away, loss, root_own, root_away = given
        lat_got = swap(lat_away, "tower", 1)
        loss_own = loss[0]
        loss_got = swap(loss_own, "tower", 1)
        root_got = swap(root_away, "tower", 1)

        latents, logits = pl.pallas_call(
            functools.partial(logits_kernel, s),
            grid_spec=pltpu.PrefetchScalarGridSpec(
                num_scalar_prefetch=1,
                grid=(steps // pair,),
                in_specs=[per_pair(rows, width), per_pair(rows, width), whole((bins, width))],
                out_specs=[per_pair(batch_rows, width), per_pair(bins, batch_rows)],
            ),
            out_shape=[
                shape((steps, batch_rows, width), BF16),
                shape((steps, bins, batch_rows), BF16),
            ],
            compiler_params=small_params,
            cost_estimate=pl.CostEstimate(
                flops=2 * steps * batch_rows * width * wide, bytes_accessed=6 * 2**20, transcendentals=0
            ),
            name="latents_and_logits",
        )(
            tower_ref,
            *[
                pltpu.with_memory_space_constraint(part, pltpu.HBM)
                for part in (lat_own, lat_got, value_own)
            ],
        )

        def in_order(mine_value, got_value, axis):
            return jnp.where(
                tower_id == 0,
                jnp.concatenate([mine_value, got_value], axis=axis),
                jnp.concatenate([got_value, mine_value], axis=axis),
            )

        row_loss = in_order(loss_own, loss_got, 0)
        grad_root = in_order(root_own, root_got, 0).astype(F32)
        return latents, logits, row_loss, grad_root

    rounds = exchange_rounds(parts)

    def unpack(digit, held):
        scalars = jnp.stack([digit, tower_id]).astype(jnp.int32)
        length = held[0].shape[0]
        block = s.reward_at // length
        at = s.reward_at - block * length
        parts_of = [part[at : at + s.shared_end - s.reward_at] for part in held]
        shared = parts_of[0]
        for other in range(1, len(held)):
            shared = jnp.where((digit ^ other) == block, parts_of[other], shared)
        shared_got = swap(shared, "tower", 1)
        return (shared, shared_got), pl.pallas_call(
            functools.partial(unpack_own_kernel, s),
            grid_spec=pltpu.PrefetchScalarGridSpec(
                num_scalar_prefetch=1,
                grid=(1,),
                in_specs=[whole(part.shape) for part in held],
                out_specs=[
                    whole((blocks, width, width)),
                    whole((blocks, width, width)),
                    whole((bins, 1, width)),
                    whole((blocks, 1, width)),
                    whole((blocks, 2, steps)),
                ],
                scratch_shapes=[
                    pltpu.VMEM((s.total, width), BF16),
                    pltpu.VMEM((s.reward_at - s.sums_at, LANES), F32),
                ],
            ),
            out_shape=[
                shape((blocks, width, width), F32),
                shape((blocks, width, width), F32),
                shape((bins, 1, width), F32),
                shape((blocks, 1, width), F32),
                shape((blocks, 2, steps), F32),
            ],
            compiler_params=small_params,
            name="unpack_own",
        )(scalars, *held)

    given = (lat_own, lat_away, loss, root_own, root_away)
    unpacked, done = exchange([own, got], rounds, parts, beside, given, unpack)
    (shared, shared_got), (grad_in, grad_out, value_t, gain_t, rms_t) = unpacked
    latents, logits, row_loss, grad_root = done
    reward_t, small_t, grad_cond = pl.pallas_call(
        functools.partial(unpack_shared_kernel, s),
        grid_spec=pltpu.PrefetchScalarGridSpec(
            num_scalar_prefetch=1,
            grid=(1,),
            in_specs=[whole(shared.shape), whole(shared.shape)],
            out_specs=[
                whole((bins, width)),
                whole((table_rows, width)),
                whole((table_rows, width)),
            ],
            scratch_shapes=[pltpu.VMEM((s.wide, width), F32)],
        ),
        out_shape=[
            shape((bins, width), F32),
            shape((table_rows, width), F32),
            shape((table_rows, width), F32),
        ],
        compiler_params=small_params,
        name="unpack_shared",
    )(tower_ref, shared, shared_got)
    layer_rms = jnp.transpose(rms_t, (2, 0, 1))[None]
    return (
        latents[None],
        jnp.swapaxes(logits, 1, 2)[None],
        row_loss,
        layer_rms,
        grad_root,
        grad_cond,
        jnp.swapaxes(gain_t, 0, 1),
        grad_in[None],
        grad_out[None],
        jnp.transpose(value_t, (1, 2, 0)),
        reward_t.T,
        small_t.T,
    )


def solution(mesh):
    placed = (
        P("batch", "tower"),
        P(),
        P("tower", None, None),
        P("tower", None, None, None),
        P("tower", None, None, None),
        P("tower", None, None),
        P(),
        P(),
        P("batch"),
        P(None, "batch"),
        P(None, "batch"),
        P(None, "batch"),
        P(None, None, "batch"),
        P(None, "batch"),
    )
    return jax.shard_map(
        body,
        mesh=mesh,
        in_specs=placed,
        out_specs=(
            P("tower", None, "batch", None),
            P("tower", None, "batch", None),
            P("batch"),
            P("tower", None, None, None),
            P("batch", "tower"),
            P(),
            P("tower", None, None),
            P("tower", None, None, None),
            P("tower", None, None, None),
            P("tower", None, None),
            P(),
            P(),
        ),
        check_vma=False,
    )
```

```python
import functools

import jax
import jax.numpy as jnp
from jax import lax
from jax.experimental import pallas as pl
from jax.experimental.pallas import tpu as pltpu
from jax.sharding import PartitionSpec as P

ACTIONS = 4
LANES = 128
MIB = 1024 * 1024
UNROLL_LIMIT = 56 * MIB
SMALL_LIMIT = 12 * MIB
epsilon = 1e-06
very_negative = -1e30
F32 = jnp.float32
BF16 = jnp.bfloat16


def natural(left, right):
    return lax.dot_general(left, right, (((1,), (0,)), ((), ())), preferred_element_type=F32)


def by_rows(left, right):
    return lax.dot_general(left, right, (((0,), (0,)), ((), ())), preferred_element_type=F32)


def by_lanes(left, right):
    return lax.dot_general(left, right, (((1,), (1,)), ((), ())), preferred_element_type=F32)


def round_up(value, unit):
    return (value + unit - 1) // unit * unit


def lane_sum(value):
    return jnp.sum(value, axis=-1, keepdims=True)


def inverse_rms(hidden):
    return lax.rsqrt(lane_sum(hidden * hidden) * (1.0 / hidden.shape[-1]) + epsilon)


def weave(*tasks):
    tasks = [(list(task)) for task in tasks]
    longest = max(len(task) for task in tasks)
    done = [0] * len(tasks)
    for turn in range(longest):
        for which, task in enumerate(tasks):
            until = (turn + 1) * len(task) // longest
            while done[which] < until:
                task[done[which]]()
                done[which] += 1


def cuts(length, unit=160):
    return [(start, min(start + unit, length)) for start in range(0, length, unit)]


class Sizes:
    def __init__(self, steps, rows, blocks, width, bins, table_rows, parts):
        self.steps, self.rows, self.blocks, self.width = steps, rows, blocks, width
        self.bins, self.table_rows, self.parts = bins, table_rows, parts
        self.calls = 2 * blocks
        self.pair = 2 if steps % 2 == 0 else 1
        self.wide = round_up(bins, 32)
        self.held = round_up(table_rows, 16)
        self.stack = (self.wide + self.held, 2 * self.wide + self.held)
        self.depth = tuple(round_up(rows_in, LANES) for rows_in in self.stack)
        half = self.wide // 2
        self.value_at = self.calls * width
        self.sums_at = self.value_at + self.wide
        self.kinds = 2 * self.calls
        self.gain_row = self.kinds + 1
        self.reward_at = self.sums_at + round_up(self.gain_row + blocks, 16)
        self.small_at = self.reward_at + half
        self.cond_at = self.small_at + self.held
        self.shared_end = self.cond_at + self.held
        self.total = round_up(self.shared_end, 16 * parts)
        self.head_rows = self.cond_at - self.value_at


def unroll_kernel(
    sizes, tower_ref,
    root_hbm, lengths_hbm, actions_hbm, codes_hbm, policy_hbm, value_bins_hbm, reward_bins_hbm,
    table_hbm, gains_hbm, in_hbm, out_hbm, value_hbm, reward_hbm, small_hbm,
    root_any, in_got, out_got, value_any, gains_got,
    lat_own, lat_away, loss, own, away, root_own_grad, root_away_grad,
    lat, entry, after, slope, side, dlat, turned, gains, lat_sems,
    root_own, root_got, lengths, actions, codes, policy, value_bins, reward_bins,
    table_in, gains_own, value_own, value_got, reward_in, small_in, sems,
    state, past0, past1, table, weights, heads0, heads1, acc0, acc1,
    logits0, logits1, cot0, cot1, sums, squares,
    carry, gain_sum, cond_sum, grads, inverse_gains, d_after_kept, d_before_kept, d_hidden_kept,
):
    turns = sizes.steps // sizes.pair
    for turn in range(turns):
        forward_turn(
            sizes, turn, tower_ref,
            root_hbm, lengths_hbm, actions_hbm, codes_hbm, policy_hbm, value_bins_hbm,
            reward_bins_hbm, table_hbm, gains_hbm, in_hbm, out_hbm, value_hbm, reward_hbm,
            small_hbm, root_any, in_got, out_got, value_any, gains_got,
            lat, entry, after, slope, side, dlat, loss, turned, gains,
            root_own, root_got, lengths, actions, codes, policy, value_bins, reward_bins,
            table_in, gains_own, value_own, value_got, reward_in, small_in, sems,
            state, past0, past1, table, weights, heads0, heads1, acc0, acc1,
            logits0, logits1, cot0, cot1, sums, squares,
        )
    tower_id = tower_ref[0]
    copies = [
        pltpu.make_async_copy(lat.at[:, tower_id], lat_own, lat_sems.at[0]),
        pltpu.make_async_copy(lat.at[:, 1 - tower_id], lat_away, lat_sems.at[1]),
    ]
    for copy in copies:
        copy.start()
    for turn in range(turns):
        backward_turn(
            sizes, turn, tower_ref,
            lat, entry, after, slope, side, dlat, actions, codes, turned, acc0, acc1, sums,
            own, away, root_own_grad, root_away_grad,
            carry, gain_sum, cond_sum, grads, gains, inverse_gains, d_after_kept, d_before_kept,
            d_hidden_kept,
        )
    for copy in copies:
        copy.wait()


def forward_turn(
    sizes, turn, tower_ref,
    root_hbm, lengths_hbm, actions_hbm, codes_hbm, policy_hbm, value_bins_hbm, reward_bins_hbm,
    table_hbm, gains_hbm, in_hbm, out_hbm, value_hbm, reward_hbm, small_hbm,
    root_any, in_got, out_got, value_any, gains_got,
    lat, entry, after, slope, side, dlat, loss, turned, gains,
    root_own, root_got, lengths, actions, codes, policy, value_bins, reward_bins,
    table_in, gains_own, value_own, value_got, reward_in, small_in, sems,
    state, past0, past1, table, weights, heads0, heads1, acc0, acc1,
    logits0, logits1, cot0, cot1, sums, squares,
):
    s = sizes
    pair = s.pair
    first_step = turn * pair
    tower_id = tower_ref[0]
    rows, width, wide = s.rows, s.width, s.wide

    if turn == 0:
        here = pl.ds(pl.multiple_of(tower_id * rows, rows), rows)

        def matrices(kind, tower):
            return weights.at[pl.ds(kind * s.calls + tower * s.blocks, s.blocks)]

        moves = [
            (in_hbm, matrices(0, tower_id)),
            (out_hbm, matrices(1, tower_id)),
            (in_got, matrices(0, 1 - tower_id)),
            (out_got, matrices(1, 1 - tower_id)),
            (value_hbm, value_own),
            (value_any, value_got),
            (reward_hbm, reward_in),
            (small_hbm, small_in),
            (table_hbm, table_in),
            (gains_hbm, gains_own),
            (root_hbm.at[here], root_own),
            (root_any.at[here], root_got),
            (actions_hbm.at[:, here], actions),
            (codes_hbm.at[:, here], codes),
            (lengths_hbm.at[:, here], lengths),
            (policy_hbm.at[:, here], policy),
            (value_bins_hbm.at[:, :, here], value_bins),
            (reward_bins_hbm.at[:, here], reward_bins),
        ]
        moves = [
            pltpu.make_async_copy(source, target, sems.at[place])
            for place, (source, target) in enumerate(moves)
        ]
        for move in moves:
            move.start()
        gains[...] = jnp.ones_like(gains)
        for target in (
            table, heads0, heads1, past0, past1, cot0, cot1, acc0, acc1, sums, squares, loss
        ):
            target[...] = jnp.zeros_like(target)
        for move in moves:
            move.wait()
        first = tower_id == 0
        state[:, 0 : width // 2] = jnp.where(first, root_own[...], root_got[...])
        state[:, width // 2 : width] = jnp.where(first, root_got[...], root_own[...])
        gains[tower_id, 0 : s.blocks, :] = gains_own[...].astype(F32)
        gains[1 - tower_id, 0 : s.blocks, :] = gains_got[...].astype(F32)
        table[0 : s.table_rows, :] = table_in[...]
        heads0[0 : s.bins, :] = jnp.where(first, value_own[...], value_got[...])
        heads1[0 : s.bins, :] = jnp.where(first, value_got[...], value_own[...])
        heads1[wide : wide + s.bins, :] = reward_in[...]
        heads0[wide : wide + s.table_rows, :] = small_in[...]
        heads1[2 * wide : 2 * wide + s.table_rows, :] = small_in[...]

    eights = lax.broadcasted_iota(jnp.int32, (8, pair * rows), 0)
    before = first_step - pair

    def pair_row(kind, at_step, lead=()):
        return jnp.concatenate(
            [kind[(slice(at_step + offset, at_step + offset + 1),) + lead] for offset in range(pair)],
            axis=1,
        )

    def live_rows(at_step):
        return jnp.concatenate(
            [(at_step + offset < lengths[...]).astype(F32) for offset in range(pair)], axis=1
        )

    kinds = []
    for offset in range(pair):
        step = first_step + offset
        kinds.append((step < lengths[...]).astype(F32))
        kinds.append(actions[step : step + 1, :].astype(F32))
        kinds.append((codes[step : step + 1, :] + ACTIONS).astype(F32))
    kinds.append(jnp.zeros((8 - len(kinds), rows), F32))
    columns = jnp.concatenate(kinds, axis=0).T

    def heads(tower, live_row, at_step, put):
        latent = past0 if tower == 0 else past1
        stack, logits, cot, acc = (
            (heads0, logits0, cot0, acc0) if tower == 0 else (heads1, logits1, cot1, acc1)
        )
        pick = lambda kind: pair_row(kind, at_step)
        value_goal = pair_row(value_bins, at_step, (tower,))
        spans = [(0, wide, 0, s.bins, value_goal)]
        if tower == 1:
            spans.append((wide, wide, 0, s.bins, pick(reward_bins)))
            spans.append((2 * wide, s.held, 0, ACTIONS, pick(policy)))
        else:
            spans.append((wide, s.held, ACTIONS, s.table_rows, pick(codes) + ACTIONS))

        def make_logits(start, stop):
            logits[start:stop, :] = by_lanes(stack[start:stop, :], latent[...])

        def eight_rows(value):
            return value.reshape(-1, 8, pair * rows)

        def mask(at, length, first, last):
            for start in range(0, length, 8):
                if start < first or start + 8 > last:
                    inside = (eights >= first - start) & (eights < last - start)
                    place = slice(at + start, at + start + 8)
                    logits[place, :] = jnp.where(inside, logits[place, :], very_negative)

        def find_top(at, start, stop, kept):
            top = jnp.max(eight_rows(logits[at + start : at + stop, :]), axis=0)
            kept["top"] = jnp.maximum(kept["top"], top) if "top" in kept else top

        def end_top(kept):
            kept["top"] = jnp.max(kept["top"], axis=0, keepdims=True)

        def make_terms(at, start, stop, goal, kept):
            place = slice(at + start, at + stop)
            value = logits[place, :]
            spot = lax.broadcasted_iota(jnp.int32, value.shape, 0)
            term = jnp.exp(value - kept["top"])
            logits[place, :] = term
            hit = spot == goal - start
            total = jnp.sum(eight_rows(term), axis=0)
            picked = jnp.sum(eight_rows(jnp.where(hit, value, 0.0)), axis=0)
            kept["total"] = kept["total"] + total if "total" in kept else total
            kept["picked"] = kept["picked"] + picked if "picked" in kept else picked

        def end_terms(kept):
            total = jnp.sum(kept["total"], axis=0, keepdims=True)
            picked = jnp.sum(kept["picked"], axis=0, keepdims=True)
            kept["scale"] = live_row / total
            row_loss = live_row * (jnp.log(total) + kept["top"] - picked)
            for offset in range(pair):
                loss[0:1, :] += row_loss[:, offset * rows : (offset + 1) * rows]

        def make_cotangent(at, start, stop, goal, kept):
            place = slice(at + start, at + stop)
            term = logits[place, :]
            spot = lax.broadcasted_iota(jnp.int32, term.shape, 0)
            hit = spot == goal - start
            cot[place, :] = (term * kept["scale"] - jnp.where(hit, live_row, 0.0)).astype(BF16)

        def make_grads(start, stop):
            acc[start:stop, :] += natural(cot[start:stop, :], latent[...])

        def make_latent():
            d_latent = by_rows(cot[...], stack[...])
            for offset in range(pair):
                put[at_step + offset, tower] = d_latent[offset * rows : (offset + 1) * rows].astype(
                    BF16
                )

        large = cuts(acc.shape[0], 320)
        pieces = [functools.partial(make_logits, *cut) for cut in large]
        for at, length, first, last, goal in spans:
            kept = {}
            each = cuts(length)
            pieces.append(functools.partial(mask, at, length, first, last))
            pieces += [functools.partial(find_top, at, *cut, kept) for cut in each]
            pieces.append(functools.partial(end_top, kept))
            pieces += [functools.partial(make_terms, at, *cut, goal, kept) for cut in each]
            pieces.append(functools.partial(end_terms, kept))
            pieces += [functools.partial(make_cotangent, at, *cut, goal, kept) for cut in each]
        return pieces + [make_latent] + [functools.partial(make_grads, *cut) for cut in large]

    def columns_of(offset, tower):
        live = columns[:, 3 * offset : 3 * offset + 1]
        return live, columns[:, 3 * offset + 1 + tower : 3 * offset + 2 + tower]

    def embedding(offset, tower):
        _, code = columns_of(offset, tower)
        spot = lax.broadcasted_iota(jnp.int32, (rows, table.shape[0]), 1)
        onehot = jnp.where(spot.astype(F32) == code, 1.0, 0.0).astype(BF16)
        return natural(onehot, table[...])

    def tower_call(offset, tower, chain):
        live, _ = columns_of(offset, tower)

        def scale_rows():
            row_squares = lane_sum(chain["hidden"] * chain["hidden"])
            return row_squares, lax.rsqrt(row_squares * (1.0 / width) + epsilon)

        def keep_squares(block, row_squares):
            place = 2 * (tower * s.blocks + block)
            total = jnp.sum(live * row_squares, axis=0, keepdims=True) * (1.0 / LANES)
            squares[first_step + offset, place : place + 1, 0:LANES] = jnp.broadcast_to(total, (1, LANES))

        def end_block(block):
            branch = chain["product"]
            chain["hidden"] = chain["hidden"] + branch
            return branch

        def keep_branch(block, branch):
            spot = 2 * (tower * s.blocks + block) + 1
            squares[first_step + offset, spot : spot + 1, :] = jnp.sum(
                branch * branch * live, axis=0, keepdims=True
            )

        def into(block):
            place = tower * s.blocks + block
            if block > 0:
                branch = end_block(block - 1)
            gained = chain["hidden"] * gains[tower, block : block + 1, :]
            chain["product"] = natural(gained.astype(BF16), weights[place])
            row_squares, inv_scale = scale_rows()
            chain["scale"] = inv_scale
            entry[first_step + offset, place] = (gained * inv_scale).astype(BF16)
            side[first_step + offset, place] = jnp.broadcast_to(inv_scale, (rows, LANES))
            if block > 0:
                keep_squares(block - 1, row_squares)
                keep_branch(block - 1, branch)

        def out_of(block):
            place = tower * s.blocks + block
            u = chain["product"] * chain["scale"]
            gate = 0.5 * jnp.tanh(0.5 * u) + 0.5
            after_rows = (u * gate).astype(BF16)
            chain["product"] = natural(after_rows, weights[s.calls + place])
            after[first_step + offset, place] = after_rows
            slope[first_step + offset, place] = (gate * (1.0 + u * (1.0 - gate))).astype(BF16)

        def finish():
            branch = end_block(s.blocks - 1)
            row_squares, inv_scale = scale_rows()
            latent = (chain["hidden"] * inv_scale).astype(BF16)
            chain[offset, tower] = latent
            following = (offset, 1) if tower == 0 else (offset + 1, 0)
            if following in chain:
                chain["hidden"] = latent.astype(F32) + chain[following]

            def keep():
                side[first_step + offset, s.calls + tower] = jnp.broadcast_to(inv_scale, (rows, LANES))
                lat[first_step + offset, tower] = latent
                keep_squares(s.blocks - 1, row_squares)
                keep_branch(s.blocks - 1, branch)
                if tower == 0:
                    total = jnp.sum(live, axis=0, keepdims=True) * (1.0 / LANES)
                    squares[first_step + offset, s.kinds : s.kinds + 1, 0:LANES] = jnp.broadcast_to(
                        total, (1, LANES)
                    )

            return keep

        pieces = []
        for block in range(s.blocks):
            pieces += [functools.partial(into, block), functools.partial(out_of, block)]
        return pieces, finish

    chain = {
        (offset, tower): embedding(offset, tower) for offset in range(pair) for tower in range(2)
    }
    chain["hidden"] = state[...].astype(F32) + chain[0, 0]
    pieces = []
    keeps = []

    def begin_next(finish, into):
        keeps.append(finish())
        into()
        keeps.pop()()

    ending = None
    for offset in range(pair):
        for tower in range(2):
            calls, finish = tower_call(offset, tower, chain)
            if ending is not None:
                calls[0] = functools.partial(begin_next, ending, calls[0])
            pieces += calls
            ending = finish
    pieces.append(lambda: ending()())

    turns = -(-2 * s.calls // (s.steps // pair))

    def turn_weights(matrix):
        turned[matrix] = weights[matrix].T

    beside = []
    if turn > 0:
        live_before = live_rows(before)
        beside += heads(1, live_before, before, dlat) + heads(0, live_before, before, dlat)
    matrices_now = range(turn * turns, min((turn + 1) * turns, 2 * s.calls))
    beside += [functools.partial(turn_weights, matrix) for matrix in matrices_now]
    weave(pieces, beside)
    at_lane = lax.broadcasted_iota(jnp.int32, sums.shape, 1)
    for offset in range(pair):
        at = slice(offset * rows, (offset + 1) * rows)
        after_state, next_state = chain[offset, 0], chain[offset, 1]
        past0[at, :] = after_state
        past1[at, :] = next_state
        if offset == pair - 1:
            state[...] = next_state
        total = lane_sum(squares[first_step + offset])
        sums[...] = jnp.where(at_lane == first_step + offset, total, sums[...])

    if turn == s.steps // pair - 1:
        live_now = live_rows(first_step)
        for piece in heads(1, live_now, first_step, dlat) + heads(0, live_now, first_step, dlat):
            piece()


def backward_turn(
    sizes, turn, tower_ref,
    lat, entry, after, slope, side, dlat, actions, codes, turned, acc0, acc1, sums,
    own, away, root_own, root_away,
    carry, gain_sum, cond_sum, grads, gains, inverse_gains, d_after_kept, d_before_kept,
    d_hidden_kept,
):
    s = sizes
    pair = s.pair
    first_step = s.steps - pair * (turn + 1)
    tower_id = tower_ref[0]
    blocks, width = s.blocks, s.width

    if turn == 0:
        inverse_gains[...] = 1.0 / gains[...]
        carry[...] = jnp.zeros_like(carry)
        grads[...] = jnp.zeros_like(grads)
        gain_sum[...] = jnp.zeros_like(gain_sum)
        cond_sum[...] = jnp.zeros_like(cond_sum)

    def over_lanes(column):
        return jnp.concatenate([column] * (width // LANES), axis=1)

    def stacked(parts):
        return jnp.concatenate(parts, axis=0)

    def add_grads(matrix, rows_of, place, kept, now):
        later = [kept[offset - 1, place] for offset in range(1, pair)]
        grads[matrix // s.calls, matrix % s.calls] += by_rows(
            stacked([rows_of[first_step + offset, place] for offset in range(pair)]), stacked([now] + later)
        )

    def add_cond(offset, tower, d_hidden):
        if offset > 0:
            d_hidden_kept[offset - 1, tower] = d_hidden.astype(BF16)
            return
        codes_of, shift = (actions, 0) if tower == 0 else (codes, ACTIONS)
        code = jnp.concatenate(
            [
                codes_of[first_step + step : first_step + step + 1, :] + shift
                for step in range(pair)
            ],
            axis=1,
        )
        spots = lax.broadcasted_iota(jnp.int32, (cond_sum.shape[0], pair * s.rows), 0)
        onehot = jnp.where(spots == code, 1.0, 0.0).astype(BF16)
        parts = [d_hidden.astype(BF16)]
        parts += [d_hidden_kept[step - 1, tower] for step in range(1, pair)]
        cond_sum[...] += natural(onehot, stacked(parts))

    behind = []

    def catch_up():
        while behind:
            behind.pop(0)()

    def tower_back(offset, tower, d_latent):
        normed = lat[first_step + offset, tower]
        normed_wide = normed.astype(F32)
        inv_scale = over_lanes(side[first_step + offset, s.calls + tower])
        base = inv_scale * d_latent
        slant = inv_scale * (lane_sum(d_latent * normed_wide) * (1.0 / width))
        for block in reversed(range(blocks)):
            place = tower * blocks + block
            matrix = tower * s.calls + block
            both = natural(
                jnp.concatenate([normed, base.astype(BF16)], axis=0), turned[s.calls + place]
            )
            d_hidden = base - slant * normed_wide
            d_branch = d_hidden.astype(BF16)
            entry_wide = entry[first_step + offset, place].astype(F32)
            inv_scale = over_lanes(side[first_step + offset, place])
            catch_up()
            d_after = both[s.rows :] - slant * both[: s.rows]
            d_before = (d_after * slope[first_step + offset, place].astype(F32)).astype(BF16)
            d_entry = natural(d_before, turned[place])
            if offset > 0:
                d_after_kept[offset - 1, place] = d_branch
                d_before_kept[offset - 1, place] = d_before
            else:
                add_grads(matrix + blocks, after, place, d_after_kept, d_branch)
                behind.append(
                    functools.partial(add_grads, matrix, entry, place, d_before_kept, d_before)
                )
            gain = gains[tower, block : block + 1, :]
            normed_wide = entry_wide * inverse_gains[tower, block : block + 1, :]
            normed = normed_wide.astype(BF16)
            product = d_entry * entry_wide
            base = d_hidden + inv_scale * (d_entry * gain)
            slant = inv_scale * (lane_sum(product) * (1.0 / width))

            def add_gain(tower=tower, block=block, product=product):
                gain_sum[tower, block : block + 1, :] += jnp.sum(product, axis=0, keepdims=True)

            behind.append(add_gain)
        d_hidden = base - slant * normed_wide
        behind.append(functools.partial(add_cond, offset, tower, d_hidden))
        return d_hidden

    def from_heads(offset, tower):
        return jnp.where(turn == 0, dlast[offset, tower], dlat[first_step + offset, tower])

    d_state = carry[...]
    for offset in reversed(range(pair)):
        for tower in (1, 0):
            d_state = tower_back(offset, tower, d_state + dlat[first_step + offset, tower].astype(F32))
    catch_up()
    carry[...] = d_state

    if turn == s.steps // pair - 1:
        left = d_state[:, 0 : width // 2].astype(BF16)
        right = d_state[:, width // 2 : width].astype(BF16)
        root_own[...] = jnp.where(tower_id == 0, left, right)
        root_away[...] = jnp.where(tower_id == 0, right, left)
        gain_sum[...] = gain_sum[...] * inverse_gains[...]
        wide, half = s.wide, s.wide // 2
        lines = lax.broadcasted_iota(jnp.int32, sums.shape, 0)
        small = acc0[wide : wide + s.held, :] + acc1[2 * wide : 2 * wide + s.held, :]
        for target, which in ((own, tower_id), (away, 1 - tower_id)):
            first = which == 0
            for matrix in range(s.calls):
                at = matrix * width
                target[at : at + width, :] = grads[which, matrix].astype(BF16)
            for start, stop in cuts(wide):
                value = jnp.where(first, acc0[start:stop, :], acc1[start:stop, :])
                target[s.value_at + start : s.value_at + stop, :] = value.astype(BF16)
            for start, stop in cuts(half):
                reward = jnp.where(
                    first,
                    acc1[wide + start : wide + stop, :],
                    acc1[wide + half + start : wide + half + stop, :],
                )
                target[s.reward_at + start : s.reward_at + stop, :] = reward.astype(BF16)
            here = jnp.where(first, small, 0.0)
            target[s.small_at : s.small_at + s.held, :] = here.astype(BF16)
            here = jnp.where(first, cond_sum[...], 0.0)
            target[s.cond_at : s.shared_end, :] = here.astype(BF16)
            kept = sums[...]
            for block in range(blocks):
                gain = gain_sum[which, block : block + 1, 0:LANES]
                kept = jnp.where(lines == s.gain_row + block, gain, kept)
            target[s.sums_at : s.reward_at, 0:LANES] = kept.astype(BF16)
            kept = jnp.zeros_like(kept)
            for block in range(blocks):
                gain = gain_sum[which, block : block + 1, LANES:]
                kept = jnp.where(lines == s.gain_row + block, gain, kept)
            target[s.sums_at : s.reward_at, LANES:] = kept.astype(BF16)
            if s.total > s.shared_end:
                target[s.shared_end :, :] = jnp.zeros((s.total - s.shared_end, width), BF16)


def logits_kernel(sizes, tower_ref, lat_own, lat_got, value_own, latents, logits):
    rows = sizes.rows
    tower_id = tower_ref[0]
    at_own = pl.ds(pl.multiple_of(tower_id * rows, rows), rows)
    at_got = pl.ds(pl.multiple_of((1 - tower_id) * rows, rows), rows)
    for offset in range(sizes.pair):
        latents[offset, at_own, :] = lat_own[offset]
        latents[offset, at_got, :] = lat_got[offset]
        logits[offset] = by_lanes(value_own[...], latents[offset]).astype(BF16)


def add_and_split_kernel(count, digit_ref, *refs):
    inputs, outputs = refs[:count], refs[count:]
    digit = digit_ref[0]
    for other, target in enumerate(outputs):
        part = digit ^ other
        total = inputs[0][part].astype(F32)
        for source in inputs[1:]:
            total = total + source[part].astype(F32)
        target[...] = total.astype(BF16)


def unpack_own_kernel(sizes, scalars, *refs):
    s = sizes
    factor = len(refs) - 7
    digit, tower_id = scalars[0], scalars[1]
    w_in, w_out, value, gain, rms, flat, held = refs[factor:]
    width = s.width
    length = refs[0].shape[0]
    for other, source in zip(others(factor), refs[:factor]):
        at = pl.multiple_of((digit ^ other) * length, 16)
        flat[pl.ds(at, length), :] = source[...]
    for block in range(s.blocks):
        at = block * width
        w_in[block] = flat[at : at + width, :].astype(F32)
        at = (s.blocks + block) * width
        w_out[block] = flat[at : at + width, :].astype(F32)
    value[:, 0, :] = flat[s.value_at : s.sums_at, :].astype(F32)[0 : s.bins]
    sums = flat[s.sums_at : s.reward_at, :].astype(F32)
    for block in range(s.blocks):
        gain[block] = sums[s.gain_row + block : s.gain_row + block + 1, :]
    held[...] = sums[:, 0:LANES]
    count = jnp.maximum(held[s.kinds : s.kinds + 1, 0 : s.steps], 1.0)
    for block in range(s.blocks):
        for kind in range(2):
            spot = tower_id * s.calls + 2 * block + kind
            square = held[pl.ds(spot, 1), 0 : s.steps]
            rms[block, kind : kind + 1, :] = jnp.sqrt(jnp.maximum(square, 0.0) / (count * width))


def unpack_shared_kernel(sizes, tower_ref, mine, got, reward, small, cond, joined):
    s = sizes
    tower_id = tower_ref[0]
    half = s.wide // 2
    joined[pl.ds(pl.multiple_of(tower_id * half, 8), half), :] = mine[0:half, :].astype(F32)
    joined[pl.ds(pl.multiple_of((1 - tower_id) * half, 8), half), :] = got[0:half, :].astype(F32)
    reward[...] = joined[0 : s.bins, :]
    for target, at in ((small, s.small_at), (cond, s.cond_at)):
        rows = slice(at - s.reward_at, at - s.reward_at + s.held)
        target[...] = (mine[rows, :].astype(F32) + got[rows, :].astype(F32))[0 : s.table_rows]


def whole(shape):
    return pl.BlockSpec(shape, lambda step, tower: (0,) * len(shape))


def swap(value, axis, mask):
    pairs = [(source, source ^ mask) for source in range(lax.axis_size(axis))]
    return lax.ppermute(value, axis, pairs)


AXES = ("tower", "batch")


def exchange_rounds(batch_size):
    factors, left = [], batch_size
    while left > 1:
        factors.append(4 if left % 4 == 0 else 2)
        left //= factors[-1]
    rounds, stride = [], 1
    for factor in factors:
        rounds.append((factor, stride))
        stride *= factor
    turned = rounds[::-1] if len(set(factors)) == 1 else rounds
    return [(one[0], (one[1], two[1])) for one, two in zip(rounds, turned)]


def swap_within(value, strides, other, batch_size):
    pairs = [
        (tower * batch_size + index, tower * batch_size + (index ^ (other * strides[tower])))
        for tower in range(2)
        for index in range(batch_size)
    ]
    return lax.ppermute(value, AXES, pairs)


def others(factor):
    return [0] + list(reversed(range(1, factor)))


def swap_all(blocks, strides, batch_size):
    return [
        swap_within(blocks[other], strides, other, batch_size) if other else blocks[0]
        for other in others(len(blocks))
    ]


def my_digit(factor, strides):
    stride = jnp.where(lax.axis_index("tower") == 0, strides[0], strides[1])
    return (lax.axis_index("batch") // stride) % factor


def add_kernel(*refs):
    total = refs[0][...].astype(F32)
    for source in refs[1:-1]:
        total = total + source[...].astype(F32)
    refs[-1][...] = total.astype(BF16)


def add_up(parts):
    return pl.pallas_call(
        add_kernel,
        out_shape=jax.ShapeDtypeStruct(parts[0].shape, BF16),
        compiler_params=pltpu.CompilerParams(vmem_limit_bytes=SMALL_LIMIT),
        name="add_up",
    )(*parts)


def exchange(value, rounds, batch_size, beside, given, last_kernel):
    factor, strides = rounds[0]
    digit = my_digit(factor, strides)
    rows, width = value[0].shape
    rows = rows // factor
    split = pl.pallas_call(
        functools.partial(add_and_split_kernel, len(value)),
        grid_spec=pltpu.PrefetchScalarGridSpec(
            num_scalar_prefetch=1,
            grid=(1,),
            in_specs=[whole((factor, rows, width))] * len(value),
            out_specs=[whole((rows, width))] * factor,
        ),
        out_shape=[pltpu.HBM((rows, width), BF16)] * factor,
        compiler_params=pltpu.CompilerParams(vmem_limit_bytes=SMALL_LIMIT),
        name="add_and_split",
    )(digit[None], *[
        pltpu.with_memory_space_constraint(part.reshape(factor, rows, width), pltpu.HBM)
        if place
        else part.reshape(factor, rows, width)
        for place, part in enumerate(value)
    ])
    split, given = lax.optimization_barrier((split, given))
    held = swap_all(split, strides, batch_size)
    done = beside(given)
    held, done = lax.optimization_barrier((held, done))
    for size, steps in rounds[1:]:
        bit = 1
        while bit < size:
            block = add_up(held)
            held = [block, swap_within(block, steps, bit, batch_size)]
            bit *= 2
    block = add_up(held)
    held = swap_all([block] * factor, strides, batch_size)
    return last_kernel(digit, held), done


def body(
    root_state, cond_table, block_gain, w_in, w_out, value_head, reward_head, small_head,
    unroll_len, actions, codes, policy_target, value_bins, reward_bins,
):
    tower_id = lax.axis_index("tower")
    other_id = 1 - tower_id
    tower_ref = tower_id.astype(jnp.int32)[None]
    steps, batch_rows = actions.shape
    blocks, width = block_gain.shape[1:]
    bins = value_head.shape[2]
    table_rows = cond_table.shape[0]
    rows = batch_rows // 2
    half = width // 2
    parts = lax.axis_size("batch")
    s = Sizes(steps, rows, blocks, width, bins, table_rows, parts)
    calls, wide, pair = s.calls, s.wide, s.pair

    root_got = swap(root_state, "tower", 1)
    in_own, out_own, gains_own = w_in[0], w_out[0], block_gain[0]
    value_own = value_head[0].T
    in_got = swap(in_own, "tower", 1)
    out_got = swap(out_own, "tower", 1)
    gains_got = swap(gains_own, "tower", 1)
    value_got = swap(value_own, "tower", 1)
    lengths = unroll_len.reshape(1, batch_rows)

    shape = jax.ShapeDtypeStruct
    per_pair = lambda *tail: pl.BlockSpec(
        (pair,) + tail, lambda turn, tower: (turn,) + (0,) * len(tail)
    )
    unroll_params = pltpu.CompilerParams(vmem_limit_bytes=UNROLL_LIMIT)
    small_params = pltpu.CompilerParams(vmem_limit_bytes=SMALL_LIMIT)
    products = steps * rows * (4 * blocks * width * width + 9 * width * wide)
    cost = pl.CostEstimate(flops=2 * products, bytes_accessed=40 * 2**20, transcendentals=0)
    lat_own, lat_away, loss, own, away, root_own, root_away = pl.pallas_call(
        functools.partial(unroll_kernel, s),
        in_specs=[pl.BlockSpec(memory_space=pltpu.SMEM)]
        + [pl.BlockSpec(memory_space=pltpu.HBM)] * 14
        + [pl.BlockSpec(memory_space=pltpu.HBM)] * 4
        + [pl.BlockSpec(memory_space=pltpu.VMEM)],
        out_specs=[pl.BlockSpec(memory_space=pltpu.HBM)] * 2
        + [pl.BlockSpec(memory_space=pltpu.VMEM)] * 5,
        scratch_shapes=[
            pltpu.VMEM((steps, 2, rows, width), BF16),
            pltpu.VMEM((steps, calls, rows, width), BF16),
            pltpu.VMEM((steps, calls, rows, width), BF16),
            pltpu.VMEM((steps, calls, rows, width), BF16),
            pltpu.VMEM((steps, calls + 2, rows, LANES), F32),
            pltpu.VMEM((steps, 2, rows, width), BF16),
            pltpu.VMEM((2 * calls, width, width), BF16),
            pltpu.VMEM((2, 16, width), F32),
            pltpu.SemaphoreType.DMA((2,)),
            pltpu.VMEM((rows, half), BF16),
            pltpu.VMEM((rows, half), BF16),
            pltpu.VMEM((1, rows), jnp.int32),
            pltpu.VMEM((steps, rows), jnp.int32),
            pltpu.VMEM((steps, rows), jnp.int32),
            pltpu.VMEM((steps, rows), jnp.int32),
            pltpu.VMEM((steps, 2, rows), jnp.int32),
            pltpu.VMEM((steps, rows), jnp.int32),
            pltpu.VMEM((table_rows, width), BF16),
            pltpu.VMEM((blocks, width), BF16),
            pltpu.VMEM((bins, width), BF16),
            pltpu.VMEM((bins, width), BF16),
            pltpu.VMEM((bins, width), BF16),
            pltpu.VMEM((table_rows, width), BF16),
            pltpu.SemaphoreType.DMA((18,)),
            pltpu.VMEM((rows, width), BF16),
            pltpu.VMEM((pair * rows, width), BF16),
            pltpu.VMEM((pair * rows, width), BF16),
            pltpu.VMEM((LANES, width), BF16),
            pltpu.VMEM((2 * calls, width, width), BF16),
            pltpu.VMEM((s.depth[0], width), BF16),
            pltpu.VMEM((s.depth[1], width), BF16),
            pltpu.VMEM((s.stack[0], width), F32),
            pltpu.VMEM((s.stack[1], width), F32),
            pltpu.VMEM((s.stack[0], pair * rows), F32),
            pltpu.VMEM((s.stack[1], pair * rows), F32),
            pltpu.VMEM((s.depth[0], pair * rows), BF16),
            pltpu.VMEM((s.depth[1], pair * rows), BF16),
            pltpu.VMEM((s.reward_at - s.sums_at, LANES), F32),
            pltpu.VMEM((steps, s.reward_at - s.sums_at, width), F32),
            pltpu.VMEM((rows, width), F32),
            pltpu.VMEM((2, 16, width), F32),
            pltpu.VMEM((s.held, width), F32),
            pltpu.VMEM((2, calls, width, width), F32),
            pltpu.VMEM((2, 16, width), F32),
            pltpu.VMEM((max(pair - 1, 1), calls, rows, width), BF16),
            pltpu.VMEM((max(pair - 1, 1), calls, rows, width), BF16),
            pltpu.VMEM((max(pair - 1, 1), 2, rows, width), BF16),
        ],
        out_shape=[
            pltpu.HBM((steps, rows, width), BF16),
            pltpu.HBM((steps, rows, width), BF16),
            shape((8, rows), F32),
            shape((s.total, width), BF16),
            shape((s.total, width), BF16),
            shape((rows, half), BF16),
            shape((rows, half), BF16),
        ],
        compiler_params=unroll_params,
        cost_estimate=cost,
        name="unroll",
    )(
        tower_ref,
        *[
            pltpu.with_memory_space_constraint(value, pltpu.HBM)
            for value in (
                root_state, lengths, actions, codes, policy_target,
                jnp.swapaxes(value_bins, 0, 1), reward_bins, cond_table, gains_own,
                in_own, out_own, value_own, reward_head.T, small_head.T,
            )
        ],
        *[
            pltpu.with_memory_space_constraint(value, pltpu.HBM)
            for value in (root_got, in_got, out_got, value_got)
        ],
        gains_got,
    )
    got = swap(away, "tower", 1)

    def beside(given):
        lat_own, lat_away, loss, root_own, root_away = given
        lat_got = swap(lat_away, "tower", 1)
        loss_own = loss[0]
        loss_got = swap(loss_own, "tower", 1)
        root_got = swap(root_away, "tower", 1)

        latents, logits = pl.pallas_call(
            functools.partial(logits_kernel, s),
            grid_spec=pltpu.PrefetchScalarGridSpec(
                num_scalar_prefetch=1,
                grid=(steps // pair,),
                in_specs=[per_pair(rows, width), per_pair(rows, width), whole((bins, width))],
                out_specs=[per_pair(batch_rows, width), per_pair(bins, batch_rows)],
            ),
            out_shape=[
                shape((steps, batch_rows, width), BF16),
                shape((steps, bins, batch_rows), BF16),
            ],
            compiler_params=small_params,
            cost_estimate=pl.CostEstimate(
                flops=2 * steps * batch_rows * width * wide, bytes_accessed=6 * 2**20, transcendentals=0
            ),
            name="latents_and_logits",
        )(
            tower_ref,
            *[
                pltpu.with_memory_space_constraint(part, pltpu.HBM)
                for part in (lat_own, lat_got, value_own)
            ],
        )

        def in_order(mine_value, got_value, axis):
            return jnp.where(
                tower_id == 0,
                jnp.concatenate([mine_value, got_value], axis=axis),
                jnp.concatenate([got_value, mine_value], axis=axis),
            )

        row_loss = in_order(loss_own, loss_got, 0)
        grad_root = in_order(root_own, root_got, 0).astype(F32)
        return latents, logits, row_loss, grad_root

    rounds = exchange_rounds(parts)

    def unpack(digit, held):
        scalars = jnp.stack([digit, tower_id]).astype(jnp.int32)
        length = held[0].shape[0]
        block = s.reward_at // length
        at = s.reward_at - block * length
        parts_of = [part[at : at + s.shared_end - s.reward_at] for part in held]
        shared = parts_of[0]
        for other, part in zip(others(len(held))[1:], parts_of[1:]):
            shared = jnp.where((digit ^ other) == block, part, shared)
        shared_got = swap(shared, "tower", 1)
        return (shared, shared_got), pl.pallas_call(
            functools.partial(unpack_own_kernel, s),
            grid_spec=pltpu.PrefetchScalarGridSpec(
                num_scalar_prefetch=1,
                grid=(1,),
                in_specs=[whole(part.shape) for part in held],
                out_specs=[
                    whole((blocks, width, width)),
                    whole((blocks, width, width)),
                    whole((bins, 1, width)),
                    whole((blocks, 1, width)),
                    whole((blocks, 2, steps)),
                ],
                scratch_shapes=[
                    pltpu.VMEM((s.total, width), BF16),
                    pltpu.VMEM((s.reward_at - s.sums_at, LANES), F32),
                ],
            ),
            out_shape=[
                shape((blocks, width, width), F32),
                shape((blocks, width, width), F32),
                shape((bins, 1, width), F32),
                shape((blocks, 1, width), F32),
                shape((blocks, 2, steps), F32),
            ],
            compiler_params=small_params,
            name="unpack_own",
        )(scalars, *held)

    given = (lat_own, lat_away, loss, root_own, root_away)
    unpacked, done = exchange([own, got], rounds, parts, beside, given, unpack)
    (shared, shared_got), (grad_in, grad_out, value_t, gain_t, rms_t) = unpacked
    latents, logits, row_loss, grad_root = done
    reward_t, small_t, grad_cond = pl.pallas_call(
        functools.partial(unpack_shared_kernel, s),
        grid_spec=pltpu.PrefetchScalarGridSpec(
            num_scalar_prefetch=1,
            grid=(1,),
            in_specs=[whole(shared.shape), whole(shared.shape)],
            out_specs=[
                whole((bins, width)),
                whole((table_rows, width)),
                whole((table_rows, width)),
            ],
            scratch_shapes=[pltpu.VMEM((s.wide, width), F32)],
        ),
        out_shape=[
            shape((bins, width), F32),
            shape((table_rows, width), F32),
            shape((table_rows, width), F32),
        ],
        compiler_params=small_params,
        name="unpack_shared",
    )(tower_ref, shared, shared_got)
    layer_rms = jnp.transpose(rms_t, (2, 0, 1))[None]
    return (
        latents[None],
        jnp.swapaxes(logits, 1, 2)[None],
        row_loss,
        layer_rms,
        grad_root,
        grad_cond,
        jnp.swapaxes(gain_t, 0, 1),
        grad_in[None],
        grad_out[None],
        jnp.transpose(value_t, (1, 2, 0)),
        reward_t.T,
        small_t.T,
    )


def solution(mesh):
    placed = (
        P("batch", "tower"),
        P(),
        P("tower", None, None),
        P("tower", None, None, None),
        P("tower", None, None, None),
        P("tower", None, None),
        P(),
        P(),
        P("batch"),
        P(None, "batch"),
        P(None, "batch"),
        P(None, "batch"),
        P(None, None, "batch"),
        P(None, "batch"),
    )
    return jax.shard_map(
        body,
        mesh=mesh,
        in_specs=placed,
        out_specs=(
            P("tower", None, "batch", None),
            P("tower", None, "batch", None),
            P("batch"),
            P("tower", None, None, None),
            P("batch", "tower"),
            P(),
            P("tower", None, None),
            P("tower", None, None, None),
            P("tower", None, None, None),
            P("tower", None, None),
            P(),
            P(),
        ),
        check_vma=False,
    )
```

```python
import functools

import jax
import jax.numpy as jnp
from jax import lax
from jax.experimental import pallas as pl
from jax.experimental.pallas import tpu as pltpu
from jax.sharding import PartitionSpec as P

ACTIONS = 4
LANES = 128
MIB = 1024 * 1024
UNROLL_LIMIT = 50 * MIB
SMALL_LIMIT = 12 * MIB
epsilon = 1e-06
very_negative = -1e30
F32 = jnp.float32
BF16 = jnp.bfloat16


def natural(left, right):
    return lax.dot_general(left, right, (((1,), (0,)), ((), ())), preferred_element_type=F32)


def by_rows(left, right):
    return lax.dot_general(left, right, (((0,), (0,)), ((), ())), preferred_element_type=F32)


def by_lanes(left, right):
    return lax.dot_general(left, right, (((1,), (1,)), ((), ())), preferred_element_type=F32)


def round_up(value, unit):
    return (value + unit - 1) // unit * unit


def lane_sum(value):
    return jnp.sum(value, axis=-1, keepdims=True)


def inverse_rms(hidden):
    return lax.rsqrt(lane_sum(hidden * hidden) * (1.0 / hidden.shape[-1]) + epsilon)


def weave(*tasks):
    tasks = [(list(task)) for task in tasks]
    longest = max(len(task) for task in tasks)
    done = [0] * len(tasks)
    for turn in range(longest):
        for which, task in enumerate(tasks):
            until = (turn + 1) * len(task) // longest
            while done[which] < until:
                task[done[which]]()
                done[which] += 1


def cuts(length, unit=160):
    return [(start, min(start + unit, length)) for start in range(0, length, unit)]


class Sizes:
    def __init__(self, steps, rows, blocks, width, bins, table_rows, parts):
        self.steps, self.rows, self.blocks, self.width = steps, rows, blocks, width
        self.bins, self.table_rows, self.parts = bins, table_rows, parts
        self.calls = 2 * blocks
        self.pair = 2 if steps % 2 == 0 else 1
        self.wide = round_up(bins, 32)
        self.held = round_up(table_rows, 16)
        self.stack = (self.wide + self.held, 2 * self.wide + self.held)
        self.depth = tuple(round_up(rows_in, LANES) for rows_in in self.stack)
        half = self.wide // 2
        self.value_at = self.calls * width
        self.sums_at = self.value_at + self.wide
        self.kinds = 2 * self.calls
        self.gain_row = self.kinds + 1
        self.reward_at = self.sums_at + round_up(self.gain_row + blocks, 16)
        self.small_at = self.reward_at + half
        self.cond_at = self.small_at + self.held
        self.shared_end = self.cond_at + self.held
        self.total = round_up(self.shared_end, 16 * parts)
        self.head_rows = self.cond_at - self.value_at


def unroll_kernel(
    sizes, tower_ref,
    root_hbm, lengths_hbm, actions_hbm, codes_hbm, policy_hbm, value_bins_hbm, reward_bins_hbm,
    table_hbm, gains_hbm, in_hbm, out_hbm, value_hbm, reward_hbm, small_hbm,
    root_any, in_got, out_got, value_any, gains_got,
    lat_own, lat_away, loss, own, away, root_own_grad, root_away_grad,
    lat, entry, after, slope, side, dlat, turned, gains, lat_sems,
    root_own, root_got, lengths, actions, codes, policy, value_bins, reward_bins,
    table_in, gains_own, value_own, value_got, reward_in, small_in, sems,
    state, past0, past1, table, weights, heads0, heads1, acc0, acc1,
    cot0, cot1, sums, squares,
    carry, gain_sum, cond_sum, grads, inverse_gains, d_after_kept, d_before_kept, d_hidden_kept,
):
    turns = sizes.steps // sizes.pair
    small, large = sizes.stack
    logits0 = grads.at[pl.ds(0, small)]
    logits1 = grads.at[pl.ds(small, large)]
    for turn in range(turns):
        forward_turn(
            sizes, turn, tower_ref,
            root_hbm, lengths_hbm, actions_hbm, codes_hbm, policy_hbm, value_bins_hbm,
            reward_bins_hbm, table_hbm, gains_hbm, in_hbm, out_hbm, value_hbm, reward_hbm,
            small_hbm, root_any, in_got, out_got, value_any, gains_got,
            lat, entry, after, slope, side, dlat, loss, turned, gains,
            root_own, root_got, lengths, actions, codes, policy, value_bins, reward_bins,
            table_in, gains_own, value_own, value_got, reward_in, small_in, sems,
            state, past0, past1, table, weights, heads0, heads1, acc0, acc1,
            logits0, logits1, cot0, cot1, sums, squares,
        )
    tower_id = tower_ref[0]
    copies = [
        pltpu.make_async_copy(lat.at[:, tower_id], lat_own, lat_sems.at[0]),
        pltpu.make_async_copy(lat.at[:, 1 - tower_id], lat_away, lat_sems.at[1]),
    ]
    for copy in copies:
        copy.start()
    for turn in range(turns):
        backward_turn(
            sizes, turn, tower_ref,
            lat, entry, after, slope, side, dlat, actions, codes, turned, acc0, acc1, sums,
            own, away, root_own_grad, root_away_grad,
            carry, gain_sum, cond_sum, grads, gains, inverse_gains, d_after_kept, d_before_kept,
            d_hidden_kept,
        )
    for copy in copies:
        copy.wait()


def forward_turn(
    sizes, turn, tower_ref,
    root_hbm, lengths_hbm, actions_hbm, codes_hbm, policy_hbm, value_bins_hbm, reward_bins_hbm,
    table_hbm, gains_hbm, in_hbm, out_hbm, value_hbm, reward_hbm, small_hbm,
    root_any, in_got, out_got, value_any, gains_got,
    lat, entry, after, slope, side, dlat, loss, turned, gains,
    root_own, root_got, lengths, actions, codes, policy, value_bins, reward_bins,
    table_in, gains_own, value_own, value_got, reward_in, small_in, sems,
    state, past0, past1, table, weights, heads0, heads1, acc0, acc1,
    logits0, logits1, cot0, cot1, sums, squares,
):
    s = sizes
    pair = s.pair
    first_step = turn * pair
    tower_id = tower_ref[0]
    rows, width, wide = s.rows, s.width, s.wide

    if turn == 0:
        here = pl.ds(pl.multiple_of(tower_id * rows, rows), rows)

        def matrices(kind, tower):
            return weights.at[pl.ds(kind * s.calls + tower * s.blocks, s.blocks)]

        moves = [
            (in_hbm, matrices(0, tower_id)),
            (out_hbm, matrices(1, tower_id)),
            (in_got, matrices(0, 1 - tower_id)),
            (out_got, matrices(1, 1 - tower_id)),
            (value_hbm, value_own),
            (value_any, value_got),
            (reward_hbm, reward_in),
            (small_hbm, small_in),
            (table_hbm, table_in),
            (gains_hbm, gains_own),
            (root_hbm.at[here], root_own),
            (root_any.at[here], root_got),
            (actions_hbm.at[:, here], actions),
            (codes_hbm.at[:, here], codes),
            (lengths_hbm.at[:, here], lengths),
            (policy_hbm.at[:, here], policy),
            (value_bins_hbm.at[:, :, here], value_bins),
            (reward_bins_hbm.at[:, here], reward_bins),
        ]
        moves = [
            pltpu.make_async_copy(source, target, sems.at[place])
            for place, (source, target) in enumerate(moves)
        ]
        for move in moves:
            move.start()
        gains[...] = jnp.ones_like(gains)
        for target in (
            table, heads0, heads1, past0, past1, cot0, cot1, acc0, acc1, sums, squares, loss
        ):
            target[...] = jnp.zeros_like(target)
        for move in moves:
            move.wait()
        first = tower_id == 0
        state[:, 0 : width // 2] = jnp.where(first, root_own[...], root_got[...])
        state[:, width // 2 : width] = jnp.where(first, root_got[...], root_own[...])
        gains[tower_id, 0 : s.blocks, :] = gains_own[...].astype(F32)
        gains[1 - tower_id, 0 : s.blocks, :] = gains_got[...].astype(F32)
        table[0 : s.table_rows, :] = table_in[...]
        heads0[0 : s.bins, :] = jnp.where(first, value_own[...], value_got[...])
        heads1[0 : s.bins, :] = jnp.where(first, value_got[...], value_own[...])
        heads1[wide : wide + s.bins, :] = reward_in[...]
        heads0[wide : wide + s.table_rows, :] = small_in[...]
        heads1[2 * wide : 2 * wide + s.table_rows, :] = small_in[...]

    eights = lax.broadcasted_iota(jnp.int32, (8, pair * rows), 0)
    before = first_step - pair

    def pair_row(kind, at_step, lead=()):
        return jnp.concatenate(
            [kind[(slice(at_step + offset, at_step + offset + 1),) + lead] for offset in range(pair)],
            axis=1,
        )

    def live_rows(at_step):
        return jnp.concatenate(
            [(at_step + offset < lengths[...]).astype(F32) for offset in range(pair)], axis=1
        )

    kinds = []
    for offset in range(pair):
        step = first_step + offset
        kinds.append((step < lengths[...]).astype(F32))
        kinds.append(actions[step : step + 1, :].astype(F32))
        kinds.append((codes[step : step + 1, :] + ACTIONS).astype(F32))
    kinds.append(jnp.zeros((8 - len(kinds), rows), F32))
    columns = jnp.concatenate(kinds, axis=0).T

    def heads(tower, live_row, at_step, put):
        latent = past0 if tower == 0 else past1
        stack, logits, cot, acc = (
            (heads0, logits0, cot0, acc0) if tower == 0 else (heads1, logits1, cot1, acc1)
        )
        pick = lambda kind: pair_row(kind, at_step)
        value_goal = pair_row(value_bins, at_step, (tower,))
        spans = [(0, wide, 0, s.bins, value_goal)]
        if tower == 1:
            spans.append((wide, wide, 0, s.bins, pick(reward_bins)))
            spans.append((2 * wide, s.held, 0, ACTIONS, pick(policy)))
        else:
            spans.append((wide, s.held, ACTIONS, s.table_rows, pick(codes) + ACTIONS))

        def make_logits(start, stop):
            logits[start:stop, :] = by_lanes(stack[start:stop, :], latent[...])

        def eight_rows(value):
            return value.reshape(-1, 8, pair * rows)

        def mask(at, length, first, last):
            for start in range(0, length, 8):
                if start < first or start + 8 > last:
                    inside = (eights >= first - start) & (eights < last - start)
                    place = slice(at + start, at + start + 8)
                    logits[place, :] = jnp.where(inside, logits[place, :], very_negative)

        def find_top(at, start, stop, kept):
            top = jnp.max(eight_rows(logits[at + start : at + stop, :]), axis=0)
            kept["top"] = jnp.maximum(kept["top"], top) if "top" in kept else top

        def end_top(kept):
            kept["top"] = jnp.max(kept["top"], axis=0, keepdims=True)

        def make_terms(at, start, stop, goal, kept):
            place = slice(at + start, at + stop)
            value = logits[place, :]
            spot = lax.broadcasted_iota(jnp.int32, value.shape, 0)
            term = jnp.exp(value - kept["top"])
            logits[place, :] = term
            hit = spot == goal - start
            total = jnp.sum(eight_rows(term), axis=0)
            picked = jnp.sum(eight_rows(jnp.where(hit, value, 0.0)), axis=0)
            kept["total"] = kept["total"] + total if "total" in kept else total
            kept["picked"] = kept["picked"] + picked if "picked" in kept else picked

        def end_terms(kept):
            total = jnp.sum(kept["total"], axis=0, keepdims=True)
            picked = jnp.sum(kept["picked"], axis=0, keepdims=True)
            kept["scale"] = live_row / total
            row_loss = live_row * (jnp.log(total) + kept["top"] - picked)
            for offset in range(pair):
                loss[0:1, :] += row_loss[:, offset * rows : (offset + 1) * rows]

        def make_cotangent(at, start, stop, goal, kept):
            place = slice(at + start, at + stop)
            term = logits[place, :]
            spot = lax.broadcasted_iota(jnp.int32, term.shape, 0)
            hit = spot == goal - start
            cot[place, :] = (term * kept["scale"] - jnp.where(hit, live_row, 0.0)).astype(BF16)

        def make_grads(start, stop):
            acc[start:stop, :] += natural(cot[start:stop, :], latent[...])

        def make_latent():
            d_latent = by_rows(cot[...], stack[...])
            for offset in range(pair):
                put[at_step + offset, tower] = d_latent[offset * rows : (offset + 1) * rows].astype(
                    BF16
                )

        large = cuts(acc.shape[0], 320)
        pieces = [functools.partial(make_logits, *cut) for cut in large]
        for at, length, first, last, goal in spans:
            kept = {}
            each = cuts(length)
            pieces.append(functools.partial(mask, at, length, first, last))
            pieces += [functools.partial(find_top, at, *cut, kept) for cut in each]
            pieces.append(functools.partial(end_top, kept))
            pieces += [functools.partial(make_terms, at, *cut, goal, kept) for cut in each]
            pieces.append(functools.partial(end_terms, kept))
            pieces += [functools.partial(make_cotangent, at, *cut, goal, kept) for cut in each]
        return pieces + [make_latent] + [functools.partial(make_grads, *cut) for cut in large]

    def columns_of(offset, tower):
        live = columns[:, 3 * offset : 3 * offset + 1]
        return live, columns[:, 3 * offset + 1 + tower : 3 * offset + 2 + tower]

    def embedding(offset, tower):
        _, code = columns_of(offset, tower)
        spot = lax.broadcasted_iota(jnp.int32, (rows, table.shape[0]), 1)
        onehot = jnp.where(spot.astype(F32) == code, 1.0, 0.0).astype(BF16)
        return natural(onehot, table[...])

    def tower_call(offset, tower, chain):
        live, _ = columns_of(offset, tower)

        def scale_rows():
            row_squares = lane_sum(chain["hidden"] * chain["hidden"])
            return row_squares, lax.rsqrt(row_squares * (1.0 / width) + epsilon)

        def keep_squares(block, row_squares):
            place = 2 * (tower * s.blocks + block)
            total = jnp.sum(live * row_squares, axis=0, keepdims=True) * (1.0 / LANES)
            squares[first_step + offset, place : place + 1, 0:LANES] = jnp.broadcast_to(total, (1, LANES))

        def end_block(block):
            branch = chain["product"]
            chain["hidden"] = chain["hidden"] + branch
            return branch

        def keep_branch(block, branch):
            spot = 2 * (tower * s.blocks + block) + 1
            squares[first_step + offset, spot : spot + 1, :] = jnp.sum(
                branch * branch * live, axis=0, keepdims=True
            )

        def into(block):
            place = tower * s.blocks + block
            if block > 0:
                branch = end_block(block - 1)
            gained = chain["hidden"] * gains[tower, block : block + 1, :]
            chain["product"] = natural(gained.astype(BF16), weights[place])
            row_squares, inv_scale = scale_rows()
            chain["scale"] = inv_scale
            entry[first_step + offset, place] = (gained * inv_scale).astype(BF16)
            side[first_step + offset, :, place : place + 1] = inv_scale
            if block > 0:
                keep_squares(block - 1, row_squares)
                keep_branch(block - 1, branch)

        def out_of(block):
            place = tower * s.blocks + block
            u = chain["product"] * chain["scale"]
            gate = 0.5 * jnp.tanh(0.5 * u) + 0.5
            after_rows = (u * gate).astype(BF16)
            chain["product"] = natural(after_rows, weights[s.calls + place])
            after[first_step + offset, place] = after_rows
            slope[first_step + offset, place] = (gate * (1.0 + u * (1.0 - gate))).astype(BF16)

        def finish():
            branch = end_block(s.blocks - 1)
            row_squares, inv_scale = scale_rows()
            latent = (chain["hidden"] * inv_scale).astype(BF16)
            chain[offset, tower] = latent
            following = (offset, 1) if tower == 0 else (offset + 1, 0)
            if following in chain:
                chain["hidden"] = latent.astype(F32) + chain[following]

            def keep():
                spot = s.calls + tower
                side[first_step + offset, :, spot : spot + 1] = inv_scale
                lat[first_step + offset, tower] = latent
                keep_squares(s.blocks - 1, row_squares)
                keep_branch(s.blocks - 1, branch)
                if tower == 0:
                    total = jnp.sum(live, axis=0, keepdims=True) * (1.0 / LANES)
                    squares[first_step + offset, s.kinds : s.kinds + 1, 0:LANES] = jnp.broadcast_to(
                        total, (1, LANES)
                    )

            return keep

        pieces = []
        for block in range(s.blocks):
            pieces += [functools.partial(into, block), functools.partial(out_of, block)]
        return pieces, finish

    chain = {
        (offset, tower): embedding(offset, tower) for offset in range(pair) for tower in range(2)
    }
    chain["hidden"] = state[...].astype(F32) + chain[0, 0]
    pieces = []
    keeps = []

    def begin_next(finish, into):
        keeps.append(finish())
        into()
        keeps.pop()()

    ending = None
    for offset in range(pair):
        for tower in range(2):
            calls, finish = tower_call(offset, tower, chain)
            if ending is not None:
                calls[0] = functools.partial(begin_next, ending, calls[0])
            pieces += calls
            ending = finish
    pieces.append(lambda: ending()())

    turns = -(-2 * s.calls // (s.steps // pair))

    def turn_weights(matrix):
        turned[matrix] = weights[matrix].T

    beside = []
    if turn > 0:
        live_before = live_rows(before)
        beside += heads(1, live_before, before, dlat) + heads(0, live_before, before, dlat)
    matrices_now = range(turn * turns, min((turn + 1) * turns, 2 * s.calls))
    beside += [functools.partial(turn_weights, matrix) for matrix in matrices_now]
    weave(pieces, beside)
    at_lane = lax.broadcasted_iota(jnp.int32, sums.shape, 1)
    for offset in range(pair):
        at = slice(offset * rows, (offset + 1) * rows)
        after_state, next_state = chain[offset, 0], chain[offset, 1]
        past0[at, :] = after_state
        past1[at, :] = next_state
        if offset == pair - 1:
            state[...] = next_state
        total = lane_sum(squares[first_step + offset])
        sums[...] = jnp.where(at_lane == first_step + offset, total, sums[...])

    if turn == s.steps // pair - 1:
        live_now = live_rows(first_step)
        for piece in heads(1, live_now, first_step, dlat) + heads(0, live_now, first_step, dlat):
            piece()


def backward_turn(
    sizes, turn, tower_ref,
    lat, entry, after, slope, side, dlat, actions, codes, turned, acc0, acc1, sums,
    own, away, root_own, root_away,
    carry, gain_sum, cond_sum, grads, gains, inverse_gains, d_after_kept, d_before_kept,
    d_hidden_kept,
):
    s = sizes
    pair = s.pair
    first_step = s.steps - pair * (turn + 1)
    tower_id = tower_ref[0]
    blocks, width = s.blocks, s.width

    if turn == 0:
        inverse_gains[...] = 1.0 / gains[...]
        carry[...] = jnp.zeros_like(carry)
        grads[...] = jnp.zeros_like(grads)
        gain_sum[...] = jnp.zeros_like(gain_sum)
        cond_sum[...] = jnp.zeros_like(cond_sum)

    def over_lanes(step, column):
        return jnp.broadcast_to(side[step, :, column : column + 1], (s.rows, width))

    def stacked(parts):
        return jnp.concatenate(parts, axis=0)

    def add_grads(matrix, rows_of, place, kept, now):
        later = [kept[offset - 1, place] for offset in range(1, pair)]
        grads[matrix * width : (matrix + 1) * width, :] += by_rows(
            stacked([rows_of[first_step + offset, place] for offset in range(pair)]), stacked([now] + later)
        )

    def add_cond(offset, tower, d_hidden):
        if offset > 0:
            d_hidden_kept[offset - 1, tower] = d_hidden.astype(BF16)
            return
        codes_of, shift = (actions, 0) if tower == 0 else (codes, ACTIONS)
        code = jnp.concatenate(
            [
                codes_of[first_step + step : first_step + step + 1, :] + shift
                for step in range(pair)
            ],
            axis=1,
        )
        spots = lax.broadcasted_iota(jnp.int32, (cond_sum.shape[0], pair * s.rows), 0)
        onehot = jnp.where(spots == code, 1.0, 0.0).astype(BF16)
        parts = [d_hidden.astype(BF16)]
        parts += [d_hidden_kept[step - 1, tower] for step in range(1, pair)]
        cond_sum[...] += natural(onehot, stacked(parts))

    behind = []

    def catch_up():
        while behind:
            behind.pop(0)()

    def tower_back(offset, tower, d_latent):
        normed = lat[first_step + offset, tower]
        normed_wide = normed.astype(F32)
        inv_scale = over_lanes(first_step + offset, s.calls + tower)
        base = inv_scale * d_latent
        slant = inv_scale * (lane_sum(d_latent * normed_wide) * (1.0 / width))
        for block in reversed(range(blocks)):
            place = tower * blocks + block
            matrix = tower * s.calls + block
            both = natural(
                jnp.concatenate([normed, base.astype(BF16)], axis=0), turned[s.calls + place]
            )
            d_hidden = base - slant * normed_wide
            d_branch = d_hidden.astype(BF16)
            entry_wide = entry[first_step + offset, place].astype(F32)
            inv_scale = over_lanes(first_step + offset, place)
            catch_up()
            d_after = both[s.rows :] - slant * both[: s.rows]
            d_before = (d_after * slope[first_step + offset, place].astype(F32)).astype(BF16)
            d_entry = natural(d_before, turned[place])
            if offset > 0:
                d_after_kept[offset - 1, place] = d_branch
                d_before_kept[offset - 1, place] = d_before
            else:
                add_grads(matrix + blocks, after, place, d_after_kept, d_branch)
                behind.append(
                    functools.partial(add_grads, matrix, entry, place, d_before_kept, d_before)
                )
            gain = gains[tower, block : block + 1, :]
            normed_wide = entry_wide * inverse_gains[tower, block : block + 1, :]
            normed = normed_wide.astype(BF16)
            product = d_entry * entry_wide
            base = d_hidden + inv_scale * (d_entry * gain)
            slant = inv_scale * (lane_sum(product) * (1.0 / width))

            def add_gain(tower=tower, block=block, product=product):
                gain_sum[tower, block : block + 1, :] += jnp.sum(product, axis=0, keepdims=True)

            behind.append(add_gain)
        d_hidden = base - slant * normed_wide
        behind.append(functools.partial(add_cond, offset, tower, d_hidden))
        return d_hidden

    def from_heads(offset, tower):
        return jnp.where(turn == 0, dlast[offset, tower], dlat[first_step + offset, tower])

    d_state = carry[...]
    for offset in reversed(range(pair)):
        for tower in (1, 0):
            d_state = tower_back(offset, tower, d_state + dlat[first_step + offset, tower].astype(F32))
    catch_up()
    carry[...] = d_state

    if turn == s.steps // pair - 1:
        left = d_state[:, 0 : width // 2].astype(BF16)
        right = d_state[:, width // 2 : width].astype(BF16)
        root_own[...] = jnp.where(tower_id == 0, left, right)
        root_away[...] = jnp.where(tower_id == 0, right, left)
        gain_sum[...] = gain_sum[...] * inverse_gains[...]
        wide, half = s.wide, s.wide // 2
        lines = lax.broadcasted_iota(jnp.int32, sums.shape, 0)
        small = acc0[wide : wide + s.held, :] + acc1[2 * wide : 2 * wide + s.held, :]
        for target, which in ((own, tower_id), (away, 1 - tower_id)):
            first = which == 0
            for matrix in range(s.calls):
                at = matrix * width
                source = pl.ds(pl.multiple_of((which * s.calls + matrix) * width, width), width)
                target[at : at + width, :] = grads[source, :].astype(BF16)
            for start, stop in cuts(wide):
                value = jnp.where(first, acc0[start:stop, :], acc1[start:stop, :])
                target[s.value_at + start : s.value_at + stop, :] = value.astype(BF16)
            for start, stop in cuts(half):
                reward = jnp.where(
                    first,
                    acc1[wide + start : wide + stop, :],
                    acc1[wide + half + start : wide + half + stop, :],
                )
                target[s.reward_at + start : s.reward_at + stop, :] = reward.astype(BF16)
            here = jnp.where(first, small, 0.0)
            target[s.small_at : s.small_at + s.held, :] = here.astype(BF16)
            here = jnp.where(first, cond_sum[...], 0.0)
            target[s.cond_at : s.shared_end, :] = here.astype(BF16)
            kept = sums[...]
            for block in range(blocks):
                gain = gain_sum[which, block : block + 1, 0:LANES]
                kept = jnp.where(lines == s.gain_row + block, gain, kept)
            target[s.sums_at : s.reward_at, 0:LANES] = kept.astype(BF16)
            kept = jnp.zeros_like(kept)
            for block in range(blocks):
                gain = gain_sum[which, block : block + 1, LANES:]
                kept = jnp.where(lines == s.gain_row + block, gain, kept)
            target[s.sums_at : s.reward_at, LANES:] = kept.astype(BF16)
            if s.total > s.shared_end:
                target[s.shared_end :, :] = jnp.zeros((s.total - s.shared_end, width), BF16)


def logits_kernel(sizes, tower_ref, lat_own, lat_got, value_own, latents, logits):
    rows = sizes.rows
    tower_id = tower_ref[0]
    at_own = pl.ds(pl.multiple_of(tower_id * rows, rows), rows)
    at_got = pl.ds(pl.multiple_of((1 - tower_id) * rows, rows), rows)
    for offset in range(sizes.pair):
        latents[offset, at_own, :] = lat_own[offset]
        latents[offset, at_got, :] = lat_got[offset]
        logits[offset] = by_lanes(value_own[...], latents[offset]).astype(BF16)


def add_and_split_kernel(count, digit_ref, *refs):
    inputs, outputs = refs[:count], refs[count:]
    digit = digit_ref[0]
    for other, target in enumerate(outputs):
        part = digit ^ other
        total = inputs[0][part].astype(F32)
        for source in inputs[1:]:
            total = total + source[part].astype(F32)
        target[...] = total.astype(BF16)


def unpack_own_kernel(sizes, scalars, *refs):
    s = sizes
    factor = len(refs) - 7
    digit, tower_id = scalars[0], scalars[1]
    w_in, w_out, value, gain, rms, flat, held = refs[factor:]
    width = s.width
    length = refs[0].shape[0]
    for other, source in enumerate(refs[:factor]):
        at = pl.multiple_of((digit ^ other) * length, 16)
        flat[pl.ds(at, length), :] = source[...]
    for block in range(s.blocks):
        at = block * width
        w_in[block] = flat[at : at + width, :].astype(F32)
        at = (s.blocks + block) * width
        w_out[block] = flat[at : at + width, :].astype(F32)
    value[:, 0, :] = flat[s.value_at : s.sums_at, :].astype(F32)[0 : s.bins]
    sums = flat[s.sums_at : s.reward_at, :].astype(F32)
    for block in range(s.blocks):
        gain[block] = sums[s.gain_row + block : s.gain_row + block + 1, :]
    held[...] = sums[:, 0:LANES]
    count = jnp.maximum(held[s.kinds : s.kinds + 1, 0 : s.steps], 1.0)
    for block in range(s.blocks):
        for kind in range(2):
            spot = tower_id * s.calls + 2 * block + kind
            square = held[pl.ds(spot, 1), 0 : s.steps]
            rms[block, kind : kind + 1, :] = jnp.sqrt(jnp.maximum(square, 0.0) / (count * width))


def unpack_shared_kernel(sizes, tower_ref, mine, got, reward, small, cond, joined):
    s = sizes
    tower_id = tower_ref[0]
    half = s.wide // 2
    joined[pl.ds(pl.multiple_of(tower_id * half, 8), half), :] = mine[0:half, :].astype(F32)
    joined[pl.ds(pl.multiple_of((1 - tower_id) * half, 8), half), :] = got[0:half, :].astype(F32)
    reward[...] = joined[0 : s.bins, :]
    for target, at in ((small, s.small_at), (cond, s.cond_at)):
        rows = slice(at - s.reward_at, at - s.reward_at + s.held)
        target[...] = (mine[rows, :].astype(F32) + got[rows, :].astype(F32))[0 : s.table_rows]


def whole(shape):
    return pl.BlockSpec(shape, lambda step, tower: (0,) * len(shape))


def swap(value, axis, mask):
    pairs = [(source, source ^ mask) for source in range(lax.axis_size(axis))]
    return lax.ppermute(value, axis, pairs)


AXES = ("tower", "batch")


def exchange_rounds(batch_size):
    factors, left = [], batch_size
    while left > 1:
        factors.append(4 if left % 4 == 0 else 2)
        left //= factors[-1]
    rounds, stride = [], 1
    for factor in factors:
        rounds.append((factor, stride))
        stride *= factor
    turned = rounds[::-1] if len(set(factors)) == 1 else rounds
    return [(one[0], (one[1], two[1])) for one, two in zip(rounds, turned)]


def swap_within(value, strides, other, batch_size):
    pairs = [
        (tower * batch_size + index, tower * batch_size + (index ^ (other * strides[tower])))
        for tower in range(2)
        for index in range(batch_size)
    ]
    return lax.ppermute(value, AXES, pairs)


def swap_all(blocks, strides, batch_size, order):
    return [
        swap_within(blocks[other], strides, other, batch_size) if other else blocks[0]
        for other in order
    ]


def my_digit(factor, strides):
    stride = jnp.where(lax.axis_index("tower") == 0, strides[0], strides[1])
    return (lax.axis_index("batch") // stride) % factor


def add_kernel(*refs):
    total = refs[0][...].astype(F32)
    for source in refs[1:-1]:
        total = total + source[...].astype(F32)
    refs[-1][...] = total.astype(BF16)


def add_up(parts):
    return pl.pallas_call(
        add_kernel,
        out_shape=jax.ShapeDtypeStruct(parts[0].shape, BF16),
        compiler_params=pltpu.CompilerParams(vmem_limit_bytes=SMALL_LIMIT),
        name="add_up",
    )(*parts)


def exchange(value, rounds, batch_size, beside, given, last_kernel):
    factor, strides = rounds[0]
    digit = my_digit(factor, strides)
    rows, width = value[0].shape
    rows = rows // factor
    split = pl.pallas_call(
        functools.partial(add_and_split_kernel, len(value)),
        grid_spec=pltpu.PrefetchScalarGridSpec(
            num_scalar_prefetch=1,
            grid=(1,),
            in_specs=[whole((factor, rows, width))] * len(value),
            out_specs=[whole((rows, width))] * factor,
        ),
        out_shape=[pltpu.HBM((rows, width), BF16)] * factor,
        compiler_params=pltpu.CompilerParams(vmem_limit_bytes=SMALL_LIMIT),
        name="add_and_split",
    )(digit[None], *[part.reshape(factor, rows, width) for part in value])
    split, given = lax.optimization_barrier((split, given))
    held = swap_all(split, strides, batch_size, [0] + list(reversed(range(1, factor))))
    done = beside(given)
    held, done = lax.optimization_barrier((held, done))
    for size, steps in rounds[1:]:
        bit = 1
        while bit < size:
            block = add_up(held)
            held = [block, swap_within(block, steps, bit, batch_size)]
            bit *= 2
    block = add_up(held)
    held = swap_all([block] * factor, strides, batch_size, range(factor))
    return last_kernel(digit, held), done


def body(
    root_state, cond_table, block_gain, w_in, w_out, value_head, reward_head, small_head,
    unroll_len, actions, codes, policy_target, value_bins, reward_bins,
):
    tower_id = lax.axis_index("tower")
    other_id = 1 - tower_id
    tower_ref = tower_id.astype(jnp.int32)[None]
    steps, batch_rows = actions.shape
    blocks, width = block_gain.shape[1:]
    bins = value_head.shape[2]
    table_rows = cond_table.shape[0]
    rows = batch_rows // 2
    half = width // 2
    parts = lax.axis_size("batch")
    s = Sizes(steps, rows, blocks, width, bins, table_rows, parts)
    calls, wide, pair = s.calls, s.wide, s.pair

    root_got = swap(root_state, "tower", 1)
    in_own, out_own, gains_own = w_in[0], w_out[0], block_gain[0]
    value_own = value_head[0].T
    in_got = swap(in_own, "tower", 1)
    out_got = swap(out_own, "tower", 1)
    gains_got = swap(gains_own, "tower", 1)
    value_got = swap(value_own, "tower", 1)
    lengths = unroll_len.reshape(1, batch_rows)

    shape = jax.ShapeDtypeStruct
    per_pair = lambda *tail: pl.BlockSpec(
        (pair,) + tail, lambda turn, tower: (turn,) + (0,) * len(tail)
    )
    unroll_params = pltpu.CompilerParams(vmem_limit_bytes=UNROLL_LIMIT)
    small_params = pltpu.CompilerParams(vmem_limit_bytes=SMALL_LIMIT)
    products = steps * rows * (4 * blocks * width * width + 9 * width * wide)
    cost = pl.CostEstimate(flops=2 * products, bytes_accessed=40 * 2**20, transcendentals=0)
    lat_own, lat_away, loss, own, away, root_own, root_away = pl.pallas_call(
        functools.partial(unroll_kernel, s),
        in_specs=[pl.BlockSpec(memory_space=pltpu.SMEM)]
        + [pl.BlockSpec(memory_space=pltpu.HBM)] * 14
        + [pl.BlockSpec(memory_space=pl.ANY)] * 4
        + [pl.BlockSpec(memory_space=pltpu.VMEM)],
        out_specs=[pl.BlockSpec(memory_space=pltpu.HBM)] * 2
        + [pl.BlockSpec(memory_space=pltpu.VMEM)] * 5,
        scratch_shapes=[
            pltpu.VMEM((steps, 2, rows, width), BF16),
            pltpu.VMEM((steps, calls, rows, width), BF16),
            pltpu.VMEM((steps, calls, rows, width), BF16),
            pltpu.VMEM((steps, calls, rows, width), BF16),
            pltpu.VMEM((steps, rows, LANES), F32),
            pltpu.VMEM((steps, 2, rows, width), BF16),
            pltpu.VMEM((2 * calls, width, width), BF16),
            pltpu.VMEM((2, 16, width), F32),
            pltpu.SemaphoreType.DMA((2,)),
            pltpu.VMEM((rows, half), BF16),
            pltpu.VMEM((rows, half), BF16),
            pltpu.VMEM((1, rows), jnp.int32),
            pltpu.VMEM((steps, rows), jnp.int32),
            pltpu.VMEM((steps, rows), jnp.int32),
            pltpu.VMEM((steps, rows), jnp.int32),
            pltpu.VMEM((steps, 2, rows), jnp.int32),
            pltpu.VMEM((steps, rows), jnp.int32),
            pltpu.VMEM((table_rows, width), BF16),
            pltpu.VMEM((blocks, width), BF16),
            pltpu.VMEM((bins, width), BF16),
            pltpu.VMEM((bins, width), BF16),
            pltpu.VMEM((bins, width), BF16),
            pltpu.VMEM((table_rows, width), BF16),
            pltpu.SemaphoreType.DMA((18,)),
            pltpu.VMEM((rows, width), BF16),
            pltpu.VMEM((pair * rows, width), BF16),
            pltpu.VMEM((pair * rows, width), BF16),
            pltpu.VMEM((LANES, width), BF16),
            pltpu.VMEM((2 * calls, width, width), BF16),
            pltpu.VMEM((s.depth[0], width), BF16),
            pltpu.VMEM((s.depth[1], width), BF16),
            pltpu.VMEM((s.stack[0], width), F32),
            pltpu.VMEM((s.stack[1], width), F32),
            pltpu.VMEM((s.depth[0], pair * rows), BF16),
            pltpu.VMEM((s.depth[1], pair * rows), BF16),
            pltpu.VMEM((s.reward_at - s.sums_at, LANES), F32),
            pltpu.VMEM((steps, s.reward_at - s.sums_at, width), F32),
            pltpu.VMEM((rows, width), F32),
            pltpu.VMEM((2, 16, width), F32),
            pltpu.VMEM((s.held, width), F32),
            pltpu.VMEM((2 * calls * width, width), F32),
            pltpu.VMEM((2, 16, width), F32),
            pltpu.VMEM((max(pair - 1, 1), calls, rows, width), BF16),
            pltpu.VMEM((max(pair - 1, 1), calls, rows, width), BF16),
            pltpu.VMEM((max(pair - 1, 1), 2, rows, width), BF16),
        ],
        out_shape=[
            pltpu.HBM((steps, rows, width), BF16),
            pltpu.HBM((steps, rows, width), BF16),
            shape((8, rows), F32),
            shape((s.total, width), BF16),
            shape((s.total, width), BF16),
            shape((rows, half), BF16),
            shape((rows, half), BF16),
        ],
        compiler_params=unroll_params,
        cost_estimate=cost,
        name="unroll",
    )(
        tower_ref,
        *[
            pltpu.with_memory_space_constraint(value, pltpu.HBM)
            for value in (
                root_state, lengths, actions, codes, policy_target,
                jnp.swapaxes(value_bins, 0, 1), reward_bins, cond_table, gains_own,
                in_own, out_own, value_own, reward_head.T, small_head.T,
            )
        ],
        root_got, in_got, out_got, value_got, gains_got,
    )
    got = swap(away, "tower", 1)

    def beside(given):
        lat_own, lat_away, loss, root_own, root_away = given
        lat_got = swap(lat_away, "tower", 1)
        loss_own = loss[0]
        loss_got = swap(loss_own, "tower", 1)
        root_got = swap(root_away, "tower", 1)

        latents, logits = pl.pallas_call(
            functools.partial(logits_kernel, s),
            grid_spec=pltpu.PrefetchScalarGridSpec(
                num_scalar_prefetch=1,
                grid=(steps // pair,),
                in_specs=[per_pair(rows, width), per_pair(rows, width), whole((bins, width))],
                out_specs=[per_pair(batch_rows, width), per_pair(bins, batch_rows)],
            ),
            out_shape=[
                shape((steps, batch_rows, width), BF16),
                shape((steps, bins, batch_rows), BF16),
            ],
            compiler_params=small_params,
            cost_estimate=pl.CostEstimate(
                flops=2 * steps * batch_rows * width * wide, bytes_accessed=6 * 2**20, transcendentals=0
            ),
            name="latents_and_logits",
        )(
            tower_ref,
            *[
                pltpu.with_memory_space_constraint(part, pltpu.HBM)
                for part in (lat_own, lat_got, value_own)
            ],
        )

        def in_order(mine_value, got_value, axis):
            return jnp.where(
                tower_id == 0,
                jnp.concatenate([mine_value, got_value], axis=axis),
                jnp.concatenate([got_value, mine_value], axis=axis),
            )

        row_loss = in_order(loss_own, loss_got, 0)
        grad_root = in_order(root_own, root_got, 0).astype(F32)
        return latents, logits, row_loss, grad_root

    rounds = exchange_rounds(parts)

    def unpack(digit, held):
        scalars = jnp.stack([digit, tower_id]).astype(jnp.int32)
        length = held[0].shape[0]
        block = s.reward_at // length
        at = s.reward_at - block * length
        parts_of = [part[at : at + s.shared_end - s.reward_at] for part in held]
        shared = parts_of[0]
        for other in range(1, len(held)):
            shared = jnp.where((digit ^ other) == block, parts_of[other], shared)
        shared_got = swap(shared, "tower", 1)
        return (shared, shared_got), pl.pallas_call(
            functools.partial(unpack_own_kernel, s),
            grid_spec=pltpu.PrefetchScalarGridSpec(
                num_scalar_prefetch=1,
                grid=(1,),
                in_specs=[whole(part.shape) for part in held],
                out_specs=[
                    whole((blocks, width, width)),
                    whole((blocks, width, width)),
                    whole((bins, 1, width)),
                    whole((blocks, 1, width)),
                    whole((blocks, 2, steps)),
                ],
                scratch_shapes=[
                    pltpu.VMEM((s.total, width), BF16),
                    pltpu.VMEM((s.reward_at - s.sums_at, LANES), F32),
                ],
            ),
            out_shape=[
                shape((blocks, width, width), F32),
                shape((blocks, width, width), F32),
                shape((bins, 1, width), F32),
                shape((blocks, 1, width), F32),
                shape((blocks, 2, steps), F32),
            ],
            compiler_params=small_params,
            name="unpack_own",
        )(scalars, *held)

    given = (lat_own, lat_away, loss, root_own, root_away)
    unpacked, done = exchange([own, got], rounds, parts, beside, given, unpack)
    (shared, shared_got), (grad_in, grad_out, value_t, gain_t, rms_t) = unpacked
    latents, logits, row_loss, grad_root = done
    reward_t, small_t, grad_cond = pl.pallas_call(
        functools.partial(unpack_shared_kernel, s),
        grid_spec=pltpu.PrefetchScalarGridSpec(
            num_scalar_prefetch=1,
            grid=(1,),
            in_specs=[whole(shared.shape), whole(shared.shape)],
            out_specs=[
                whole((bins, width)),
                whole((table_rows, width)),
                whole((table_rows, width)),
            ],
            scratch_shapes=[pltpu.VMEM((s.wide, width), F32)],
        ),
        out_shape=[
            shape((bins, width), F32),
            shape((table_rows, width), F32),
            shape((table_rows, width), F32),
        ],
        compiler_params=small_params,
        name="unpack_shared",
    )(tower_ref, shared, shared_got)
    layer_rms = jnp.transpose(rms_t, (2, 0, 1))[None]
    return (
        latents[None],
        jnp.swapaxes(logits, 1, 2)[None],
        row_loss,
        layer_rms,
        grad_root,
        grad_cond,
        jnp.swapaxes(gain_t, 0, 1),
        grad_in[None],
        grad_out[None],
        jnp.transpose(value_t, (1, 2, 0)),
        reward_t.T,
        small_t.T,
    )


def solution(mesh):
    placed = (
        P("batch", "tower"),
        P(),
        P("tower", None, None),
        P("tower", None, None, None),
        P("tower", None, None, None),
        P("tower", None, None),
        P(),
        P(),
        P("batch"),
        P(None, "batch"),
        P(None, "batch"),
        P(None, "batch"),
        P(None, None, "batch"),
        P(None, "batch"),
    )
    return jax.shard_map(
        body,
        mesh=mesh,
        in_specs=placed,
        out_specs=(
            P("tower", None, "batch", None),
            P("tower", None, "batch", None),
            P("batch"),
            P("tower", None, None, None),
            P("batch", "tower"),
            P(),
            P("tower", None, None),
            P("tower", None, None, None),
            P("tower", None, None, None),
            P("tower", None, None),
            P(),
            P(),
        ),
        check_vma=False,
    )
```

```python
import functools

import jax
import jax.numpy as jnp
from jax import lax
from jax.experimental import pallas as pl
from jax.experimental.pallas import tpu as pltpu
from jax.sharding import PartitionSpec as P

ACTIONS = 4
LANES = 128
MIB = 1024 * 1024
UNROLL_LIMIT = 50 * MIB
SMALL_LIMIT = 12 * MIB
epsilon = 1e-06
very_negative = -1e30
F32 = jnp.float32
BF16 = jnp.bfloat16


def natural(left, right):
    return lax.dot_general(left, right, (((1,), (0,)), ((), ())), preferred_element_type=F32)


def by_rows(left, right):
    return lax.dot_general(left, right, (((0,), (0,)), ((), ())), preferred_element_type=F32)


def by_lanes(left, right):
    return lax.dot_general(left, right, (((1,), (1,)), ((), ())), preferred_element_type=F32)


def round_up(value, unit):
    return (value + unit - 1) // unit * unit


def lane_sum(value):
    return jnp.sum(value, axis=-1, keepdims=True)


def inverse_rms(hidden):
    return lax.rsqrt(lane_sum(hidden * hidden) * (1.0 / hidden.shape[-1]) + epsilon)


def weave(*tasks):
    tasks = [(list(task)) for task in tasks]
    longest = max(len(task) for task in tasks)
    done = [0] * len(tasks)
    for turn in range(longest):
        for which, task in enumerate(tasks):
            until = (turn + 1) * len(task) // longest
            while done[which] < until:
                task[done[which]]()
                done[which] += 1


def cuts(length, unit=160):
    return [(start, min(start + unit, length)) for start in range(0, length, unit)]


class Sizes:
    def __init__(self, steps, rows, blocks, width, bins, table_rows, parts):
        self.steps, self.rows, self.blocks, self.width = steps, rows, blocks, width
        self.bins, self.table_rows, self.parts = bins, table_rows, parts
        self.calls = 2 * blocks
        self.pair = 2 if steps % 2 == 0 else 1
        self.wide = round_up(bins, 32)
        self.held = round_up(table_rows, 16)
        self.stack = (self.wide + self.held, 2 * self.wide + self.held)
        self.depth = tuple(round_up(rows_in, LANES) for rows_in in self.stack)
        half = self.wide // 2
        self.value_at = self.calls * width
        self.sums_at = self.value_at + self.wide
        self.kinds = 2 * self.calls
        self.gain_row = self.kinds + 1
        self.reward_at = self.sums_at + round_up(self.gain_row + blocks, 16)
        self.small_at = self.reward_at + half
        self.cond_at = self.small_at + self.held
        self.shared_end = self.cond_at + self.held
        self.total = round_up(self.shared_end, 16 * parts)
        self.head_rows = self.cond_at - self.value_at


def unroll_kernel(
    sizes, tower_ref,
    root_hbm, lengths_hbm, actions_hbm, codes_hbm, policy_hbm, value_bins_hbm, reward_bins_hbm,
    table_hbm, gains_hbm, in_hbm, out_hbm, value_hbm, reward_hbm, small_hbm,
    root_any, in_got, out_got, value_any, gains_got,
    lat_own, lat_away, loss, own, away, root_own_grad, root_away_grad,
    lat, entry, after, slope, side, dlat, turned, gains, lat_sems,
    root_own, root_got, lengths, actions, codes, policy, value_bins, reward_bins,
    table_in, gains_own, value_own, value_got, reward_in, small_in, sems,
    state, past0, past1, table, weights, heads0, heads1, acc0, acc1,
    cot0, cot1, sums, squares,
    carry, gain_sum, cond_sum, grads, inverse_gains, d_after_kept, d_before_kept, d_hidden_kept,
):
    turns = sizes.steps // sizes.pair
    small, large = sizes.stack
    logits0 = grads.at[pl.ds(0, small)]
    logits1 = grads.at[pl.ds(small, large)]
    for turn in range(turns):
        forward_turn(
            sizes, turn, tower_ref,
            root_hbm, lengths_hbm, actions_hbm, codes_hbm, policy_hbm, value_bins_hbm,
            reward_bins_hbm, table_hbm, gains_hbm, in_hbm, out_hbm, value_hbm, reward_hbm,
            small_hbm, root_any, in_got, out_got, value_any, gains_got,
            lat, entry, after, slope, side, dlat, loss, turned, gains,
            root_own, root_got, lengths, actions, codes, policy, value_bins, reward_bins,
            table_in, gains_own, value_own, value_got, reward_in, small_in, sems,
            state, past0, past1, table, weights, heads0, heads1, acc0, acc1,
            logits0, logits1, cot0, cot1, sums, squares,
        )
    tower_id = tower_ref[0]
    copies = [
        pltpu.make_async_copy(lat.at[:, tower_id], lat_own, lat_sems.at[0]),
        pltpu.make_async_copy(lat.at[:, 1 - tower_id], lat_away, lat_sems.at[1]),
    ]
    for copy in copies:
        copy.start()

    def one_backward(turn, is_first):
        backward_turn(
            sizes, turn, is_first,
            lat, entry, after, slope, side, dlat, actions, codes, turned,
            carry, gain_sum, cond_sum, grads, gains, inverse_gains, d_after_kept, d_before_kept,
            d_hidden_kept,
        )

    def later_backward(turn, _):
        one_backward(turn, False)
        return 0

    one_backward(0, True)
    lax.fori_loop(1, turns, later_backward, 0)
    finish_backward(
        sizes, tower_ref, acc0, acc1, sums, own, away, root_own_grad, root_away_grad,
        carry, gain_sum, cond_sum, grads, inverse_gains,
    )
    for copy in copies:
        copy.wait()


def forward_turn(
    sizes, turn, tower_ref,
    root_hbm, lengths_hbm, actions_hbm, codes_hbm, policy_hbm, value_bins_hbm, reward_bins_hbm,
    table_hbm, gains_hbm, in_hbm, out_hbm, value_hbm, reward_hbm, small_hbm,
    root_any, in_got, out_got, value_any, gains_got,
    lat, entry, after, slope, side, dlat, loss, turned, gains,
    root_own, root_got, lengths, actions, codes, policy, value_bins, reward_bins,
    table_in, gains_own, value_own, value_got, reward_in, small_in, sems,
    state, past0, past1, table, weights, heads0, heads1, acc0, acc1,
    logits0, logits1, cot0, cot1, sums, squares,
):
    s = sizes
    pair = s.pair
    first_step = turn * pair
    tower_id = tower_ref[0]
    rows, width, wide = s.rows, s.width, s.wide

    if turn == 0:
        here = pl.ds(pl.multiple_of(tower_id * rows, rows), rows)

        def matrices(kind, tower):
            return weights.at[pl.ds(kind * s.calls + tower * s.blocks, s.blocks)]

        moves = [
            (in_hbm, matrices(0, tower_id)),
            (out_hbm, matrices(1, tower_id)),
            (in_got, matrices(0, 1 - tower_id)),
            (out_got, matrices(1, 1 - tower_id)),
            (value_hbm, value_own),
            (value_any, value_got),
            (reward_hbm, reward_in),
            (small_hbm, small_in),
            (table_hbm, table_in),
            (gains_hbm, gains_own),
            (root_hbm.at[here], root_own),
            (root_any.at[here], root_got),
            (actions_hbm.at[:, here], actions),
            (codes_hbm.at[:, here], codes),
            (lengths_hbm.at[:, here], lengths),
            (policy_hbm.at[:, here], policy),
            (value_bins_hbm.at[:, :, here], value_bins),
            (reward_bins_hbm.at[:, here], reward_bins),
        ]
        moves = [
            pltpu.make_async_copy(source, target, sems.at[place])
            for place, (source, target) in enumerate(moves)
        ]
        for move in moves:
            move.start()
        gains[...] = jnp.ones_like(gains)
        for target in (
            table, sums, squares, loss
        ):
            target[...] = jnp.zeros_like(target)
        for stack, cot, rows_used in ((heads0, cot0, s.stack[0]), (heads1, cot1, s.stack[1])):
            start = rows_used - s.held
            stack[start:, :] = jnp.zeros((stack.shape[0] - start, width), BF16)
            for end in range(wide, start + 1, wide):
                stack[end - 16 : end, :] = jnp.zeros((16, width), BF16)
            cot[rows_used:, :] = jnp.zeros((cot.shape[0] - rows_used, pair * rows), BF16)
        for move in moves:
            move.wait()
        first = tower_id == 0
        state[:, 0 : width // 2] = jnp.where(first, root_own[...], root_got[...])
        state[:, width // 2 : width] = jnp.where(first, root_got[...], root_own[...])
        gains[tower_id, 0 : s.blocks, :] = gains_own[...].astype(F32)
        gains[1 - tower_id, 0 : s.blocks, :] = gains_got[...].astype(F32)
        table[0 : s.table_rows, :] = table_in[...]
        heads0[0 : s.bins, :] = jnp.where(first, value_own[...], value_got[...])
        heads1[0 : s.bins, :] = jnp.where(first, value_got[...], value_own[...])
        heads1[wide : wide + s.bins, :] = reward_in[...]
        heads0[wide : wide + s.table_rows, :] = small_in[...]
        heads1[2 * wide : 2 * wide + s.table_rows, :] = small_in[...]

    eights = lax.broadcasted_iota(jnp.int32, (8, pair * rows), 0)
    before = first_step - pair

    def pair_row(kind, at_step, lead=()):
        return jnp.concatenate(
            [kind[(slice(at_step + offset, at_step + offset + 1),) + lead] for offset in range(pair)],
            axis=1,
        )

    def live_rows(at_step):
        return jnp.concatenate(
            [(at_step + offset < lengths[...]).astype(F32) for offset in range(pair)], axis=1
        )

    kinds = []
    for offset in range(pair):
        step = first_step + offset
        kinds.append((step < lengths[...]).astype(F32))
        kinds.append(actions[step : step + 1, :].astype(F32))
        kinds.append((codes[step : step + 1, :] + ACTIONS).astype(F32))
    kinds.append(jnp.zeros((8 - len(kinds), rows), F32))
    columns = jnp.concatenate(kinds, axis=0).T

    def heads(tower, live_row, at_step, put):
        latent = past0 if tower == 0 else past1
        stack, logits, cot, acc = (
            (heads0, logits0, cot0, acc0) if tower == 0 else (heads1, logits1, cot1, acc1)
        )
        pick = lambda kind: pair_row(kind, at_step)
        value_goal = pair_row(value_bins, at_step, (tower,))
        spans = [(0, wide, 0, s.bins, value_goal)]
        if tower == 1:
            spans.append((wide, wide, 0, s.bins, pick(reward_bins)))
            spans.append((2 * wide, s.held, 0, ACTIONS, pick(policy)))
        else:
            spans.append((wide, s.held, ACTIONS, s.table_rows, pick(codes) + ACTIONS))

        def make_logits(start, stop):
            logits[start:stop, :] = by_lanes(stack[start:stop, :], latent[...])

        def eight_rows(value):
            return value.reshape(-1, 8, pair * rows)

        def mask(at, length, first, last):
            for start in range(0, length, 8):
                if start < first or start + 8 > last:
                    inside = (eights >= first - start) & (eights < last - start)
                    place = slice(at + start, at + start + 8)
                    logits[place, :] = jnp.where(inside, logits[place, :], very_negative)

        def find_top(at, start, stop, kept):
            top = jnp.max(eight_rows(logits[at + start : at + stop, :]), axis=0)
            kept["top"] = jnp.maximum(kept["top"], top) if "top" in kept else top

        def end_top(kept):
            kept["top"] = jnp.max(kept["top"], axis=0, keepdims=True)

        def make_terms(at, start, stop, goal, kept):
            place = slice(at + start, at + stop)
            value = logits[place, :]
            spot = lax.broadcasted_iota(jnp.int32, value.shape, 0)
            term = jnp.exp(value - kept["top"])
            logits[place, :] = term
            hit = spot == goal - start
            total = jnp.sum(eight_rows(term), axis=0)
            picked = jnp.sum(eight_rows(jnp.where(hit, value, 0.0)), axis=0)
            kept["total"] = kept["total"] + total if "total" in kept else total
            kept["picked"] = kept["picked"] + picked if "picked" in kept else picked

        def end_terms(kept):
            total = jnp.sum(kept["total"], axis=0, keepdims=True)
            picked = jnp.sum(kept["picked"], axis=0, keepdims=True)
            kept["scale"] = live_row / total
            row_loss = live_row * (jnp.log(total) + kept["top"] - picked)
            for offset in range(pair):
                loss[0:1, :] += row_loss[:, offset * rows : (offset + 1) * rows]

        def make_cotangent(at, start, stop, goal, kept):
            place = slice(at + start, at + stop)
            term = logits[place, :]
            spot = lax.broadcasted_iota(jnp.int32, term.shape, 0)
            hit = spot == goal - start
            cot[place, :] = (term * kept["scale"] - jnp.where(hit, live_row, 0.0)).astype(BF16)

        def make_grads(start, stop):
            product = natural(cot[start:stop, :], latent[...])
            if at_step > 0:
                product = acc[start:stop, :] + product
            acc[start:stop, :] = product

        def make_latent():
            d_latent = by_rows(cot[...], stack[...])
            for offset in range(pair):
                put[at_step + offset, tower] = d_latent[offset * rows : (offset + 1) * rows].astype(
                    BF16
                )

        large = cuts(acc.shape[0], 320)
        pieces = [functools.partial(make_logits, *cut) for cut in large]
        for at, length, first, last, goal in spans:
            kept = {}
            each = cuts(length)
            pieces.append(functools.partial(mask, at, length, first, last))
            pieces += [functools.partial(find_top, at, *cut, kept) for cut in each]
            pieces.append(functools.partial(end_top, kept))
            pieces += [functools.partial(make_terms, at, *cut, goal, kept) for cut in each]
            pieces.append(functools.partial(end_terms, kept))
            pieces += [functools.partial(make_cotangent, at, *cut, goal, kept) for cut in each]
        return pieces + [make_latent] + [functools.partial(make_grads, *cut) for cut in large]

    def columns_of(offset, tower):
        live = columns[:, 3 * offset : 3 * offset + 1]
        return live, columns[:, 3 * offset + 1 + tower : 3 * offset + 2 + tower]

    def embedding(offset, tower):
        _, code = columns_of(offset, tower)
        spot = lax.broadcasted_iota(jnp.int32, (rows, table.shape[0]), 1)
        onehot = jnp.where(spot.astype(F32) == code, 1.0, 0.0).astype(BF16)
        return natural(onehot, table[...])

    def tower_call(offset, tower, chain):
        live, _ = columns_of(offset, tower)

        def scale_rows():
            row_squares = lane_sum(chain["hidden"] * chain["hidden"])
            return row_squares, lax.rsqrt(row_squares * (1.0 / width) + epsilon)

        def keep_squares(block, row_squares):
            place = 2 * (tower * s.blocks + block)
            total = jnp.sum(live * row_squares, axis=0, keepdims=True) * (1.0 / LANES)
            squares[first_step + offset, place : place + 1, 0:LANES] = jnp.broadcast_to(total, (1, LANES))

        def end_block(block):
            branch = chain["product"]
            chain["hidden"] = chain["hidden"] + branch
            return branch

        def keep_branch(block, branch):
            spot = 2 * (tower * s.blocks + block) + 1
            squares[first_step + offset, spot : spot + 1, :] = jnp.sum(
                branch * branch * live, axis=0, keepdims=True
            )

        def into(block):
            place = tower * s.blocks + block
            if block > 0:
                branch = end_block(block - 1)
            gained = chain["hidden"] * gains[tower, block : block + 1, :]
            chain["product"] = natural(gained.astype(BF16), weights[place])
            row_squares, inv_scale = scale_rows()
            chain["scale"] = inv_scale
            entry[first_step + offset, place] = (gained * inv_scale).astype(BF16)
            side[first_step + offset, :, place : place + 1] = inv_scale
            if block > 0:
                keep_squares(block - 1, row_squares)
                keep_branch(block - 1, branch)

        def out_of(block):
            place = tower * s.blocks + block
            u = chain["product"] * chain["scale"]
            gate = 0.5 * jnp.tanh(0.5 * u) + 0.5
            after_rows = (u * gate).astype(BF16)
            chain["product"] = natural(after_rows, weights[s.calls + place])
            after[first_step + offset, place] = after_rows
            slope[first_step + offset, place] = (gate * (1.0 + u * (1.0 - gate))).astype(BF16)

        def finish():
            branch = end_block(s.blocks - 1)
            row_squares, inv_scale = scale_rows()
            latent = (chain["hidden"] * inv_scale).astype(BF16)
            chain[offset, tower] = latent
            following = (offset, 1) if tower == 0 else (offset + 1, 0)
            if following in chain:
                chain["hidden"] = latent.astype(F32) + chain[following]

            def keep():
                spot = s.calls + tower
                side[first_step + offset, :, spot : spot + 1] = inv_scale
                lat[first_step + offset, tower] = latent
                keep_squares(s.blocks - 1, row_squares)
                keep_branch(s.blocks - 1, branch)
                if tower == 0:
                    total = jnp.sum(live, axis=0, keepdims=True) * (1.0 / LANES)
                    squares[first_step + offset, s.kinds : s.kinds + 1, 0:LANES] = jnp.broadcast_to(
                        total, (1, LANES)
                    )

            return keep

        pieces = []
        for block in range(s.blocks):
            pieces += [functools.partial(into, block), functools.partial(out_of, block)]
        return pieces, finish

    chain = {
        (offset, tower): embedding(offset, tower) for offset in range(pair) for tower in range(2)
    }
    chain["hidden"] = state[...].astype(F32) + chain[0, 0]
    pieces = []
    keeps = []

    def begin_next(finish, into):
        keeps.append(finish())
        into()
        keeps.pop()()

    ending = None
    for offset in range(pair):
        for tower in range(2):
            calls, finish = tower_call(offset, tower, chain)
            if ending is not None:
                calls[0] = functools.partial(begin_next, ending, calls[0])
            pieces += calls
            ending = finish
    pieces.append(lambda: ending()())

    turns = -(-2 * s.calls // (s.steps // pair))

    def turn_weights(matrix):
        turned[matrix] = weights[matrix].T

    beside = []
    if turn > 0:
        live_before = live_rows(before)
        beside += heads(1, live_before, before, dlat) + heads(0, live_before, before, dlat)
    matrices_now = range(turn * turns, min((turn + 1) * turns, 2 * s.calls))
    beside += [functools.partial(turn_weights, matrix) for matrix in matrices_now]
    weave(pieces, beside)
    at_lane = lax.broadcasted_iota(jnp.int32, sums.shape, 1)
    for offset in range(pair):
        at = slice(offset * rows, (offset + 1) * rows)
        after_state, next_state = chain[offset, 0], chain[offset, 1]
        past0[at, :] = after_state
        past1[at, :] = next_state
        if offset == pair - 1:
            state[...] = next_state
        total = lane_sum(squares[first_step + offset])
        sums[...] = jnp.where(at_lane == first_step + offset, total, sums[...])

    if turn == s.steps // pair - 1:
        live_now = live_rows(first_step)
        for piece in heads(1, live_now, first_step, dlat) + heads(0, live_now, first_step, dlat):
            piece()


def backward_turn(
    sizes, turn, is_first,
    lat, entry, after, slope, side, dlat, actions, codes, turned,
    carry, gain_sum, cond_sum, grads, gains, inverse_gains, d_after_kept, d_before_kept,
    d_hidden_kept,
):
    s = sizes
    pair = s.pair
    first_step = s.steps - pair * (turn + 1)
    blocks, width = s.blocks, s.width
    if is_first:
        inverse_gains[...] = 1.0 / gains[...]
        carry[...] = jnp.zeros_like(carry)
        gain_sum[...] = jnp.zeros_like(gain_sum)
        cond_sum[...] = jnp.zeros_like(cond_sum)

    def over_lanes(step, column):
        return jnp.broadcast_to(side[step, :, column : column + 1], (s.rows, width))

    def stacked(parts):
        return jnp.concatenate(parts, axis=0)

    def add_grads(matrix, rows_of, place, kept, now):
        later = [kept[offset - 1, place] for offset in range(1, pair)]
        product = by_rows(
            stacked([rows_of[first_step + offset, place] for offset in range(pair)]),
            stacked([now] + later),
        )
        at = slice(matrix * width, (matrix + 1) * width)
        if not is_first:
            product = grads[at, :] + product
        grads[at, :] = product

    def add_cond(offset, tower, d_hidden):
        if offset > 0:
            d_hidden_kept[offset - 1, tower] = d_hidden.astype(BF16)
            return
        codes_of, shift = (actions, 0) if tower == 0 else (codes, ACTIONS)
        code = jnp.concatenate(
            [
                codes_of[pl.ds(first_step + step, 1), :] + shift
                for step in range(pair)
            ],
            axis=1,
        )
        spots = lax.broadcasted_iota(jnp.int32, (cond_sum.shape[0], pair * s.rows), 0)
        onehot = jnp.where(spots == code, 1.0, 0.0).astype(BF16)
        parts = [d_hidden.astype(BF16)]
        parts += [d_hidden_kept[step - 1, tower] for step in range(1, pair)]
        cond_sum[...] += natural(onehot, stacked(parts))

    behind = []

    def catch_up():
        while behind:
            behind.pop(0)()

    def tower_back(offset, tower, d_latent):
        normed = lat[first_step + offset, tower]
        normed_wide = normed.astype(F32)
        inv_scale = over_lanes(first_step + offset, s.calls + tower)
        base = inv_scale * d_latent
        slant = inv_scale * (lane_sum(d_latent * normed_wide) * (1.0 / width))
        for block in reversed(range(blocks)):
            place = tower * blocks + block
            matrix = tower * s.calls + block
            both = natural(
                jnp.concatenate([normed, base.astype(BF16)], axis=0), turned[s.calls + place]
            )
            d_hidden = base - slant * normed_wide
            d_branch = d_hidden.astype(BF16)
            entry_wide = entry[first_step + offset, place].astype(F32)
            inv_scale = over_lanes(first_step + offset, place)
            catch_up()
            d_after = both[s.rows :] - slant * both[: s.rows]
            d_before = (d_after * slope[first_step + offset, place].astype(F32)).astype(BF16)
            d_entry = natural(d_before, turned[place])
            if offset > 0:
                d_after_kept[offset - 1, place] = d_branch
                d_before_kept[offset - 1, place] = d_before
            else:
                add_grads(matrix + blocks, after, place, d_after_kept, d_branch)
                behind.append(
                    functools.partial(add_grads, matrix, entry, place, d_before_kept, d_before)
                )
            gain = gains[tower, block : block + 1, :]
            normed_wide = entry_wide * inverse_gains[tower, block : block + 1, :]
            normed = normed_wide.astype(BF16)
            product = d_entry * entry_wide
            base = d_hidden + inv_scale * (d_entry * gain)
            slant = inv_scale * (lane_sum(product) * (1.0 / width))

            def add_gain(tower=tower, block=block, product=product):
                gain_sum[tower, block : block + 1, :] += jnp.sum(product, axis=0, keepdims=True)

            behind.append(add_gain)
        d_hidden = base - slant * normed_wide
        behind.append(functools.partial(add_cond, offset, tower, d_hidden))
        return d_hidden

    def from_heads(offset, tower):
        return jnp.where(turn == 0, dlast[offset, tower], dlat[first_step + offset, tower])

    d_state = carry[...]
    for offset in reversed(range(pair)):
        for tower in (1, 0):
            d_state = tower_back(offset, tower, d_state + dlat[first_step + offset, tower].astype(F32))
    catch_up()
    carry[...] = d_state


def finish_backward(
    sizes, tower_ref, acc0, acc1, sums, own, away, root_own, root_away,
    carry, gain_sum, cond_sum, grads, inverse_gains,
):
    s = sizes
    tower_id = tower_ref[0]
    blocks, width = s.blocks, s.width
    d_state = carry[...]
    left = d_state[:, 0 : width // 2].astype(BF16)
    right = d_state[:, width // 2 : width].astype(BF16)
    root_own[...] = jnp.where(tower_id == 0, left, right)
    root_away[...] = jnp.where(tower_id == 0, right, left)
    gain_sum[...] = gain_sum[...] * inverse_gains[...]
    wide, half = s.wide, s.wide // 2
    lines = lax.broadcasted_iota(jnp.int32, sums.shape, 0)
    small = acc0[wide : wide + s.held, :] + acc1[2 * wide : 2 * wide + s.held, :]
    for target, which in ((own, tower_id), (away, 1 - tower_id)):
        first = which == 0

        def put_matrix(matrix, _, target=target, which=which):
            source = pl.ds(pl.multiple_of((which * s.calls + matrix) * width, width), width)
            at = pl.ds(pl.multiple_of(matrix * width, width), width)
            target[at, :] = grads[source, :].astype(BF16)
            return 0

        lax.fori_loop(0, s.calls, put_matrix, 0)
        for start, stop in cuts(wide):
            value = jnp.where(first, acc0[start:stop, :], acc1[start:stop, :])
            target[s.value_at + start : s.value_at + stop, :] = value.astype(BF16)
        for start, stop in cuts(half):
            reward = jnp.where(
                first,
                acc1[wide + start : wide + stop, :],
                acc1[wide + half + start : wide + half + stop, :],
            )
            target[s.reward_at + start : s.reward_at + stop, :] = reward.astype(BF16)
        here = jnp.where(first, small, 0.0)
        target[s.small_at : s.small_at + s.held, :] = here.astype(BF16)
        here = jnp.where(first, cond_sum[...], 0.0)
        target[s.cond_at : s.shared_end, :] = here.astype(BF16)
        kept = sums[...]
        for block in range(blocks):
            gain = gain_sum[which, block : block + 1, 0:LANES]
            kept = jnp.where(lines == s.gain_row + block, gain, kept)
        target[s.sums_at : s.reward_at, 0:LANES] = kept.astype(BF16)
        kept = jnp.zeros_like(kept)
        for block in range(blocks):
            gain = gain_sum[which, block : block + 1, LANES:]
            kept = jnp.where(lines == s.gain_row + block, gain, kept)
        target[s.sums_at : s.reward_at, LANES:] = kept.astype(BF16)
        if s.total > s.shared_end:
            target[s.shared_end :, :] = jnp.zeros((s.total - s.shared_end, width), BF16)


def logits_kernel(sizes, tower_ref, lat_own, lat_got, value_own, latents, logits):
    rows = sizes.rows
    tower_id = tower_ref[0]
    at_own = pl.ds(pl.multiple_of(tower_id * rows, rows), rows)
    at_got = pl.ds(pl.multiple_of((1 - tower_id) * rows, rows), rows)
    for offset in range(sizes.pair):
        latents[offset, at_own, :] = lat_own[offset]
        latents[offset, at_got, :] = lat_got[offset]
        logits[offset] = by_lanes(value_own[...], latents[offset]).astype(BF16)


def add_and_split_kernel(count, digit_ref, *refs):
    inputs, outputs = refs[:count], refs[count:]
    digit = digit_ref[0]
    for other, target in enumerate(outputs):
        part = digit ^ other
        total = inputs[0][part].astype(F32)
        for source in inputs[1:]:
            total = total + source[part].astype(F32)
        target[...] = total.astype(BF16)


def unpack_own_kernel(sizes, scalars, *refs):
    s = sizes
    factor = len(refs) - 7
    digit, tower_id = scalars[0], scalars[1]
    w_in, w_out, value, gain, rms, flat, held = refs[factor:]
    width = s.width
    length = refs[0].shape[0]
    for other, source in enumerate(refs[:factor]):
        at = pl.multiple_of((digit ^ other) * length, 16)
        flat[pl.ds(at, length), :] = source[...]
    for block in range(s.blocks):
        at = block * width
        w_in[block] = flat[at : at + width, :].astype(F32)
        at = (s.blocks + block) * width
        w_out[block] = flat[at : at + width, :].astype(F32)
    value[:, 0, :] = flat[s.value_at : s.sums_at, :].astype(F32)[0 : s.bins]
    sums = flat[s.sums_at : s.reward_at, :].astype(F32)
    for block in range(s.blocks):
        gain[block] = sums[s.gain_row + block : s.gain_row + block + 1, :]
    held[...] = sums[:, 0:LANES]
    count = jnp.maximum(held[s.kinds : s.kinds + 1, 0 : s.steps], 1.0)
    for block in range(s.blocks):
        for kind in range(2):
            spot = tower_id * s.calls + 2 * block + kind
            square = held[pl.ds(spot, 1), 0 : s.steps]
            rms[block, kind : kind + 1, :] = jnp.sqrt(jnp.maximum(square, 0.0) / (count * width))


def unpack_shared_kernel(sizes, tower_ref, mine, got, reward, small, cond, joined):
    s = sizes
    tower_id = tower_ref[0]
    half = s.wide // 2
    joined[pl.ds(pl.multiple_of(tower_id * half, 8), half), :] = mine[0:half, :].astype(F32)
    joined[pl.ds(pl.multiple_of((1 - tower_id) * half, 8), half), :] = got[0:half, :].astype(F32)
    reward[...] = joined[0 : s.bins, :]
    for target, at in ((small, s.small_at), (cond, s.cond_at)):
        rows = slice(at - s.reward_at, at - s.reward_at + s.held)
        target[...] = (mine[rows, :].astype(F32) + got[rows, :].astype(F32))[0 : s.table_rows]


def whole(shape):
    return pl.BlockSpec(shape, lambda step, tower: (0,) * len(shape))


def swap(value, axis, mask):
    pairs = [(source, source ^ mask) for source in range(lax.axis_size(axis))]
    return lax.ppermute(value, axis, pairs)


AXES = ("tower", "batch")


def exchange_rounds(batch_size):
    factors, left = [], batch_size
    while left > 1:
        factors.append(4 if left % 4 == 0 else 2)
        left //= factors[-1]
    rounds, stride = [], 1
    for factor in factors:
        rounds.append((factor, stride))
        stride *= factor
    turned = rounds[::-1] if len(set(factors)) == 1 else rounds
    return [(one[0], (one[1], two[1])) for one, two in zip(rounds, turned)]


def swap_within(value, strides, other, batch_size):
    pairs = [
        (tower * batch_size + index, tower * batch_size + (index ^ (other * strides[tower])))
        for tower in range(2)
        for index in range(batch_size)
    ]
    return lax.ppermute(value, AXES, pairs)


def swap_all(blocks, strides, batch_size, order):
    return [
        swap_within(blocks[other], strides, other, batch_size) if other else blocks[0]
        for other in order
    ]


def my_digit(factor, strides):
    stride = jnp.where(lax.axis_index("tower") == 0, strides[0], strides[1])
    return (lax.axis_index("batch") // stride) % factor


def add_kernel(*refs):
    total = refs[0][...].astype(F32)
    for source in refs[1:-1]:
        total = total + source[...].astype(F32)
    refs[-1][...] = total.astype(BF16)


def add_up(parts):
    return pl.pallas_call(
        add_kernel,
        out_shape=jax.ShapeDtypeStruct(parts[0].shape, BF16),
        compiler_params=pltpu.CompilerParams(vmem_limit_bytes=SMALL_LIMIT),
        name="add_up",
    )(*parts)


def exchange(value, rounds, batch_size, beside, given, last_kernel):
    factor, strides = rounds[0]
    digit = my_digit(factor, strides)
    rows, width = value[0].shape
    rows = rows // factor
    split = pl.pallas_call(
        functools.partial(add_and_split_kernel, len(value)),
        grid_spec=pltpu.PrefetchScalarGridSpec(
            num_scalar_prefetch=1,
            grid=(1,),
            in_specs=[whole((factor, rows, width))] * len(value),
            out_specs=[whole((rows, width))] * factor,
        ),
        out_shape=[pltpu.HBM((rows, width), BF16)] * factor,
        compiler_params=pltpu.CompilerParams(vmem_limit_bytes=SMALL_LIMIT),
        name="add_and_split",
    )(digit[None], *[part.reshape(factor, rows, width) for part in value])
    split, given = lax.optimization_barrier((split, given))
    held = swap_all(split, strides, batch_size, [0] + list(reversed(range(1, factor))))
    done = beside(given)
    held, done = lax.optimization_barrier((held, done))
    for size, steps in rounds[1:]:
        bit = 1
        while bit < size:
            block = add_up(held)
            held = [block, swap_within(block, steps, bit, batch_size)]
            bit *= 2
    block = add_up(held)
    held = swap_all([block] * factor, strides, batch_size, range(factor))
    return last_kernel(digit, held), done


def body(
    root_state, cond_table, block_gain, w_in, w_out, value_head, reward_head, small_head,
    unroll_len, actions, codes, policy_target, value_bins, reward_bins,
):
    tower_id = lax.axis_index("tower")
    other_id = 1 - tower_id
    tower_ref = tower_id.astype(jnp.int32)[None]
    steps, batch_rows = actions.shape
    blocks, width = block_gain.shape[1:]
    bins = value_head.shape[2]
    table_rows = cond_table.shape[0]
    rows = batch_rows // 2
    half = width // 2
    parts = lax.axis_size("batch")
    s = Sizes(steps, rows, blocks, width, bins, table_rows, parts)
    calls, wide, pair = s.calls, s.wide, s.pair

    root_got = swap(root_state, "tower", 1)
    in_own, out_own, gains_own = w_in[0], w_out[0], block_gain[0]
    value_own = value_head[0].T
    in_got = swap(in_own, "tower", 1)
    out_got = swap(out_own, "tower", 1)
    gains_got = swap(gains_own, "tower", 1)
    value_got = swap(value_own, "tower", 1)
    lengths = unroll_len.reshape(1, batch_rows)

    shape = jax.ShapeDtypeStruct
    per_pair = lambda *tail: pl.BlockSpec(
        (pair,) + tail, lambda turn, tower: (turn,) + (0,) * len(tail)
    )
    unroll_params = pltpu.CompilerParams(vmem_limit_bytes=UNROLL_LIMIT)
    small_params = pltpu.CompilerParams(vmem_limit_bytes=SMALL_LIMIT)
    products = steps * rows * (4 * blocks * width * width + 9 * width * wide)
    cost = pl.CostEstimate(flops=2 * products, bytes_accessed=40 * 2**20, transcendentals=0)
    lat_own, lat_away, loss, own, away, root_own, root_away = pl.pallas_call(
        functools.partial(unroll_kernel, s),
        in_specs=[pl.BlockSpec(memory_space=pltpu.SMEM)]
        + [pl.BlockSpec(memory_space=pltpu.HBM)] * 14
        + [pl.BlockSpec(memory_space=pl.ANY)] * 4
        + [pl.BlockSpec(memory_space=pltpu.VMEM)],
        out_specs=[pl.BlockSpec(memory_space=pltpu.HBM)] * 2
        + [pl.BlockSpec(memory_space=pltpu.VMEM)] * 5,
        scratch_shapes=[
            pltpu.VMEM((steps, 2, rows, width), BF16),
            pltpu.VMEM((steps, calls, rows, width), BF16),
            pltpu.VMEM((steps, calls, rows, width), BF16),
            pltpu.VMEM((steps, calls, rows, width), BF16),
            pltpu.VMEM((steps, rows, LANES), F32),
            pltpu.VMEM((steps, 2, rows, width), BF16),
            pltpu.VMEM((2 * calls, width, width), BF16),
            pltpu.VMEM((2, 16, width), F32),
            pltpu.SemaphoreType.DMA((2,)),
            pltpu.VMEM((rows, half), BF16),
            pltpu.VMEM((rows, half), BF16),
            pltpu.VMEM((1, rows), jnp.int32),
            pltpu.VMEM((steps, rows), jnp.int32),
            pltpu.VMEM((steps, rows), jnp.int32),
            pltpu.VMEM((steps, rows), jnp.int32),
            pltpu.VMEM((steps, 2, rows), jnp.int32),
            pltpu.VMEM((steps, rows), jnp.int32),
            pltpu.VMEM((table_rows, width), BF16),
            pltpu.VMEM((blocks, width), BF16),
            pltpu.VMEM((bins, width), BF16),
            pltpu.VMEM((bins, width), BF16),
            pltpu.VMEM((bins, width), BF16),
            pltpu.VMEM((table_rows, width), BF16),
            pltpu.SemaphoreType.DMA((18,)),
            pltpu.VMEM((rows, width), BF16),
            pltpu.VMEM((pair * rows, width), BF16),
            pltpu.VMEM((pair * rows, width), BF16),
            pltpu.VMEM((LANES, width), BF16),
            pltpu.VMEM((2 * calls, width, width), BF16),
            pltpu.VMEM((s.depth[0], width), BF16),
            pltpu.VMEM((s.depth[1], width), BF16),
            pltpu.VMEM((s.stack[0], width), F32),
            pltpu.VMEM((s.stack[1], width), F32),
            pltpu.VMEM((s.depth[0], pair * rows), BF16),
            pltpu.VMEM((s.depth[1], pair * rows), BF16),
            pltpu.VMEM((s.reward_at - s.sums_at, LANES), F32),
            pltpu.VMEM((steps, s.reward_at - s.sums_at, width), F32),
            pltpu.VMEM((rows, width), F32),
            pltpu.VMEM((2, 16, width), F32),
            pltpu.VMEM((s.held, width), F32),
            pltpu.VMEM((2 * calls * width, width), F32),
            pltpu.VMEM((2, 16, width), F32),
            pltpu.VMEM((max(pair - 1, 1), calls, rows, width), BF16),
            pltpu.VMEM((max(pair - 1, 1), calls, rows, width), BF16),
            pltpu.VMEM((max(pair - 1, 1), 2, rows, width), BF16),
        ],
        out_shape=[
            pltpu.HBM((steps, rows, width), BF16),
            pltpu.HBM((steps, rows, width), BF16),
            shape((8, rows), F32),
            shape((s.total, width), BF16),
            shape((s.total, width), BF16),
            shape((rows, half), BF16),
            shape((rows, half), BF16),
        ],
        compiler_params=unroll_params,
        cost_estimate=cost,
        name="unroll",
    )(
        tower_ref,
        *[
            pltpu.with_memory_space_constraint(value, pltpu.HBM)
            for value in (
                root_state, lengths, actions, codes, policy_target,
                jnp.swapaxes(value_bins, 0, 1), reward_bins, cond_table, gains_own,
                in_own, out_own, value_own, reward_head.T, small_head.T,
            )
        ],
        root_got, in_got, out_got, value_got, gains_got,
    )
    got = swap(away, "tower", 1)

    def beside(given):
        lat_own, lat_away, loss, root_own, root_away = given
        lat_got = swap(lat_away, "tower", 1)
        loss_own = loss[0]
        loss_got = swap(loss_own, "tower", 1)
        root_got = swap(root_away, "tower", 1)

        latents, logits = pl.pallas_call(
            functools.partial(logits_kernel, s),
            grid_spec=pltpu.PrefetchScalarGridSpec(
                num_scalar_prefetch=1,
                grid=(steps // pair,),
                in_specs=[per_pair(rows, width), per_pair(rows, width), whole((bins, width))],
                out_specs=[per_pair(batch_rows, width), per_pair(bins, batch_rows)],
            ),
            out_shape=[
                shape((steps, batch_rows, width), BF16),
                shape((steps, bins, batch_rows), BF16),
            ],
            compiler_params=small_params,
            cost_estimate=pl.CostEstimate(
                flops=2 * steps * batch_rows * width * wide, bytes_accessed=6 * 2**20, transcendentals=0
            ),
            name="latents_and_logits",
        )(
            tower_ref,
            *[
                pltpu.with_memory_space_constraint(part, pltpu.HBM)
                for part in (lat_own, lat_got, value_own)
            ],
        )

        def in_order(mine_value, got_value, axis):
            return jnp.where(
                tower_id == 0,
                jnp.concatenate([mine_value, got_value], axis=axis),
                jnp.concatenate([got_value, mine_value], axis=axis),
            )

        row_loss = in_order(loss_own, loss_got, 0)
        grad_root = in_order(root_own, root_got, 0).astype(F32)
        return latents, logits, row_loss, grad_root

    rounds = exchange_rounds(parts)

    def unpack(digit, held):
        scalars = jnp.stack([digit, tower_id]).astype(jnp.int32)
        length = held[0].shape[0]
        block = s.reward_at // length
        at = s.reward_at - block * length
        parts_of = [part[at : at + s.shared_end - s.reward_at] for part in held]
        shared = parts_of[0]
        for other in range(1, len(held)):
            shared = jnp.where((digit ^ other) == block, parts_of[other], shared)
        shared_got = swap(shared, "tower", 1)
        return (shared, shared_got), pl.pallas_call(
            functools.partial(unpack_own_kernel, s),
            grid_spec=pltpu.PrefetchScalarGridSpec(
                num_scalar_prefetch=1,
                grid=(1,),
                in_specs=[whole(part.shape) for part in held],
                out_specs=[
                    whole((blocks, width, width)),
                    whole((blocks, width, width)),
                    whole((bins, 1, width)),
                    whole((blocks, 1, width)),
                    whole((blocks, 2, steps)),
                ],
                scratch_shapes=[
                    pltpu.VMEM((s.total, width), BF16),
                    pltpu.VMEM((s.reward_at - s.sums_at, LANES), F32),
                ],
            ),
            out_shape=[
                shape((blocks, width, width), F32),
                shape((blocks, width, width), F32),
                shape((bins, 1, width), F32),
                shape((blocks, 1, width), F32),
                shape((blocks, 2, steps), F32),
            ],
            compiler_params=small_params,
            name="unpack_own",
        )(scalars, *held)

    given = (lat_own, lat_away, loss, root_own, root_away)
    unpacked, done = exchange([own, got], rounds, parts, beside, given, unpack)
    (shared, shared_got), (grad_in, grad_out, value_t, gain_t, rms_t) = unpacked
    latents, logits, row_loss, grad_root = done
    reward_t, small_t, grad_cond = pl.pallas_call(
        functools.partial(unpack_shared_kernel, s),
        grid_spec=pltpu.PrefetchScalarGridSpec(
            num_scalar_prefetch=1,
            grid=(1,),
            in_specs=[whole(shared.shape), whole(shared.shape)],
            out_specs=[
                whole((bins, width)),
                whole((table_rows, width)),
                whole((table_rows, width)),
            ],
            scratch_shapes=[pltpu.VMEM((s.wide, width), F32)],
        ),
        out_shape=[
            shape((bins, width), F32),
            shape((table_rows, width), F32),
            shape((table_rows, width), F32),
        ],
        compiler_params=small_params,
        name="unpack_shared",
    )(tower_ref, shared, shared_got)
    layer_rms = jnp.transpose(rms_t, (2, 0, 1))[None]
    return (
        latents[None],
        jnp.swapaxes(logits, 1, 2)[None],
        row_loss,
        layer_rms,
        grad_root,
        grad_cond,
        jnp.swapaxes(gain_t, 0, 1),
        grad_in[None],
        grad_out[None],
        jnp.transpose(value_t, (1, 2, 0)),
        reward_t.T,
        small_t.T,
    )


def solution(mesh):
    placed = (
        P("batch", "tower"),
        P(),
        P("tower", None, None),
        P("tower", None, None, None),
        P("tower", None, None, None),
        P("tower", None, None),
        P(),
        P(),
        P("batch"),
        P(None, "batch"),
        P(None, "batch"),
        P(None, "batch"),
        P(None, None, "batch"),
        P(None, "batch"),
    )
    return jax.shard_map(
        body,
        mesh=mesh,
        in_specs=placed,
        out_specs=(
            P("tower", None, "batch", None),
            P("tower", None, "batch", None),
            P("batch"),
            P("tower", None, None, None),
            P("batch", "tower"),
            P(),
            P("tower", None, None),
            P("tower", None, None, None),
            P("tower", None, None, None),
            P("tower", None, None),
            P(),
            P(),
        ),
        check_vma=False,
    )
```

```python
import functools

import jax
import jax.numpy as jnp
from jax import lax
from jax.experimental import pallas as pl
from jax.experimental.pallas import tpu as pltpu
from jax.sharding import PartitionSpec as P

ACTIONS = 4
LANES = 128
MIB = 1024 * 1024
UNROLL_LIMIT = 50 * MIB
SMALL_LIMIT = 12 * MIB
epsilon = 1e-06
very_negative = -1e30
F32 = jnp.float32
BF16 = jnp.bfloat16


def natural(left, right):
    return lax.dot_general(left, right, (((1,), (0,)), ((), ())), preferred_element_type=F32)


def by_rows(left, right):
    return lax.dot_general(left, right, (((0,), (0,)), ((), ())), preferred_element_type=F32)


def by_lanes(left, right):
    return lax.dot_general(left, right, (((1,), (1,)), ((), ())), preferred_element_type=F32)


def round_up(value, unit):
    return (value + unit - 1) // unit * unit


def lane_sum(value):
    return jnp.sum(value, axis=-1, keepdims=True)


def inverse_rms(hidden):
    return lax.rsqrt(lane_sum(hidden * hidden) * (1.0 / hidden.shape[-1]) + epsilon)


def weave(*tasks):
    tasks = [(list(task)) for task in tasks]
    longest = max(len(task) for task in tasks)
    done = [0] * len(tasks)
    for turn in range(longest):
        for which, task in enumerate(tasks):
            until = (turn + 1) * len(task) // longest
            while done[which] < until:
                task[done[which]]()
                done[which] += 1


def cuts(length, unit=320):
    return [(start, min(start + unit, length)) for start in range(0, length, unit)]


class Sizes:
    def __init__(self, steps, rows, blocks, width, bins, table_rows, parts):
        self.steps, self.rows, self.blocks, self.width = steps, rows, blocks, width
        self.bins, self.table_rows, self.parts = bins, table_rows, parts
        self.calls = 2 * blocks
        self.pair = 2 if steps % 2 == 0 else 1
        self.wide = round_up(bins, 32)
        self.held = round_up(table_rows, 16)
        self.stack = (self.wide + self.held, 2 * self.wide + self.held)
        self.depth = tuple(round_up(rows_in, LANES) for rows_in in self.stack)
        half = self.wide // 2
        self.value_at = self.calls * width
        self.sums_at = self.value_at + self.wide
        self.kinds = 2 * self.calls
        self.gain_row = self.kinds + 1
        self.reward_at = self.sums_at + round_up(self.gain_row + blocks, 16)
        self.small_at = self.reward_at + half
        self.cond_at = self.small_at + self.held
        self.shared_end = self.cond_at + self.held
        self.total = round_up(self.shared_end, 16 * parts)
        self.head_rows = self.cond_at - self.value_at


def unroll_kernel(
    sizes, tower_ref,
    root_hbm, lengths_hbm, actions_hbm, codes_hbm, policy_hbm, value_bins_hbm, reward_bins_hbm,
    table_hbm, gains_hbm, in_hbm, out_hbm, value_hbm, reward_hbm, small_hbm,
    root_any, in_got, out_got, value_any, gains_got,
    lat_own, lat_away, loss, own, away, root_own_grad, root_away_grad,
    lat, entry, after, slope, side, dlat, turned, gains, lat_sems,
    root_own, root_got, lengths, actions, codes, policy, value_bins, reward_bins,
    table_in, gains_own, value_own, value_got, reward_in, small_in, sems,
    state, past0, past1, table, weights, heads0, heads1, acc0, acc1,
    cot0, cot1, sums, squares,
    carry, gain_sum, cond_sum, grads, inverse_gains, d_after_kept, d_before_kept, d_hidden_kept,
):
    turns = sizes.steps // sizes.pair
    small, large = sizes.stack
    logits0 = grads.at[pl.ds(0, small)]
    logits1 = grads.at[pl.ds(small, large)]
    for turn in range(turns):
        forward_turn(
            sizes, turn, tower_ref,
            root_hbm, lengths_hbm, actions_hbm, codes_hbm, policy_hbm, value_bins_hbm,
            reward_bins_hbm, table_hbm, gains_hbm, in_hbm, out_hbm, value_hbm, reward_hbm,
            small_hbm, root_any, in_got, out_got, value_any, gains_got,
            lat, entry, after, slope, side, dlat, loss, turned, gains,
            root_own, root_got, lengths, actions, codes, policy, value_bins, reward_bins,
            table_in, gains_own, value_own, value_got, reward_in, small_in, sems,
            state, past0, past1, table, weights, heads0, heads1, acc0, acc1,
            logits0, logits1, cot0, cot1, sums, squares,
        )
    tower_id = tower_ref[0]
    copies = [
        pltpu.make_async_copy(lat.at[:, tower_id], lat_own, lat_sems.at[0]),
        pltpu.make_async_copy(lat.at[:, 1 - tower_id], lat_away, lat_sems.at[1]),
    ]
    for copy in copies:
        copy.start()

    def one_backward(turn, is_first):
        backward_turn(
            sizes, turn, is_first,
            lat, entry, after, slope, side, dlat, actions, codes, turned,
            carry, gain_sum, cond_sum, grads, gains, inverse_gains, d_after_kept, d_before_kept,
            d_hidden_kept,
        )

    def later_backward(turn, _):
        one_backward(turn, False)
        return 0

    one_backward(0, True)
    lax.fori_loop(1, turns, later_backward, 0)
    finish_backward(
        sizes, tower_ref, acc0, acc1, sums, own, away, root_own_grad, root_away_grad,
        carry, gain_sum, cond_sum, grads, inverse_gains,
    )
    for copy in copies:
        copy.wait()


def forward_turn(
    sizes, turn, tower_ref,
    root_hbm, lengths_hbm, actions_hbm, codes_hbm, policy_hbm, value_bins_hbm, reward_bins_hbm,
    table_hbm, gains_hbm, in_hbm, out_hbm, value_hbm, reward_hbm, small_hbm,
    root_any, in_got, out_got, value_any, gains_got,
    lat, entry, after, slope, side, dlat, loss, turned, gains,
    root_own, root_got, lengths, actions, codes, policy, value_bins, reward_bins,
    table_in, gains_own, value_own, value_got, reward_in, small_in, sems,
    state, past0, past1, table, weights, heads0, heads1, acc0, acc1,
    logits0, logits1, cot0, cot1, sums, squares,
):
    s = sizes
    pair = s.pair
    first_step = turn * pair
    tower_id = tower_ref[0]
    rows, width, wide = s.rows, s.width, s.wide

    if turn == 0:
        here = pl.ds(pl.multiple_of(tower_id * rows, rows), rows)

        def matrices(kind, tower):
            return weights.at[pl.ds(kind * s.calls + tower * s.blocks, s.blocks)]

        moves = [
            (in_hbm, matrices(0, tower_id)),
            (out_hbm, matrices(1, tower_id)),
            (in_got, matrices(0, 1 - tower_id)),
            (out_got, matrices(1, 1 - tower_id)),
            (value_hbm, value_own),
            (value_any, value_got),
            (reward_hbm, reward_in),
            (small_hbm, small_in),
            (table_hbm, table_in),
            (gains_hbm, gains_own),
            (root_hbm.at[here], root_own),
            (root_any.at[here], root_got),
            (actions_hbm.at[:, here], actions),
            (codes_hbm.at[:, here], codes),
            (lengths_hbm.at[:, here], lengths),
            (policy_hbm.at[:, here], policy),
            (value_bins_hbm.at[:, :, here], value_bins),
            (reward_bins_hbm.at[:, here], reward_bins),
        ]
        moves = [
            pltpu.make_async_copy(source, target, sems.at[place])
            for place, (source, target) in enumerate(moves)
        ]
        for move in moves:
            move.start()
        gains[...] = jnp.ones_like(gains)
        for target in (
            table, sums, squares, loss
        ):
            target[...] = jnp.zeros_like(target)
        for stack, cot, rows_used in ((heads0, cot0, s.stack[0]), (heads1, cot1, s.stack[1])):
            start = rows_used - s.held
            stack[start:, :] = jnp.zeros((stack.shape[0] - start, width), BF16)
            for end in range(wide, start + 1, wide):
                stack[end - 16 : end, :] = jnp.zeros((16, width), BF16)
            cot[rows_used:, :] = jnp.zeros((cot.shape[0] - rows_used, pair * rows), BF16)
        for move in moves:
            move.wait()
        first = tower_id == 0
        state[:, 0 : width // 2] = jnp.where(first, root_own[...], root_got[...])
        state[:, width // 2 : width] = jnp.where(first, root_got[...], root_own[...])
        gains[tower_id, 0 : s.blocks, :] = gains_own[...].astype(F32)
        gains[1 - tower_id, 0 : s.blocks, :] = gains_got[...].astype(F32)
        table[0 : s.table_rows, :] = table_in[...]
        heads0[0 : s.bins, :] = jnp.where(first, value_own[...], value_got[...])
        heads1[0 : s.bins, :] = jnp.where(first, value_got[...], value_own[...])
        heads1[wide : wide + s.bins, :] = reward_in[...]
        heads0[wide : wide + s.table_rows, :] = small_in[...]
        heads1[2 * wide : 2 * wide + s.table_rows, :] = small_in[...]

    eights = lax.broadcasted_iota(jnp.int32, (8, pair * rows), 0)
    before = first_step - pair

    def pair_row(kind, at_step, lead=()):
        return jnp.concatenate(
            [kind[(slice(at_step + offset, at_step + offset + 1),) + lead] for offset in range(pair)],
            axis=1,
        )

    def live_rows(at_step):
        return jnp.concatenate(
            [(at_step + offset < lengths[...]).astype(F32) for offset in range(pair)], axis=1
        )

    kinds = []
    for offset in range(pair):
        step = first_step + offset
        kinds.append((step < lengths[...]).astype(F32))
        kinds.append(actions[step : step + 1, :].astype(F32))
        kinds.append((codes[step : step + 1, :] + ACTIONS).astype(F32))
    kinds.append(jnp.zeros((8 - len(kinds), rows), F32))
    columns = jnp.concatenate(kinds, axis=0).T

    def heads(tower, live_row, at_step, put):
        latent = past0 if tower == 0 else past1
        stack, logits, cot, acc = (
            (heads0, logits0, cot0, acc0) if tower == 0 else (heads1, logits1, cot1, acc1)
        )
        pick = lambda kind: pair_row(kind, at_step)
        value_goal = pair_row(value_bins, at_step, (tower,))
        spans = [(0, wide, 0, s.bins, value_goal)]
        if tower == 1:
            spans.append((wide, wide, 0, s.bins, pick(reward_bins)))
            spans.append((2 * wide, s.held, 0, ACTIONS, pick(policy)))
        else:
            spans.append((wide, s.held, ACTIONS, s.table_rows, pick(codes) + ACTIONS))

        def make_logits(start, stop):
            logits[start:stop, :] = by_lanes(stack[start:stop, :], latent[...])

        def eight_rows(value):
            return value.reshape(-1, 8, pair * rows)

        def mask(at, length, first, last):
            for start in range(0, length, 8):
                if start < first or start + 8 > last:
                    inside = (eights >= first - start) & (eights < last - start)
                    place = slice(at + start, at + start + 8)
                    logits[place, :] = jnp.where(inside, logits[place, :], very_negative)

        def find_top(at, start, stop, kept):
            top = jnp.max(eight_rows(logits[at + start : at + stop, :]), axis=0)
            kept["top"] = jnp.maximum(kept["top"], top) if "top" in kept else top

        def end_top(kept):
            kept["top"] = jnp.max(kept["top"], axis=0, keepdims=True)

        def make_terms(at, start, stop, goal, kept):
            place = slice(at + start, at + stop)
            value = logits[place, :]
            spot = lax.broadcasted_iota(jnp.int32, value.shape, 0)
            term = jnp.exp(value - kept["top"])
            logits[place, :] = term
            hit = spot == goal - start
            total = jnp.sum(eight_rows(term), axis=0)
            picked = jnp.sum(eight_rows(jnp.where(hit, value, 0.0)), axis=0)
            kept["total"] = kept["total"] + total if "total" in kept else total
            kept["picked"] = kept["picked"] + picked if "picked" in kept else picked

        def end_terms(kept):
            total = jnp.sum(kept["total"], axis=0, keepdims=True)
            picked = jnp.sum(kept["picked"], axis=0, keepdims=True)
            kept["scale"] = live_row / total
            row_loss = live_row * (jnp.log(total) + kept["top"] - picked)
            for offset in range(pair):
                loss[0:1, :] += row_loss[:, offset * rows : (offset + 1) * rows]

        def make_cotangent(at, start, stop, goal, kept):
            place = slice(at + start, at + stop)
            term = logits[place, :]
            spot = lax.broadcasted_iota(jnp.int32, term.shape, 0)
            hit = spot == goal - start
            cot[place, :] = (term * kept["scale"] - jnp.where(hit, live_row, 0.0)).astype(BF16)

        def make_grads(start, stop):
            product = natural(cot[start:stop, :], latent[...])
            if at_step > 0:
                product = acc[start:stop, :] + product
            acc[start:stop, :] = product

        def make_latent():
            d_latent = by_rows(cot[...], stack[...])
            for offset in range(pair):
                put[at_step + offset, tower] = d_latent[offset * rows : (offset + 1) * rows].astype(
                    BF16
                )

        large = cuts(acc.shape[0], 320)
        pieces = [functools.partial(make_logits, *cut) for cut in large]
        for at, length, first, last, goal in spans:
            kept = {}
            each = cuts(length)
            pieces.append(functools.partial(mask, at, length, first, last))
            pieces += [functools.partial(find_top, at, *cut, kept) for cut in each]
            pieces.append(functools.partial(end_top, kept))
            pieces += [functools.partial(make_terms, at, *cut, goal, kept) for cut in each]
            pieces.append(functools.partial(end_terms, kept))
            pieces += [functools.partial(make_cotangent, at, *cut, goal, kept) for cut in each]
        return pieces + [make_latent] + [functools.partial(make_grads, *cut) for cut in large]

    def columns_of(offset, tower):
        live = columns[:, 3 * offset : 3 * offset + 1]
        return live, columns[:, 3 * offset + 1 + tower : 3 * offset + 2 + tower]

    def embedding(offset, tower):
        _, code = columns_of(offset, tower)
        spot = lax.broadcasted_iota(jnp.int32, (rows, table.shape[0]), 1)
        onehot = jnp.where(spot.astype(F32) == code, 1.0, 0.0).astype(BF16)
        return natural(onehot, table[...])

    def tower_call(offset, tower, chain):
        live, _ = columns_of(offset, tower)

        def scale_rows():
            row_squares = lane_sum(chain["hidden"] * chain["hidden"])
            return row_squares, lax.rsqrt(row_squares * (1.0 / width) + epsilon)

        def keep_squares(block, row_squares):
            place = 2 * (tower * s.blocks + block)
            total = jnp.sum(live * row_squares, axis=0, keepdims=True) * (1.0 / LANES)
            squares[first_step + offset, place : place + 1, 0:LANES] = jnp.broadcast_to(total, (1, LANES))

        def end_block(block):
            branch = chain["product"]
            chain["hidden"] = chain["hidden"] + branch
            return branch

        def keep_branch(block, branch):
            spot = 2 * (tower * s.blocks + block) + 1
            squares[first_step + offset, spot : spot + 1, :] = jnp.sum(
                branch * branch * live, axis=0, keepdims=True
            )

        def into(block):
            place = tower * s.blocks + block
            if block > 0:
                branch = end_block(block - 1)
            gained = chain["hidden"] * gains[tower, block : block + 1, :]
            chain["product"] = natural(gained.astype(BF16), weights[place])
            row_squares, inv_scale = scale_rows()
            chain["scale"] = inv_scale
            entry[first_step + offset, place] = (gained * inv_scale).astype(BF16)
            side[first_step + offset, :, place : place + 1] = inv_scale
            if block > 0:
                keep_squares(block - 1, row_squares)
                keep_branch(block - 1, branch)

        def out_of(block):
            place = tower * s.blocks + block
            u = chain["product"] * chain["scale"]
            gate = 0.5 * jnp.tanh(0.5 * u) + 0.5
            after_rows = (u * gate).astype(BF16)
            chain["product"] = natural(after_rows, weights[s.calls + place])
            after[first_step + offset, place] = after_rows
            slope[first_step + offset, place] = (gate * (1.0 + u * (1.0 - gate))).astype(BF16)

        def finish():
            branch = end_block(s.blocks - 1)
            row_squares, inv_scale = scale_rows()
            latent = (chain["hidden"] * inv_scale).astype(BF16)
            chain[offset, tower] = latent
            following = (offset, 1) if tower == 0 else (offset + 1, 0)
            if following in chain:
                chain["hidden"] = latent.astype(F32) + chain[following]

            def keep():
                spot = s.calls + tower
                side[first_step + offset, :, spot : spot + 1] = inv_scale
                lat[first_step + offset, tower] = latent
                keep_squares(s.blocks - 1, row_squares)
                keep_branch(s.blocks - 1, branch)
                if tower == 0:
                    total = jnp.sum(live, axis=0, keepdims=True) * (1.0 / LANES)
                    squares[first_step + offset, s.kinds : s.kinds + 1, 0:LANES] = jnp.broadcast_to(
                        total, (1, LANES)
                    )

            return keep

        pieces = []
        for block in range(s.blocks):
            pieces += [functools.partial(into, block), functools.partial(out_of, block)]
        return pieces, finish

    chain = {
        (offset, tower): embedding(offset, tower) for offset in range(pair) for tower in range(2)
    }
    chain["hidden"] = state[...].astype(F32) + chain[0, 0]
    pieces = []
    keeps = []

    def begin_next(finish, into):
        keeps.append(finish())
        into()
        keeps.pop()()

    ending = None
    for offset in range(pair):
        for tower in range(2):
            calls, finish = tower_call(offset, tower, chain)
            if ending is not None:
                calls[0] = functools.partial(begin_next, ending, calls[0])
            pieces += calls
            ending = finish
    pieces.append(lambda: ending()())

    turns = -(-2 * s.calls // (s.steps // pair))

    def turn_weights(matrix):
        turned[matrix] = weights[matrix].T

    beside = []
    if turn > 0:
        live_before = live_rows(before)
        beside += heads(1, live_before, before, dlat) + heads(0, live_before, before, dlat)
    matrices_now = range(turn * turns, min((turn + 1) * turns, 2 * s.calls))
    beside += [functools.partial(turn_weights, matrix) for matrix in matrices_now]
    weave(pieces, beside)
    at_lane = lax.broadcasted_iota(jnp.int32, sums.shape, 1)
    for offset in range(pair):
        at = slice(offset * rows, (offset + 1) * rows)
        after_state, next_state = chain[offset, 0], chain[offset, 1]
        past0[at, :] = after_state
        past1[at, :] = next_state
        if offset == pair - 1:
            state[...] = next_state
        total = lane_sum(squares[first_step + offset])
        sums[...] = jnp.where(at_lane == first_step + offset, total, sums[...])

    if turn == s.steps // pair - 1:
        live_now = live_rows(first_step)
        for piece in heads(1, live_now, first_step, dlat) + heads(0, live_now, first_step, dlat):
            piece()


def backward_turn(
    sizes, turn, is_first,
    lat, entry, after, slope, side, dlat, actions, codes, turned,
    carry, gain_sum, cond_sum, grads, gains, inverse_gains, d_after_kept, d_before_kept,
    d_hidden_kept,
):
    s = sizes
    pair = s.pair
    first_step = s.steps - pair * (turn + 1)
    blocks, width = s.blocks, s.width
    if is_first:
        inverse_gains[...] = 1.0 / gains[...]
        carry[...] = jnp.zeros_like(carry)
        gain_sum[...] = jnp.zeros_like(gain_sum)
        cond_sum[...] = jnp.zeros_like(cond_sum)

    def over_lanes(step, column):
        return jnp.broadcast_to(side[step, :, column : column + 1], (s.rows, width))

    def stacked(parts):
        return jnp.concatenate(parts, axis=0)

    def add_grads(matrix, rows_of, place, kept, now):
        later = [kept[offset - 1, place] for offset in range(1, pair)]
        product = by_rows(
            stacked([rows_of[first_step + offset, place] for offset in range(pair)]),
            stacked([now] + later),
        )
        at = slice(matrix * width, (matrix + 1) * width)
        if not is_first:
            product = grads[at, :] + product
        grads[at, :] = product

    def add_cond(offset, tower, d_hidden):
        if offset > 0:
            d_hidden_kept[offset - 1, tower] = d_hidden.astype(BF16)
            return
        codes_of, shift = (actions, 0) if tower == 0 else (codes, ACTIONS)
        code = jnp.concatenate(
            [
                codes_of[pl.ds(first_step + step, 1), :] + shift
                for step in range(pair)
            ],
            axis=1,
        )
        spots = lax.broadcasted_iota(jnp.int32, (cond_sum.shape[0], pair * s.rows), 0)
        onehot = jnp.where(spots == code, 1.0, 0.0).astype(BF16)
        parts = [d_hidden.astype(BF16)]
        parts += [d_hidden_kept[step - 1, tower] for step in range(1, pair)]
        cond_sum[...] += natural(onehot, stacked(parts))

    behind = []

    def catch_up():
        while behind:
            behind.pop(0)()

    def tower_back(offset, tower, d_latent):
        normed = lat[first_step + offset, tower]
        normed_wide = normed.astype(F32)
        inv_scale = over_lanes(first_step + offset, s.calls + tower)
        base = inv_scale * d_latent
        slant = inv_scale * (lane_sum(d_latent * normed_wide) * (1.0 / width))
        for block in reversed(range(blocks)):
            place = tower * blocks + block
            matrix = tower * s.calls + block
            both = natural(
                jnp.concatenate([normed, base.astype(BF16)], axis=0), turned[s.calls + place]
            )
            d_hidden = base - slant * normed_wide
            d_branch = d_hidden.astype(BF16)
            entry_wide = entry[first_step + offset, place].astype(F32)
            inv_scale = over_lanes(first_step + offset, place)
            catch_up()
            d_after = both[s.rows :] - slant * both[: s.rows]
            d_before = (d_after * slope[first_step + offset, place].astype(F32)).astype(BF16)
            d_entry = natural(d_before, turned[place])
            if offset > 0:
                d_after_kept[offset - 1, place] = d_branch
                d_before_kept[offset - 1, place] = d_before
            else:
                add_grads(matrix + blocks, after, place, d_after_kept, d_branch)
                behind.append(
                    functools.partial(add_grads, matrix, entry, place, d_before_kept, d_before)
                )
            gain = gains[tower, block : block + 1, :]
            normed_wide = entry_wide * inverse_gains[tower, block : block + 1, :]
            normed = normed_wide.astype(BF16)
            product = d_entry * entry_wide
            base = d_hidden + inv_scale * (d_entry * gain)
            slant = inv_scale * (lane_sum(product) * (1.0 / width))

            def add_gain(tower=tower, block=block, product=product):
                gain_sum[tower, block : block + 1, :] += jnp.sum(product, axis=0, keepdims=True)

            behind.append(add_gain)
        d_hidden = base - slant * normed_wide
        behind.append(functools.partial(add_cond, offset, tower, d_hidden))
        return d_hidden

    def from_heads(offset, tower):
        return jnp.where(turn == 0, dlast[offset, tower], dlat[first_step + offset, tower])

    d_state = carry[...]
    for offset in reversed(range(pair)):
        for tower in (1, 0):
            d_state = tower_back(offset, tower, d_state + dlat[first_step + offset, tower].astype(F32))
    catch_up()
    carry[...] = d_state


def finish_backward(
    sizes, tower_ref, acc0, acc1, sums, own, away, root_own, root_away,
    carry, gain_sum, cond_sum, grads, inverse_gains,
):
    s = sizes
    tower_id = tower_ref[0]
    blocks, width = s.blocks, s.width
    d_state = carry[...]
    left = d_state[:, 0 : width // 2].astype(BF16)
    right = d_state[:, width // 2 : width].astype(BF16)
    root_own[...] = jnp.where(tower_id == 0, left, right)
    root_away[...] = jnp.where(tower_id == 0, right, left)
    gain_sum[...] = gain_sum[...] * inverse_gains[...]
    wide, half = s.wide, s.wide // 2
    lines = lax.broadcasted_iota(jnp.int32, sums.shape, 0)
    small = acc0[wide : wide + s.held, :] + acc1[2 * wide : 2 * wide + s.held, :]
    for target, which in ((own, tower_id), (away, 1 - tower_id)):
        first = which == 0

        def put_matrix(matrix, _, target=target, which=which):
            source = pl.ds(pl.multiple_of((which * s.calls + matrix) * width, width), width)
            at = pl.ds(pl.multiple_of(matrix * width, width), width)
            target[at, :] = grads[source, :].astype(BF16)
            return 0

        lax.fori_loop(0, s.calls, put_matrix, 0)
        for start, stop in cuts(wide):
            value = jnp.where(first, acc0[start:stop, :], acc1[start:stop, :])
            target[s.value_at + start : s.value_at + stop, :] = value.astype(BF16)
        for start, stop in cuts(half):
            reward = jnp.where(
                first,
                acc1[wide + start : wide + stop, :],
                acc1[wide + half + start : wide + half + stop, :],
            )
            target[s.reward_at + start : s.reward_at + stop, :] = reward.astype(BF16)
        here = jnp.where(first, small, 0.0)
        target[s.small_at : s.small_at + s.held, :] = here.astype(BF16)
        here = jnp.where(first, cond_sum[...], 0.0)
        target[s.cond_at : s.shared_end, :] = here.astype(BF16)
        kept = sums[...]
        for block in range(blocks):
            gain = gain_sum[which, block : block + 1, 0:LANES]
            kept = jnp.where(lines == s.gain_row + block, gain, kept)
        target[s.sums_at : s.reward_at, 0:LANES] = kept.astype(BF16)
        kept = jnp.zeros_like(kept)
        for block in range(blocks):
            gain = gain_sum[which, block : block + 1, LANES:]
            kept = jnp.where(lines == s.gain_row + block, gain, kept)
        target[s.sums_at : s.reward_at, LANES:] = kept.astype(BF16)
        if s.total > s.shared_end:
            target[s.shared_end :, :] = jnp.zeros((s.total - s.shared_end, width), BF16)


def logits_kernel(sizes, tower_ref, lat_own, lat_got, value_own, latents, logits):
    rows = sizes.rows
    tower_id = tower_ref[0]
    at_own = pl.ds(pl.multiple_of(tower_id * rows, rows), rows)
    at_got = pl.ds(pl.multiple_of((1 - tower_id) * rows, rows), rows)
    for offset in range(sizes.pair):
        latents[offset, at_own, :] = lat_own[offset]
        latents[offset, at_got, :] = lat_got[offset]
        logits[offset] = by_lanes(value_own[...], latents[offset]).astype(BF16)


def add_and_split_kernel(count, digit_ref, *refs):
    inputs, outputs = refs[:count], refs[count:]
    digit = digit_ref[0]
    for other, target in enumerate(outputs):
        part = digit ^ other
        total = inputs[0][part].astype(F32)
        for source in inputs[1:]:
            total = total + source[part].astype(F32)
        target[...] = total.astype(BF16)


def unpack_own_kernel(sizes, scalars, *refs):
    s = sizes
    factor = len(refs) - 7
    digit, tower_id = scalars[0], scalars[1]
    w_in, w_out, value, gain, rms, flat, held = refs[factor:]
    width = s.width
    length = refs[0].shape[0]
    for other, source in enumerate(refs[:factor]):
        at = pl.multiple_of((digit ^ other) * length, 16)
        flat[pl.ds(at, length), :] = source[...]
    for block in range(s.blocks):
        at = block * width
        w_in[block] = flat[at : at + width, :].astype(F32)
        at = (s.blocks + block) * width
        w_out[block] = flat[at : at + width, :].astype(F32)
    value[:, 0, :] = flat[s.value_at : s.sums_at, :].astype(F32)[0 : s.bins]
    sums = flat[s.sums_at : s.reward_at, :].astype(F32)
    for block in range(s.blocks):
        gain[block] = sums[s.gain_row + block : s.gain_row + block + 1, :]
    held[...] = sums[:, 0:LANES]
    count = jnp.maximum(held[s.kinds : s.kinds + 1, 0 : s.steps], 1.0)
    for block in range(s.blocks):
        for kind in range(2):
            spot = tower_id * s.calls + 2 * block + kind
            square = held[pl.ds(spot, 1), 0 : s.steps]
            rms[block, kind : kind + 1, :] = jnp.sqrt(jnp.maximum(square, 0.0) / (count * width))


def unpack_shared_kernel(sizes, tower_ref, mine, got, reward, small, cond, joined):
    s = sizes
    tower_id = tower_ref[0]
    half = s.wide // 2
    joined[pl.ds(pl.multiple_of(tower_id * half, 8), half), :] = mine[0:half, :].astype(F32)
    joined[pl.ds(pl.multiple_of((1 - tower_id) * half, 8), half), :] = got[0:half, :].astype(F32)
    reward[...] = joined[0 : s.bins, :]
    for target, at in ((small, s.small_at), (cond, s.cond_at)):
        rows = slice(at - s.reward_at, at - s.reward_at + s.held)
        target[...] = (mine[rows, :].astype(F32) + got[rows, :].astype(F32))[0 : s.table_rows]


def whole(shape):
    return pl.BlockSpec(shape, lambda step, tower: (0,) * len(shape))


def swap(value, axis, mask):
    pairs = [(source, source ^ mask) for source in range(lax.axis_size(axis))]
    return lax.ppermute(value, axis, pairs)


AXES = ("tower", "batch")


def exchange_rounds(batch_size):
    factors, left = [], batch_size
    while left > 1:
        factors.append(4 if left % 4 == 0 else 2)
        left //= factors[-1]
    rounds, stride = [], 1
    for factor in factors:
        rounds.append((factor, stride))
        stride *= factor
    turned = rounds[::-1] if len(set(factors)) == 1 else rounds
    return [(one[0], (one[1], two[1])) for one, two in zip(rounds, turned)]


def swap_within(value, strides, other, batch_size):
    pairs = [
        (tower * batch_size + index, tower * batch_size + (index ^ (other * strides[tower])))
        for tower in range(2)
        for index in range(batch_size)
    ]
    return lax.ppermute(value, AXES, pairs)


def swap_all(blocks, strides, batch_size, order):
    return [
        swap_within(blocks[other], strides, other, batch_size) if other else blocks[0]
        for other in order
    ]


def my_digit(factor, strides):
    stride = jnp.where(lax.axis_index("tower") == 0, strides[0], strides[1])
    return (lax.axis_index("batch") // stride) % factor


def add_kernel(*refs):
    total = refs[0][...].astype(F32)
    for source in refs[1:-1]:
        total = total + source[...].astype(F32)
    refs[-1][...] = total.astype(BF16)


def add_up(parts):
    return pl.pallas_call(
        add_kernel,
        out_shape=jax.ShapeDtypeStruct(parts[0].shape, BF16),
        compiler_params=pltpu.CompilerParams(vmem_limit_bytes=SMALL_LIMIT),
        name="add_up",
    )(*parts)


def exchange(value, rounds, batch_size, beside, given, last_kernel):
    factor, strides = rounds[0]
    digit = my_digit(factor, strides)
    rows, width = value[0].shape
    rows = rows // factor
    split = pl.pallas_call(
        functools.partial(add_and_split_kernel, len(value)),
        grid_spec=pltpu.PrefetchScalarGridSpec(
            num_scalar_prefetch=1,
            grid=(1,),
            in_specs=[whole((factor, rows, width))] * len(value),
            out_specs=[whole((rows, width))] * factor,
        ),
        out_shape=[pltpu.HBM((rows, width), BF16)] * factor,
        compiler_params=pltpu.CompilerParams(vmem_limit_bytes=SMALL_LIMIT),
        name="add_and_split",
    )(digit[None], *[part.reshape(factor, rows, width) for part in value])
    split, given = lax.optimization_barrier((split, given))
    held = swap_all(split, strides, batch_size, [0] + list(reversed(range(1, factor))))
    done = beside(given)
    held, done = lax.optimization_barrier((held, done))
    for size, steps in rounds[1:]:
        bit = 1
        while bit < size:
            block = add_up(held)
            held = [block, swap_within(block, steps, bit, batch_size)]
            bit *= 2
    block = add_up(held)
    held = swap_all([block] * factor, strides, batch_size, range(factor))
    return last_kernel(digit, held), done


def body(
    root_state, cond_table, block_gain, w_in, w_out, value_head, reward_head, small_head,
    unroll_len, actions, codes, policy_target, value_bins, reward_bins,
):
    tower_id = lax.axis_index("tower")
    other_id = 1 - tower_id
    tower_ref = tower_id.astype(jnp.int32)[None]
    steps, batch_rows = actions.shape
    blocks, width = block_gain.shape[1:]
    bins = value_head.shape[2]
    table_rows = cond_table.shape[0]
    rows = batch_rows // 2
    half = width // 2
    parts = lax.axis_size("batch")
    s = Sizes(steps, rows, blocks, width, bins, table_rows, parts)
    calls, wide, pair = s.calls, s.wide, s.pair

    root_got = swap(root_state, "tower", 1)
    in_own, out_own, gains_own = w_in[0], w_out[0], block_gain[0]
    value_own = value_head[0].T
    in_got = swap(in_own, "tower", 1)
    out_got = swap(out_own, "tower", 1)
    gains_got = swap(gains_own, "tower", 1)
    value_got = swap(value_own, "tower", 1)
    lengths = unroll_len.reshape(1, batch_rows)

    shape = jax.ShapeDtypeStruct
    per_pair = lambda *tail: pl.BlockSpec(
        (pair,) + tail, lambda turn, tower: (turn,) + (0,) * len(tail)
    )
    unroll_params = pltpu.CompilerParams(vmem_limit_bytes=UNROLL_LIMIT)
    small_params = pltpu.CompilerParams(vmem_limit_bytes=SMALL_LIMIT)
    products = steps * rows * (4 * blocks * width * width + 9 * width * wide)
    cost = pl.CostEstimate(flops=2 * products, bytes_accessed=40 * 2**20, transcendentals=0)
    lat_own, lat_away, loss, own, away, root_own, root_away = pl.pallas_call(
        functools.partial(unroll_kernel, s),
        in_specs=[pl.BlockSpec(memory_space=pltpu.SMEM)]
        + [pl.BlockSpec(memory_space=pltpu.HBM)] * 14
        + [pl.BlockSpec(memory_space=pl.ANY)] * 4
        + [pl.BlockSpec(memory_space=pltpu.VMEM)],
        out_specs=[pl.BlockSpec(memory_space=pltpu.HBM)] * 2
        + [pl.BlockSpec(memory_space=pltpu.VMEM)] * 5,
        scratch_shapes=[
            pltpu.VMEM((steps, 2, rows, width), BF16),
            pltpu.VMEM((steps, calls, rows, width), BF16),
            pltpu.VMEM((steps, calls, rows, width), BF16),
            pltpu.VMEM((steps, calls, rows, width), BF16),
            pltpu.VMEM((steps, rows, LANES), F32),
            pltpu.VMEM((steps, 2, rows, width), BF16),
            pltpu.VMEM((2 * calls, width, width), BF16),
            pltpu.VMEM((2, 16, width), F32),
            pltpu.SemaphoreType.DMA((2,)),
            pltpu.VMEM((rows, half), BF16),
            pltpu.VMEM((rows, half), BF16),
            pltpu.VMEM((1, rows), jnp.int32),
            pltpu.VMEM((steps, rows), jnp.int32),
            pltpu.VMEM((steps, rows), jnp.int32),
            pltpu.VMEM((steps, rows), jnp.int32),
            pltpu.VMEM((steps, 2, rows), jnp.int32),
            pltpu.VMEM((steps, rows), jnp.int32),
            pltpu.VMEM((table_rows, width), BF16),
            pltpu.VMEM((blocks, width), BF16),
            pltpu.VMEM((bins, width), BF16),
            pltpu.VMEM((bins, width), BF16),
            pltpu.VMEM((bins, width), BF16),
            pltpu.VMEM((table_rows, width), BF16),
            pltpu.SemaphoreType.DMA((18,)),
            pltpu.VMEM((rows, width), BF16),
            pltpu.VMEM((pair * rows, width), BF16),
            pltpu.VMEM((pair * rows, width), BF16),
            pltpu.VMEM((LANES, width), BF16),
            pltpu.VMEM((2 * calls, width, width), BF16),
            pltpu.VMEM((s.depth[0], width), BF16),
            pltpu.VMEM((s.depth[1], width), BF16),
            pltpu.VMEM((s.stack[0], width), F32),
            pltpu.VMEM((s.stack[1], width), F32),
            pltpu.VMEM((s.depth[0], pair * rows), BF16),
            pltpu.VMEM((s.depth[1], pair * rows), BF16),
            pltpu.VMEM((s.reward_at - s.sums_at, LANES), F32),
            pltpu.VMEM((steps, s.reward_at - s.sums_at, width), F32),
            pltpu.VMEM((rows, width), F32),
            pltpu.VMEM((2, 16, width), F32),
            pltpu.VMEM((s.held, width), F32),
            pltpu.VMEM((2 * calls * width, width), F32),
            pltpu.VMEM((2, 16, width), F32),
            pltpu.VMEM((max(pair - 1, 1), calls, rows, width), BF16),
            pltpu.VMEM((max(pair - 1, 1), calls, rows, width), BF16),
            pltpu.VMEM((max(pair - 1, 1), 2, rows, width), BF16),
        ],
        out_shape=[
            pltpu.HBM((steps, rows, width), BF16),
            pltpu.HBM((steps, rows, width), BF16),
            shape((8, rows), F32),
            shape((s.total, width), BF16),
            shape((s.total, width), BF16),
            shape((rows, half), BF16),
            shape((rows, half), BF16),
        ],
        compiler_params=unroll_params,
        cost_estimate=cost,
        name="unroll",
    )(
        tower_ref,
        *[
            pltpu.with_memory_space_constraint(value, pltpu.HBM)
            for value in (
                root_state, lengths, actions, codes, policy_target,
                jnp.swapaxes(value_bins, 0, 1), reward_bins, cond_table, gains_own,
                in_own, out_own, value_own, reward_head.T, small_head.T,
            )
        ],
        root_got, in_got, out_got, value_got, gains_got,
    )
    got = swap(away, "tower", 1)

    def beside(given):
        lat_own, lat_away, loss, root_own, root_away = given
        lat_got = swap(lat_away, "tower", 1)
        loss_own = loss[0]
        loss_got = swap(loss_own, "tower", 1)
        root_got = swap(root_away, "tower", 1)

        latents, logits = pl.pallas_call(
            functools.partial(logits_kernel, s),
            grid_spec=pltpu.PrefetchScalarGridSpec(
                num_scalar_prefetch=1,
                grid=(steps // pair,),
                in_specs=[per_pair(rows, width), per_pair(rows, width), whole((bins, width))],
                out_specs=[per_pair(batch_rows, width), per_pair(bins, batch_rows)],
            ),
            out_shape=[
                shape((steps, batch_rows, width), BF16),
                shape((steps, bins, batch_rows), BF16),
            ],
            compiler_params=small_params,
            cost_estimate=pl.CostEstimate(
                flops=2 * steps * batch_rows * width * wide, bytes_accessed=6 * 2**20, transcendentals=0
            ),
            name="latents_and_logits",
        )(
            tower_ref,
            *[
                pltpu.with_memory_space_constraint(part, pltpu.HBM)
                for part in (lat_own, lat_got, value_own)
            ],
        )

        def in_order(mine_value, got_value, axis):
            return jnp.where(
                tower_id == 0,
                jnp.concatenate([mine_value, got_value], axis=axis),
                jnp.concatenate([got_value, mine_value], axis=axis),
            )

        row_loss = in_order(loss_own, loss_got, 0)
        grad_root = in_order(root_own, root_got, 0).astype(F32)
        return latents, logits, row_loss, grad_root

    rounds = exchange_rounds(parts)

    def unpack(digit, held):
        scalars = jnp.stack([digit, tower_id]).astype(jnp.int32)
        length = held[0].shape[0]
        block = s.reward_at // length
        at = s.reward_at - block * length
        parts_of = [part[at : at + s.shared_end - s.reward_at] for part in held]
        shared = parts_of[0]
        for other in range(1, len(held)):
            shared = jnp.where((digit ^ other) == block, parts_of[other], shared)
        shared_got = swap(shared, "tower", 1)
        return (shared, shared_got), pl.pallas_call(
            functools.partial(unpack_own_kernel, s),
            grid_spec=pltpu.PrefetchScalarGridSpec(
                num_scalar_prefetch=1,
                grid=(1,),
                in_specs=[whole(part.shape) for part in held],
                out_specs=[
                    whole((blocks, width, width)),
                    whole((blocks, width, width)),
                    whole((bins, 1, width)),
                    whole((blocks, 1, width)),
                    whole((blocks, 2, steps)),
                ],
                scratch_shapes=[
                    pltpu.VMEM((s.total, width), BF16),
                    pltpu.VMEM((s.reward_at - s.sums_at, LANES), F32),
                ],
            ),
            out_shape=[
                shape((blocks, width, width), F32),
                shape((blocks, width, width), F32),
                shape((bins, 1, width), F32),
                shape((blocks, 1, width), F32),
                shape((blocks, 2, steps), F32),
            ],
            compiler_params=small_params,
            name="unpack_own",
        )(scalars, *held)

    given = (lat_own, lat_away, loss, root_own, root_away)
    unpacked, done = exchange([own, got], rounds, parts, beside, given, unpack)
    (shared, shared_got), (grad_in, grad_out, value_t, gain_t, rms_t) = unpacked
    latents, logits, row_loss, grad_root = done
    reward_t, small_t, grad_cond = pl.pallas_call(
        functools.partial(unpack_shared_kernel, s),
        grid_spec=pltpu.PrefetchScalarGridSpec(
            num_scalar_prefetch=1,
            grid=(1,),
            in_specs=[whole(shared.shape), whole(shared.shape)],
            out_specs=[
                whole((bins, width)),
                whole((table_rows, width)),
                whole((table_rows, width)),
            ],
            scratch_shapes=[pltpu.VMEM((s.wide, width), F32)],
        ),
        out_shape=[
            shape((bins, width), F32),
            shape((table_rows, width), F32),
            shape((table_rows, width), F32),
        ],
        compiler_params=small_params,
        name="unpack_shared",
    )(tower_ref, shared, shared_got)
    layer_rms = jnp.transpose(rms_t, (2, 0, 1))[None]
    return (
        latents[None],
        jnp.swapaxes(logits, 1, 2)[None],
        row_loss,
        layer_rms,
        grad_root,
        grad_cond,
        jnp.swapaxes(gain_t, 0, 1),
        grad_in[None],
        grad_out[None],
        jnp.transpose(value_t, (1, 2, 0)),
        reward_t.T,
        small_t.T,
    )


def solution(mesh):
    placed = (
        P("batch", "tower"),
        P(),
        P("tower", None, None),
        P("tower", None, None, None),
        P("tower", None, None, None),
        P("tower", None, None),
        P(),
        P(),
        P("batch"),
        P(None, "batch"),
        P(None, "batch"),
        P(None, "batch"),
        P(None, None, "batch"),
        P(None, "batch"),
    )
    return jax.shard_map(
        body,
        mesh=mesh,
        in_specs=placed,
        out_specs=(
            P("tower", None, "batch", None),
            P("tower", None, "batch", None),
            P("batch"),
            P("tower", None, None, None),
            P("batch", "tower"),
            P(),
            P("tower", None, None),
            P("tower", None, None, None),
            P("tower", None, None, None),
            P("tower", None, None),
            P(),
            P(),
        ),
        check_vma=False,
    )
```
